32 devices in a mesh: dp: 16 (over z, y, core), tensor: 2 (over x).
Axes of the slice: x: 2, y: 2, z: 4, core: 2. Of those that a mesh axis runs over, the one named last changes fastest.
Arguments:
- tokens: bfloat16 [4096, 2048], P(('dp', 'tensor')), may hold values from -6 to 6
- attention_gain: bfloat16 [2048], P(('dp', 'tensor')), may hold values from 0.5 to 1.5
- expert_norm_gain: bfloat16 [2048], P(('dp', 'tensor')), may hold values from 0.5 to 1.5
- query_projection: bfloat16 [2048, 2048], P('dp', 'tensor'), may hold values from -0.125 to 0.125
- key_projection: bfloat16 [2048, 512], P('dp', 'tensor'), may hold values from -0.125 to 0.125
- value_projection: bfloat16 [2048, 512], P('dp', 'tensor'), may hold values from -0.125 to 0.125
- output_projection: bfloat16 [2048, 2048], P('tensor', 'dp'), may hold values from -0.5 to 0.5
- router: bfloat16 [2048, 16], P(('dp', 'tensor')), may hold values from -0.0625 to 0.0625
- shared_gate_matrix: bfloat16 [2048, 2816], P('dp', 'tensor'), may hold values from -0.125 to 0.125
- shared_up_matrix: bfloat16 [2048, 2816], P('dp', 'tensor'), may hold values from -0.125 to 0.125
- shared_down_matrix: bfloat16 [2816, 2048], P('tensor', 'dp'), may hold values from -0.109375 to 0.109375
- expert_gate_matrix: bfloat16 [16, 2048, 1408], P('dp', None, 'tensor'), may hold values from -0.125 to 0.125
- expert_up_matrix: bfloat16 [16, 2048, 1408], P('dp', None, 'tensor'), may hold values from -0.125 to 0.125
- expert_down_matrix: bfloat16 [16, 1408, 2048], P('dp', 'tensor'), may hold values from -0.15625 to 0.15625
- document_lengths: int32 [16, 4], P('dp'), may hold values from 1 to 160, 256 in all within a row
- expert_indices: int32 [4096, 6], P('dp'), may hold values from 0 to 15, all different within a row; in each aligned block of 256 rows (0 to 255, 256 to 511, ...) at most 128 rows name the same one
- cotangent: bfloat16 [4096, 2048], P(('dp', 'tensor')), may hold values from -6 to 6
Outputs:
- output: bfloat16 [4096, 2048], P(('dp', 'tensor'))
- grad_tokens: float32 [4096, 2048], P(('dp', 'tensor'))
- grad_gain_attn: float32 [2048], P(('dp', 'tensor'))
- grad_gain_ffn: float32 [2048], P(('dp', 'tensor'))
- grad_w_query: float32 [2048, 2048], P('dp', 'tensor')
- grad_w_key: float32 [2048, 512], P('dp', 'tensor')
- grad_w_value: float32 [2048, 512], P('dp', 'tensor')
- grad_w_out: float32 [2048, 2048], P('tensor', 'dp')
- grad_router: float32 [2048, 16], P(('dp', 'tensor'))
- grad_w_sgate: float32 [2048, 2816], P('dp', 'tensor')
- grad_w_sup: float32 [2048, 2816], P('dp', 'tensor')
- grad_w_sdown: float32 [2816, 2048], P('tensor', 'dp')
- grad_w_egate: float32 [16, 2048, 1408], P('dp', None, 'tensor')
- grad_w_eup: float32 [16, 2048, 1408], P('dp', None, 'tensor')
- grad_w_edown: float32 [16, 1408, 2048], P('dp', 'tensor')
The draws below stay inside these ranges and needn't reach their ends.
Inputs may be any that keep to these rules, and one draw needn't show every extreme that they name: `expert_indices`: each row names 6 different experts; in each aligned block of 256 rows (one sequence) no expert is named by more than 128 rows. `document_lengths`: each row sums to 256.
All inputs are finite; a program needn't handle non-finite values.
Results may differ from the reference program's by a relative error of at most 0.017.
Values may be sent and summed in bfloat16 or wider, within the bound.
A program may use at most 256 MiB of HBM per device.

```python
import math
import jax
import jax.numpy as jnp
import numpy as np
from jax import lax

MODEL_WIDTH = 2048
QUERY_HEADS = 16
KEY_VALUE_HEADS = 4
HEAD_SIZE = 128
EXPERT_HIDDEN = 1408
SH = 2816
TOP = 6
ROUTED_EXPERTS = 16
SEQ = 256
DOCS = 4
EXPERT_ROW_LIMIT = 128
TOKENS = 4096
N_DP = 16
N_TENSOR = 2


def block_levels(key, extent, shards, least, largest):
    def one(position, parts):
        steps = jax.random.uniform(jax.random.fold_in(jax.random.fold_in(key, 6), position), (parts,), jnp.float32, least / len(shards), largest / len(shards))
        return jnp.repeat(jnp.exp(steps), extent[position] // parts).reshape((-1,) + (1,) * (len(extent) - position - 1))

    loudness = one(*shards[0])
    for cut in shards[1:]:
        loudness = loudness * one(*cut)
    return loudness


def length_profile(number_of, total, reach, skew):
    portions = [(1 << 20) // math.isqrt(standing ** skew) + 1 for standing in range(2, number_of + 1)]
    surplus, given = total - reach - (number_of - 1), [1] * (number_of - 1)
    while surplus > 0:
        candidates = [i for i in range(number_of - 1) if given[i] < reach]
        mass, remaining = sum([portions[i] for i in candidates]), surplus
        for i in candidates:
            extra = min(reach - given[i], max(1, remaining * portions[i] // mass), surplus)
            given[i] = given[i] + extra
            surplus = surplus - extra
    return np.array([reach] + given)


def uneven_parts(stream_key, amount, total, reach, lean):
    if amount == 2:
        one = jax.random.randint(stream_key, (), max(1, total - reach), min(reach, total - 1) + 1)
        return jnp.stack([one, total - one])
    sizes = jnp.asarray(length_profile(amount, total, reach, lean), jnp.int32)
    twos = (amount - 1) // 2
    donor, taker = sizes[1:1 + 2 * twos:2], sizes[2:2 + 2 * twos:2]
    margin = jnp.minimum(donor - 1, reach - taker)
    moved = jax.random.randint(jax.random.fold_in(stream_key, 1), (twos,), 0, 1 << 20) % (margin + 1)
    sizes = sizes.at[1:1 + 2 * twos:2].set(donor - moved).at[2:2 + 2 * twos:2].set(taker + moved)
    return sizes[jax.random.permutation(jax.random.fold_in(stream_key, 2), amount)]


def assign_block(stream_key, own, number, rows, number_of, top, limit, slope):
    order = jax.random.permutation(stream_key, number_of)
    packed, common = portions_of(number_of, rows * top, limit, slope, True), portions_of(number_of, rows * top, limit, slope, False)
    places = jnp.arange(number_of)

    def named(lengths, offset_by):
        used = int((lengths > 0).sum())
        fixed = max(1, used // 4)
        moved = fixed + (places - fixed + offset_by * (used - fixed)) % max(1, number_of - fixed)
        return jnp.zeros((number_of,), jnp.int32).at[order[jnp.where(places < fixed, places, moved)]].set(jnp.asarray(lengths, jnp.int32))

    lengths = jnp.where(number % 4 == 0, named(packed, number // 4), named(common, number - number // 4 - 1))
    mixed = jax.random.permutation(jax.random.fold_in(own, 3), number_of)
    donor, taker = mixed[0:number_of // 2 * 2:2], mixed[1:number_of // 2 * 2:2]
    margin = jnp.minimum(lengths[donor] - 1, limit - lengths[taker]) // 2
    margin = jnp.where((donor == order[0]) | (taker == order[0]) | (lengths[taker] == 0), 0, jnp.maximum(margin, 0))
    moved = jax.random.randint(jax.random.fold_in(own, 4), (number_of // 2,), 0, 1 << 20) % (margin + 1)
    lengths = lengths.at[donor].add(-moved).at[taker].add(moved)
    items = jnp.searchsorted(jnp.cumsum(lengths), jnp.arange(rows * top), side="right").astype(jnp.int32)
    table = items.reshape(top, rows).T
    table = table[jax.random.permutation(jax.random.fold_in(own, 1), rows)]
    offset_by = jax.random.randint(jax.random.fold_in(own, 2), (rows, 1), 0, top)
    return jnp.take_along_axis(table, (jnp.arange(top)[None, :] + offset_by) % top, axis=1)


def portions_of(count, total, bound, slope, full):
    loads = [(1 << 20) // math.isqrt(rank ** slope) + 1 for rank in range(1, count + 1)]
    largest = bound if full else min(bound, max(-(-total // count), total * loads[0] // sum(loads)))
    least = 1 if total - largest >= count - 1 else 0
    counts, surplus = [largest] + [least] * (count - 1), total - largest - least * (count - 1)
    while surplus > 0:
        candidates = [i for i in range(1, count) if counts[i] < largest] or [i for i in range(1, count) if counts[i] < bound]
        mass, left = sum([loads[i] for i in candidates]), surplus
        for i in candidates:
            more = min(bound - counts[i], max(1, left * loads[i] // mass), surplus)
            counts[i] = counts[i] + more
            surplus = surplus - more
    return np.array(counts)


def scatter_about(stream_key, dims, spread, limit, split=(), kind=jnp.bfloat16):
    values = jax.random.normal(stream_key, dims, jnp.float32) * spread
    if len(split) > 0:
        values = block_levels(stream_key, dims, split, -0.22, 0.18) * values
    return jnp.clip(values, min=-limit, max=limit).astype(kind)


def setup_inputs(seed: int = 0) -> dict:
    key_list = jax.random.split(jax.random.key(seed), 18)
    tokens = scatter_about(key_list[0], (TOKENS, MODEL_WIDTH), 1.0, 6.0, ((0, 32),))
    attention_gain = jnp.clip(1.0 + 0.1 * jax.random.normal(key_list[1], (MODEL_WIDTH,), jnp.float32), 0.5, 1.5).astype(jnp.bfloat16)
    expert_norm_gain = jnp.clip(1.0 + 0.1 * jax.random.normal(key_list[2], (MODEL_WIDTH,), jnp.float32), 0.5, 1.5).astype(jnp.bfloat16)
    query_projection = scatter_about(key_list[3], (MODEL_WIDTH, QUERY_HEADS * HEAD_SIZE), MODEL_WIDTH ** -0.5, 0.125, ((0, 16), (1, 2)))
    key_projection = scatter_about(key_list[4], (MODEL_WIDTH, KEY_VALUE_HEADS * HEAD_SIZE), MODEL_WIDTH ** -0.5, 0.125, ((0, 16), (1, 2)))
    value_projection = scatter_about(key_list[5], (MODEL_WIDTH, KEY_VALUE_HEADS * HEAD_SIZE), MODEL_WIDTH ** -0.5, 0.125, ((0, 16), (1, 2)))
    output_projection = scatter_about(key_list[6], (QUERY_HEADS * HEAD_SIZE, MODEL_WIDTH), (QUERY_HEADS * HEAD_SIZE // 16) ** -0.5, 0.5, ((0, 2), (1, 16)))
    router = scatter_about(key_list[7], (MODEL_WIDTH, ROUTED_EXPERTS), (4 * MODEL_WIDTH) ** -0.5, 0.0625, ((0, 32),))
    shared_gate_matrix = scatter_about(key_list[8], (MODEL_WIDTH, SH), MODEL_WIDTH ** -0.5, 0.125, ((0, 16), (1, 2)))
    shared_up_matrix = scatter_about(key_list[9], (MODEL_WIDTH, SH), MODEL_WIDTH ** -0.5, 0.125, ((0, 16), (1, 2)))
    shared_down_matrix = scatter_about(key_list[10], (SH, MODEL_WIDTH), SH ** -0.5, 0.109375, ((0, 2), (1, 16)))
    expert_gate_matrix = scatter_about(key_list[11], (ROUTED_EXPERTS, MODEL_WIDTH, EXPERT_HIDDEN), MODEL_WIDTH ** -0.5, 0.125, ((0, 16), (2, 2)))
    expert_up_matrix = scatter_about(key_list[12], (ROUTED_EXPERTS, MODEL_WIDTH, EXPERT_HIDDEN), MODEL_WIDTH ** -0.5, 0.125, ((0, 16), (2, 2)))
    expert_down_matrix = scatter_about(key_list[13], (ROUTED_EXPERTS, EXPERT_HIDDEN, MODEL_WIDTH), EXPERT_HIDDEN ** -0.5, 0.15625, ((0, 16), (1, 2)))
    document_lengths = jax.vmap(lambda own: uneven_parts(own, DOCS, SEQ, 5 * SEQ // 8, 1))(jax.random.split(key_list[14], N_DP)).reshape((N_DP, DOCS)).astype(jnp.int32)
    expert_indices_keys = jax.random.split(jax.random.fold_in(key_list[15], 1), TOKENS // SEQ)
    expert_indices_turns = jax.random.permutation(jax.random.fold_in(key_list[15], 3), TOKENS // SEQ)
    expert_indices = jax.vmap(lambda own, number: assign_block(jax.random.fold_in(key_list[15], 2), own, number, SEQ, ROUTED_EXPERTS, TOP, EXPERT_ROW_LIMIT, 1))(expert_indices_keys, expert_indices_turns).reshape((TOKENS, TOP))
    cotangent = scatter_about(key_list[16], (TOKENS, MODEL_WIDTH), 1.0, 6.0, ((0, 32),))
    return {"tokens": tokens, "attention_gain": attention_gain, "expert_norm_gain": expert_norm_gain, "query_projection": query_projection, "key_projection": key_projection, "value_projection": value_projection, "output_projection": output_projection, "router": router, "shared_gate_matrix": shared_gate_matrix, "shared_up_matrix": shared_up_matrix, "shared_down_matrix": shared_down_matrix, "expert_gate_matrix": expert_gate_matrix, "expert_up_matrix": expert_up_matrix, "expert_down_matrix": expert_down_matrix, "document_lengths": document_lengths, "expert_indices": expert_indices, "cotangent": cotangent}


@jax.custom_vjp
def reduced_precision(v):
    return lax.optimization_barrier(v.astype(jnp.bfloat16)).astype(jnp.float32)

@jax.custom_vjp
def reduced_precision_backward(v):
    return v

def low_keep(v):
    return (reduced_precision(v), None)

def low_pass(kept, grad):
    return (grad,)

def back_keep(v):
    return (v, None)

def back_low(kept, grad):
    return (reduced_precision(grad),)
reduced_precision.defvjp(low_keep, low_pass)
reduced_precision_backward.defvjp(back_keep, back_low)
norm_eps = 1e-06
rope_base = 600000.0
neg_big = -1e+30
highest = lax.Precision.HIGHEST

def matrix_product(left, right):
    return jnp.dot(left, right, precision=highest)

def silu(argument):
    return argument * jax.nn.sigmoid(argument)

def rotation(sequence_length, head_dim):
    half_dim = head_dim // 2
    frequency = jnp.exp(jnp.arange(half_dim, dtype=jnp.float32) * (-2.0 * math.log(rope_base) / head_dim))
    angles = jnp.arange(sequence_length, dtype=jnp.float32)[:, None] * frequency[None, :]
    return (jnp.cos(angles), jnp.sin(angles))

def apply_rotary(tensor, rotary_cosine, rotary_sine):
    half_dim = tensor.shape[-1] // 2
    first_half = tensor[..., :half_dim]
    second_half = tensor[..., half_dim:]
    cos_rows = rotary_cosine[:, None, :]
    sin_rows = rotary_sine[:, None, :]
    return jnp.concatenate([first_half * cos_rows - second_half * sin_rows, second_half * cos_rows + first_half * sin_rows], axis=-1)

def attend(normalized, doc_ids, query_matrix, key_matrix, value_matrix, output_matrix, rotary_cosine, rotary_sine):
    sequence_length = normalized.shape[0]
    query_unrotated = reduced_precision_backward(matrix_product(normalized, query_matrix)).reshape(sequence_length, QUERY_HEADS, HEAD_SIZE)
    key_unrotated = reduced_precision_backward(matrix_product(normalized, key_matrix)).reshape(sequence_length, KEY_VALUE_HEADS, HEAD_SIZE)
    rows_of_query = reduced_precision(apply_rotary(query_unrotated, rotary_cosine, rotary_sine)).reshape(sequence_length, KEY_VALUE_HEADS, QUERY_HEADS // KEY_VALUE_HEADS, HEAD_SIZE)
    key_rows = reduced_precision(apply_rotary(key_unrotated, rotary_cosine, rotary_sine))
    rows_of_value = reduced_precision(reduced_precision_backward(matrix_product(normalized, value_matrix))).reshape(sequence_length, KEY_VALUE_HEADS, HEAD_SIZE)
    scores = reduced_precision_backward(jnp.einsum('qkgd,skd->kgqs', rows_of_query, key_rows, precision=highest) * HEAD_SIZE ** (-0.5))
    positions = jnp.arange(sequence_length, dtype=jnp.int32)
    allowed = (doc_ids[:, None] == doc_ids[None, :]) & (positions[:, None] >= positions[None, :])
    scores = jnp.where(allowed, scores, neg_big)
    row_max = lax.optimization_barrier(jnp.max(scores, axis=-1, keepdims=True))
    exp_scores = jnp.exp(scores - row_max)
    attn_probs = exp_scores / lax.optimization_barrier(jnp.sum(exp_scores, axis=-1, keepdims=True))
    mixed_heads = jnp.einsum('kgqs,skd->qkgd', reduced_precision(attn_probs), rows_of_value, precision=highest)
    mixed_heads = reduced_precision(reduced_precision_backward(mixed_heads.reshape(sequence_length, QUERY_HEADS * HEAD_SIZE)))
    return reduced_precision_backward(matrix_product(mixed_heads, output_matrix))

def rows_per_expert(normalized, expert_gate_weight, expert_up_weight, expert_down_weight, rows_of_token, filled_slots):
    gathered_rows = normalized[rows_of_token] * filled_slots[:, None]
    partition_width = EXPERT_HIDDEN // N_TENSOR
    result = jnp.zeros((gathered_rows.shape[0], MODEL_WIDTH), jnp.float32)
    for part_index in range(N_TENSOR):
        starting_column = part_index * partition_width
        dispatched_rows = reduced_precision_backward(gathered_rows)
        gate_preactivation = reduced_precision_backward(matrix_product(dispatched_rows, expert_gate_weight[:, starting_column:starting_column + partition_width]))
        up_preactivation = reduced_precision_backward(matrix_product(dispatched_rows, expert_up_weight[:, starting_column:starting_column + partition_width]))
        hidden = reduced_precision(silu(gate_preactivation) * up_preactivation)
        result = result + reduced_precision(reduced_precision_backward(matrix_product(hidden, expert_down_weight[starting_column:starting_column + partition_width])))
    return result

def slot_tables(expert_indices):
    flat_ids = expert_indices.reshape(N_DP, SEQ * TOP)
    onehot = (flat_ids[:, :, None] == jnp.arange(ROUTED_EXPERTS, dtype=jnp.int32)[None, None, :]).astype(jnp.int32)
    slot_rank = lax.optimization_barrier(jnp.sum(onehot * (jnp.cumsum(onehot, axis=1) - 1), axis=-1))
    source_index = jnp.arange(N_DP, dtype=jnp.int32)[:, None]
    slot_index = (flat_ids * (N_DP * EXPERT_ROW_LIMIT) + source_index * EXPERT_ROW_LIMIT + slot_rank).reshape(-1)
    pair_index = jnp.arange(N_DP * SEQ * TOP, dtype=jnp.int32)
    row_total = ROUTED_EXPERTS * N_DP * EXPERT_ROW_LIMIT
    rows_of_token = jnp.zeros((row_total,), jnp.int32).at[slot_index].set(pair_index // TOP)
    assign_rows = jnp.zeros((row_total,), jnp.int32).at[slot_index].set(pair_index)
    filled_slots = jnp.zeros((row_total,), jnp.float32).at[slot_index].set(1.0)
    return (rows_of_token, assign_rows, filled_slots)

def reference(tokens, attention_gain, expert_norm_gain, query_projection, key_projection, value_projection, output_projection, router, shared_gate_matrix, shared_up_matrix, shared_down_matrix, expert_gate_matrix, expert_up_matrix, expert_down_matrix, document_lengths, expert_indices, cotangent):
    rows_of_token, assign_rows, filled_slots = slot_tables(expert_indices)
    doc_ends = jnp.cumsum(document_lengths, axis=1)
    positions = jnp.arange(SEQ, dtype=jnp.int32)
    doc_ids = lax.optimization_barrier(jnp.sum((positions[None, :, None] >= doc_ends[:, None, :]).astype(jnp.int32), axis=-1))
    rotary_cosine, rotary_sine = rotation(SEQ, HEAD_SIZE)
    chosen = expert_indices[:, :, None] == jnp.arange(ROUTED_EXPERTS, dtype=jnp.int32)[None, None, :]
    float_values = tuple((make_array.astype(jnp.float32) for make_array in (tokens, attention_gain, expert_norm_gain, query_projection, key_projection, value_projection, output_projection, router, shared_gate_matrix, shared_up_matrix, shared_down_matrix, expert_gate_matrix, expert_up_matrix, expert_down_matrix)))

    def forward_pass(input_values, first_gain, second_gain, query_matrix, key_matrix, value_matrix, output_matrix, router_matrix, shared_gate_weight, shared_up_weight, shared_down_weight, expert_gate_weight, expert_up_weight, expert_down_weight):
        scale_one = lax.rsqrt(lax.optimization_barrier(jnp.mean(input_values * input_values, axis=-1, keepdims=True)) + norm_eps)
        normed_one = reduced_precision(input_values * scale_one * first_gain)

        def attend_one(pieces):
            return attend(pieces[0], pieces[1], query_matrix, key_matrix, value_matrix, output_matrix, rotary_cosine, rotary_sine)
        attn_out = lax.map(jax.checkpoint(attend_one), (normed_one.reshape(N_DP, SEQ, MODEL_WIDTH), doc_ids)).reshape(TOKENS, MODEL_WIDTH)
        residual = input_values + attn_out
        scale_two = lax.rsqrt(lax.optimization_barrier(jnp.mean(residual * residual, axis=-1, keepdims=True)) + norm_eps)
        normed_two = reduced_precision(residual * scale_two * second_gain)
        logits = reduced_precision_backward(matrix_product(normed_two, router_matrix))
        selected = lax.optimization_barrier(jnp.sum(jnp.where(chosen, logits[:, None, :], 0.0), axis=-1))
        top_max = lax.optimization_barrier(jnp.max(selected, axis=-1, keepdims=True))
        gate_exp = jnp.exp(selected - top_max)
        gate_probs = gate_exp / lax.optimization_barrier(jnp.sum(gate_exp, axis=-1, keepdims=True))
        gate_shared = reduced_precision_backward(matrix_product(normed_two, shared_gate_weight))
        up_shared = reduced_precision_backward(matrix_product(normed_two, shared_up_weight))
        hidden_shared = reduced_precision(silu(gate_shared) * up_shared)
        shared_out = matrix_product(hidden_shared, shared_down_weight)

        def single_expert(pieces):
            return rows_per_expert(normed_two, pieces[0], pieces[1], pieces[2], pieces[3], pieces[4])
        expert_output = lax.map(jax.checkpoint(single_expert), (expert_gate_weight, expert_up_weight, expert_down_weight, rows_of_token.reshape(ROUTED_EXPERTS, N_DP * EXPERT_ROW_LIMIT), filled_slots.reshape(ROUTED_EXPERTS, N_DP * EXPERT_ROW_LIMIT)))
        gate_slots = gate_probs.reshape(-1)[assign_rows] * filled_slots
        routed = jnp.zeros((TOKENS, MODEL_WIDTH), jnp.float32).at[rows_of_token].add(gate_slots[:, None] * expert_output.reshape(-1, MODEL_WIDTH))
        ffn_out = reduced_precision_backward(shared_out + routed)
        return residual + ffn_out
    output, pullback = jax.vjp(forward_pass, *float_values)
    gradients = pullback(cotangent.astype(jnp.float32))
    return (output.astype(jnp.bfloat16), gradients[0], gradients[1], gradients[2], gradients[3], gradients[4], gradients[5], gradients[6], gradients[7], gradients[8], gradients[9], gradients[10], gradients[11], gradients[12], gradients[13])
```

```python
import functools
import math

import jax
import jax.numpy as jnp
from jax import lax
from jax.experimental import pallas as pl
from jax.experimental.pallas import tpu as pltpu
from jax.sharding import PartitionSpec as P

HEAD_SIZE = 128
DP, TENSOR = ("dp", "tensor")


norm_eps = 1e-06
rope_base = 600000.0
neg_big = -1e30


def silu(argument):
    return argument * jax.nn.sigmoid(argument)


def silu_slope(argument):
    sigmoid_of = jax.nn.sigmoid(argument)
    return sigmoid_of * (1.0 + argument * (1.0 - sigmoid_of))


def rotation(sequence_length, head_dim):
    half_dim = head_dim // 2
    frequency = jnp.exp(
        jnp.arange(half_dim, dtype=jnp.float32) * (-2.0 * math.log(rope_base) / head_dim)
    )
    angles = jnp.arange(sequence_length, dtype=jnp.float32)[:, None] * frequency[None, :]
    return (jnp.cos(angles), jnp.sin(angles))


def apply_rotary(tensor, rotary_cosine, rotary_sine):
    half_dim = tensor.shape[-1] // 2
    first_half = tensor[..., :half_dim]
    second_half = tensor[..., half_dim:]
    cos_rows = rotary_cosine[:, None, :]
    sin_rows = rotary_sine[:, None, :]
    return jnp.concatenate(
        [
            first_half * cos_rows - second_half * sin_rows,
            second_half * cos_rows + first_half * sin_rows,
        ],
        axis=-1,
    )


def rotate_back(tensor, rotary_cosine, rotary_sine):
    return apply_rotary(tensor, rotary_cosine, -rotary_sine)


def rms_back(grad_normed, source, scale_rows, gain_full):
    weighted = grad_normed * gain_full
    cubed = scale_rows * scale_rows * scale_rows
    grad_source = scale_rows * weighted - source * cubed * jnp.mean(
        source * weighted, axis=-1, keepdims=True
    )
    grad_gain = jnp.sum(grad_normed * source * scale_rows, axis=0)
    return (grad_source, grad_gain)


def widen(sharded):
    return lax.all_gather(sharded, TENSOR, axis=0, tiled=True)


def narrow(partial_sum):
    return lax.psum_scatter(partial_sum, TENSOR, scatter_dimension=0, tiled=True)


def dense_fetch(
    query_projection,
    key_projection,
    value_projection,
    output_projection,
    shared_gate_matrix,
    shared_up_matrix,
    shared_down_matrix,
):
    return (
        lax.all_gather(query_projection, DP, axis=0, tiled=True),
        lax.all_gather(key_projection, DP, axis=0, tiled=True),
        lax.all_gather(value_projection, DP, axis=0, tiled=True),
        lax.all_gather(output_projection, DP, axis=1, tiled=True),
        lax.all_gather(shared_gate_matrix, DP, axis=0, tiled=True),
        lax.all_gather(shared_up_matrix, DP, axis=0, tiled=True),
        lax.all_gather(shared_down_matrix, DP, axis=1, tiled=True),
    )


def expert_up_output(received_rows, expert_gate_matrix, expert_up_matrix, expert_down_matrix):
    gate_preactivation = jnp.einsum(
        "miwy,iyh->miwh", received_rows, expert_gate_matrix, preferred_element_type=jnp.float32
    )
    up_preactivation = jnp.einsum(
        "miwy,iyh->miwh", received_rows, expert_up_matrix, preferred_element_type=jnp.float32
    )
    hidden = (silu(gate_preactivation) * up_preactivation).astype(jnp.bfloat16)
    produced_rows = jnp.einsum(
        "sxcf,xfd->sxcd", hidden, expert_down_matrix, preferred_element_type=jnp.float32
    ).astype(jnp.bfloat16)
    return (produced_rows, gate_preactivation, up_preactivation)


def expert_gradients(
    received,
    received_gradient,
    gate_preactivation,
    up_preactivation,
    expert_gate_matrix,
    expert_up_matrix,
    expert_down_matrix,
):
    hidden_expert = (silu(gate_preactivation) * up_preactivation).astype(jnp.bfloat16)
    expert_down_gradient = jnp.einsum(
        "sxcf,sxcd->xfd", hidden_expert, received_gradient, preferred_element_type=jnp.float32
    )
    grad_hidden_e = jnp.einsum(
        "sxcd,xfd->sxcf", received_gradient, expert_down_matrix, preferred_element_type=jnp.float32
    )
    grad_gate_e = (grad_hidden_e * up_preactivation * silu_slope(gate_preactivation)).astype(
        jnp.bfloat16
    )
    expert_up_hidden_gradient = (grad_hidden_e * silu(gate_preactivation)).astype(jnp.bfloat16)
    expert_gate_gradient = jnp.einsum(
        "gayi,gayr->air", received, grad_gate_e, preferred_element_type=jnp.float32
    )
    expert_up_gradient = jnp.einsum(
        "gayi,gayr->air", received, expert_up_hidden_gradient, preferred_element_type=jnp.float32
    )
    output_rows_gradient = (
        jnp.einsum(
            "zkjh,klh->zkjl", grad_gate_e, expert_gate_matrix, preferred_element_type=jnp.float32
        )
        + jnp.einsum(
            "zkjh,klh->zkjl",
            expert_up_hidden_gradient,
            expert_up_matrix,
            preferred_element_type=jnp.float32,
        )
    ).astype(jnp.bfloat16)
    return (expert_gate_gradient, expert_up_gradient, expert_down_gradient, output_rows_gradient)


def exchange_plan(
    tokens,
    attention_gain,
    expert_norm_gain,
    query_projection,
    key_projection,
    value_projection,
    output_projection,
    router,
    shared_gate_matrix,
    shared_up_matrix,
    shared_down_matrix,
    expert_gate_matrix,
    expert_up_matrix,
    expert_down_matrix,
    document_lengths,
    expert_indices,
    cotangent,
):
    n_tensor = lax.axis_size(TENSOR)
    n_dp = lax.axis_size(DP)
    tensor_pos = lax.axis_index(TENSOR)
    own_rows = tokens.shape[0]
    sequence_length = own_rows * n_tensor
    model_dim = tokens.shape[1]
    exp_dev = expert_gate_matrix.shape[0]
    experts = exp_dev * n_dp
    top_k = expert_indices.shape[1]
    capacity = max(2, sequence_length * top_k * 4 // (3 * experts))
    slot_total = experts * capacity
    router_full, gain_first, gain_second = (
        lax.all_gather(router, (DP, TENSOR), axis=0, tiled=True),
        lax.all_gather(attention_gain, (DP, TENSOR), axis=0, tiled=True),
        lax.all_gather(expert_norm_gain, (DP, TENSOR), axis=0, tiled=True),
    )
    first_gain = gain_first.astype(jnp.float32)
    second_gain = gain_second.astype(jnp.float32)
    fetched = dense_fetch(
        query_projection,
        key_projection,
        value_projection,
        output_projection,
        shared_gate_matrix,
        shared_up_matrix,
        shared_down_matrix,
    )
    query_all, key_all, value_all, out_all, sgate_all, sup_all, sdown_all = fetched
    input_values = tokens.astype(jnp.float32)
    scale_one = lax.rsqrt(jnp.mean(input_values * input_values, axis=-1, keepdims=True) + norm_eps)
    normed_one = (input_values * scale_one * first_gain).astype(jnp.bfloat16)
    full_one = widen(normed_one)
    q_heads = query_all.shape[1] // HEAD_SIZE
    kv_heads = key_all.shape[1] // HEAD_SIZE
    group_size = q_heads // kv_heads
    rotary_cosine, rotary_sine = rotation(sequence_length, HEAD_SIZE)
    query_unrotated = jnp.dot(full_one, query_all, preferred_element_type=jnp.float32).reshape(
        sequence_length, q_heads, HEAD_SIZE
    )
    key_unrotated = jnp.dot(full_one, key_all, preferred_element_type=jnp.float32).reshape(
        sequence_length, kv_heads, HEAD_SIZE
    )
    rows_of_query = (
        apply_rotary(query_unrotated, rotary_cosine, rotary_sine)
        .astype(jnp.bfloat16)
        .reshape(sequence_length, kv_heads, group_size, HEAD_SIZE)
    )
    key_rows = apply_rotary(key_unrotated, rotary_cosine, rotary_sine).astype(jnp.bfloat16)
    rows_of_value = (
        jnp.dot(full_one, value_all, preferred_element_type=jnp.float32)
        .astype(jnp.bfloat16)
        .reshape(sequence_length, kv_heads, HEAD_SIZE)
    )
    doc_ends = jnp.cumsum(document_lengths[0])
    positions = jnp.arange(sequence_length, dtype=jnp.int32)
    doc_ids = jnp.sum((positions[:, None] >= doc_ends[None, :]).astype(jnp.int32), axis=-1)
    score_scale = HEAD_SIZE ** (-0.5)

    def block_scores(start_row, end_row):
        scores = (
            jnp.einsum(
                "qkgd,skd->kgqs", rows_of_query, key_rows, preferred_element_type=jnp.float32
            )
            * score_scale
        )
        allowed = (doc_ids[start_row:end_row, None] == doc_ids[None, :end_row]) & (
            positions[start_row:end_row, None] >= positions[None, :end_row]
        )
        return (scores, allowed)

    block_index = 0
    start_row = block_index * sequence_length
    end_row = start_row + sequence_length
    scores, allowed = block_scores(start_row, end_row)
    scores = jnp.where(allowed, scores, neg_big)
    row_max = jnp.max(scores, axis=-1, keepdims=True)
    exp_scores = jnp.exp(scores - row_max)
    row_sum = jnp.sum(exp_scores, axis=-1, keepdims=True)
    lse_blocks = [row_max + jnp.log(row_sum)]
    attn_probs = (exp_scores / row_sum).astype(jnp.bfloat16)
    out_blocks = jnp.einsum(
        "kgqs,skd->qkgd", attn_probs, rows_of_value, preferred_element_type=jnp.float32
    )
    mixed_heads = out_blocks.reshape(sequence_length, q_heads * HEAD_SIZE).astype(jnp.bfloat16)
    attn_part = jnp.dot(mixed_heads, out_all, preferred_element_type=jnp.float32)
    residual = input_values + narrow(attn_part)
    scale_two = lax.rsqrt(jnp.mean(residual * residual, axis=-1, keepdims=True) + norm_eps)
    normed_two = (residual * scale_two * second_gain).astype(jnp.bfloat16)
    full_two = widen(normed_two)
    logits = jnp.dot(full_two, router_full, preferred_element_type=jnp.float32)
    chosen = expert_indices[:, :, None] == jnp.arange(experts, dtype=jnp.int32)[None, None, :]
    selected = jnp.sum(jnp.where(chosen, logits[:, None, :], 0.0), axis=-1)
    top_max = jnp.max(selected, axis=-1, keepdims=True)
    gate_exp = jnp.exp(selected - top_max)
    gate_probs = gate_exp / jnp.sum(gate_exp, axis=-1, keepdims=True)
    gate_shared = jnp.dot(full_two, sgate_all, preferred_element_type=jnp.float32)
    up_shared = jnp.dot(full_two, sup_all, preferred_element_type=jnp.float32)
    hidden_shared = (silu(gate_shared) * up_shared).astype(jnp.bfloat16)
    shared_part = jnp.dot(hidden_shared, sdown_all, preferred_element_type=jnp.float32)
    flat_ids = expert_indices.reshape(-1)
    onehot = (flat_ids[:, None] == jnp.arange(experts, dtype=jnp.int32)[None, :]).astype(jnp.int32)
    slot_rank = jnp.sum(onehot * (jnp.cumsum(onehot, axis=0) - 1), axis=-1)
    slot_index = flat_ids * capacity + slot_rank
    pair_index = jnp.arange(sequence_length * top_k, dtype=jnp.int32)
    token_of_slot = jnp.zeros((slot_total,), jnp.int32).at[slot_index].set(pair_index // top_k)
    slot_used = jnp.zeros((slot_total,), jnp.bool_).at[slot_index].set(True)
    gate_of_slot = jnp.zeros((slot_total,), jnp.float32).at[slot_index].set(gate_probs.reshape(-1))
    outgoing = jnp.where(slot_used[:, None], full_two[token_of_slot], 0).reshape(
        n_dp, exp_dev, capacity, model_dim
    )
    received_rows = lax.all_to_all(outgoing, DP, split_axis=0, concat_axis=0, tiled=True)
    produced_rows, gate_preactivation, up_preactivation = expert_up_output(
        received_rows, expert_gate_matrix, expert_up_matrix, expert_down_matrix
    )
    sent_home = lax.all_to_all(produced_rows, DP, split_axis=0, concat_axis=0, tiled=True)
    returned, received, gate_preactivation, up_preactivation = (
        sent_home,
        received_rows,
        gate_preactivation,
        up_preactivation,
    )
    picked = returned.reshape(slot_total, model_dim)[slot_index].reshape(
        sequence_length, top_k, model_dim
    )
    routed_part = jnp.einsum("sk,skd->sd", gate_probs, picked, preferred_element_type=jnp.float32)
    ffn_own = narrow(shared_part + routed_part)
    output = (residual + ffn_own).astype(jnp.bfloat16)
    weights_back = dense_fetch(
        query_projection,
        key_projection,
        value_projection,
        output_projection,
        shared_gate_matrix,
        shared_up_matrix,
        shared_down_matrix,
    )
    query_back, key_back, value_back, out_back, sgate_back, sup_back, sdown_back = weights_back
    grad_out = cotangent.astype(jnp.float32)
    grad_ffn = widen(cotangent)
    grad_hidden_sh = jnp.dot(grad_ffn, sdown_back.T, preferred_element_type=jnp.float32)
    grad_sdown = jnp.dot(hidden_shared.T, grad_ffn, preferred_element_type=jnp.float32)
    grad_gate_sh = (grad_hidden_sh * up_shared * silu_slope(gate_shared)).astype(jnp.bfloat16)
    grad_up_sh = (grad_hidden_sh * silu(gate_shared)).astype(jnp.bfloat16)
    grad_sgate = jnp.dot(full_two.T, grad_gate_sh, preferred_element_type=jnp.float32)
    grad_sup = jnp.dot(full_two.T, grad_up_sh, preferred_element_type=jnp.float32)
    grad_normed_part = jnp.dot(
        grad_gate_sh, sgate_back.T, preferred_element_type=jnp.float32
    ) + jnp.dot(grad_up_sh, sup_back.T, preferred_element_type=jnp.float32)
    grad_gates_part = jnp.einsum("sd,skd->sk", grad_ffn, picked, preferred_element_type=jnp.float32)
    grad_slot = (
        jnp.where(slot_used[:, None], grad_ffn[token_of_slot] * gate_of_slot[:, None], 0.0)
        .astype(jnp.bfloat16)
        .reshape(n_dp, exp_dev, capacity, model_dim)
    )
    received_gradient = lax.all_to_all(grad_slot, DP, split_axis=0, concat_axis=0, tiled=True)
    expert_gate_gradient, expert_up_gradient, expert_down_gradient, output_rows_gradient = (
        expert_gradients(
            received,
            received_gradient,
            gate_preactivation,
            up_preactivation,
            expert_gate_matrix,
            expert_up_matrix,
            expert_down_matrix,
        )
    )
    grad_returned = lax.all_to_all(
        output_rows_gradient, DP, split_axis=0, concat_axis=0, tiled=True
    )
    grad_picked = grad_returned.reshape(slot_total, model_dim)[slot_index].reshape(
        sequence_length, top_k, model_dim
    )
    grad_normed_part = grad_normed_part + jnp.sum(grad_picked, axis=1, dtype=jnp.float32)
    grad_normed_two, grad_gates = (
        lax.psum_scatter(
            grad_normed_part.astype(jnp.bfloat16), TENSOR, scatter_dimension=0, tiled=True
        ).astype(jnp.float32),
        lax.psum_scatter(
            grad_gates_part.astype(jnp.bfloat16), TENSOR, scatter_dimension=0, tiled=True
        ).astype(jnp.float32),
    )
    row_start = tensor_pos * own_rows
    gates_own = lax.dynamic_slice_in_dim(gate_probs, row_start, own_rows, 0)
    chosen_own = lax.dynamic_slice_in_dim(chosen, row_start, own_rows, 0)
    grad_selected = gates_own * (
        grad_gates - jnp.sum(gates_own * grad_gates, axis=-1, keepdims=True)
    )
    grad_logits = jnp.sum(jnp.where(chosen_own, grad_selected[:, :, None], 0.0), axis=1).astype(
        jnp.bfloat16
    )
    grad_normed_two = grad_normed_two + jnp.dot(
        grad_logits, router_full.T, preferred_element_type=jnp.float32
    )
    grad_router_part = jnp.dot(normed_two.T, grad_logits, preferred_element_type=jnp.float32)
    grad_residual, grad_gain_two = rms_back(grad_normed_two, residual, scale_two, second_gain)
    grad_residual = grad_residual + grad_out
    grad_attn = widen(grad_residual.astype(jnp.bfloat16))
    grad_wout = jnp.dot(mixed_heads.T, grad_attn, preferred_element_type=jnp.float32)
    grad_mixed = (
        jnp.dot(grad_attn, out_back.T, preferred_element_type=jnp.float32)
        .astype(jnp.bfloat16)
        .reshape(sequence_length, kv_heads, group_size, HEAD_SIZE)
    )
    grad_keys = jnp.zeros((sequence_length, kv_heads, HEAD_SIZE), jnp.float32)
    grad_values = jnp.zeros((sequence_length, kv_heads, HEAD_SIZE), jnp.float32)
    block_index = 0
    start_row = block_index * sequence_length
    end_row = start_row + sequence_length
    scores, allowed = block_scores(start_row, end_row)
    attn_probs = jnp.where(allowed, jnp.exp(scores - lse_blocks[block_index]), 0.0)
    probs_low = attn_probs.astype(jnp.bfloat16)
    grad_values = grad_values.at[:end_row].add(
        jnp.einsum("kgqs,qkgd->skd", probs_low, grad_mixed, preferred_element_type=jnp.float32)
    )
    grad_probs = jnp.einsum(
        "qkgd,skd->kgqs", grad_mixed, rows_of_value, preferred_element_type=jnp.float32
    )
    inner_sum = jnp.sum(attn_probs * grad_probs, axis=-1, keepdims=True)
    grad_scores = (attn_probs * (grad_probs - inner_sum)).astype(jnp.bfloat16)
    grad_query_blocks = (
        jnp.einsum("kgqs,skd->qkgd", grad_scores, key_rows, preferred_element_type=jnp.float32)
        * score_scale
    )
    grad_keys = grad_keys.at[:end_row].add(
        jnp.einsum("kgqs,qkgd->skd", grad_scores, rows_of_query, preferred_element_type=jnp.float32)
        * score_scale
    )
    grad_query = grad_query_blocks.reshape(sequence_length, q_heads, HEAD_SIZE)
    grad_q_raw = (
        rotate_back(grad_query, rotary_cosine, rotary_sine)
        .astype(jnp.bfloat16)
        .reshape(sequence_length, q_heads * HEAD_SIZE)
    )
    grad_k_raw = (
        rotate_back(grad_keys, rotary_cosine, rotary_sine)
        .astype(jnp.bfloat16)
        .reshape(sequence_length, kv_heads * HEAD_SIZE)
    )
    grad_v_low = grad_values.astype(jnp.bfloat16).reshape(sequence_length, kv_heads * HEAD_SIZE)
    grad_wquery = jnp.dot(full_one.T, grad_q_raw, preferred_element_type=jnp.float32)
    grad_wkey = jnp.dot(full_one.T, grad_k_raw, preferred_element_type=jnp.float32)
    grad_wvalue = jnp.dot(full_one.T, grad_v_low, preferred_element_type=jnp.float32)
    grad_normed_one_part = (
        jnp.dot(grad_q_raw, query_back.T, preferred_element_type=jnp.float32)
        + jnp.dot(grad_k_raw, key_back.T, preferred_element_type=jnp.float32)
        + jnp.dot(grad_v_low, value_back.T, preferred_element_type=jnp.float32)
    )
    grad_normed_one = narrow(grad_normed_one_part)
    grad_inputs, grad_gain_one = rms_back(grad_normed_one, input_values, scale_one, first_gain)
    grad_inputs = grad_inputs + grad_residual
    dense_sums = (
        lax.psum_scatter(grad_wquery, DP, scatter_dimension=0, tiled=True),
        lax.psum_scatter(grad_wkey, DP, scatter_dimension=0, tiled=True),
        lax.psum_scatter(grad_wvalue, DP, scatter_dimension=0, tiled=True),
        lax.psum_scatter(grad_wout, DP, scatter_dimension=1, tiled=True),
        lax.psum_scatter(grad_sgate, DP, scatter_dimension=0, tiled=True),
        lax.psum_scatter(grad_sup, DP, scatter_dimension=0, tiled=True),
        lax.psum_scatter(grad_sdown, DP, scatter_dimension=1, tiled=True),
    )
    small_sums = (
        lax.psum_scatter(grad_router_part, (DP, TENSOR), scatter_dimension=0, tiled=True),
        lax.psum_scatter(grad_gain_one, (DP, TENSOR), scatter_dimension=0, tiled=True),
        lax.psum_scatter(grad_gain_two, (DP, TENSOR), scatter_dimension=0, tiled=True),
    )
    return (
        output,
        grad_inputs,
        small_sums[1],
        small_sums[2],
        dense_sums[0],
        dense_sums[1],
        dense_sums[2],
        dense_sums[3],
        small_sums[0],
        dense_sums[4],
        dense_sums[5],
        dense_sums[6],
        expert_gate_gradient,
        expert_up_gradient,
        expert_down_gradient,
    )


MESH = pl.DeviceIdType.MESH
ANY = pl.BlockSpec(memory_space=pl.ANY)


def when(condition, body):
    if condition is None:
        body()
    else:
        pl.when(condition)(body)


class Spot:
    def __init__(self, n_planes):
        dp = lax.axis_index(DP)
        self.x = lax.axis_index(TENSOR)
        self.dp = dp
        self.core = dp % 2
        self.y = (dp // 2) % 2
        self.z = dp // 4
        self.n_planes = n_planes
        self.has_up = self.z < n_planes - 1
        self.has_down = self.z > 0
        self.up = (dp + 4, self.x)
        self.down = (dp - 4, self.x)
        self.side = (dp + 2 - 4 * self.y, self.x)
        self.across = (dp, 1 - self.x)
        self.twin = (dp + 1 - 2 * self.core, self.x)

    def far_first(self):
        low, high = 0 * self.z, 0 * self.z + self.n_planes - 1
        order = []
        for _ in range(self.n_planes):
            take_low = (self.z - low >= high - self.z).astype(jnp.int32)
            order.append(take_low * low + (1 - take_low) * high)
            low, high = low + take_low, high - (1 - take_low)
        return order

    def greet(self):
        barrier = pltpu.get_barrier_semaphore()
        fixed = [self.side, self.twin, self.across]
        for device in fixed:
            pl.semaphore_signal(barrier, inc=1, device_id=device, device_id_type=MESH)
        for condition, device in ((self.has_up, self.up), (self.has_down, self.down)):

            @pl.when(condition)
            def _(device=device):
                pl.semaphore_signal(barrier, inc=1, device_id=device, device_id_type=MESH)

        ends = self.has_up.astype(jnp.int32) + self.has_down.astype(jnp.int32)
        pl.semaphore_wait(barrier, len(fixed) + ends)


class Copies:
    def __init__(self, groups, n_planes, n_pieces, send, recv):
        self.base = {name: i * n_planes for i, name in enumerate(groups)}
        self.n_pieces = n_pieces
        self.send, self.recv = send, recv
        self.open = []

    def copy(self, group, s, piece, src, dst, device, arrival=None):
        return pltpu.make_async_remote_copy(
            src_ref=src,
            dst_ref=dst,
            send_sem=self.send.at[self.base[group] + s, piece],
            recv_sem=self.recv.at[self.base[arrival or group] + s, piece],
            device_id=device,
            device_id_type=MESH,
        )

    def start(self, condition, group, s, sources, targets, device, arrival=None):
        def body():
            for i, (src, dst) in enumerate(zip(sources, targets)):
                self.copy(group, s, i, src, dst, device, arrival).start()

        when(condition, body)
        self.open.append((condition, group, s, sources, targets, device, arrival))

    def arrive(self, group, s, targets, device):
        for i, dst in enumerate(targets):
            self.copy(group, s, i, dst, dst, device).wait_recv()

    def close(self):
        for condition, group, s, sources, targets, device, arrival in self.open:

            def body():
                for i, (src, dst) in enumerate(zip(sources, targets)):
                    self.copy(group, s, i, src, dst, device, arrival).wait_send()

            when(condition, body)


SPREAD_GROUPS = (
    "z", "z_down", "y_all", "y_half", "x_all", "x_half", "c_own", "c_y", "c_x", "c_xh", "c_yh",
)


def spread(spot, copies, own, views, use_x):
    order = spot.far_first()[::-1]
    y, x, core = spot.y, spot.x, spot.core

    def at(s, yy, xx, part="all", cc=None):
        return views(s, yy, core if cc is None else cc, xx, part)

    def onward(s, sources):
        copies.start(None, "y_all", s, sources, at(s, y, x), spot.side)
        if use_x:
            copies.start(None, "x_all", s, sources, at(s, y, x), spot.across)
        copies.start(None, "c_own", s, sources, at(s, y, x), spot.twin)

    def column(j):
        s = order[j]
        here = at(s, y, x)
        copies.arrive("z", s, here, spot.up)
        copies.start((s > spot.z) & spot.has_down, "z_down", s, here, here, spot.down, "z")
        copies.start((s < spot.z) & spot.has_up, "z", s, here, here, spot.up)
        onward(s, here)

    def sides(j):
        s = order[j]
        there = at(s, 1 - y, x)
        copies.arrive("y_all", s, there, spot.side)
        if use_x:
            part = at(s, 1 - y, x, "first")
            copies.start(None, "x_half", s, part, part, spot.across)
        copies.start(None, "c_y", s, there, there, spot.twin)
        if use_x:
            there = at(s, y, 1 - x)
            copies.arrive("x_all", s, there, spot.across)
            part = at(s, y, 1 - x, "second")
            copies.start(None, "y_half", s, part, part, spot.side)
            copies.start(None, "c_x", s, there, there, spot.twin)

    def corner(j):
        if not use_x:
            return
        s = order[j]
        part = at(s, 1 - y, 1 - x, "first")
        copies.arrive("x_half", s, part, spot.across)
        copies.start(None, "c_xh", s, part, part, spot.twin)
        part = at(s, 1 - y, 1 - x, "second")
        copies.arrive("y_half", s, part, spot.side)
        copies.start(None, "c_yh", s, part, part, spot.twin)

    here = at(spot.z, y, x)
    copies.start(spot.has_up, "z", spot.z, own, here, spot.up)
    copies.start(spot.has_down, "z_down", spot.z, own, here, spot.down, "z")
    onward(spot.z, own)
    n = spot.n_planes
    for step in range(1, n + 2):
        if step < n:
            column(step)
        if 0 <= step - 1 < n:
            sides(step - 1)
        if 0 <= step - 2 < n:
            corner(step - 2)
    other = 1 - core
    for s in range(n):
        copies.arrive("c_own", s, at(s, y, x, cc=other), spot.twin)
        copies.arrive("c_y", s, at(s, 1 - y, x, cc=other), spot.twin)
        if use_x:
            copies.arrive("c_x", s, at(s, y, 1 - x, cc=other), spot.twin)
            copies.arrive("c_xh", s, at(s, 1 - y, 1 - x, "first", cc=other), spot.twin)
            copies.arrive("c_yh", s, at(s, 1 - y, 1 - x, "second", cc=other), spot.twin)
    copies.close()


def dp_of(s, yy, cc):
    return (s * 2 + yy) * 2 + cc


def gather_kernel(n_planes, n, *refs):
    ins, outs, (send, recv, local) = refs[:n], refs[n : 2 * n], refs[2 * n :]
    spot = Spot(n_planes)
    half = ins[0].shape[0] // 2

    def views(s, yy, cc, xx, part):
        b = dp_of(s, yy, cc) * 2 + xx
        if part == "all":
            return [o.at[b] for o in outs]
        if part == "first":
            return [outs[0].at[b, pl.ds(0, half)]] + [o.at[b] for o in outs[1:]]
        return [outs[0].at[b, pl.ds(half, half)]]

    own = [
        pltpu.make_async_copy(ins[i], outs[i].at[spot.dp * 2 + spot.x], local.at[i])
        for i in range(n)
    ]
    for c in own:
        c.start()
    spot.greet()
    copies = Copies(SPREAD_GROUPS, n_planes, n, send, recv)
    spread(spot, copies, list(ins), views, True)
    for c in own:
        c.wait()


def gather_everywhere(arrays, n_dp, collective_id):
    n, n_planes = len(arrays), n_dp // 4
    sems = (len(SPREAD_GROUPS) * n_planes, n)
    return pl.pallas_call(
        functools.partial(gather_kernel, n_planes, n),
        out_shape=[jax.ShapeDtypeStruct((2 * n_dp,) + a.shape, a.dtype) for a in arrays],
        in_specs=[ANY] * n,
        out_specs=[ANY] * n,
        scratch_shapes=[
            pltpu.SemaphoreType.DMA(sems),
            pltpu.SemaphoreType.DMA(sems),
            pltpu.SemaphoreType.DMA((n,)),
        ],
        compiler_params=pltpu.CompilerParams(collective_id=collective_id, has_side_effects=True),
    )(*arrays)


def fetch_kernel(n_planes, axes, *refs):
    n = len(axes)
    ins, (tokens, small), outs = refs[:n], refs[n : n + 2], refs[n + 2 : 2 * n + 2]
    sequence, smalls = refs[2 * n + 2 : 2 * n + 4]
    send, recv, local, x_send, x_recv = refs[2 * n + 4 :]
    spot = Spot(n_planes)

    def views(s, yy, cc, xx, part):
        i = dp_of(s, yy, cc)
        places = []
        for o, a, axis in zip(outs, ins, axes):
            size = a.shape[axis]
            span = pl.ds(pl.multiple_of(i * size, size), size)
            places.append(o.at[span] if axis == 0 else o.at[:, span])
        return places + [smalls.at[xx, i]]

    sources = list(ins) + [small]
    mine = views(spot.z, spot.y, spot.core, spot.x, "all")
    own = [pltpu.make_async_copy(a, v, local.at[i]) for i, (a, v) in enumerate(zip(sources, mine))]
    own.append(pltpu.make_async_copy(tokens, sequence.at[spot.x], local.at[n + 1]))
    for c in own:
        c.start()
    spot.greet()

    def across(i, src, dst):
        return pltpu.make_async_remote_copy(
            src_ref=src, dst_ref=dst, send_sem=x_send.at[i], recv_sem=x_recv.at[i],
            device_id=spot.across, device_id_type=MESH,
        )

    across(0, tokens, sequence.at[spot.x]).start()
    copies = Copies(SPREAD_GROUPS, n_planes, n + 1, send, recv)
    spread(spot, copies, sources, views, False)
    for c in own:
        c.wait()
    across(1, smalls.at[spot.x], smalls.at[spot.x]).start()
    across(0, tokens, sequence.at[spot.x]).wait_send()
    across(1, smalls.at[spot.x], smalls.at[spot.x]).wait_send()
    across(0, sequence.at[1 - spot.x], sequence.at[1 - spot.x]).wait_recv()
    across(1, smalls.at[1 - spot.x], smalls.at[1 - spot.x]).wait_recv()


def fetch(arrays, axes, tokens, small, n_dp, collective_id):
    n, n_planes = len(arrays), n_dp // 4
    sems = (len(SPREAD_GROUPS) * n_planes, n + 1)

    def whole(a, axis):
        shape = list(a.shape)
        shape[axis] *= n_dp
        return jax.ShapeDtypeStruct(tuple(shape), a.dtype)

    return pl.pallas_call(
        functools.partial(fetch_kernel, n_planes, axes),
        out_shape=[whole(a, axis) for a, axis in zip(arrays, axes)]
        + [
            jax.ShapeDtypeStruct((2,) + tokens.shape, tokens.dtype),
            jax.ShapeDtypeStruct((2, n_dp) + small.shape, small.dtype),
        ],
        in_specs=[ANY] * (n + 2),
        out_specs=[ANY] * (n + 2),
        scratch_shapes=[
            pltpu.SemaphoreType.DMA(sems),
            pltpu.SemaphoreType.DMA(sems),
            pltpu.SemaphoreType.DMA((n + 2,)),
            pltpu.SemaphoreType.DMA((2,)),
            pltpu.SemaphoreType.DMA((2,)),
        ],
        compiler_params=pltpu.CompilerParams(collective_id=collective_id, has_side_effects=True),
    )(*arrays, tokens, small)


REDUCE_GROUPS = ("c_yx", "c_y", "c_x", "c_own", "x_half", "y_half", "y_all", "x_all", "z_up", "z_down")


def add_up(target, sources):
    rows = target.shape[0]
    step = 16 if rows % 16 == 0 else rows

    def body(i, carry):
        span = pl.ds(pl.multiple_of(i * step, step), step)
        total = sources[0][span, :].astype(jnp.float32)
        for source in sources[1:]:
            total = total + source[span, :].astype(jnp.float32)
        target[span, :] = total.astype(target.dtype)
        return carry

    lax.fori_loop(0, rows // step, body, 0)


class Sums:
    @staticmethod
    def scratch(shapes, dtypes, n_planes, use_x):
        n = len(shapes)
        kinds = 4 if use_x else 2
        out = []
        for i, (shape, dtype) in enumerate(zip(shapes, dtypes)):
            half = (shape[0] // 2, shape[1]) if i == 0 else shape
            out.append(pltpu.VMEM((kinds, n_planes) + shape, dtype))
            out.append(pltpu.VMEM((kinds, n_planes) + shape, dtype))
            out.append(pltpu.VMEM((n_planes,) + shape, dtype))
            out.append(pltpu.VMEM((n_planes,) + shape, dtype))
            out.append(pltpu.VMEM((n_planes,) + shape, dtype))
            if use_x:
                out.append(pltpu.VMEM((n_planes,) + shape, dtype))
                out.append(pltpu.VMEM((n_planes,) + half, dtype))
                out.append(pltpu.VMEM((n_planes,) + (half if i == 0 else (8, 128)), dtype))
        sems = (len(REDUCE_GROUPS) * n_planes, n)
        out.append(pltpu.SemaphoreType.DMA(sems))
        out.append(pltpu.SemaphoreType.DMA(sems))
        out.append(pltpu.SemaphoreType.DMA((kinds * n_planes, n)))
        return out


def reduce_scatter(spot, ins, outs, scratch, use_x):
    n, n_planes = len(outs), spot.n_planes
    per = 8 if use_x else 5
    send, recv, local = scratch[n * per :]
    sets = [scratch[i * per : (i + 1) * per] for i in range(n)]
    mine = [s[0] for s in sets]
    twin = [s[1] for s in sets]
    above = [s[2] for s in sets]
    below = [s[3] for s in sets]
    side = [s[4] for s in sets]
    across = [s[5] for s in sets] if use_x else None
    first = [s[6] for s in sets] if use_x else None
    second = [sets[0][7]] if use_x else None
    copies = Copies(REDUCE_GROUPS, n_planes, n, send, recv)
    y, x, core = spot.y, spot.x, spot.core
    order = spot.far_first()
    kinds = (["c_yx", "c_y", "c_x", "c_own"] if use_x else ["c_y", "c_own"])
    places = {"c_yx": (1 - y, 1 - x), "c_y": (1 - y, x), "c_x": (y, 1 - x), "c_own": (y, x)}

    def load(k, j):
        s = order[j]
        yy, xx = places[kinds[k]]
        for i, ref in enumerate(ins(s, yy, core, xx)):
            yield pltpu.make_async_copy(ref, mine[i].at[k, s], local.at[k * n_planes + s, i])

    for j in range(n_planes):
        for k in range(len(kinds)):
            for c in load(k, j):
                c.start()
    spot.greet()
    for j in range(n_planes):
        s = order[j]
        for k, name in enumerate(kinds):
            yy, xx = places[name]
            copies.start(None, name, s, ins(s, yy, 1 - core, xx), [t.at[k, s] for t in twin], spot.twin)

    def ready(k, j):
        s = order[j]
        for c in load(k, j):
            c.wait()
        copies.arrive(kinds[k], s, [t.at[k, s] for t in twin], spot.twin)

    half = sets[0][0].shape[2] // 2

    def corner(j):
        s = order[j]
        ready(0, j)
        for i in range(n):
            add_up(mine[i].at[0, s], [mine[i].at[0, s], twin[i].at[0, s]])
        head = [mine[0].at[0, s, pl.ds(0, half)]] + [m.at[0, s] for m in mine[1:]]
        copies.start(None, "x_half", s, head, [f.at[s] for f in first], spot.across)
        copies.start(None, "y_half", s, [mine[0].at[0, s, pl.ds(half, half)]], [second[0].at[s]], spot.side)

    def sides(j):
        s = order[j]
        k = kinds.index("c_y")
        ready(k, j)
        if use_x:
            copies.arrive("x_half", s, [f.at[s] for f in first], spot.across)
            for i in range(n):
                if i == 0:
                    a, b = pl.ds(0, half), pl.ds(half, half)
                    add_up(mine[0].at[k, s, a], [mine[0].at[k, s, a], twin[0].at[k, s, a], first[0].at[s]])
                    add_up(mine[0].at[k, s, b], [mine[0].at[k, s, b], twin[0].at[k, s, b]])
                else:
                    add_up(mine[i].at[k, s], [mine[i].at[k, s], twin[i].at[k, s], first[i].at[s]])
        else:
            for i in range(n):
                add_up(mine[i].at[k, s], [mine[i].at[k, s], twin[i].at[k, s]])
        copies.start(None, "y_all", s, [m.at[k, s] for m in mine], [t.at[s] for t in side], spot.side)
        if not use_x:
            return
        k = kinds.index("c_x")
        ready(k, j)
        copies.arrive("y_half", s, [second[0].at[s]], spot.side)
        for i in range(n):
            if i == 0:
                a, b = pl.ds(0, half), pl.ds(half, half)
                add_up(mine[0].at[k, s, a], [mine[0].at[k, s, a], twin[0].at[k, s, a]])
                add_up(mine[0].at[k, s, b], [mine[0].at[k, s, b], twin[0].at[k, s, b], second[0].at[s]])
            else:
                add_up(mine[i].at[k, s], [mine[i].at[k, s], twin[i].at[k, s]])
        copies.start(None, "x_all", s, [m.at[k, s] for m in mine], [t.at[s] for t in across], spot.across)

    def column(j):
        s = order[j]
        k = kinds.index("c_own")
        ready(k, j)
        copies.arrive("y_all", s, [t.at[s] for t in side], spot.side)
        if use_x:
            copies.arrive("x_all", s, [t.at[s] for t in across], spot.across)
        here = [[mine[i].at[k, s], twin[i].at[k, s], side[i].at[s]] + ([across[i].at[s]] if use_x else []) for i in range(n)]
        if j == n_planes - 1:
            from_above = [t.at[s] for t in above]
            from_below = [t.at[s] for t in below]

            def wait_above():
                copies.arrive("z_down", s, from_above, spot.up)

            def wait_below():
                copies.arrive("z_up", s, from_below, spot.down)

            when(spot.has_up, wait_above)
            when(spot.has_down, wait_below)

            def both():
                for i in range(n):
                    add_up(outs[i], here[i] + [from_above[i], from_below[i]])

            def one_above():
                for i in range(n):
                    add_up(outs[i], here[i] + [from_above[i]])

            def one_below():
                for i in range(n):
                    add_up(outs[i], here[i] + [from_below[i]])

            when(spot.has_up & spot.has_down, both)
            when(spot.has_up & (spot.z == 0), one_above)
            when(spot.has_down & (spot.z == n_planes - 1), one_below)
            return
        goes_down = s < spot.z
        goes_up = s > spot.z
        for goes, more, group, buffers, device, source in (
            (goes_down, spot.has_up, "z_down", above, spot.down, spot.up),
            (goes_up, spot.has_down, "z_up", below, spot.up, spot.down),
        ):
            arrived = [t.at[s] for t in buffers]

            def partial():
                copies.arrive(group, s, arrived, source)
                for i in range(n):
                    add_up(mine[i].at[k, s], here[i] + [arrived[i]])

            def alone():
                for i in range(n):
                    add_up(mine[i].at[k, s], here[i])

            when(goes & more, partial)
            when(goes & jnp.logical_not(more), alone)
            copies.start(goes, group, s, [m.at[k, s] for m in mine], [t.at[s] for t in buffers], device)

    for step in range(n_planes + 2):
        if use_x and step < n_planes:
            corner(step)
        if 0 <= step - 1 < n_planes:
            sides(step - 1)
        if 0 <= step - 2 < n_planes:
            column(step - 2)
    copies.close()


def sum_kernel(n_planes, n, *refs):
    ins, outs, scratch = refs[:n], refs[n : 2 * n], refs[2 * n :]
    spot = Spot(n_planes)

    def blocks(s, yy, cc, xx):
        return [a.at[dp_of(s, yy, cc) * 2 + xx] for a in ins]

    reduce_scatter(spot, blocks, outs, scratch, True)


def sum_everywhere(arrays, out_dtypes, n_dp, collective_id):
    n, n_planes = len(arrays), n_dp // 4
    shapes = [a.shape[1:] for a in arrays]
    return pl.pallas_call(
        functools.partial(sum_kernel, n_planes, n),
        out_shape=[jax.ShapeDtypeStruct(s, t) for s, t in zip(shapes, out_dtypes)],
        in_specs=[ANY] * n,
        out_specs=[pl.BlockSpec(memory_space=pltpu.VMEM)] * n,
        scratch_shapes=Sums.scratch(shapes, [a.dtype for a in arrays], n_planes, True),
        compiler_params=pltpu.CompilerParams(
            collective_id=collective_id, has_side_effects=True, vmem_limit_bytes=56 << 20
        ),
    )(*arrays)


def return_kernel(n_planes, axes, *refs):
    n = len(axes)
    ins, outs = refs[:n], refs[n : 2 * n]
    scratch, (tile_sum, tile_in, x_send, x_recv) = refs[2 * n : -4], refs[-4:]
    spot = Spot(n_planes)

    def blocks(s, yy, cc, xx):
        i = dp_of(s, yy, cc)
        places = []
        for j, (a, o, axis) in enumerate(zip(ins, outs, axes)):
            size = o.shape[axis] * (2 if j == n - 1 else 1)
            span = pl.ds(pl.multiple_of(i * size, size), size)
            places.append(a.at[span] if axis == 0 else a.at[:, span])
        return places

    reduce_scatter(spot, blocks, list(outs[:-1]) + [tile_sum], scratch, False)
    rows = tile_in.shape[0]
    swap = pltpu.make_async_remote_copy(
        src_ref=tile_sum.at[pl.ds(pl.multiple_of((1 - spot.x) * rows, rows), rows)], dst_ref=tile_in,
        send_sem=x_send, recv_sem=x_recv, device_id=spot.across, device_id_type=MESH,
    )
    swap.start()
    swap.wait()
    outs[-1][...] = tile_sum[pl.ds(pl.multiple_of(spot.x * rows, rows), rows), :] + tile_in[...]


def sum_back(arrays, axes, n_dp, collective_id):
    n, n_planes = len(arrays), n_dp // 4

    def part(a, axis):
        shape = list(a.shape)
        shape[axis] //= n_dp
        return tuple(shape)

    shapes = [part(a, axis) for a, axis in zip(arrays, axes)]
    tile = (shapes[-1][0] // 2, shapes[-1][1])
    return pl.pallas_call(
        functools.partial(return_kernel, n_planes, axes),
        out_shape=[jax.ShapeDtypeStruct(s, jnp.float32) for s in shapes[:-1] + [tile]],
        in_specs=[ANY] * n,
        out_specs=[pl.BlockSpec(memory_space=pltpu.VMEM)] * n,
        scratch_shapes=Sums.scratch(shapes, [a.dtype for a in arrays], n_planes, False)
        + [
            pltpu.VMEM(shapes[-1], jnp.float32),
            pltpu.VMEM(tile, jnp.float32),
            pltpu.SemaphoreType.DMA(()),
            pltpu.SemaphoreType.DMA(()),
        ],
        compiler_params=pltpu.CompilerParams(
            collective_id=collective_id, has_side_effects=True, vmem_limit_bytes=56 << 20
        ),
    )(*arrays)


def swap_halves(own, x):
    return lax.ppermute(own, TENSOR, [(0, 1), (1, 0)])


def halves_sum(partial, rows, x):
    kept = lax.dynamic_slice_in_dim(partial, x * rows, rows, 0)
    given = lax.dynamic_slice_in_dim(partial, (1 - x) * rows, rows, 0).astype(jnp.bfloat16)
    return kept + swap_halves(given, x).astype(jnp.float32)


def gather_plan(
    tokens,
    attention_gain,
    expert_norm_gain,
    query_projection,
    key_projection,
    value_projection,
    output_projection,
    router,
    shared_gate_matrix,
    shared_up_matrix,
    shared_down_matrix,
    expert_gate_matrix,
    expert_up_matrix,
    expert_down_matrix,
    document_lengths,
    expert_indices,
    cotangent,
):
    n_dp = lax.axis_size(DP)
    x = lax.axis_index(TENSOR)
    dp = lax.axis_index(DP)
    own_rows, model_dim = tokens.shape
    sequence_length = own_rows * 2
    experts = n_dp
    top_k = expert_indices.shape[1]
    capacity = sequence_length * top_k * 4 // (3 * experts)
    bf16, f32 = jnp.bfloat16, jnp.float32

    def dot(a, b):
        return jnp.dot(a, b, preferred_element_type=f32)

    width = attention_gain.shape[0]
    small = jnp.concatenate([attention_gain, expert_norm_gain, router.reshape(-1)])
    small = jnp.pad(small, (0, -small.shape[0] % 2048)).reshape(-1, 128)
    axes = (0, 0, 0, 1)
    query_all, key_all, value_all, out_all, sequence, smalls = fetch(
        [query_projection, key_projection, value_projection, output_projection],
        axes, tokens, small, n_dp, 1,
    )
    flat = smalls.swapaxes(0, 1).reshape(2 * n_dp, -1)
    first_gain = flat[:, :width].reshape(-1).astype(f32)
    second_gain = flat[:, width : 2 * width].reshape(-1).astype(f32)
    router_full = flat[:, 2 * width : (2 + experts) * width].reshape(model_dim, experts)

    hidden = shared_gate_matrix.shape[1] // n_dp
    hidden_pad = -(-hidden // 16) * 16

    def slices(transposed):
        blocks = transposed.reshape(n_dp, hidden, -1)
        return jnp.pad(blocks, ((0, 0), (0, hidden_pad - hidden), (0, 0)))

    shared_out = jnp.stack(
        [slices(shared_gate_matrix.T), slices(shared_up_matrix.T), slices(shared_down_matrix)], axis=1
    )
    shared_in = lax.all_to_all(shared_out, DP, split_axis=0, concat_axis=0, tiled=True)
    shared_rows = jnp.moveaxis(shared_in, 0, 2).reshape(3, hidden_pad, model_dim)
    sgate_t, sup_t, sdown = shared_rows[0], shared_rows[1], shared_rows[2]

    full_tokens = sequence.reshape(sequence_length, model_dim).astype(f32)
    full_scale = lax.rsqrt(jnp.mean(full_tokens * full_tokens, axis=-1, keepdims=True) + norm_eps)
    full_one = (full_tokens * full_scale * first_gain).astype(bf16)
    input_values = tokens.astype(f32)
    scale_one = lax.dynamic_slice_in_dim(full_scale, x * own_rows, own_rows, 0)
    q_heads = query_all.shape[1] // HEAD_SIZE
    kv_heads = key_all.shape[1] // HEAD_SIZE
    group_size = q_heads // kv_heads
    rotary_cosine, rotary_sine = rotation(sequence_length, HEAD_SIZE)
    query_unrotated = dot(full_one, query_all).reshape(sequence_length, q_heads, HEAD_SIZE)
    key_unrotated = dot(full_one, key_all).reshape(sequence_length, kv_heads, HEAD_SIZE)
    rows_of_query = (
        apply_rotary(query_unrotated, rotary_cosine, rotary_sine)
        .astype(bf16)
        .reshape(sequence_length, kv_heads, group_size, HEAD_SIZE)
    )
    key_rows = apply_rotary(key_unrotated, rotary_cosine, rotary_sine).astype(bf16)
    rows_of_value = dot(full_one, value_all).astype(bf16).reshape(sequence_length, kv_heads, HEAD_SIZE)
    doc_ends = jnp.cumsum(document_lengths[0])
    positions = jnp.arange(sequence_length, dtype=jnp.int32)
    doc_ids = jnp.sum((positions[:, None] >= doc_ends[None, :]).astype(jnp.int32), axis=-1)
    score_scale = HEAD_SIZE ** (-0.5)
    allowed = (doc_ids[:, None] == doc_ids[None, :]) & (positions[:, None] >= positions[None, :])
    scores = (
        jnp.einsum("qkgd,skd->kgqs", rows_of_query, key_rows, preferred_element_type=f32) * score_scale
    )
    scores = jnp.where(allowed, scores, neg_big)
    exp_scores = jnp.exp(scores - jnp.max(scores, axis=-1, keepdims=True))
    attn_probs = exp_scores / jnp.sum(exp_scores, axis=-1, keepdims=True)
    probs_low = attn_probs.astype(bf16)
    mixed_heads = (
        jnp.einsum("kgqs,skd->qkgd", probs_low, rows_of_value, preferred_element_type=f32)
        .reshape(sequence_length, q_heads * HEAD_SIZE)
        .astype(bf16)
    )
    residual = input_values + halves_sum(dot(mixed_heads, out_all), own_rows, x)

    scale_two = lax.rsqrt(jnp.mean(residual * residual, axis=-1, keepdims=True) + norm_eps)
    normed_two = (residual * scale_two * second_gain).astype(bf16)
    logits = dot(normed_two, router_full)
    own_indices = lax.dynamic_slice_in_dim(expert_indices, x * own_rows, own_rows, 0)
    chosen = own_indices[:, :, None] == jnp.arange(experts, dtype=jnp.int32)[None, None, :]
    selected = jnp.sum(jnp.where(chosen, logits[:, None, :], 0.0), axis=-1)
    gate_exp = jnp.exp(selected - jnp.max(selected, axis=-1, keepdims=True))
    gate_probs = gate_exp / jnp.sum(gate_exp, axis=-1, keepdims=True)
    gates = jnp.sum(jnp.where(chosen, gate_probs[:, :, None], 0.0), axis=1)

    (cotangent_all,) = gather_everywhere([cotangent], n_dp, 3)
    normed_all, gates_all = gather_everywhere([normed_two, gates.T], n_dp, 2)

    normed_seq = normed_all.reshape(n_dp, sequence_length, model_dim)
    grad_seq = cotangent_all.reshape(n_dp, sequence_length, model_dim)
    gate_seq = lax.dynamic_index_in_dim(gates_all, dp, 1, keepdims=False).reshape(n_dp, sequence_length)
    routed = gate_seq > 0.0
    rank = jnp.cumsum(routed.astype(jnp.int32), axis=1) - 1
    pick = (rank[:, None, :] == jnp.arange(capacity, dtype=jnp.int32)[None, :, None]) & routed[:, None, :]
    pick_low = pick.astype(bf16)
    rows = n_dp * capacity
    received = jnp.einsum("sjt,std->sjd", pick_low, normed_seq, preferred_element_type=f32)
    received = received.astype(bf16).reshape(rows, model_dim)
    grad_rows = jnp.einsum("sjt,std->sjd", pick_low, grad_seq, preferred_element_type=f32)
    grad_rows = grad_rows.astype(bf16).reshape(rows, model_dim)
    gate_rows = jnp.sum(jnp.where(pick, gate_seq[:, None, :], 0.0), axis=-1).reshape(rows, 1)
    w_gate, w_up, w_down = expert_gate_matrix[0], expert_up_matrix[0], expert_down_matrix[0]
    gate_pre = dot(received, w_gate)
    up_pre = dot(received, w_up)
    hidden_rows = silu(gate_pre) * up_pre
    gated_hidden = (hidden_rows * gate_rows).astype(bf16)
    produced = dot(gated_hidden, w_down).astype(bf16)
    grad_hidden = dot(grad_rows, w_down.T)
    grad_gate_rows = jnp.sum(hidden_rows * grad_hidden, axis=-1).reshape(n_dp, capacity)
    grad_hidden = grad_hidden * gate_rows
    grad_gate = (grad_hidden * up_pre * silu_slope(gate_pre)).astype(bf16)
    grad_up = (grad_hidden * silu(gate_pre)).astype(bf16)
    grad_received = (dot(grad_gate, w_gate.T) + dot(grad_up, w_up.T)).astype(bf16)
    expert_gate_gradient = dot(received.T, grad_gate)[None]
    expert_up_gradient = dot(received.T, grad_up)[None]
    expert_down_gradient = dot(gated_hidden.T, grad_rows)[None]

    normed_flat = normed_all.reshape(-1, model_dim)
    grad_flat = cotangent_all.reshape(-1, model_dim)
    gate_shared = dot(normed_flat, sgate_t.T)
    up_shared = dot(normed_flat, sup_t.T)
    hidden_shared = (silu(gate_shared) * up_shared).astype(bf16)
    grad_hidden_sh = dot(grad_flat, sdown.T)
    grad_gate_sh = (grad_hidden_sh * up_shared * silu_slope(gate_shared)).astype(bf16)
    grad_up_sh = (grad_hidden_sh * silu(gate_shared)).astype(bf16)
    shared_grads = jnp.stack(
        [dot(grad_gate_sh.T, normed_flat), dot(grad_up_sh.T, normed_flat), dot(hidden_shared.T, grad_flat)]
    ).astype(bf16)

    def scatter(rows_out, shared_part):
        back = jnp.einsum(
            "sjt,sjd->std", pick_low, rows_out.reshape(n_dp, capacity, model_dim), preferred_element_type=f32
        )
        total = back.reshape(-1, model_dim) + shared_part
        return total.astype(bf16).reshape(2 * n_dp, own_rows, model_dim)

    output_parts = scatter(produced, dot(hidden_shared, sdown))
    normed_parts = scatter(grad_received, dot(grad_gate_sh, sgate_t) + dot(grad_up_sh, sup_t))
    grad_gate_tokens = jnp.sum(jnp.where(pick, grad_gate_rows[:, :, None], 0.0), axis=1)
    grad_gate_parts = jnp.where(
        jnp.arange(experts)[None, :, None] == dp, grad_gate_tokens.reshape(2 * n_dp, 1, own_rows), 0.0
    )
    grad_normed_two, grad_gates_t = sum_everywhere([normed_parts, grad_gate_parts], [f32, f32], n_dp, 4)
    (ffn_own,) = sum_everywhere([output_parts], [f32], n_dp, 5)
    output = (residual + ffn_own).astype(bf16)

    grad_gates = grad_gates_t.T
    grad_logits = (
        gates * (grad_gates - jnp.sum(gates * grad_gates, axis=-1, keepdims=True))
    ).astype(bf16)
    grad_normed_two = grad_normed_two + dot(grad_logits, router_full.T)
    grad_router_part = dot(normed_two.T, grad_logits)
    grad_residual, grad_gain_two = rms_back(grad_normed_two, residual, scale_two, second_gain)
    grad_residual = grad_residual + cotangent.astype(f32)
    grad_low = grad_residual.astype(bf16)
    grad_other = swap_halves(grad_low, x)
    grad_attn = jnp.where(
        x == 0, jnp.concatenate([grad_low, grad_other]), jnp.concatenate([grad_other, grad_low])
    )

    grad_wout = dot(mixed_heads.T, grad_attn)
    grad_mixed = (
        dot(grad_attn, out_all.T).astype(bf16).reshape(sequence_length, kv_heads, group_size, HEAD_SIZE)
    )
    grad_values = jnp.einsum("kgqs,qkgd->skd", probs_low, grad_mixed, preferred_element_type=f32)
    grad_probs = jnp.einsum("qkgd,skd->kgqs", grad_mixed, rows_of_value, preferred_element_type=f32)
    inner_sum = jnp.sum(attn_probs * grad_probs, axis=-1, keepdims=True)
    grad_scores = (attn_probs * (grad_probs - inner_sum)).astype(bf16)
    grad_query = (
        jnp.einsum("kgqs,skd->qkgd", grad_scores, key_rows, preferred_element_type=f32) * score_scale
    ).reshape(sequence_length, q_heads, HEAD_SIZE)
    grad_keys = (
        jnp.einsum("kgqs,qkgd->skd", grad_scores, rows_of_query, preferred_element_type=f32) * score_scale
    )
    grad_q_raw = rotate_back(grad_query, rotary_cosine, rotary_sine).astype(bf16)
    grad_q_raw = grad_q_raw.reshape(sequence_length, q_heads * HEAD_SIZE)
    grad_k_raw = rotate_back(grad_keys, rotary_cosine, rotary_sine).astype(bf16)
    grad_k_raw = grad_k_raw.reshape(sequence_length, kv_heads * HEAD_SIZE)
    grad_v_low = grad_values.astype(bf16).reshape(sequence_length, kv_heads * HEAD_SIZE)
    grad_wquery = dot(full_one.T, grad_q_raw).astype(bf16)
    grad_wkey = dot(full_one.T, grad_k_raw).astype(bf16)
    grad_wvalue = dot(full_one.T, grad_v_low).astype(bf16)
    grad_normed_one = halves_sum(
        dot(grad_q_raw, query_all.T) + dot(grad_k_raw, key_all.T) + dot(grad_v_low, value_all.T), own_rows, x
    )
    grad_inputs, grad_gain_one = rms_back(grad_normed_one, input_values, scale_one, first_gain)
    grad_inputs = grad_inputs + grad_residual

    def by_owner(v):
        return v.reshape(2 * n_dp, -1)

    tiles = jnp.concatenate([by_owner(grad_gain_one), by_owner(grad_gain_two), by_owner(grad_router_part)], axis=1)
    tiles = jnp.pad(tiles, ((0, 0), (0, -tiles.shape[1] % 2048)))
    small_rows = tiles.shape[1] // 128
    sums = sum_back(
        [grad_wquery, grad_wkey, grad_wvalue, grad_wout.astype(bf16), tiles.reshape(-1, 128)],
        axes + (0,), n_dp, 6,
    )
    mine = sums[4].reshape(-1)
    gain_one_own, gain_two_own = mine[:width], mine[width : 2 * width]
    router_own = mine[2 * width : (2 + experts) * width].reshape(width, experts)
    returned = lax.all_to_all(
        shared_grads.reshape(3, hidden_pad, n_dp, -1).transpose(2, 0, 1, 3),
        DP, split_axis=0, concat_axis=0, tiled=True,
    )[:, :, :hidden]
    returned = returned.transpose(1, 0, 2, 3).reshape(3, n_dp * hidden, -1).astype(f32)
    return (
        output,
        grad_inputs,
        gain_one_own,
        gain_two_own,
        sums[0],
        sums[1],
        sums[2],
        sums[3],
        router_own,
        returned[0].T,
        returned[1].T,
        returned[2],
        expert_gate_gradient,
        expert_up_gradient,
        expert_down_gradient,
    )


def shards(*arguments):
    tokens, expert_gate_matrix = arguments[0], arguments[11]
    n_dp, n_tensor = lax.axis_size(DP), lax.axis_size(TENSOR)
    gathered = n_dp * n_tensor * tokens.shape[0] * tokens.shape[1] * 2
    if n_tensor == 2 and n_dp % 4 == 0 and expert_gate_matrix.shape[0] == 1 and gathered <= 32 << 20:
        return gather_plan(*arguments)
    return exchange_plan(*arguments)


def solution(mesh):
    placed = (
        P((DP, TENSOR), None),
        P((DP, TENSOR)),
        P((DP, TENSOR)),
        P(DP, TENSOR),
        P(DP, TENSOR),
        P(DP, TENSOR),
        P(TENSOR, DP),
        P((DP, TENSOR), None),
        P(DP, TENSOR),
        P(DP, TENSOR),
        P(TENSOR, DP),
        P(DP, None, TENSOR),
        P(DP, None, TENSOR),
        P(DP, TENSOR, None),
        P(DP, None),
        P(DP, None),
        P((DP, TENSOR), None),
    )
    return jax.shard_map(
        shards,
        mesh=mesh,
        in_specs=placed,
        out_specs=(
            P((DP, TENSOR), None),
            P((DP, TENSOR), None),
            P((DP, TENSOR)),
            P((DP, TENSOR)),
            P(DP, TENSOR),
            P(DP, TENSOR),
            P(DP, TENSOR),
            P(TENSOR, DP),
            P((DP, TENSOR), None),
            P(DP, TENSOR),
            P(DP, TENSOR),
            P(TENSOR, DP),
            P(DP, None, TENSOR),
            P(DP, None, TENSOR),
            P(DP, TENSOR, None),
        ),
        check_vma=False,
    )
```

```python
import functools
import math

import jax
import jax.numpy as jnp
from jax import lax
from jax.experimental import pallas as pl
from jax.experimental.pallas import tpu as pltpu
from jax.sharding import PartitionSpec as P

HEAD_SIZE = 128
DP, TENSOR = ("dp", "tensor")


norm_eps = 1e-06
rope_base = 600000.0
neg_big = -1e30


def silu(argument):
    return argument * jax.nn.sigmoid(argument)


def silu_slope(argument):
    sigmoid_of = jax.nn.sigmoid(argument)
    return sigmoid_of * (1.0 + argument * (1.0 - sigmoid_of))


def rotation(sequence_length, head_dim):
    half_dim = head_dim // 2
    frequency = jnp.exp(
        jnp.arange(half_dim, dtype=jnp.float32) * (-2.0 * math.log(rope_base) / head_dim)
    )
    angles = jnp.arange(sequence_length, dtype=jnp.float32)[:, None] * frequency[None, :]
    return (jnp.cos(angles), jnp.sin(angles))


def apply_rotary(tensor, rotary_cosine, rotary_sine):
    half_dim = tensor.shape[-1] // 2
    first_half = tensor[..., :half_dim]
    second_half = tensor[..., half_dim:]
    cos_rows = rotary_cosine[:, None, :]
    sin_rows = rotary_sine[:, None, :]
    return jnp.concatenate(
        [
            first_half * cos_rows - second_half * sin_rows,
            second_half * cos_rows + first_half * sin_rows,
        ],
        axis=-1,
    )


def rotate_back(tensor, rotary_cosine, rotary_sine):
    return apply_rotary(tensor, rotary_cosine, -rotary_sine)


def rms_back(grad_normed, source, scale_rows, gain_full):
    weighted = grad_normed * gain_full
    cubed = scale_rows * scale_rows * scale_rows
    grad_source = scale_rows * weighted - source * cubed * jnp.mean(
        source * weighted, axis=-1, keepdims=True
    )
    grad_gain = jnp.sum(grad_normed * source * scale_rows, axis=0)
    return (grad_source, grad_gain)


def widen(sharded):
    return lax.all_gather(sharded, TENSOR, axis=0, tiled=True)


def narrow(partial_sum):
    return lax.psum_scatter(partial_sum, TENSOR, scatter_dimension=0, tiled=True)


def dense_fetch(
    query_projection,
    key_projection,
    value_projection,
    output_projection,
    shared_gate_matrix,
    shared_up_matrix,
    shared_down_matrix,
):
    return (
        lax.all_gather(query_projection, DP, axis=0, tiled=True),
        lax.all_gather(key_projection, DP, axis=0, tiled=True),
        lax.all_gather(value_projection, DP, axis=0, tiled=True),
        lax.all_gather(output_projection, DP, axis=1, tiled=True),
        lax.all_gather(shared_gate_matrix, DP, axis=0, tiled=True),
        lax.all_gather(shared_up_matrix, DP, axis=0, tiled=True),
        lax.all_gather(shared_down_matrix, DP, axis=1, tiled=True),
    )


def expert_up_output(received_rows, expert_gate_matrix, expert_up_matrix, expert_down_matrix):
    gate_preactivation = jnp.einsum(
        "miwy,iyh->miwh", received_rows, expert_gate_matrix, preferred_element_type=jnp.float32
    )
    up_preactivation = jnp.einsum(
        "miwy,iyh->miwh", received_rows, expert_up_matrix, preferred_element_type=jnp.float32
    )
    hidden = (silu(gate_preactivation) * up_preactivation).astype(jnp.bfloat16)
    produced_rows = jnp.einsum(
        "sxcf,xfd->sxcd", hidden, expert_down_matrix, preferred_element_type=jnp.float32
    ).astype(jnp.bfloat16)
    return (produced_rows, gate_preactivation, up_preactivation)


def expert_gradients(
    received,
    received_gradient,
    gate_preactivation,
    up_preactivation,
    expert_gate_matrix,
    expert_up_matrix,
    expert_down_matrix,
):
    hidden_expert = (silu(gate_preactivation) * up_preactivation).astype(jnp.bfloat16)
    expert_down_gradient = jnp.einsum(
        "sxcf,sxcd->xfd", hidden_expert, received_gradient, preferred_element_type=jnp.float32
    )
    grad_hidden_e = jnp.einsum(
        "sxcd,xfd->sxcf", received_gradient, expert_down_matrix, preferred_element_type=jnp.float32
    )
    grad_gate_e = (grad_hidden_e * up_preactivation * silu_slope(gate_preactivation)).astype(
        jnp.bfloat16
    )
    expert_up_hidden_gradient = (grad_hidden_e * silu(gate_preactivation)).astype(jnp.bfloat16)
    expert_gate_gradient = jnp.einsum(
        "gayi,gayr->air", received, grad_gate_e, preferred_element_type=jnp.float32
    )
    expert_up_gradient = jnp.einsum(
        "gayi,gayr->air", received, expert_up_hidden_gradient, preferred_element_type=jnp.float32
    )
    output_rows_gradient = (
        jnp.einsum(
            "zkjh,klh->zkjl", grad_gate_e, expert_gate_matrix, preferred_element_type=jnp.float32
        )
        + jnp.einsum(
            "zkjh,klh->zkjl",
            expert_up_hidden_gradient,
            expert_up_matrix,
            preferred_element_type=jnp.float32,
        )
    ).astype(jnp.bfloat16)
    return (expert_gate_gradient, expert_up_gradient, expert_down_gradient, output_rows_gradient)


def exchange_plan(
    tokens,
    attention_gain,
    expert_norm_gain,
    query_projection,
    key_projection,
    value_projection,
    output_projection,
    router,
    shared_gate_matrix,
    shared_up_matrix,
    shared_down_matrix,
    expert_gate_matrix,
    expert_up_matrix,
    expert_down_matrix,
    document_lengths,
    expert_indices,
    cotangent,
):
    n_tensor = lax.axis_size(TENSOR)
    n_dp = lax.axis_size(DP)
    tensor_pos = lax.axis_index(TENSOR)
    own_rows = tokens.shape[0]
    sequence_length = own_rows * n_tensor
    model_dim = tokens.shape[1]
    exp_dev = expert_gate_matrix.shape[0]
    experts = exp_dev * n_dp
    top_k = expert_indices.shape[1]
    capacity = max(2, sequence_length * top_k * 4 // (3 * experts))
    slot_total = experts * capacity
    router_full, gain_first, gain_second = (
        lax.all_gather(router, (DP, TENSOR), axis=0, tiled=True),
        lax.all_gather(attention_gain, (DP, TENSOR), axis=0, tiled=True),
        lax.all_gather(expert_norm_gain, (DP, TENSOR), axis=0, tiled=True),
    )
    first_gain = gain_first.astype(jnp.float32)
    second_gain = gain_second.astype(jnp.float32)
    fetched = dense_fetch(
        query_projection,
        key_projection,
        value_projection,
        output_projection,
        shared_gate_matrix,
        shared_up_matrix,
        shared_down_matrix,
    )
    query_all, key_all, value_all, out_all, sgate_all, sup_all, sdown_all = fetched
    input_values = tokens.astype(jnp.float32)
    scale_one = lax.rsqrt(jnp.mean(input_values * input_values, axis=-1, keepdims=True) + norm_eps)
    normed_one = (input_values * scale_one * first_gain).astype(jnp.bfloat16)
    full_one = widen(normed_one)
    q_heads = query_all.shape[1] // HEAD_SIZE
    kv_heads = key_all.shape[1] // HEAD_SIZE
    group_size = q_heads // kv_heads
    rotary_cosine, rotary_sine = rotation(sequence_length, HEAD_SIZE)
    query_unrotated = jnp.dot(full_one, query_all, preferred_element_type=jnp.float32).reshape(
        sequence_length, q_heads, HEAD_SIZE
    )
    key_unrotated = jnp.dot(full_one, key_all, preferred_element_type=jnp.float32).reshape(
        sequence_length, kv_heads, HEAD_SIZE
    )
    rows_of_query = (
        apply_rotary(query_unrotated, rotary_cosine, rotary_sine)
        .astype(jnp.bfloat16)
        .reshape(sequence_length, kv_heads, group_size, HEAD_SIZE)
    )
    key_rows = apply_rotary(key_unrotated, rotary_cosine, rotary_sine).astype(jnp.bfloat16)
    rows_of_value = (
        jnp.dot(full_one, value_all, preferred_element_type=jnp.float32)
        .astype(jnp.bfloat16)
        .reshape(sequence_length, kv_heads, HEAD_SIZE)
    )
    doc_ends = jnp.cumsum(document_lengths[0])
    positions = jnp.arange(sequence_length, dtype=jnp.int32)
    doc_ids = jnp.sum((positions[:, None] >= doc_ends[None, :]).astype(jnp.int32), axis=-1)
    score_scale = HEAD_SIZE ** (-0.5)

    def block_scores(start_row, end_row):
        scores = (
            jnp.einsum(
                "qkgd,skd->kgqs", rows_of_query, key_rows, preferred_element_type=jnp.float32
            )
            * score_scale
        )
        allowed = (doc_ids[start_row:end_row, None] == doc_ids[None, :end_row]) & (
            positions[start_row:end_row, None] >= positions[None, :end_row]
        )
        return (scores, allowed)

    block_index = 0
    start_row = block_index * sequence_length
    end_row = start_row + sequence_length
    scores, allowed = block_scores(start_row, end_row)
    scores = jnp.where(allowed, scores, neg_big)
    row_max = jnp.max(scores, axis=-1, keepdims=True)
    exp_scores = jnp.exp(scores - row_max)
    row_sum = jnp.sum(exp_scores, axis=-1, keepdims=True)
    lse_blocks = [row_max + jnp.log(row_sum)]
    attn_probs = (exp_scores / row_sum).astype(jnp.bfloat16)
    out_blocks = jnp.einsum(
        "kgqs,skd->qkgd", attn_probs, rows_of_value, preferred_element_type=jnp.float32
    )
    mixed_heads = out_blocks.reshape(sequence_length, q_heads * HEAD_SIZE).astype(jnp.bfloat16)
    attn_part = jnp.dot(mixed_heads, out_all, preferred_element_type=jnp.float32)
    residual = input_values + narrow(attn_part)
    scale_two = lax.rsqrt(jnp.mean(residual * residual, axis=-1, keepdims=True) + norm_eps)
    normed_two = (residual * scale_two * second_gain).astype(jnp.bfloat16)
    full_two = widen(normed_two)
    logits = jnp.dot(full_two, router_full, preferred_element_type=jnp.float32)
    chosen = expert_indices[:, :, None] == jnp.arange(experts, dtype=jnp.int32)[None, None, :]
    selected = jnp.sum(jnp.where(chosen, logits[:, None, :], 0.0), axis=-1)
    top_max = jnp.max(selected, axis=-1, keepdims=True)
    gate_exp = jnp.exp(selected - top_max)
    gate_probs = gate_exp / jnp.sum(gate_exp, axis=-1, keepdims=True)
    gate_shared = jnp.dot(full_two, sgate_all, preferred_element_type=jnp.float32)
    up_shared = jnp.dot(full_two, sup_all, preferred_element_type=jnp.float32)
    hidden_shared = (silu(gate_shared) * up_shared).astype(jnp.bfloat16)
    shared_part = jnp.dot(hidden_shared, sdown_all, preferred_element_type=jnp.float32)
    flat_ids = expert_indices.reshape(-1)
    onehot = (flat_ids[:, None] == jnp.arange(experts, dtype=jnp.int32)[None, :]).astype(jnp.int32)
    slot_rank = jnp.sum(onehot * (jnp.cumsum(onehot, axis=0) - 1), axis=-1)
    slot_index = flat_ids * capacity + slot_rank
    pair_index = jnp.arange(sequence_length * top_k, dtype=jnp.int32)
    token_of_slot = jnp.zeros((slot_total,), jnp.int32).at[slot_index].set(pair_index // top_k)
    slot_used = jnp.zeros((slot_total,), jnp.bool_).at[slot_index].set(True)
    gate_of_slot = jnp.zeros((slot_total,), jnp.float32).at[slot_index].set(gate_probs.reshape(-1))
    outgoing = jnp.where(slot_used[:, None], full_two[token_of_slot], 0).reshape(
        n_dp, exp_dev, capacity, model_dim
    )
    received_rows = lax.all_to_all(outgoing, DP, split_axis=0, concat_axis=0, tiled=True)
    produced_rows, gate_preactivation, up_preactivation = expert_up_output(
        received_rows, expert_gate_matrix, expert_up_matrix, expert_down_matrix
    )
    sent_home = lax.all_to_all(produced_rows, DP, split_axis=0, concat_axis=0, tiled=True)
    returned, received, gate_preactivation, up_preactivation = (
        sent_home,
        received_rows,
        gate_preactivation,
        up_preactivation,
    )
    picked = returned.reshape(slot_total, model_dim)[slot_index].reshape(
        sequence_length, top_k, model_dim
    )
    routed_part = jnp.einsum("sk,skd->sd", gate_probs, picked, preferred_element_type=jnp.float32)
    ffn_own = narrow(shared_part + routed_part)
    output = (residual + ffn_own).astype(jnp.bfloat16)
    weights_back = dense_fetch(
        query_projection,
        key_projection,
        value_projection,
        output_projection,
        shared_gate_matrix,
        shared_up_matrix,
        shared_down_matrix,
    )
    query_back, key_back, value_back, out_back, sgate_back, sup_back, sdown_back = weights_back
    grad_out = cotangent.astype(jnp.float32)
    grad_ffn = widen(cotangent)
    grad_hidden_sh = jnp.dot(grad_ffn, sdown_back.T, preferred_element_type=jnp.float32)
    grad_sdown = jnp.dot(hidden_shared.T, grad_ffn, preferred_element_type=jnp.float32)
    grad_gate_sh = (grad_hidden_sh * up_shared * silu_slope(gate_shared)).astype(jnp.bfloat16)
    grad_up_sh = (grad_hidden_sh * silu(gate_shared)).astype(jnp.bfloat16)
    grad_sgate = jnp.dot(full_two.T, grad_gate_sh, preferred_element_type=jnp.float32)
    grad_sup = jnp.dot(full_two.T, grad_up_sh, preferred_element_type=jnp.float32)
    grad_normed_part = jnp.dot(
        grad_gate_sh, sgate_back.T, preferred_element_type=jnp.float32
    ) + jnp.dot(grad_up_sh, sup_back.T, preferred_element_type=jnp.float32)
    grad_gates_part = jnp.einsum("sd,skd->sk", grad_ffn, picked, preferred_element_type=jnp.float32)
    grad_slot = (
        jnp.where(slot_used[:, None], grad_ffn[token_of_slot] * gate_of_slot[:, None], 0.0)
        .astype(jnp.bfloat16)
        .reshape(n_dp, exp_dev, capacity, model_dim)
    )
    received_gradient = lax.all_to_all(grad_slot, DP, split_axis=0, concat_axis=0, tiled=True)
    expert_gate_gradient, expert_up_gradient, expert_down_gradient, output_rows_gradient = (
        expert_gradients(
            received,
            received_gradient,
            gate_preactivation,
            up_preactivation,
            expert_gate_matrix,
            expert_up_matrix,
            expert_down_matrix,
        )
    )
    grad_returned = lax.all_to_all(
        output_rows_gradient, DP, split_axis=0, concat_axis=0, tiled=True
    )
    grad_picked = grad_returned.reshape(slot_total, model_dim)[slot_index].reshape(
        sequence_length, top_k, model_dim
    )
    grad_normed_part = grad_normed_part + jnp.sum(grad_picked, axis=1, dtype=jnp.float32)
    grad_normed_two, grad_gates = (
        lax.psum_scatter(
            grad_normed_part.astype(jnp.bfloat16), TENSOR, scatter_dimension=0, tiled=True
        ).astype(jnp.float32),
        lax.psum_scatter(
            grad_gates_part.astype(jnp.bfloat16), TENSOR, scatter_dimension=0, tiled=True
        ).astype(jnp.float32),
    )
    row_start = tensor_pos * own_rows
    gates_own = lax.dynamic_slice_in_dim(gate_probs, row_start, own_rows, 0)
    chosen_own = lax.dynamic_slice_in_dim(chosen, row_start, own_rows, 0)
    grad_selected = gates_own * (
        grad_gates - jnp.sum(gates_own * grad_gates, axis=-1, keepdims=True)
    )
    grad_logits = jnp.sum(jnp.where(chosen_own, grad_selected[:, :, None], 0.0), axis=1).astype(
        jnp.bfloat16
    )
    grad_normed_two = grad_normed_two + jnp.dot(
        grad_logits, router_full.T, preferred_element_type=jnp.float32
    )
    grad_router_part = jnp.dot(normed_two.T, grad_logits, preferred_element_type=jnp.float32)
    grad_residual, grad_gain_two = rms_back(grad_normed_two, residual, scale_two, second_gain)
    grad_residual = grad_residual + grad_out
    grad_attn = widen(grad_residual.astype(jnp.bfloat16))
    grad_wout = jnp.dot(mixed_heads.T, grad_attn, preferred_element_type=jnp.float32)
    grad_mixed = (
        jnp.dot(grad_attn, out_back.T, preferred_element_type=jnp.float32)
        .astype(jnp.bfloat16)
        .reshape(sequence_length, kv_heads, group_size, HEAD_SIZE)
    )
    grad_keys = jnp.zeros((sequence_length, kv_heads, HEAD_SIZE), jnp.float32)
    grad_values = jnp.zeros((sequence_length, kv_heads, HEAD_SIZE), jnp.float32)
    block_index = 0
    start_row = block_index * sequence_length
    end_row = start_row + sequence_length
    scores, allowed = block_scores(start_row, end_row)
    attn_probs = jnp.where(allowed, jnp.exp(scores - lse_blocks[block_index]), 0.0)
    probs_low = attn_probs.astype(jnp.bfloat16)
    grad_values = grad_values.at[:end_row].add(
        jnp.einsum("kgqs,qkgd->skd", probs_low, grad_mixed, preferred_element_type=jnp.float32)
    )
    grad_probs = jnp.einsum(
        "qkgd,skd->kgqs", grad_mixed, rows_of_value, preferred_element_type=jnp.float32
    )
    inner_sum = jnp.sum(attn_probs * grad_probs, axis=-1, keepdims=True)
    grad_scores = (attn_probs * (grad_probs - inner_sum)).astype(jnp.bfloat16)
    grad_query_blocks = (
        jnp.einsum("kgqs,skd->qkgd", grad_scores, key_rows, preferred_element_type=jnp.float32)
        * score_scale
    )
    grad_keys = grad_keys.at[:end_row].add(
        jnp.einsum("kgqs,qkgd->skd", grad_scores, rows_of_query, preferred_element_type=jnp.float32)
        * score_scale
    )
    grad_query = grad_query_blocks.reshape(sequence_length, q_heads, HEAD_SIZE)
    grad_q_raw = (
        rotate_back(grad_query, rotary_cosine, rotary_sine)
        .astype(jnp.bfloat16)
        .reshape(sequence_length, q_heads * HEAD_SIZE)
    )
    grad_k_raw = (
        rotate_back(grad_keys, rotary_cosine, rotary_sine)
        .astype(jnp.bfloat16)
        .reshape(sequence_length, kv_heads * HEAD_SIZE)
    )
    grad_v_low = grad_values.astype(jnp.bfloat16).reshape(sequence_length, kv_heads * HEAD_SIZE)
    grad_wquery = jnp.dot(full_one.T, grad_q_raw, preferred_element_type=jnp.float32)
    grad_wkey = jnp.dot(full_one.T, grad_k_raw, preferred_element_type=jnp.float32)
    grad_wvalue = jnp.dot(full_one.T, grad_v_low, preferred_element_type=jnp.float32)
    grad_normed_one_part = (
        jnp.dot(grad_q_raw, query_back.T, preferred_element_type=jnp.float32)
        + jnp.dot(grad_k_raw, key_back.T, preferred_element_type=jnp.float32)
        + jnp.dot(grad_v_low, value_back.T, preferred_element_type=jnp.float32)
    )
    grad_normed_one = narrow(grad_normed_one_part)
    grad_inputs, grad_gain_one = rms_back(grad_normed_one, input_values, scale_one, first_gain)
    grad_inputs = grad_inputs + grad_residual
    dense_sums = (
        lax.psum_scatter(grad_wquery, DP, scatter_dimension=0, tiled=True),
        lax.psum_scatter(grad_wkey, DP, scatter_dimension=0, tiled=True),
        lax.psum_scatter(grad_wvalue, DP, scatter_dimension=0, tiled=True),
        lax.psum_scatter(grad_wout, DP, scatter_dimension=1, tiled=True),
        lax.psum_scatter(grad_sgate, DP, scatter_dimension=0, tiled=True),
        lax.psum_scatter(grad_sup, DP, scatter_dimension=0, tiled=True),
        lax.psum_scatter(grad_sdown, DP, scatter_dimension=1, tiled=True),
    )
    small_sums = (
        lax.psum_scatter(grad_router_part, (DP, TENSOR), scatter_dimension=0, tiled=True),
        lax.psum_scatter(grad_gain_one, (DP, TENSOR), scatter_dimension=0, tiled=True),
        lax.psum_scatter(grad_gain_two, (DP, TENSOR), scatter_dimension=0, tiled=True),
    )
    return (
        output,
        grad_inputs,
        small_sums[1],
        small_sums[2],
        dense_sums[0],
        dense_sums[1],
        dense_sums[2],
        dense_sums[3],
        small_sums[0],
        dense_sums[4],
        dense_sums[5],
        dense_sums[6],
        expert_gate_gradient,
        expert_up_gradient,
        expert_down_gradient,
    )


MESH = pl.DeviceIdType.MESH
ANY = pl.BlockSpec(memory_space=pl.ANY)


def when(condition, body):
    if condition is None:
        body()
    else:
        pl.when(condition)(body)


class Spot:
    def __init__(self, n_planes):
        dp = lax.axis_index(DP)
        self.x = lax.axis_index(TENSOR)
        self.dp = dp
        self.core = dp % 2
        self.y = (dp // 2) % 2
        self.z = dp // 4
        self.n_planes = n_planes
        self.has_up = self.z < n_planes - 1
        self.has_down = self.z > 0
        self.up = (dp + 4, self.x)
        self.down = (dp - 4, self.x)
        self.side = (dp + 2 - 4 * self.y, self.x)
        self.across = (dp, 1 - self.x)
        self.twin = (dp + 1 - 2 * self.core, self.x)

    def far_first(self):
        low, high = 0 * self.z, 0 * self.z + self.n_planes - 1
        order = []
        for _ in range(self.n_planes):
            take_low = (self.z - low >= high - self.z).astype(jnp.int32)
            order.append(take_low * low + (1 - take_low) * high)
            low, high = low + take_low, high - (1 - take_low)
        return order

    def greet(self):
        barrier = pltpu.get_barrier_semaphore()
        fixed = [self.side, self.twin, self.across]
        for device in fixed:
            pl.semaphore_signal(barrier, inc=1, device_id=device, device_id_type=MESH)
        for condition, device in ((self.has_up, self.up), (self.has_down, self.down)):

            @pl.when(condition)
            def _(device=device):
                pl.semaphore_signal(barrier, inc=1, device_id=device, device_id_type=MESH)

        ends = self.has_up.astype(jnp.int32) + self.has_down.astype(jnp.int32)
        pl.semaphore_wait(barrier, len(fixed) + ends)


class Copies:
    def __init__(self, n_planes, send, recv):
        self.n_planes, self.send, self.recv = n_planes, send, recv
        self.open = []

    def copy(self, group, s, piece, src, dst, device, arrival=None):
        arrival = group if arrival is None else arrival
        return pltpu.make_async_remote_copy(
            src_ref=src,
            dst_ref=dst,
            send_sem=self.send.at[group * self.n_planes + s, piece],
            recv_sem=self.recv.at[arrival * self.n_planes + s, piece],
            device_id=device,
            device_id_type=MESH,
        )

    def start(self, condition, group, s, sources, targets, device, arrival=None):
        def body():
            for i, (src, dst) in enumerate(zip(sources, targets)):
                self.copy(group, s, i, src, dst, device, arrival).start()

        when(condition, body)
        self.open.append((condition, group, s, sources, targets, device, arrival))

    def arrive(self, group, s, targets, device):
        for i, dst in enumerate(targets):
            self.copy(group, s, i, dst, dst, device).wait_recv()

    def close(self):
        for condition, group, s, sources, targets, device, arrival in self.open:

            def body():
                for i, (src, dst) in enumerate(zip(sources, targets)):
                    self.copy(group, s, i, src, dst, device, arrival).wait_send()

            when(condition, body)


(Z_UP, Z_DOWN, Y_ALL, Y_HALF, X_ALL, X_HALF, C_OWN, C_Y, C_X, C_XH, C_YH) = range(11)
(ALL, FIRST, SECOND) = range(3)


class Spread:
    def __init__(self, spot, copies, own, views, use_x):
        self.spot, self.copies, self.own, self.use_x = spot, copies, own, use_x
        self.order = spot.far_first()[::-1]
        y, x, core = spot.y, spot.x, spot.core

        def places(s, cc):
            return (
                views(s, y, cc, x, ALL),
                views(s, 1 - y, cc, x, ALL),
                views(s, 1 - y, cc, x, FIRST),
                views(s, y, cc, 1 - x, ALL),
                views(s, y, cc, 1 - x, SECOND),
                views(s, 1 - y, cc, 1 - x, FIRST),
                views(s, 1 - y, cc, 1 - x, SECOND),
            )

        self.mine = [places(s, core) for s in self.order]
        self.twins = [places(s, 1 - core) for s in self.order]
        self.goes_down = [(s > spot.z) & spot.has_down for s in self.order]
        self.goes_up = [(s < spot.z) & spot.has_up for s in self.order]

    def onward(self, j, sources):
        s, here, spot, start = self.order[j], self.mine[j][0], self.spot, self.copies.start
        start(None, Y_ALL, s, sources, here, spot.side)
        if self.use_x:
            start(None, X_ALL, s, sources, here, spot.across)
        start(None, C_OWN, s, sources, here, spot.twin)

    def begin(self):
        spot, here = self.spot, self.mine[0][0]
        self.copies.start(spot.has_up, Z_UP, spot.z, self.own, here, spot.up)
        self.copies.start(spot.has_down, Z_DOWN, spot.z, self.own, here, spot.down, Z_UP)
        self.onward(0, self.own)

    def relay(self, j, goes=None):
        s, here, spot = self.order[j], self.mine[j][0], self.spot
        goes_down, goes_up = goes or (self.goes_down[j], self.goes_up[j])
        self.copies.arrive(Z_UP, s, here, spot.up)
        self.copies.start(goes_down, Z_DOWN, s, here, here, spot.down, Z_UP)
        self.copies.start(goes_up, Z_UP, s, here, here, spot.up)

    def column(self, j):
        if j < len(self.order):
            self.relay(j)
            self.onward(j, self.mine[j][0])

    def side(self, j):
        s, (_, there, part, *_), spot = self.order[j], self.mine[j], self.spot
        self.copies.arrive(Y_ALL, s, there, spot.side)
        if self.use_x:
            self.copies.start(None, X_HALF, s, part, part, spot.across)
        self.copies.start(None, C_Y, s, there, there, spot.twin)

    def across(self, j):
        s, (_, _, _, there, part, *_), spot = self.order[j], self.mine[j], self.spot
        self.copies.arrive(X_ALL, s, there, spot.across)
        self.copies.start(None, Y_HALF, s, part, part, spot.side)
        self.copies.start(None, C_X, s, there, there, spot.twin)

    def sides(self, j):
        if 0 <= j < len(self.order):
            self.side(j)
            if self.use_x:
                self.across(j)

    def corner(self, j):
        if not self.use_x or not 0 <= j < len(self.order):
            return
        s, (_, _, _, _, _, first, second), spot = self.order[j], self.mine[j], self.spot
        self.copies.arrive(X_HALF, s, first, spot.across)
        self.copies.start(None, C_XH, s, first, first, spot.twin)
        self.copies.arrive(Y_HALF, s, second, spot.side)
        self.copies.start(None, C_YH, s, second, second, spot.twin)

    def twin_near(self, j):
        s, there, spot = self.order[j], self.twins[j], self.spot
        self.copies.arrive(C_OWN, s, there[0], spot.twin)
        if self.use_x:
            self.copies.arrive(C_X, s, there[3], spot.twin)

    def twin_far(self, j):
        s, there, spot = self.order[j], self.twins[j], self.spot
        self.copies.arrive(C_Y, s, there[1], spot.twin)
        if self.use_x:
            self.copies.arrive(C_XH, s, there[5], spot.twin)
            self.copies.arrive(C_YH, s, there[6], spot.twin)

    def twin_all(self):
        for j in range(len(self.order)):
            self.twin_near(j)
            self.twin_far(j)

    def stage(self, step):
        self.column(step)
        self.sides(step - 1)
        self.corner(step - 2)

    def run(self):
        self.begin()
        for step in range(1, len(self.order) + 2):
            self.stage(step)
        self.twin_all()
        self.copies.close()


def dp_of(s, yy, cc):
    return (s * 2 + yy) * 2 + cc


def fetch_kernel(n_planes, axes, *refs):
    n = len(axes)
    ins, (tokens, small, grads), outs = refs[:n], refs[n : n + 3], refs[n + 3 : 2 * n + 3]
    sequence, smalls, all_grads = refs[2 * n + 3 : 2 * n + 6]
    send, recv, local, x_send, x_recv, g_send, g_recv = refs[2 * n + 6 :]
    spot = Spot(n_planes)

    def views(s, yy, cc, xx, part):
        i = dp_of(s, yy, cc)
        places = []
        for o, a, axis in zip(outs, ins, axes):
            size = a.shape[axis]
            span = pl.ds(pl.multiple_of(i * size, size), size)
            places.append(o.at[span] if axis == 0 else o.at[:, span])
        return places + [smalls.at[xx, i]]

    sources = list(ins) + [small]
    mine = views(spot.z, spot.y, spot.core, spot.x, ALL)
    own = [pltpu.make_async_copy(a, v, local.at[i]) for i, (a, v) in enumerate(zip(sources, mine))]
    own.append(pltpu.make_async_copy(tokens, sequence.at[spot.x], local.at[n + 1]))
    own.append(pltpu.make_async_copy(grads, all_grads.at[spot.dp * 2 + spot.x], local.at[n + 2]))
    half = grads.shape[0] // 2

    def grad_views(s, yy, cc, xx, part):
        b = dp_of(s, yy, cc) * 2 + xx
        if part == ALL:
            return [all_grads.at[b]]
        return [all_grads.at[b, pl.ds(0 if part == FIRST else half, half)]]

    for c in own:
        c.start()
    spot.greet()

    def across(i, src, dst):
        return pltpu.make_async_remote_copy(
            src_ref=src, dst_ref=dst, send_sem=x_send.at[i], recv_sem=x_recv.at[i],
            device_id=spot.across, device_id_type=MESH,
        )

    across(0, tokens, sequence.at[spot.x]).start()
    copies = Copies(n_planes, send, recv)
    weights = Spread(spot, copies, sources, views, False)
    gradients = Spread(spot, Copies(n_planes, g_send, g_recv), [grads], grad_views, True)
    weights.begin()
    gradients.begin()
    for step in range(1, n_planes + 2):
        weights.stage(step)
        gradients.stage(step)
    weights.twin_all()
    gradients.twin_all()
    weights.copies.close()
    gradients.copies.close()
    for c in own:
        c.wait()
    across(1, smalls.at[spot.x], smalls.at[spot.x]).start()
    across(0, tokens, sequence.at[spot.x]).wait_send()
    across(1, smalls.at[spot.x], smalls.at[spot.x]).wait_send()
    across(0, sequence.at[1 - spot.x], sequence.at[1 - spot.x]).wait_recv()
    across(1, smalls.at[1 - spot.x], smalls.at[1 - spot.x]).wait_recv()


def fetch(arrays, axes, tokens, small, grads, n_dp, collective_id):
    n, n_planes = len(arrays), n_dp // 4
    sems = (11 * n_planes, n + 1)

    def whole(a, axis):
        shape = list(a.shape)
        shape[axis] *= n_dp
        return jax.ShapeDtypeStruct(tuple(shape), a.dtype)

    return pl.pallas_call(
        functools.partial(fetch_kernel, n_planes, axes),
        out_shape=[whole(a, axis) for a, axis in zip(arrays, axes)]
        + [
            jax.ShapeDtypeStruct((2,) + tokens.shape, tokens.dtype),
            jax.ShapeDtypeStruct((2, n_dp) + small.shape, small.dtype),
            jax.ShapeDtypeStruct((2 * n_dp,) + grads.shape, grads.dtype),
        ],
        in_specs=[ANY] * (n + 3),
        out_specs=[ANY] * (n + 3),
        scratch_shapes=[
            pltpu.SemaphoreType.DMA(sems),
            pltpu.SemaphoreType.DMA(sems),
            pltpu.SemaphoreType.DMA((n + 3,)),
            pltpu.SemaphoreType.DMA((2,)),
            pltpu.SemaphoreType.DMA((2,)),
            pltpu.SemaphoreType.DMA((11 * n_planes, 1)),
            pltpu.SemaphoreType.DMA((11 * n_planes, 1)),
        ],
        compiler_params=pltpu.CompilerParams(collective_id=collective_id, has_side_effects=True),
    )(*arrays, tokens, small, grads)


(T_YX, T_Y, T_X, T_OWN, R_XHALF, R_YHALF, R_YALL, R_XALL, R_UP, R_DOWN) = range(10)


def add_up(target, sources):
    rows = target.shape[0]
    step = 16 if rows % 16 == 0 else rows

    def body(i, carry):
        span = pl.ds(pl.multiple_of(i * step, step), step)
        total = sources[0][span, :].astype(jnp.float32)
        for source in sources[1:]:
            total = total + source[span, :].astype(jnp.float32)
        target[span, :] = total.astype(target.dtype)
        return carry

    lax.fori_loop(0, rows // step, body, 0)


class Reduce:
    @staticmethod
    def scratch(shapes, dtypes, n_planes, use_x):
        n = len(shapes)
        kinds = 4 if use_x else 2
        out = []
        for i, (shape, dtype) in enumerate(zip(shapes, dtypes)):
            half = (shape[0] // 2, shape[1]) if i == 0 else shape
            out.append(pltpu.VMEM((kinds, n_planes) + shape, dtype))
            out.append(pltpu.VMEM((kinds, n_planes) + shape, dtype))
            out.append(pltpu.VMEM((n_planes,) + shape, dtype))
            out.append(pltpu.VMEM((n_planes,) + shape, dtype))
            out.append(pltpu.VMEM((n_planes,) + shape, dtype))
            if use_x:
                out.append(pltpu.VMEM((n_planes,) + shape, dtype))
                out.append(pltpu.VMEM((n_planes,) + half, dtype))
                out.append(pltpu.VMEM((n_planes,) + (half if i == 0 else (8, 128)), dtype))
        sems = (10 * n_planes, n)
        out.append(pltpu.SemaphoreType.DMA(sems))
        out.append(pltpu.SemaphoreType.DMA(sems))
        out.append(pltpu.SemaphoreType.DMA((kinds * n_planes, n)))
        return out

    @staticmethod
    def n_scratch(n, use_x):
        return n * (8 if use_x else 5) + 3

    def __init__(self, spot, blocks, outs, scratch, use_x):
        self.spot, self.outs, self.use_x = spot, outs, use_x
        self.n, self.n_planes = len(outs), spot.n_planes
        per = 8 if use_x else 5
        send, recv, self.local = scratch[self.n * per :]
        sets = [scratch[i * per : (i + 1) * per] for i in range(self.n)]
        self.mine = [s[0] for s in sets]
        self.twin = [s[1] for s in sets]
        self.above = [s[2] for s in sets]
        self.below = [s[3] for s in sets]
        self.near = [s[4] for s in sets]
        self.across = [s[5] for s in sets] if use_x else None
        self.first = [s[6] for s in sets] if use_x else None
        self.second = sets[0][7] if use_x else None
        self.half = sets[0][0].shape[2] // 2
        self.copies = Copies(self.n_planes, send, recv)
        y, x, core = spot.y, spot.x, spot.core
        self.order = spot.far_first()
        places = {T_YX: (1 - y, 1 - x), T_Y: (1 - y, x), T_X: (y, 1 - x), T_OWN: (y, x)}
        self.kinds = [T_YX, T_Y, T_X, T_OWN] if use_x else [T_Y, T_OWN]
        self.terms = {(k, j): blocks(s, places[k][0], core, places[k][1]) for k in self.kinds for j, s in enumerate(self.order)}
        self.others = {(k, j): blocks(s, places[k][0], 1 - core, places[k][1]) for k in self.kinds for j, s in enumerate(self.order)}

    def load(self, kind, j):
        k = self.kinds.index(kind)
        s = self.order[j]
        return [
            pltpu.make_async_copy(ref, self.mine[i].at[k, s], self.local.at[k * self.n_planes + s, i])
            for i, ref in enumerate(self.terms[kind, j])
        ]

    def start_loads(self):
        for j in range(self.n_planes):
            for kind in self.kinds:
                for c in self.load(kind, j):
                    c.start()

    def start_twins(self):
        for j in range(self.n_planes):
            s = self.order[j]
            for k, kind in enumerate(self.kinds):
                self.copies.start(None, kind, s, self.others[kind, j], [t.at[k, s] for t in self.twin], self.spot.twin)

    def ready(self, kind, j):
        k, s = self.kinds.index(kind), self.order[j]
        for c in self.load(kind, j):
            c.wait()
        self.copies.arrive(kind, s, [t.at[k, s] for t in self.twin], self.spot.twin)
        return [m.at[k, s] for m in self.mine], [t.at[k, s] for t in self.twin]

    def corner(self, j):
        if not self.use_x or not 0 <= j < self.n_planes:
            return
        s, half = self.order[j], self.half
        mine, twin = self.ready(T_YX, j)
        for m, t in zip(mine, twin):
            add_up(m, [m, t])
        head = [mine[0].at[pl.ds(0, half)]] + mine[1:]
        self.copies.start(None, R_XHALF, s, head, [f.at[s] for f in self.first], self.spot.across)
        tail = [mine[0].at[pl.ds(half, half)]]
        self.copies.start(None, R_YHALF, s, tail, [self.second.at[s]], self.spot.side)

    def side(self, j):
        s, half = self.order[j], self.half
        mine, twin = self.ready(T_Y, j)
        if self.use_x:
            first = [f.at[s] for f in self.first]
            self.copies.arrive(R_XHALF, s, first, self.spot.across)
        for i, (m, t) in enumerate(zip(mine, twin)):
            if not self.use_x:
                add_up(m, [m, t])
            elif i == 0:
                a, b = pl.ds(0, half), pl.ds(half, half)
                add_up(m.at[a], [m.at[a], t.at[a], first[0]])
                add_up(m.at[b], [m.at[b], t.at[b]])
            else:
                add_up(m, [m, t, first[i]])
        self.copies.start(None, R_YALL, s, mine, [t.at[s] for t in self.near], self.spot.side)

    def over(self, j):
        s, half = self.order[j], self.half
        mine, twin = self.ready(T_X, j)
        second = self.second.at[s]
        self.copies.arrive(R_YHALF, s, [second], self.spot.side)
        for i, (m, t) in enumerate(zip(mine, twin)):
            if i == 0:
                a, b = pl.ds(0, half), pl.ds(half, half)
                add_up(m.at[a], [m.at[a], t.at[a]])
                add_up(m.at[b], [m.at[b], t.at[b], second])
            else:
                add_up(m, [m, t])
        self.copies.start(None, R_XALL, s, mine, [t.at[s] for t in self.across], self.spot.across)

    def sides(self, j):
        if 0 <= j < self.n_planes:
            self.side(j)
            if self.use_x:
                self.over(j)

    def column(self, j):
        if not 0 <= j < self.n_planes:
            return
        s, spot, copies, n = self.order[j], self.spot, self.copies, self.n
        mine, twin = self.ready(T_OWN, j)
        near = [t.at[s] for t in self.near]
        copies.arrive(R_YALL, s, near, spot.side)
        here = [[m, t, a] for m, t, a in zip(mine, twin, near)]
        if self.use_x:
            across = [t.at[s] for t in self.across]
            copies.arrive(R_XALL, s, across, spot.across)
            here = [h + [a] for h, a in zip(here, across)]
        above = [t.at[s] for t in self.above]
        below = [t.at[s] for t in self.below]

        def add_all(targets, *more):
            for i in range(n):
                add_up(targets[i], here[i] + [m[i] for m in more])

        if j == self.n_planes - 1:
            when(spot.has_up, lambda: copies.arrive(R_DOWN, s, above, spot.up))
            when(spot.has_down, lambda: copies.arrive(R_UP, s, below, spot.down))
            when(spot.has_up & spot.has_down, lambda: add_all(self.outs, above, below))
            when(spot.z == 0, lambda: add_all(self.outs, above))
            when(spot.z == self.n_planes - 1, lambda: add_all(self.outs, below))
            return
        for goes, more, group, buffers, device, source in (
            (s < spot.z, spot.has_up, R_DOWN, above, spot.down, spot.up),
            (s > spot.z, spot.has_down, R_UP, below, spot.up, spot.down),
        ):

            def partial():
                copies.arrive(group, s, buffers, source)
                add_all(mine, buffers)

            when(goes & more, partial)
            when(goes & jnp.logical_not(more), lambda: add_all(mine))
            copies.start(goes, group, s, mine, buffers, device)

    def stage(self, step):
        self.corner(step)
        self.sides(step - 1)
        self.column(step - 2)

    def close(self):
        self.copies.close()


def sum_kernel(n_planes, n, *refs):
    ins, outs, scratch = refs[:n], refs[n : 2 * n], refs[2 * n :]
    spot = Spot(n_planes)

    def blocks(s, yy, cc, xx):
        return [a.at[dp_of(s, yy, cc) * 2 + xx] for a in ins]

    net = Reduce(spot, blocks, outs, scratch, True)
    net.start_loads()
    spot.greet()
    net.start_twins()
    for step in range(n_planes + 2):
        net.stage(step)
    net.close()


def sum_everywhere(arrays, out_dtypes, n_dp, collective_id):
    n, n_planes = len(arrays), n_dp // 4
    shapes = [a.shape[1:] for a in arrays]
    return pl.pallas_call(
        functools.partial(sum_kernel, n_planes, n),
        out_shape=[jax.ShapeDtypeStruct(s, t) for s, t in zip(shapes, out_dtypes)],
        in_specs=[ANY] * n,
        out_specs=[pl.BlockSpec(memory_space=pltpu.VMEM)] * n,
        scratch_shapes=Reduce.scratch(shapes, [a.dtype for a in arrays], n_planes, True),
        compiler_params=pltpu.CompilerParams(
            collective_id=collective_id, has_side_effects=True, vmem_limit_bytes=56 << 20
        ),
    )(*arrays)


def return_kernel(n_planes, axes, *refs):
    n = len(axes)
    ins, parts, outs, out_sum = refs[:n], refs[n], refs[n + 1 : 2 * n + 1], refs[2 * n + 1]
    scratch, (tile_sum, tile_in, x_send, x_recv) = refs[2 * n + 2 : -4], refs[-4:]
    spot = Spot(n_planes)

    def blocks(s, yy, cc, xx):
        i = dp_of(s, yy, cc)
        places = []
        for j, (a, o, axis) in enumerate(zip(ins, outs, axes)):
            size = o.shape[axis] * (2 if j == n - 1 else 1)
            span = pl.ds(pl.multiple_of(i * size, size), size)
            places.append(a.at[span] if axis == 0 else a.at[:, span])
        return places

    cut = Reduce.n_scratch(n, False)
    weights = Reduce(spot, blocks, list(outs[:-1]) + [tile_sum], scratch[:cut], False)
    tokens = Reduce(
        spot, lambda s, yy, cc, xx: [parts.at[dp_of(s, yy, cc) * 2 + xx]], [out_sum], scratch[cut:], True
    )
    weights.start_loads()
    tokens.start_loads()
    spot.greet()
    weights.start_twins()
    tokens.start_twins()
    for step in range(n_planes + 2):
        weights.sides(step)
        tokens.corner(step)
        tokens.sides(step - 1)
        weights.column(step - 1)
        tokens.column(step - 2)
    rows = tile_in.shape[0]
    swap = pltpu.make_async_remote_copy(
        src_ref=tile_sum.at[pl.ds(pl.multiple_of((1 - spot.x) * rows, rows), rows)], dst_ref=tile_in,
        send_sem=x_send, recv_sem=x_recv, device_id=spot.across, device_id_type=MESH,
    )
    swap.start()
    swap.wait()
    outs[-1][...] = tile_sum[pl.ds(pl.multiple_of(spot.x * rows, rows), rows), :] + tile_in[...]
    weights.close()
    tokens.close()


def sum_back(arrays, axes, parts, n_dp, collective_id):
    n, n_planes = len(arrays), n_dp // 4

    def part(a, axis):
        shape = list(a.shape)
        shape[axis] //= n_dp
        return tuple(shape)

    shapes = [part(a, axis) for a, axis in zip(arrays, axes)]
    tile = (shapes[-1][0] // 2, shapes[-1][1])
    block = parts.shape[1:]
    return pl.pallas_call(
        functools.partial(return_kernel, n_planes, axes),
        out_shape=[jax.ShapeDtypeStruct(s, jnp.float32) for s in shapes[:-1] + [tile, block]],
        in_specs=[ANY] * (n + 1),
        out_specs=[pl.BlockSpec(memory_space=pltpu.VMEM)] * (n + 1),
        scratch_shapes=Reduce.scratch(shapes, [a.dtype for a in arrays], n_planes, False)
        + Reduce.scratch([block], [parts.dtype], n_planes, True)
        + [
            pltpu.VMEM(shapes[-1], jnp.float32),
            pltpu.VMEM(tile, jnp.float32),
            pltpu.SemaphoreType.DMA(()),
            pltpu.SemaphoreType.DMA(()),
        ],
        compiler_params=pltpu.CompilerParams(
            collective_id=collective_id, has_side_effects=True, vmem_limit_bytes=60 << 20
        ),
    )(*arrays, parts)
UNIT = 2


def dot_t(a, b):
    return lax.dot_general(a, b, (((1,), (1,)), ((), ())), preferred_element_type=jnp.float32)


def dot_f32(a, b):
    return lax.dot_general(a, b, (((1,), (0,)), ((), ())), preferred_element_type=jnp.float32)


class ExpertWork:
    def __init__(self, expert, weights, scratch):
        self.expert = expert
        self.w_gate, self.w_up, self.w_down, self.shared = weights
        (
            self.tokens, self.grads, self.rows, self.grad_rows, self.hidden, self.pre, self.left_out,
            self.left_grad, self.right_out, self.right_grad, self.out, self.back, self.shared_hidden,
        ) = scratch

    @staticmethod
    def scratch(model, width, capacity, own_rows):
        bf16 = jnp.bfloat16
        seq = 2 * own_rows
        return [
            pltpu.VMEM((2, 2 * UNIT, own_rows, model), bf16),
            pltpu.VMEM((2, 2 * UNIT, own_rows, model), bf16),
            pltpu.VMEM((2, UNIT * capacity, model), bf16),
            pltpu.VMEM((2, UNIT * capacity, model), bf16),
            pltpu.VMEM((2, 3, UNIT * capacity, width), bf16),
            pltpu.VMEM((3, UNIT * capacity, width), jnp.float32),
            pltpu.VMEM((UNIT, seq, capacity + 128), bf16),
            pltpu.VMEM((UNIT, seq, capacity + 256), bf16),
            pltpu.VMEM((UNIT, capacity + 128, model), bf16),
            pltpu.VMEM((UNIT, capacity + 256, model), bf16),
            pltpu.VMEM((2, 2 * UNIT, own_rows, model), bf16),
            pltpu.VMEM((2, 2 * UNIT, own_rows, model), bf16),
            pltpu.VMEM((2, UNIT * seq, 384), bf16),
        ]

    def prepare(self):
        capacity = self.rows.shape[1] // UNIT
        for q in range(UNIT):
            self.right_out[q, pl.ds(capacity, 128), :] = self.shared[pl.ds(256, 128), :]
            self.right_grad[q, pl.ds(capacity, 256), :] = self.shared[pl.ds(0, 256), :]

    def run(self, slot, unit, gates, grad_gates, hook):
        bf16, f32 = jnp.bfloat16, jnp.float32
        own_rows, model = self.tokens.shape[2:]
        seq = 2 * own_rows
        capacity = self.rows.shape[1] // UNIT
        experts = gates.shape[1]
        column = 1024
        n_columns = model // column
        first = unit * (2 * UNIT)
        before = lax.broadcasted_iota(jnp.int32, (seq, seq), 0) <= lax.broadcasted_iota(jnp.int32, (seq, seq), 1)
        before = before.astype(f32).astype(bf16)
        slots = lax.broadcasted_iota(jnp.int32, (capacity, seq), 0)
        picks, row_gates = [], []
        for q in range(UNIT):
            g = jnp.concatenate(
                [gates[first + 2 * q + h, pl.ds(self.expert, 1), :] for h in range(2)], axis=1
            )
            g = jnp.broadcast_to(g, (8, seq))
            taken = (g > 0.0).astype(f32)
            rank = dot_f32(taken.astype(bf16), before).astype(jnp.int32) - 1
            hit = (slots == rank[:1]) & (g[:1] > 0.0)
            pick = hit.astype(f32)
            picks.append(pick)
            row_gates.append(jnp.sum(pick * g[:1], axis=1, keepdims=True))
            self.left_out[q, :, pl.ds(0, capacity)] = pick.T.astype(bf16)
            self.left_grad[q, :, pl.ds(0, capacity)] = pick.T.astype(bf16)
            low = pick.astype(bf16)

            span = pl.ds(q * capacity, capacity)
            for source, target in ((self.tokens, self.rows), (self.grads, self.grad_rows)):
                whole = source[slot, pl.ds(2 * q, 2)].reshape(seq, model)
                target[slot, span] = dot_f32(low, whole).astype(bf16)
        hook(1)
        row_gate = jnp.concatenate(row_gates, axis=0)
        rows, grad_rows = self.rows.at[slot], self.grad_rows.at[slot]
        self.pre[0] = dot_f32(rows[...], self.w_gate[...])
        self.pre[1] = dot_f32(rows[...], self.w_up[...])
        self.pre[2] = dot_t(grad_rows[...], self.w_down[...])
        hook(2)
        step = 32
        parts = []
        for r in range(UNIT * capacity // step):
            span = pl.ds(r * step, step)
            gate_pre, up_pre, grad_hidden = self.pre[0, span], self.pre[1, span], self.pre[2, span]
            gate = row_gate[r * step : (r + 1) * step]
            sig = jax.nn.sigmoid(gate_pre)
            act = gate_pre * sig
            hidden = act * up_pre
            parts.append(jnp.sum(hidden * grad_hidden, axis=1, keepdims=True))
            grad_hidden = grad_hidden * gate
            self.hidden[slot, 0, span] = (hidden * gate).astype(bf16)
            slope = sig * (1.0 + gate_pre * (1.0 - sig))
            self.hidden[slot, 1, span] = (grad_hidden * up_pre * slope).astype(bf16)
            self.hidden[slot, 2, span] = (grad_hidden * act).astype(bf16)
        grad_gate_rows = jnp.concatenate(parts, axis=0)
        mine = lax.broadcasted_iota(jnp.int32, (experts, own_rows), 0) == self.expert
        for q in range(UNIT):
            per_token = jnp.sum(picks[q] * grad_gate_rows[q * capacity : (q + 1) * capacity], axis=0, keepdims=True)
            for h in range(2):
                part = jnp.broadcast_to(per_token[:, h * own_rows : (h + 1) * own_rows], (experts, own_rows))
                grad_gates[first + 2 * q + h] = jnp.where(mine, part, 0.0)

        for q in range(UNIT):
            blocks = pl.ds(2 * q, 2)
            whole = self.tokens[slot, blocks].reshape(seq, model)
            grad = self.grads[slot, blocks].reshape(seq, model)
            pre = dot_t(whole, self.shared[pl.ds(0, 256), :])
            grad_hidden = dot_t(grad, self.shared[pl.ds(256, 128), :])
            gate_pre, up_pre = pre[:, :128], pre[:, 128:]
            sig = jax.nn.sigmoid(gate_pre)
            act = gate_pre * sig
            hidden = (act * up_pre).astype(bf16)
            grad_gate = (grad_hidden * up_pre * sig * (1.0 + gate_pre * (1.0 - sig))).astype(bf16)
            grad_up = (grad_hidden * act).astype(bf16)
            span = pl.ds(q * seq, seq)
            self.shared_hidden[slot, span, pl.ds(0, 128)] = hidden
            self.shared_hidden[slot, span, pl.ds(128, 128)] = grad_gate
            self.shared_hidden[slot, span, pl.ds(256, 128)] = grad_up
            self.left_out[q, :, pl.ds(capacity, 128)] = hidden
            self.left_grad[q, :, pl.ds(capacity, 128)] = grad_gate
            self.left_grad[q, :, pl.ds(capacity + 128, 128)] = grad_up

        hook(3)

        def combine(c, carry):
            cols = pl.ds(pl.multiple_of(c * column, column), column)
            made = dot_f32(self.hidden[slot, 0], self.w_down[:, cols]).astype(bf16)
            back = dot_t(self.hidden[slot, 1], self.w_gate[cols, :])
            back = (back + dot_t(self.hidden[slot, 2], self.w_up[cols, :])).astype(bf16)
            for q in range(UNIT):
                span = slice(q * capacity, (q + 1) * capacity)
                self.right_out[q, pl.ds(0, capacity), cols] = made[span]
                self.right_grad[q, pl.ds(0, capacity), cols] = back[span]
                out = dot_f32(self.left_out[q], self.right_out[q, :, cols]).astype(bf16)
                self.out[slot, pl.ds(2 * q, 2), :, cols] = out.reshape(2, own_rows, column)
                out = dot_f32(self.left_grad[q], self.right_grad[q, :, cols]).astype(bf16)
                self.back[slot, pl.ds(2 * q, 2), :, cols] = out.reshape(2, own_rows, column)

            @pl.when(c == n_columns // 2)
            def _():
                hook(4)

            return carry

        lax.fori_loop(0, n_columns, combine, 0)


def expert_kernel(n_dp, *refs):
    own, own_gates, grads, w_gate, w_up, w_down, shared = refs[:7]
    normed, out_parts, back_parts, grad_gates, rows_out, grad_rows_out, hidden_out, shared_out = refs[7:15]
    scratch, (gates, load, store, local, send, recv) = refs[15:-6], refs[-6:]
    n_planes = n_dp // 4
    spot = Spot(n_planes)
    half = own.shape[0] // 2

    def views(s, yy, cc, xx, part):
        b = dp_of(s, yy, cc) * 2 + xx
        if part == ALL:
            return [normed.at[b], gates.at[b]]
        if part == FIRST:
            return [normed.at[b, pl.ds(0, half)], gates.at[b]]
        return [normed.at[b, pl.ds(half, half)]]

    kept = [
        pltpu.make_async_copy(a, v, local.at[i])
        for i, (a, v) in enumerate(zip((own, own_gates), views(spot.z, spot.y, spot.core, spot.x, ALL)))
    ]
    for c in kept:
        c.start()
    spot.greet()
    copies = Copies(n_planes, send, recv)
    net = Spread(spot, copies, [own, own_gates], views, True)
    net.begin()
    work = ExpertWork(spot.dp, (w_gate, w_up, w_down, shared), scratch)
    work.prepare()
    n_units = n_dp // UNIT
    blocks = 2 * UNIT
    rows = work.rows.shape[1]
    seqs = work.shared_hidden.shape[1]
    order = net.order

    def unit_of(i):
        s = 0 * i
        for j, plane in enumerate(order):
            s = s + (i // 2 == j).astype(jnp.int32) * plane
        yy = spot.y + (i % 2) * (1 - 2 * spot.y)
        return s * 2 + yy

    def loads(u, slot):
        span = pl.ds(u * blocks, blocks)
        return [
            pltpu.make_async_copy(normed.at[span], work.tokens.at[slot], load.at[slot, 0]),
            pltpu.make_async_copy(grads.at[span], work.grads.at[slot], load.at[slot, 1]),
        ]

    def stores(u, slot):
        span = pl.ds(u * blocks, blocks)
        some = pl.ds(pl.multiple_of(u * rows, rows), rows)
        pairs = [
            (work.out.at[slot], out_parts.at[span]),
            (work.back.at[slot], back_parts.at[span]),
            (work.rows.at[slot], rows_out.at[some]),
            (work.grad_rows.at[slot], grad_rows_out.at[some]),
            (work.hidden.at[slot], hidden_out.at[:, some]),
            (work.shared_hidden.at[slot], shared_out.at[pl.ds(pl.multiple_of(u * seqs, seqs), seqs)]),
        ]
        return [pltpu.make_async_copy(a, b, store.at[slot, i]) for i, (a, b) in enumerate(pairs)]

    def load_unit(i):
        loads(unit_of(jnp.int32(i)), i % 2)[0].start()

    def near(j):
        net.twin_near(j)
        load_unit(2 * j)

    def far(j):
        net.twin_far(j)
        load_unit(2 * j + 1)

    def on(j):
        net.onward(j, net.mine[j][0])

    middle = spot.has_up & spot.has_down
    end = jnp.logical_not(middle)

    goes = {
        (j, c): (net.goes_down[j] & (middle if c else end), net.goes_up[j] & (middle if c else end))
        for j in range(1, n_planes)
        for c in (0, 1)
    }

    def relay(j, c):
        pl.when(middle if c else end)(functools.partial(net.relay, j, goes[j, c]))

    plan = {
        (0, 0): [(on, 1)],
        (0, 1): [(net.corner, 0)],
        (0, 2): [(far, 0)],
        (0, 4): [(relay, 2, 0), (relay, 3, 1)],
        (1, 0): [(net.sides, 1)],
        (1, 1): [(on, 2)],
        (1, 2): [(near, 1)],
        (1, 3): [(net.corner, 1)],
        (2, 0): [(far, 1)],
        (2, 3): [(net.sides, 2), (relay, 3, 0)],
        (2, 4): [(on, 3)],
        (3, 0): [(near, 2)],
        (3, 1): [(net.corner, 2)],
        (4, 0): [(net.sides, 3), (far, 2)],
        (4, 3): [(net.corner, 3)],
        (5, 0): [(near, 3)],
        (6, 0): [(far, 3)],
    }

    net.relay(1)
    relay(2, 1)
    net.sides(0)
    for c in kept:
        c.wait()
    near(0)
    loads(unit_of(jnp.int32(0)), 0)[1].start()

    def body(i, carry):
        slot = i % 2
        u = unit_of(i)

        def hook(point):
            for (k, at), actions in plan.items():
                if at == point:

                    @pl.when(i == k)
                    def _(actions=actions):
                        for action, *values in actions:
                            action(*values)

        hook(0)

        @pl.when(i + 1 < n_units)
        def _():
            loads(unit_of(i + 1), 1 - slot)[1].start()

        for c in loads(u, slot):
            c.wait()

        @pl.when(i >= 2)
        def _():
            for c in stores(unit_of(i - 2), slot):
                c.wait()

        work.run(slot, u, gates, grad_gates, hook)
        for c in stores(u, slot):
            c.start()
        return carry

    lax.fori_loop(0, n_units, body, 0)
    for i in (n_units - 2, n_units - 1):
        for c in stores(unit_of(jnp.int32(i)), i % 2):
            c.wait()
    copies.close()


def expert_call(own, own_gates, grads, w_gate, w_up, w_down, shared, n_dp, capacity, collective_id):
    own_rows, model = own.shape
    blocks = 2 * n_dp
    width = w_gate.shape[1]
    bf16 = jnp.bfloat16
    rows = n_dp * capacity
    n_planes = n_dp // 4
    vmem = pl.BlockSpec(memory_space=pltpu.VMEM)
    everyone = jax.ShapeDtypeStruct((blocks, own_rows, model), bf16)
    all_gates = (blocks,) + own_gates.shape
    return pl.pallas_call(
        functools.partial(expert_kernel, n_dp),
        out_shape=[
            everyone,
            everyone,
            everyone,
            jax.ShapeDtypeStruct(all_gates, jnp.float32),
            jax.ShapeDtypeStruct((rows, model), bf16),
            jax.ShapeDtypeStruct((rows, model), bf16),
            jax.ShapeDtypeStruct((3, rows, width), bf16),
            jax.ShapeDtypeStruct((blocks * own_rows, 384), bf16),
        ],
        in_specs=[ANY, ANY, ANY, vmem, vmem, vmem, vmem],
        out_specs=[ANY, ANY, ANY, vmem, ANY, ANY, ANY, ANY],
        scratch_shapes=ExpertWork.scratch(model, width, capacity, own_rows)
        + [
            pltpu.VMEM(all_gates, jnp.float32),
            pltpu.SemaphoreType.DMA((2, 2)),
            pltpu.SemaphoreType.DMA((2, 6)),
            pltpu.SemaphoreType.DMA((2,)),
            pltpu.SemaphoreType.DMA((11 * n_planes, 2)),
            pltpu.SemaphoreType.DMA((11 * n_planes, 2)),
        ],
        compiler_params=pltpu.CompilerParams(
            collective_id=collective_id, has_side_effects=True, vmem_limit_bytes=60 << 20
        ),
    )(own, own_gates, grads, w_gate, w_up, w_down, shared)


def swap_halves(own, x):
    return lax.ppermute(own, TENSOR, [(0, 1), (1, 0)])


def halves_sum(partial, rows, x):
    kept = lax.dynamic_slice_in_dim(partial, x * rows, rows, 0)
    given = lax.dynamic_slice_in_dim(partial, (1 - x) * rows, rows, 0).astype(jnp.bfloat16)
    return kept + swap_halves(given, x).astype(jnp.float32)


def gather_plan(
    tokens,
    attention_gain,
    expert_norm_gain,
    query_projection,
    key_projection,
    value_projection,
    output_projection,
    router,
    shared_gate_matrix,
    shared_up_matrix,
    shared_down_matrix,
    expert_gate_matrix,
    expert_up_matrix,
    expert_down_matrix,
    document_lengths,
    expert_indices,
    cotangent,
):
    n_dp = lax.axis_size(DP)
    x = lax.axis_index(TENSOR)
    dp = lax.axis_index(DP)
    own_rows, model_dim = tokens.shape
    sequence_length = own_rows * 2
    experts = n_dp
    top_k = expert_indices.shape[1]
    capacity = sequence_length * top_k * 4 // (3 * experts)
    bf16, f32 = jnp.bfloat16, jnp.float32

    def dot(a, b):
        return jnp.dot(a, b, preferred_element_type=f32)

    width = attention_gain.shape[0]
    small = jnp.concatenate([attention_gain, expert_norm_gain, router.reshape(-1)])
    small = jnp.pad(small, (0, -small.shape[0] % 2048)).reshape(-1, 128)
    axes = (0, 0, 0, 1)
    query_all, key_all, value_all, out_all, sequence, smalls, cotangent_all = fetch(
        [query_projection, key_projection, value_projection, output_projection],
        axes, tokens, small, cotangent, n_dp, 1,
    )
    flat = smalls.swapaxes(0, 1).reshape(2 * n_dp, -1)
    first_gain = flat[:, :width].reshape(-1).astype(f32)
    second_gain = flat[:, width : 2 * width].reshape(-1).astype(f32)
    router_full = flat[:, 2 * width : (2 + experts) * width].reshape(model_dim, experts)

    hidden = shared_gate_matrix.shape[1] // n_dp
    hidden_pad = -(-hidden // 16) * 16

    def slices(transposed):
        blocks = transposed.reshape(n_dp, hidden, -1)
        return jnp.pad(blocks, ((0, 0), (0, hidden_pad - hidden), (0, 0)))

    shared_out = jnp.stack(
        [slices(shared_gate_matrix.T), slices(shared_up_matrix.T), slices(shared_down_matrix)], axis=1
    )
    shared_in = lax.all_to_all(shared_out, DP, split_axis=0, concat_axis=0, tiled=True)
    shared_rows = jnp.moveaxis(shared_in, 0, 2).reshape(3, hidden_pad, model_dim)

    full_tokens = sequence.reshape(sequence_length, model_dim).astype(f32)
    full_scale = lax.rsqrt(jnp.mean(full_tokens * full_tokens, axis=-1, keepdims=True) + norm_eps)
    full_one = (full_tokens * full_scale * first_gain).astype(bf16)
    input_values = tokens.astype(f32)
    scale_one = lax.dynamic_slice_in_dim(full_scale, x * own_rows, own_rows, 0)
    q_heads = query_all.shape[1] // HEAD_SIZE
    kv_heads = key_all.shape[1] // HEAD_SIZE
    group_size = q_heads // kv_heads
    rotary_cosine, rotary_sine = rotation(sequence_length, HEAD_SIZE)
    query_unrotated = dot(full_one, query_all).reshape(sequence_length, q_heads, HEAD_SIZE)
    key_unrotated = dot(full_one, key_all).reshape(sequence_length, kv_heads, HEAD_SIZE)
    rows_of_query = (
        apply_rotary(query_unrotated, rotary_cosine, rotary_sine)
        .astype(bf16)
        .reshape(sequence_length, kv_heads, group_size, HEAD_SIZE)
    )
    key_rows = apply_rotary(key_unrotated, rotary_cosine, rotary_sine).astype(bf16)
    rows_of_value = dot(full_one, value_all).astype(bf16).reshape(sequence_length, kv_heads, HEAD_SIZE)
    doc_ends = jnp.cumsum(document_lengths[0])
    positions = jnp.arange(sequence_length, dtype=jnp.int32)
    doc_ids = jnp.sum((positions[:, None] >= doc_ends[None, :]).astype(jnp.int32), axis=-1)
    score_scale = HEAD_SIZE ** (-0.5)
    allowed = (doc_ids[:, None] == doc_ids[None, :]) & (positions[:, None] >= positions[None, :])
    scores = (
        jnp.einsum("qkgd,skd->kgqs", rows_of_query, key_rows, preferred_element_type=f32) * score_scale
    )
    scores = jnp.where(allowed, scores, neg_big)
    exp_scores = jnp.exp(scores - jnp.max(scores, axis=-1, keepdims=True))
    attn_probs = exp_scores / jnp.sum(exp_scores, axis=-1, keepdims=True)
    probs_low = attn_probs.astype(bf16)
    mixed_heads = (
        jnp.einsum("kgqs,skd->qkgd", probs_low, rows_of_value, preferred_element_type=f32)
        .reshape(sequence_length, q_heads * HEAD_SIZE)
        .astype(bf16)
    )
    residual = input_values + halves_sum(dot(mixed_heads, out_all), own_rows, x)

    scale_two = lax.rsqrt(jnp.mean(residual * residual, axis=-1, keepdims=True) + norm_eps)
    normed_two = (residual * scale_two * second_gain).astype(bf16)
    logits = dot(normed_two, router_full)
    own_indices = lax.dynamic_slice_in_dim(expert_indices, x * own_rows, own_rows, 0)
    chosen = own_indices[:, :, None] == jnp.arange(experts, dtype=jnp.int32)[None, None, :]
    selected = jnp.sum(jnp.where(chosen, logits[:, None, :], 0.0), axis=-1)
    gate_exp = jnp.exp(selected - jnp.max(selected, axis=-1, keepdims=True))
    gate_probs = gate_exp / jnp.sum(gate_exp, axis=-1, keepdims=True)
    gates = jnp.sum(jnp.where(chosen, gate_probs[:, :, None], 0.0), axis=1)


    shared_rows = jnp.pad(shared_rows, ((0, 0), (0, 128 - hidden_pad), (0, 0))).reshape(384, model_dim)
    normed_all, output_parts, normed_parts, grad_gate_parts, received, grad_rows, hidden_rows, shared_hidden = (
        expert_call(
            normed_two, gates.T, cotangent_all, expert_gate_matrix[0], expert_up_matrix[0], expert_down_matrix[0],
            shared_rows, n_dp, capacity, 2,
        )
    )
    expert_gate_gradient = dot(received.T, hidden_rows[1])[None]
    expert_up_gradient = dot(received.T, hidden_rows[2])[None]
    expert_down_gradient = dot(hidden_rows[0].T, grad_rows)[None]
    normed_flat = normed_all.reshape(-1, model_dim)
    grad_flat = cotangent_all.reshape(-1, model_dim)
    shared_grads = jnp.concatenate(
        [dot(shared_hidden[:, 128:].T, normed_flat), dot(shared_hidden[:, :128].T, grad_flat)]
    ).astype(bf16)
    shared_grads = shared_grads.reshape(3, 128, model_dim)[:, :hidden_pad]
    grad_normed_two, grad_gates_t = sum_everywhere([normed_parts, grad_gate_parts], [f32, f32], n_dp, 4)

    grad_gates = grad_gates_t.T
    grad_logits = (
        gates * (grad_gates - jnp.sum(gates * grad_gates, axis=-1, keepdims=True))
    ).astype(bf16)
    grad_normed_two = grad_normed_two + dot(grad_logits, router_full.T)
    grad_router_part = dot(normed_two.T, grad_logits)
    grad_residual, grad_gain_two = rms_back(grad_normed_two, residual, scale_two, second_gain)
    grad_residual = grad_residual + cotangent.astype(f32)
    grad_low = grad_residual.astype(bf16)
    grad_other = swap_halves(grad_low, x)
    grad_attn = jnp.where(
        x == 0, jnp.concatenate([grad_low, grad_other]), jnp.concatenate([grad_other, grad_low])
    )

    grad_wout = dot(mixed_heads.T, grad_attn)
    grad_mixed = (
        dot(grad_attn, out_all.T).astype(bf16).reshape(sequence_length, kv_heads, group_size, HEAD_SIZE)
    )
    grad_values = jnp.einsum("kgqs,qkgd->skd", probs_low, grad_mixed, preferred_element_type=f32)
    grad_probs = jnp.einsum("qkgd,skd->kgqs", grad_mixed, rows_of_value, preferred_element_type=f32)
    inner_sum = jnp.sum(attn_probs * grad_probs, axis=-1, keepdims=True)
    grad_scores = (attn_probs * (grad_probs - inner_sum)).astype(bf16)
    grad_query = (
        jnp.einsum("kgqs,skd->qkgd", grad_scores, key_rows, preferred_element_type=f32) * score_scale
    ).reshape(sequence_length, q_heads, HEAD_SIZE)
    grad_keys = (
        jnp.einsum("kgqs,qkgd->skd", grad_scores, rows_of_query, preferred_element_type=f32) * score_scale
    )
    grad_q_raw = rotate_back(grad_query, rotary_cosine, rotary_sine).astype(bf16)
    grad_q_raw = grad_q_raw.reshape(sequence_length, q_heads * HEAD_SIZE)
    grad_k_raw = rotate_back(grad_keys, rotary_cosine, rotary_sine).astype(bf16)
    grad_k_raw = grad_k_raw.reshape(sequence_length, kv_heads * HEAD_SIZE)
    grad_v_low = grad_values.astype(bf16).reshape(sequence_length, kv_heads * HEAD_SIZE)
    grad_wquery = dot(full_one.T, grad_q_raw).astype(bf16)
    grad_wkey = dot(full_one.T, grad_k_raw).astype(bf16)
    grad_wvalue = dot(full_one.T, grad_v_low).astype(bf16)
    grad_normed_one = halves_sum(
        dot(grad_q_raw, query_all.T) + dot(grad_k_raw, key_all.T) + dot(grad_v_low, value_all.T), own_rows, x
    )
    grad_inputs, grad_gain_one = rms_back(grad_normed_one, input_values, scale_one, first_gain)
    grad_inputs = grad_inputs + grad_residual

    def by_owner(v):
        return v.reshape(2 * n_dp, -1)

    tiles = jnp.concatenate([by_owner(grad_gain_one), by_owner(grad_gain_two), by_owner(grad_router_part)], axis=1)
    tiles = jnp.pad(tiles, ((0, 0), (0, -tiles.shape[1] % 2048)))
    small_rows = tiles.shape[1] // 128
    sums = sum_back(
        [grad_wquery, grad_wkey, grad_wvalue, grad_wout.astype(bf16), tiles.reshape(-1, 128)],
        axes + (0,), output_parts, n_dp, 6,
    )
    output = (residual + sums[5]).astype(bf16)
    mine = sums[4].reshape(-1)
    gain_one_own, gain_two_own = mine[:width], mine[width : 2 * width]
    router_own = mine[2 * width : (2 + experts) * width].reshape(width, experts)
    returned = lax.all_to_all(
        shared_grads.reshape(3, hidden_pad, n_dp, -1).transpose(2, 0, 1, 3),
        DP, split_axis=0, concat_axis=0, tiled=True,
    )[:, :, :hidden]
    returned = returned.transpose(1, 0, 2, 3).reshape(3, n_dp * hidden, -1).astype(f32)
    return (
        output,
        grad_inputs,
        gain_one_own,
        gain_two_own,
        sums[0],
        sums[1],
        sums[2],
        sums[3],
        router_own,
        returned[0].T,
        returned[1].T,
        returned[2],
        expert_gate_gradient,
        expert_up_gradient,
        expert_down_gradient,
    )


def shards(*arguments):
    tokens, expert_gate_matrix = arguments[0], arguments[11]
    n_dp, n_tensor = lax.axis_size(DP), lax.axis_size(TENSOR)
    gathered = n_dp * n_tensor * tokens.shape[0] * tokens.shape[1] * 2
    if n_tensor == 2 and n_dp % 4 == 0 and expert_gate_matrix.shape[0] == 1 and gathered <= 32 << 20:
        return gather_plan(*arguments)
    return exchange_plan(*arguments)


def solution(mesh):
    placed = (
        P((DP, TENSOR), None),
        P((DP, TENSOR)),
        P((DP, TENSOR)),
        P(DP, TENSOR),
        P(DP, TENSOR),
        P(DP, TENSOR),
        P(TENSOR, DP),
        P((DP, TENSOR), None),
        P(DP, TENSOR),
        P(DP, TENSOR),
        P(TENSOR, DP),
        P(DP, None, TENSOR),
        P(DP, None, TENSOR),
        P(DP, TENSOR, None),
        P(DP, None),
        P(DP, None),
        P((DP, TENSOR), None),
    )
    return jax.shard_map(
        shards,
        mesh=mesh,
        in_specs=placed,
        out_specs=(
            P((DP, TENSOR), None),
            P((DP, TENSOR), None),
            P((DP, TENSOR)),
            P((DP, TENSOR)),
            P(DP, TENSOR),
            P(DP, TENSOR),
            P(DP, TENSOR),
            P(TENSOR, DP),
            P((DP, TENSOR), None),
            P(DP, TENSOR),
            P(DP, TENSOR),
            P(TENSOR, DP),
            P(DP, None, TENSOR),
            P(DP, None, TENSOR),
            P(DP, TENSOR, None),
        ),
        check_vma=False,
    )
```

```python
import functools
import math

import jax
import jax.numpy as jnp
from jax import lax
from jax.experimental import pallas as pl
from jax.experimental.pallas import tpu as pltpu
from jax.sharding import PartitionSpec as P

HEAD_SIZE = 128
DP, TENSOR = ("dp", "tensor")


norm_eps = 1e-06
rope_base = 600000.0
neg_big = -1e30


def silu(argument):
    return argument * jax.nn.sigmoid(argument)


def silu_slope(argument):
    sigmoid_of = jax.nn.sigmoid(argument)
    return sigmoid_of * (1.0 + argument * (1.0 - sigmoid_of))


def rotation(sequence_length, head_dim):
    half_dim = head_dim // 2
    frequency = jnp.exp(
        jnp.arange(half_dim, dtype=jnp.float32) * (-2.0 * math.log(rope_base) / head_dim)
    )
    angles = jnp.arange(sequence_length, dtype=jnp.float32)[:, None] * frequency[None, :]
    return (jnp.cos(angles), jnp.sin(angles))


def apply_rotary(tensor, rotary_cosine, rotary_sine):
    half_dim = tensor.shape[-1] // 2
    first_half = tensor[..., :half_dim]
    second_half = tensor[..., half_dim:]
    cos_rows = rotary_cosine[:, None, :]
    sin_rows = rotary_sine[:, None, :]
    return jnp.concatenate(
        [
            first_half * cos_rows - second_half * sin_rows,
            second_half * cos_rows + first_half * sin_rows,
        ],
        axis=-1,
    )


def rotate_back(tensor, rotary_cosine, rotary_sine):
    return apply_rotary(tensor, rotary_cosine, -rotary_sine)


def rms_back(grad_normed, source, scale_rows, gain_full):
    weighted = grad_normed * gain_full
    cubed = scale_rows * scale_rows * scale_rows
    grad_source = scale_rows * weighted - source * cubed * jnp.mean(
        source * weighted, axis=-1, keepdims=True
    )
    grad_gain = jnp.sum(grad_normed * source * scale_rows, axis=0)
    return (grad_source, grad_gain)


def widen(sharded):
    return lax.all_gather(sharded, TENSOR, axis=0, tiled=True)


def narrow(partial_sum):
    return lax.psum_scatter(partial_sum, TENSOR, scatter_dimension=0, tiled=True)


def dense_fetch(
    query_projection,
    key_projection,
    value_projection,
    output_projection,
    shared_gate_matrix,
    shared_up_matrix,
    shared_down_matrix,
):
    return (
        lax.all_gather(query_projection, DP, axis=0, tiled=True),
        lax.all_gather(key_projection, DP, axis=0, tiled=True),
        lax.all_gather(value_projection, DP, axis=0, tiled=True),
        lax.all_gather(output_projection, DP, axis=1, tiled=True),
        lax.all_gather(shared_gate_matrix, DP, axis=0, tiled=True),
        lax.all_gather(shared_up_matrix, DP, axis=0, tiled=True),
        lax.all_gather(shared_down_matrix, DP, axis=1, tiled=True),
    )


def expert_up_output(received_rows, expert_gate_matrix, expert_up_matrix, expert_down_matrix):
    gate_preactivation = jnp.einsum(
        "miwy,iyh->miwh", received_rows, expert_gate_matrix, preferred_element_type=jnp.float32
    )
    up_preactivation = jnp.einsum(
        "miwy,iyh->miwh", received_rows, expert_up_matrix, preferred_element_type=jnp.float32
    )
    hidden = (silu(gate_preactivation) * up_preactivation).astype(jnp.bfloat16)
    produced_rows = jnp.einsum(
        "sxcf,xfd->sxcd", hidden, expert_down_matrix, preferred_element_type=jnp.float32
    ).astype(jnp.bfloat16)
    return (produced_rows, gate_preactivation, up_preactivation)


def expert_gradients(
    received,
    received_gradient,
    gate_preactivation,
    up_preactivation,
    expert_gate_matrix,
    expert_up_matrix,
    expert_down_matrix,
):
    hidden_expert = (silu(gate_preactivation) * up_preactivation).astype(jnp.bfloat16)
    expert_down_gradient = jnp.einsum(
        "sxcf,sxcd->xfd", hidden_expert, received_gradient, preferred_element_type=jnp.float32
    )
    grad_hidden_e = jnp.einsum(
        "sxcd,xfd->sxcf", received_gradient, expert_down_matrix, preferred_element_type=jnp.float32
    )
    grad_gate_e = (grad_hidden_e * up_preactivation * silu_slope(gate_preactivation)).astype(
        jnp.bfloat16
    )
    expert_up_hidden_gradient = (grad_hidden_e * silu(gate_preactivation)).astype(jnp.bfloat16)
    expert_gate_gradient = jnp.einsum(
        "gayi,gayr->air", received, grad_gate_e, preferred_element_type=jnp.float32
    )
    expert_up_gradient = jnp.einsum(
        "gayi,gayr->air", received, expert_up_hidden_gradient, preferred_element_type=jnp.float32
    )
    output_rows_gradient = (
        jnp.einsum(
            "zkjh,klh->zkjl", grad_gate_e, expert_gate_matrix, preferred_element_type=jnp.float32
        )
        + jnp.einsum(
            "zkjh,klh->zkjl",
            expert_up_hidden_gradient,
            expert_up_matrix,
            preferred_element_type=jnp.float32,
        )
    ).astype(jnp.bfloat16)
    return (expert_gate_gradient, expert_up_gradient, expert_down_gradient, output_rows_gradient)


def exchange_plan(
    tokens,
    attention_gain,
    expert_norm_gain,
    query_projection,
    key_projection,
    value_projection,
    output_projection,
    router,
    shared_gate_matrix,
    shared_up_matrix,
    shared_down_matrix,
    expert_gate_matrix,
    expert_up_matrix,
    expert_down_matrix,
    document_lengths,
    expert_indices,
    cotangent,
):
    n_tensor = lax.axis_size(TENSOR)
    n_dp = lax.axis_size(DP)
    tensor_pos = lax.axis_index(TENSOR)
    own_rows = tokens.shape[0]
    sequence_length = own_rows * n_tensor
    model_dim = tokens.shape[1]
    exp_dev = expert_gate_matrix.shape[0]
    experts = exp_dev * n_dp
    top_k = expert_indices.shape[1]
    capacity = max(2, sequence_length * top_k * 4 // (3 * experts))
    slot_total = experts * capacity
    router_full, gain_first, gain_second = (
        lax.all_gather(router, (DP, TENSOR), axis=0, tiled=True),
        lax.all_gather(attention_gain, (DP, TENSOR), axis=0, tiled=True),
        lax.all_gather(expert_norm_gain, (DP, TENSOR), axis=0, tiled=True),
    )
    first_gain = gain_first.astype(jnp.float32)
    second_gain = gain_second.astype(jnp.float32)
    fetched = dense_fetch(
        query_projection,
        key_projection,
        value_projection,
        output_projection,
        shared_gate_matrix,
        shared_up_matrix,
        shared_down_matrix,
    )
    query_all, key_all, value_all, out_all, sgate_all, sup_all, sdown_all = fetched
    input_values = tokens.astype(jnp.float32)
    scale_one = lax.rsqrt(jnp.mean(input_values * input_values, axis=-1, keepdims=True) + norm_eps)
    normed_one = (input_values * scale_one * first_gain).astype(jnp.bfloat16)
    full_one = widen(normed_one)
    q_heads = query_all.shape[1] // HEAD_SIZE
    kv_heads = key_all.shape[1] // HEAD_SIZE
    group_size = q_heads // kv_heads
    rotary_cosine, rotary_sine = rotation(sequence_length, HEAD_SIZE)
    query_unrotated = jnp.dot(full_one, query_all, preferred_element_type=jnp.float32).reshape(
        sequence_length, q_heads, HEAD_SIZE
    )
    key_unrotated = jnp.dot(full_one, key_all, preferred_element_type=jnp.float32).reshape(
        sequence_length, kv_heads, HEAD_SIZE
    )
    rows_of_query = (
        apply_rotary(query_unrotated, rotary_cosine, rotary_sine)
        .astype(jnp.bfloat16)
        .reshape(sequence_length, kv_heads, group_size, HEAD_SIZE)
    )
    key_rows = apply_rotary(key_unrotated, rotary_cosine, rotary_sine).astype(jnp.bfloat16)
    rows_of_value = (
        jnp.dot(full_one, value_all, preferred_element_type=jnp.float32)
        .astype(jnp.bfloat16)
        .reshape(sequence_length, kv_heads, HEAD_SIZE)
    )
    doc_ends = jnp.cumsum(document_lengths[0])
    positions = jnp.arange(sequence_length, dtype=jnp.int32)
    doc_ids = jnp.sum((positions[:, None] >= doc_ends[None, :]).astype(jnp.int32), axis=-1)
    score_scale = HEAD_SIZE ** (-0.5)

    def block_scores(start_row, end_row):
        scores = (
            jnp.einsum(
                "qkgd,skd->kgqs", rows_of_query, key_rows, preferred_element_type=jnp.float32
            )
            * score_scale
        )
        allowed = (doc_ids[start_row:end_row, None] == doc_ids[None, :end_row]) & (
            positions[start_row:end_row, None] >= positions[None, :end_row]
        )
        return (scores, allowed)

    block_index = 0
    start_row = block_index * sequence_length
    end_row = start_row + sequence_length
    scores, allowed = block_scores(start_row, end_row)
    scores = jnp.where(allowed, scores, neg_big)
    row_max = jnp.max(scores, axis=-1, keepdims=True)
    exp_scores = jnp.exp(scores - row_max)
    row_sum = jnp.sum(exp_scores, axis=-1, keepdims=True)
    lse_blocks = [row_max + jnp.log(row_sum)]
    attn_probs = (exp_scores / row_sum).astype(jnp.bfloat16)
    out_blocks = jnp.einsum(
        "kgqs,skd->qkgd", attn_probs, rows_of_value, preferred_element_type=jnp.float32
    )
    mixed_heads = out_blocks.reshape(sequence_length, q_heads * HEAD_SIZE).astype(jnp.bfloat16)
    attn_part = jnp.dot(mixed_heads, out_all, preferred_element_type=jnp.float32)
    residual = input_values + narrow(attn_part)
    scale_two = lax.rsqrt(jnp.mean(residual * residual, axis=-1, keepdims=True) + norm_eps)
    normed_two = (residual * scale_two * second_gain).astype(jnp.bfloat16)
    full_two = widen(normed_two)
    logits = jnp.dot(full_two, router_full, preferred_element_type=jnp.float32)
    chosen = expert_indices[:, :, None] == jnp.arange(experts, dtype=jnp.int32)[None, None, :]
    selected = jnp.sum(jnp.where(chosen, logits[:, None, :], 0.0), axis=-1)
    top_max = jnp.max(selected, axis=-1, keepdims=True)
    gate_exp = jnp.exp(selected - top_max)
    gate_probs = gate_exp / jnp.sum(gate_exp, axis=-1, keepdims=True)
    gate_shared = jnp.dot(full_two, sgate_all, preferred_element_type=jnp.float32)
    up_shared = jnp.dot(full_two, sup_all, preferred_element_type=jnp.float32)
    hidden_shared = (silu(gate_shared) * up_shared).astype(jnp.bfloat16)
    shared_part = jnp.dot(hidden_shared, sdown_all, preferred_element_type=jnp.float32)
    flat_ids = expert_indices.reshape(-1)
    onehot = (flat_ids[:, None] == jnp.arange(experts, dtype=jnp.int32)[None, :]).astype(jnp.int32)
    slot_rank = jnp.sum(onehot * (jnp.cumsum(onehot, axis=0) - 1), axis=-1)
    slot_index = flat_ids * capacity + slot_rank
    pair_index = jnp.arange(sequence_length * top_k, dtype=jnp.int32)
    token_of_slot = jnp.zeros((slot_total,), jnp.int32).at[slot_index].set(pair_index // top_k)
    slot_used = jnp.zeros((slot_total,), jnp.bool_).at[slot_index].set(True)
    gate_of_slot = jnp.zeros((slot_total,), jnp.float32).at[slot_index].set(gate_probs.reshape(-1))
    outgoing = jnp.where(slot_used[:, None], full_two[token_of_slot], 0).reshape(
        n_dp, exp_dev, capacity, model_dim
    )
    received_rows = lax.all_to_all(outgoing, DP, split_axis=0, concat_axis=0, tiled=True)
    produced_rows, gate_preactivation, up_preactivation = expert_up_output(
        received_rows, expert_gate_matrix, expert_up_matrix, expert_down_matrix
    )
    sent_home = lax.all_to_all(produced_rows, DP, split_axis=0, concat_axis=0, tiled=True)
    returned, received, gate_preactivation, up_preactivation = (
        sent_home,
        received_rows,
        gate_preactivation,
        up_preactivation,
    )
    picked = returned.reshape(slot_total, model_dim)[slot_index].reshape(
        sequence_length, top_k, model_dim
    )
    routed_part = jnp.einsum("sk,skd->sd", gate_probs, picked, preferred_element_type=jnp.float32)
    ffn_own = narrow(shared_part + routed_part)
    output = (residual + ffn_own).astype(jnp.bfloat16)
    weights_back = dense_fetch(
        query_projection,
        key_projection,
        value_projection,
        output_projection,
        shared_gate_matrix,
        shared_up_matrix,
        shared_down_matrix,
    )
    query_back, key_back, value_back, out_back, sgate_back, sup_back, sdown_back = weights_back
    grad_out = cotangent.astype(jnp.float32)
    grad_ffn = widen(cotangent)
    grad_hidden_sh = jnp.dot(grad_ffn, sdown_back.T, preferred_element_type=jnp.float32)
    grad_sdown = jnp.dot(hidden_shared.T, grad_ffn, preferred_element_type=jnp.float32)
    grad_gate_sh = (grad_hidden_sh * up_shared * silu_slope(gate_shared)).astype(jnp.bfloat16)
    grad_up_sh = (grad_hidden_sh * silu(gate_shared)).astype(jnp.bfloat16)
    grad_sgate = jnp.dot(full_two.T, grad_gate_sh, preferred_element_type=jnp.float32)
    grad_sup = jnp.dot(full_two.T, grad_up_sh, preferred_element_type=jnp.float32)
    grad_normed_part = jnp.dot(
        grad_gate_sh, sgate_back.T, preferred_element_type=jnp.float32
    ) + jnp.dot(grad_up_sh, sup_back.T, preferred_element_type=jnp.float32)
    grad_gates_part = jnp.einsum("sd,skd->sk", grad_ffn, picked, preferred_element_type=jnp.float32)
    grad_slot = (
        jnp.where(slot_used[:, None], grad_ffn[token_of_slot] * gate_of_slot[:, None], 0.0)
        .astype(jnp.bfloat16)
        .reshape(n_dp, exp_dev, capacity, model_dim)
    )
    received_gradient = lax.all_to_all(grad_slot, DP, split_axis=0, concat_axis=0, tiled=True)
    expert_gate_gradient, expert_up_gradient, expert_down_gradient, output_rows_gradient = (
        expert_gradients(
            received,
            received_gradient,
            gate_preactivation,
            up_preactivation,
            expert_gate_matrix,
            expert_up_matrix,
            expert_down_matrix,
        )
    )
    grad_returned = lax.all_to_all(
        output_rows_gradient, DP, split_axis=0, concat_axis=0, tiled=True
    )
    grad_picked = grad_returned.reshape(slot_total, model_dim)[slot_index].reshape(
        sequence_length, top_k, model_dim
    )
    grad_normed_part = grad_normed_part + jnp.sum(grad_picked, axis=1, dtype=jnp.float32)
    grad_normed_two, grad_gates = (
        lax.psum_scatter(
            grad_normed_part.astype(jnp.bfloat16), TENSOR, scatter_dimension=0, tiled=True
        ).astype(jnp.float32),
        lax.psum_scatter(
            grad_gates_part.astype(jnp.bfloat16), TENSOR, scatter_dimension=0, tiled=True
        ).astype(jnp.float32),
    )
    row_start = tensor_pos * own_rows
    gates_own = lax.dynamic_slice_in_dim(gate_probs, row_start, own_rows, 0)
    chosen_own = lax.dynamic_slice_in_dim(chosen, row_start, own_rows, 0)
    grad_selected = gates_own * (
        grad_gates - jnp.sum(gates_own * grad_gates, axis=-1, keepdims=True)
    )
    grad_logits = jnp.sum(jnp.where(chosen_own, grad_selected[:, :, None], 0.0), axis=1).astype(
        jnp.bfloat16
    )
    grad_normed_two = grad_normed_two + jnp.dot(
        grad_logits, router_full.T, preferred_element_type=jnp.float32
    )
    grad_router_part = jnp.dot(normed_two.T, grad_logits, preferred_element_type=jnp.float32)
    grad_residual, grad_gain_two = rms_back(grad_normed_two, residual, scale_two, second_gain)
    grad_residual = grad_residual + grad_out
    grad_attn = widen(grad_residual.astype(jnp.bfloat16))
    grad_wout = jnp.dot(mixed_heads.T, grad_attn, preferred_element_type=jnp.float32)
    grad_mixed = (
        jnp.dot(grad_attn, out_back.T, preferred_element_type=jnp.float32)
        .astype(jnp.bfloat16)
        .reshape(sequence_length, kv_heads, group_size, HEAD_SIZE)
    )
    grad_keys = jnp.zeros((sequence_length, kv_heads, HEAD_SIZE), jnp.float32)
    grad_values = jnp.zeros((sequence_length, kv_heads, HEAD_SIZE), jnp.float32)
    block_index = 0
    start_row = block_index * sequence_length
    end_row = start_row + sequence_length
    scores, allowed = block_scores(start_row, end_row)
    attn_probs = jnp.where(allowed, jnp.exp(scores - lse_blocks[block_index]), 0.0)
    probs_low = attn_probs.astype(jnp.bfloat16)
    grad_values = grad_values.at[:end_row].add(
        jnp.einsum("kgqs,qkgd->skd", probs_low, grad_mixed, preferred_element_type=jnp.float32)
    )
    grad_probs = jnp.einsum(
        "qkgd,skd->kgqs", grad_mixed, rows_of_value, preferred_element_type=jnp.float32
    )
    inner_sum = jnp.sum(attn_probs * grad_probs, axis=-1, keepdims=True)
    grad_scores = (attn_probs * (grad_probs - inner_sum)).astype(jnp.bfloat16)
    grad_query_blocks = (
        jnp.einsum("kgqs,skd->qkgd", grad_scores, key_rows, preferred_element_type=jnp.float32)
        * score_scale
    )
    grad_keys = grad_keys.at[:end_row].add(
        jnp.einsum("kgqs,qkgd->skd", grad_scores, rows_of_query, preferred_element_type=jnp.float32)
        * score_scale
    )
    grad_query = grad_query_blocks.reshape(sequence_length, q_heads, HEAD_SIZE)
    grad_q_raw = (
        rotate_back(grad_query, rotary_cosine, rotary_sine)
        .astype(jnp.bfloat16)
        .reshape(sequence_length, q_heads * HEAD_SIZE)
    )
    grad_k_raw = (
        rotate_back(grad_keys, rotary_cosine, rotary_sine)
        .astype(jnp.bfloat16)
        .reshape(sequence_length, kv_heads * HEAD_SIZE)
    )
    grad_v_low = grad_values.astype(jnp.bfloat16).reshape(sequence_length, kv_heads * HEAD_SIZE)
    grad_wquery = jnp.dot(full_one.T, grad_q_raw, preferred_element_type=jnp.float32)
    grad_wkey = jnp.dot(full_one.T, grad_k_raw, preferred_element_type=jnp.float32)
    grad_wvalue = jnp.dot(full_one.T, grad_v_low, preferred_element_type=jnp.float32)
    grad_normed_one_part = (
        jnp.dot(grad_q_raw, query_back.T, preferred_element_type=jnp.float32)
        + jnp.dot(grad_k_raw, key_back.T, preferred_element_type=jnp.float32)
        + jnp.dot(grad_v_low, value_back.T, preferred_element_type=jnp.float32)
    )
    grad_normed_one = narrow(grad_normed_one_part)
    grad_inputs, grad_gain_one = rms_back(grad_normed_one, input_values, scale_one, first_gain)
    grad_inputs = grad_inputs + grad_residual
    dense_sums = (
        lax.psum_scatter(grad_wquery, DP, scatter_dimension=0, tiled=True),
        lax.psum_scatter(grad_wkey, DP, scatter_dimension=0, tiled=True),
        lax.psum_scatter(grad_wvalue, DP, scatter_dimension=0, tiled=True),
        lax.psum_scatter(grad_wout, DP, scatter_dimension=1, tiled=True),
        lax.psum_scatter(grad_sgate, DP, scatter_dimension=0, tiled=True),
        lax.psum_scatter(grad_sup, DP, scatter_dimension=0, tiled=True),
        lax.psum_scatter(grad_sdown, DP, scatter_dimension=1, tiled=True),
    )
    small_sums = (
        lax.psum_scatter(grad_router_part, (DP, TENSOR), scatter_dimension=0, tiled=True),
        lax.psum_scatter(grad_gain_one, (DP, TENSOR), scatter_dimension=0, tiled=True),
        lax.psum_scatter(grad_gain_two, (DP, TENSOR), scatter_dimension=0, tiled=True),
    )
    return (
        output,
        grad_inputs,
        small_sums[1],
        small_sums[2],
        dense_sums[0],
        dense_sums[1],
        dense_sums[2],
        dense_sums[3],
        small_sums[0],
        dense_sums[4],
        dense_sums[5],
        dense_sums[6],
        expert_gate_gradient,
        expert_up_gradient,
        expert_down_gradient,
    )


MESH = pl.DeviceIdType.MESH
ANY = pl.BlockSpec(memory_space=pl.ANY)


def when(condition, body):
    if condition is None:
        body()
    else:
        pl.when(condition)(body)


class Spot:
    def __init__(self, n_planes):
        dp = lax.axis_index(DP)
        self.x = lax.axis_index(TENSOR)
        self.dp = dp
        self.core = dp % 2
        self.y = (dp // 2) % 2
        self.z = dp // 4
        self.n_planes = n_planes
        self.has_up = self.z < n_planes - 1
        self.has_down = self.z > 0
        self.up = (dp + 4, self.x)
        self.down = (dp - 4, self.x)
        self.side = (dp + 2 - 4 * self.y, self.x)
        self.across = (dp, 1 - self.x)
        self.twin = (dp + 1 - 2 * self.core, self.x)

    def far_first(self):
        low, high = 0 * self.z, 0 * self.z + self.n_planes - 1
        order = []
        for _ in range(self.n_planes):
            take_low = (self.z - low >= high - self.z).astype(jnp.int32)
            order.append(take_low * low + (1 - take_low) * high)
            low, high = low + take_low, high - (1 - take_low)
        return order

    def greet(self):
        barrier = pltpu.get_barrier_semaphore()
        fixed = [self.side, self.twin, self.across]
        for device in fixed:
            pl.semaphore_signal(barrier, inc=1, device_id=device, device_id_type=MESH)
        for condition, device in ((self.has_up, self.up), (self.has_down, self.down)):

            @pl.when(condition)
            def _(device=device):
                pl.semaphore_signal(barrier, inc=1, device_id=device, device_id_type=MESH)

        ends = self.has_up.astype(jnp.int32) + self.has_down.astype(jnp.int32)
        pl.semaphore_wait(barrier, len(fixed) + ends)


class Copies:
    def __init__(self, n_planes, send, recv):
        self.n_planes, self.send, self.recv = n_planes, send, recv
        self.open = []

    def copy(self, group, s, piece, src, dst, device, arrival=None):
        arrival = group if arrival is None else arrival
        return pltpu.make_async_remote_copy(
            src_ref=src,
            dst_ref=dst,
            send_sem=self.send.at[group * self.n_planes + s, piece],
            recv_sem=self.recv.at[arrival * self.n_planes + s, piece],
            device_id=device,
            device_id_type=MESH,
        )

    def start(self, condition, group, s, sources, targets, device, arrival=None):
        def body():
            for i, (src, dst) in enumerate(zip(sources, targets)):
                self.copy(group, s, i, src, dst, device, arrival).start()

        when(condition, body)
        self.open.append((condition, group, s, sources, targets, device, arrival))

    def arrive(self, group, s, targets, device):
        for i, dst in enumerate(targets):
            self.copy(group, s, i, dst, dst, device).wait_recv()

    def close(self):
        for condition, group, s, sources, targets, device, arrival in self.open:

            def body():
                for i, (src, dst) in enumerate(zip(sources, targets)):
                    self.copy(group, s, i, src, dst, device, arrival).wait_send()

            when(condition, body)


(Z_UP, Z_DOWN, Y_ALL, Y_HALF, X_ALL, X_HALF, C_OWN, C_Y, C_X, C_XH, C_YH) = range(11)
(ALL, FIRST, SECOND) = range(3)


class Spread:
    def __init__(self, spot, copies, own, views, use_x):
        self.spot, self.copies, self.own, self.use_x = spot, copies, own, use_x
        self.order = spot.far_first()[::-1]
        y, x, core = spot.y, spot.x, spot.core

        def places(s, cc):
            return (
                views(s, y, cc, x, ALL),
                views(s, 1 - y, cc, x, ALL),
                views(s, 1 - y, cc, x, FIRST),
                views(s, y, cc, 1 - x, ALL),
                views(s, y, cc, 1 - x, SECOND),
                views(s, 1 - y, cc, 1 - x, FIRST),
                views(s, 1 - y, cc, 1 - x, SECOND),
            )

        self.mine = [places(s, core) for s in self.order]
        self.twins = [places(s, 1 - core) for s in self.order]
        self.goes_down = [(s > spot.z) & spot.has_down for s in self.order]
        self.goes_up = [(s < spot.z) & spot.has_up for s in self.order]

    def place(self, j):
        return self.own if j == 0 else self.mine[j][0]

    def onward_y(self, j):
        self.copies.start(None, Y_ALL, self.order[j], self.place(j), self.mine[j][0], self.spot.side)

    def onward_x(self, j):
        self.copies.start(None, X_ALL, self.order[j], self.place(j), self.mine[j][0], self.spot.across)

    def onward_twin(self, j):
        self.copies.start(None, C_OWN, self.order[j], self.place(j), self.mine[j][0], self.spot.twin)

    def onward(self, j):
        self.onward_y(j)
        if self.use_x:
            self.onward_x(j)
        self.onward_twin(j)

    def begin_z(self):
        spot, here = self.spot, self.mine[0][0]
        self.copies.start(spot.has_up, Z_UP, spot.z, self.own, here, spot.up)
        self.copies.start(spot.has_down, Z_DOWN, spot.z, self.own, here, spot.down, Z_UP)

    def begin(self):
        self.begin_z()
        self.onward(0)

    def relay(self, j, goes=None):
        s, here, spot = self.order[j], self.mine[j][0], self.spot
        goes_down, goes_up = goes or (self.goes_down[j], self.goes_up[j])
        self.copies.arrive(Z_UP, s, here, spot.up)
        self.copies.start(goes_down, Z_DOWN, s, here, here, spot.down, Z_UP)
        self.copies.start(goes_up, Z_UP, s, here, here, spot.up)

    def column(self, j):
        if j < len(self.order):
            self.relay(j)
            self.onward(j)

    def from_side(self, j):
        s, there, spot = self.order[j], self.mine[j][1], self.spot
        self.copies.arrive(Y_ALL, s, there, spot.side)
        self.copies.start(None, C_Y, s, there, there, spot.twin)

    def from_across(self, j):
        s, there, spot = self.order[j], self.mine[j][3], self.spot
        self.copies.arrive(X_ALL, s, there, spot.across)
        self.copies.start(None, C_X, s, there, there, spot.twin)

    def over_x(self, j):
        part = self.mine[j][2]
        self.copies.start(None, X_HALF, self.order[j], part, part, self.spot.across)

    def over_y(self, j):
        part = self.mine[j][4]
        self.copies.start(None, Y_HALF, self.order[j], part, part, self.spot.side)

    def side(self, j):
        self.from_side(j)
        if self.use_x:
            self.over_x(j)

    def across(self, j):
        self.from_across(j)
        self.over_y(j)

    def sides(self, j):
        if 0 <= j < len(self.order):
            self.side(j)
            if self.use_x:
                self.across(j)

    def corner(self, j):
        if not self.use_x or not 0 <= j < len(self.order):
            return
        s, spot = self.order[j], self.spot
        first, second = self.mine[j][5:]
        self.copies.arrive(X_HALF, s, first, spot.across)
        self.copies.start(None, C_XH, s, first, first, spot.twin)
        self.copies.arrive(Y_HALF, s, second, spot.side)
        self.copies.start(None, C_YH, s, second, second, spot.twin)

    def twin_near(self, j):
        s, there, spot = self.order[j], self.twins[j], self.spot
        self.copies.arrive(C_OWN, s, there[0], spot.twin)
        if self.use_x:
            self.copies.arrive(C_X, s, there[3], spot.twin)

    def twin_side(self, j):
        self.copies.arrive(C_Y, self.order[j], self.twins[j][1], self.spot.twin)

    def twin_corner(self, j):
        self.copies.arrive(C_XH, self.order[j], self.twins[j][5], self.spot.twin)
        self.copies.arrive(C_YH, self.order[j], self.twins[j][6], self.spot.twin)

    def twin_far(self, j):
        self.twin_side(j)
        if self.use_x:
            self.twin_corner(j)

    def twin_all(self):
        for j in range(len(self.order)):
            self.twin_near(j)
            self.twin_far(j)

    def stage(self, step):
        self.column(step)
        self.sides(step - 1)
        self.corner(step - 2)

    def run(self):
        self.begin()
        for step in range(1, len(self.order) + 2):
            self.stage(step)
        self.twin_all()
        self.copies.close()


def dp_of(s, yy, cc):
    return (s * 2 + yy) * 2 + cc


def plain_dot(a, b, contract):
    return lax.dot_general(a, b, (contract, ((), ())), preferred_element_type=jnp.float32)


ROWS_COLUMNS = ((1,), (0,))
ROWS_ROWS = ((1,), (1,))
COLUMNS_COLUMNS = ((0,), (0,))


def turn(heads, cosine, sine):
    return heads * cosine + pltpu.roll(heads, heads.shape[1] // 2, 1) * sine


def front_kernel(n_planes, axes, *refs):
    n = len(axes)
    shards_in, (tokens, tile, grads, chosen, cosine, sine, allowed) = refs[:n], refs[n : n + 7]
    outs = refs[n + 7 : 2 * n + 7]
    (
        all_grads, params, normed_one, query, key, value, probs, mixed, residual, normed_two, gates,
    ) = refs[2 * n + 7 : 2 * n + 18]
    (
        wq, wk, wv, wo, sequence, pair, sent, received, w_send, w_recv, p_send, p_recv, g_send, g_recv, local,
        load, x_send, x_recv,
    ) = refs[2 * n + 18 :]
    spot = Spot(n_planes)
    x = spot.x
    bf16, f32 = jnp.bfloat16, jnp.float32
    own_rows, model = tokens.shape

    def weight_views(s, yy, cc, xx, part):
        i = dp_of(s, yy, cc)
        places = []
        for o, a, axis in zip(outs, shards_in, axes):
            size = a.shape[axis]
            span = pl.ds(pl.multiple_of(i * size, size), size)
            places.append(o.at[span] if axis == 0 else o.at[:, span])
        return places

    def param_views(s, yy, cc, xx, part):
        size = tile.shape[1]
        return [params.at[:, pl.ds(pl.multiple_of(dp_of(s, yy, cc) * size, size), size)]]

    def grad_views(s, yy, cc, xx, part):
        b = dp_of(s, yy, cc) * 2 + xx
        if part == ALL:
            return [all_grads.at[b]]
        return [all_grads.at[b, pl.ds(0 if part == FIRST else own_rows // 2, own_rows // 2)]]

    def mine(views):
        return views(spot.z, spot.y, spot.core, x, ALL)

    def swap(i, src, dst):
        return pltpu.make_async_remote_copy(
            src_ref=src, dst_ref=dst, send_sem=x_send.at[i], recv_sem=x_recv.at[i],
            device_id=spot.across, device_id_type=MESH,
        )

    kept = list(zip(list(shards_in) + [tokens, grads, tile], mine(weight_views) + [sequence.at[x]] + mine(grad_views) + [pair.at[x]]))
    kept = [pltpu.make_async_copy(a, b, local.at[i]) for i, (a, b) in enumerate(kept)]
    for c in kept:
        c.start()
    spot.greet()
    swaps = [swap(0, tile, pair.at[x]), swap(1, tokens, sequence.at[x]), swap(2, sent, received)]
    swaps[0].start()
    weights = Spread(spot, Copies(n_planes, w_send, w_recv), list(shards_in), weight_views, False)
    small = Spread(spot, Copies(n_planes, p_send, p_recv), mine(param_views), param_views, False)
    net = Spread(spot, Copies(n_planes, g_send, g_recv), [grads], grad_views, True)
    weights.begin()
    swaps[1].start()
    for c in kept:
        c.wait()
    swap(0, pair.at[1 - x], pair.at[1 - x]).wait_recv()
    mine(param_views)[0][...] = pair[0] + pair[1]
    small.begin()
    net.onward_x(0)
    net.onward_twin(0)
    for step in range(1, n_planes + 1):
        weights.stage(step)
        small.stage(step)
        if step == n_planes - 1:
            net.begin_z()
    net.onward_y(0)
    net.from_across(0)

    def column(j):
        net.relay(j)
        net.onward_x(j)
        net.onward_twin(j)

    column(1)

    small.twin_all()
    swap(1, sequence.at[1 - x], sequence.at[1 - x]).wait_recv()

    experts = chosen.shape[0]
    first_gain = params[experts : experts + 1, :].astype(f32)
    step = 32
    for h in range(2):
        for r in range(own_rows // step):
            rows = sequence[h, pl.ds(r * step, step)].astype(f32)
            scale = lax.rsqrt(jnp.mean(rows * rows, axis=1, keepdims=True) + norm_eps)
            normed_one[pl.ds(h * own_rows + r * step, step)] = (rows * scale * first_gain).astype(bf16)
    weights.twin_all()
    loads = [pltpu.make_async_copy(a, b, load.at[i]) for i, (a, b) in enumerate(zip(outs, (wq, wk, wv, wo)))]
    for c in loads:
        c.start()
    heads, head_dim = query.shape[1] // cosine.shape[1], cosine.shape[1]
    kv_heads = key.shape[1] // head_dim
    group = heads // kv_heads
    for c in loads[:3]:
        c.wait()
    cos, sin = cosine[...], sine[...]
    raw = plain_dot(normed_one[...], wk[...], ROWS_COLUMNS)
    for g in range(kv_heads):
        span = slice(g * head_dim, (g + 1) * head_dim)
        key[:, span] = turn(raw[:, span], cos, sin).astype(bf16)
    value[...] = plain_dot(normed_one[...], wv[...], ROWS_COLUMNS).astype(bf16)
    raw = plain_dot(normed_one[...], wq[...], ROWS_COLUMNS)
    for h in range(heads):
        span = slice(h * head_dim, (h + 1) * head_dim)
        query[:, span] = turn(raw[:, span], cos, sin).astype(bf16)
    net.from_side(0)
    net.onward_y(1)
    column(2)
    net.from_across(1)
    may = allowed[...] > 0.0
    for h in range(heads):
        span = slice(h * head_dim, (h + 1) * head_dim)
        shared = slice(h // group * head_dim, (h // group + 1) * head_dim)
        scores = plain_dot(query[:, span], key[:, shared], ROWS_ROWS) * (head_dim ** -0.5)
        scores = jnp.where(may, scores, neg_big)
        weight = jnp.exp(scores - jnp.max(scores, axis=1, keepdims=True))
        weight = weight / jnp.sum(weight, axis=1, keepdims=True)
        probs[h] = weight
        mixed[:, span] = plain_dot(weight.astype(bf16), value[:, shared], ROWS_COLUMNS).astype(bf16)
    loads[3].wait()
    other = mixed[pl.ds(pl.multiple_of((1 - x) * own_rows, own_rows), own_rows), :]
    sent[...] = plain_dot(other, wo[...], ROWS_COLUMNS).astype(bf16)
    swaps[2].start()
    other = mixed[pl.ds(pl.multiple_of(x * own_rows, own_rows), own_rows), :]
    residual[...] = plain_dot(other, wo[...], ROWS_COLUMNS)
    net.from_side(1)
    net.onward_y(2)
    column(3)
    net.from_across(2)
    swap(2, received, received).wait_recv()
    second_gain = params[experts + 1 : experts + 2, :].astype(f32)
    for r in range(own_rows // step):
        span = pl.ds(r * step, step)
        rows = sequence[x, span].astype(f32) + (residual[span] + received[span].astype(f32))
        residual[span] = rows
        scale = lax.rsqrt(jnp.mean(rows * rows, axis=1, keepdims=True) + norm_eps)
        normed_two[span] = (rows * scale * second_gain).astype(bf16)
    logits = plain_dot(params[:experts, :], normed_two[...], ROWS_ROWS)
    picked = chosen[...] > 0.0
    top = jnp.max(jnp.where(picked, logits, neg_big), axis=0, keepdims=True)
    weight = jnp.where(picked, jnp.exp(jnp.where(picked, logits - top, 0.0)), 0.0)
    gates[...] = weight / jnp.sum(weight, axis=0, keepdims=True)

    net.from_side(2)
    net.from_across(3)
    for j in range(n_planes):
        net.twin_near(j)
        if j < n_planes - 1:
            net.twin_side(j)
    for each in (weights, small, net):
        each.copies.close()
    for c in swaps:
        c.wait_send()


def front(arrays, axes, tokens, tile, grads, chosen, cosine, sine, allowed, n_dp, collective_id):
    n, n_planes = len(arrays), n_dp // 4
    bf16, f32 = jnp.bfloat16, jnp.float32
    shape = jax.ShapeDtypeStruct

    def whole(a, axis):
        full = list(a.shape)
        full[axis] *= n_dp
        return shape(tuple(full), a.dtype)

    own_rows, model = tokens.shape
    seq = 2 * own_rows
    experts = chosen.shape[0]
    wide, narrow_ = arrays[0].shape[1], arrays[1].shape[1]
    heads = wide // cosine.shape[1]
    gathered = [whole(a, axis) for a, axis in zip(arrays, axes)]
    vmem = pl.BlockSpec(memory_space=pltpu.VMEM)
    dma = pltpu.SemaphoreType.DMA
    return pl.pallas_call(
        functools.partial(front_kernel, n_planes, axes),
        out_shape=gathered
        + [
            shape((2 * n_dp,) + grads.shape, bf16),
            shape((tile.shape[0], tile.shape[1] * n_dp), bf16),
            shape((seq, model), bf16),
            shape((seq, wide), bf16),
            shape((seq, narrow_), bf16),
            shape((seq, narrow_), bf16),
            shape((heads, seq, seq), f32),
            shape((seq, wide), bf16),
            shape((own_rows, model), f32),
            shape((own_rows, model), bf16),
            shape((experts, own_rows), f32),
        ],
        in_specs=[ANY] * (n + 3) + [vmem] * 4,
        out_specs=[ANY] * (n + 1) + [vmem] * 10,
        scratch_shapes=[pltpu.VMEM(g.shape, bf16) for g in gathered]
        + [
            pltpu.VMEM((2, own_rows, model), bf16),
            pltpu.VMEM((2,) + tile.shape, bf16),
            pltpu.VMEM((own_rows, model), bf16),
            pltpu.VMEM((own_rows, model), bf16),
        ]
        + [dma((11 * n_planes, n))] * 2
        + [dma((11 * n_planes, 1))] * 4
        + [dma((n + 3,)), dma((n,)), dma((3,)), dma((3,))],
        compiler_params=pltpu.CompilerParams(
            collective_id=collective_id, has_side_effects=True, vmem_limit_bytes=56 << 20
        ),
        cost_estimate=pl.CostEstimate(
            flops=6 * seq * model * wide, bytes_accessed=16 * n_dp * own_rows * model, transcendentals=heads * seq * seq
        ),
    )(*arrays, tokens, tile, grads, chosen, cosine, sine, allowed)


(T_YX, T_Y, T_X, T_OWN, R_XHALF, R_YHALF, R_YALL, R_XALL, R_UP, R_DOWN) = range(10)


def add_up(target, sources):
    rows = target.shape[0]
    step = 16 if rows % 16 == 0 else rows

    def body(i, carry):
        span = pl.ds(pl.multiple_of(i * step, step), step)
        total = sources[0][span, :].astype(jnp.float32)
        for source in sources[1:]:
            total = total + source[span, :].astype(jnp.float32)
        target[span, :] = total.astype(target.dtype)
        return carry

    lax.fori_loop(0, rows // step, body, 0)


class Reduce:
    @staticmethod
    def scratch(shapes, dtypes, n_planes, use_x, cut=0, direct=False):
        kinds = 4 if use_x else 2
        out = []
        for i, (shape, dtype) in enumerate(zip(shapes, dtypes)):
            rows = cut if i == 0 else shape[0]
            out.append(pltpu.VMEM((kinds, n_planes) + shape, dtype))
            out.append(pltpu.VMEM((n_planes + 1,) + shape, dtype))
            out.append(pltpu.VMEM((n_planes,) + shape, dtype))
            if not direct:
                out.append(pltpu.VMEM((kinds, 2) + shape, dtype))
            if use_x:
                out.append(pltpu.VMEM((n_planes,) + shape, dtype))
                out.append(pltpu.VMEM((n_planes, rows) + shape[1:], dtype))
                if i == 0 and cut < shape[0]:
                    out.append(pltpu.VMEM((n_planes, shape[0] - cut) + shape[1:], dtype))
        n = len(shapes)
        out.append(pltpu.SemaphoreType.DMA((10 * n_planes, n)))
        out.append(pltpu.SemaphoreType.DMA((10 * n_planes, n)))
        out.append(pltpu.SemaphoreType.DMA((kinds * n_planes, n)))
        return out

    def __init__(self, spot, blocks, outs, scratch, use_x, cut=0, direct=False):
        self.spot, self.outs, self.use_x, self.direct = spot, outs, use_x, direct
        self.n, self.n_planes, self.cut = len(outs), spot.n_planes, cut
        left = list(scratch)
        self.twin, self.line, self.near, self.ring, self.across, self.first = [], [], [], [], [], []
        self.second = None
        for i in range(self.n):
            self.twin.append(left.pop(0))
            self.line.append(left.pop(0))
            self.near.append(left.pop(0))
            if not direct:
                self.ring.append(left.pop(0))
            if use_x:
                self.across.append(left.pop(0))
                self.first.append(left.pop(0))
                if i == 0 and cut < self.near[0].shape[1]:
                    self.second = left.pop(0)
        send, recv, self.local = left
        self.copies = Copies(self.n_planes, send, recv)
        y, x, core = spot.y, spot.x, spot.core
        self.order = spot.far_first()
        places = {T_YX: (1 - y, 1 - x), T_Y: (1 - y, x), T_X: (y, 1 - x), T_OWN: (y, x)}
        self.kinds = [T_YX, T_Y, T_X, T_OWN] if use_x else [T_Y, T_OWN]
        every = [(k, j) for j in range(self.n_planes) for k in self.kinds]
        self.terms = {(k, j): blocks(self.order[j], places[k][0], core, places[k][1]) for k, j in every}
        self.others = {(k, j): blocks(self.order[j], places[k][0], 1 - core, places[k][1]) for k, j in every}

    def load(self, kind, j):
        k, s = self.kinds.index(kind), self.order[j]
        return [
            pltpu.make_async_copy(ref, self.ring[i].at[k, j % 2], self.local.at[k * self.n_planes + s, i])
            for i, ref in enumerate(self.terms[kind, j])
        ]

    def start_load(self, kind, j):
        if not self.direct and j < self.n_planes:
            for c in self.load(kind, j):
                c.start()

    def start_loads(self):
        for j in range(2):
            for kind in self.kinds:
                self.start_load(kind, j)

    def start_twins(self):
        for j in range(self.n_planes):
            s = self.order[j]
            for k, kind in enumerate(self.kinds):
                self.copies.start(None, kind, s, self.others[kind, j], [t.at[k, s] for t in self.twin], self.spot.twin)

    def ready(self, kind, j):
        k, s = self.kinds.index(kind), self.order[j]
        twin = [t.at[k, s] for t in self.twin]
        self.copies.arrive(kind, s, twin, self.spot.twin)
        if self.direct:
            return twin, self.terms[kind, j]
        for c in self.load(kind, j):
            c.wait()
        return twin, [r.at[k, j % 2] for r in self.ring]

    def corner(self, j):
        if not self.use_x or not 0 <= j < self.n_planes:
            return
        s, cut = self.order[j], self.cut
        twin, mine = self.ready(T_YX, j)
        for m, t in zip(mine, twin):
            add_up(t, [m, t])
        self.start_load(T_YX, j + 2)
        head = twin if self.second is None else [twin[0].at[pl.ds(0, cut)]] + twin[1:]
        self.copies.start(None, R_XHALF, s, head, [f.at[s] for f in self.first], self.spot.across)
        if self.second is not None:
            tail = [twin[0].at[pl.ds(cut, self.second.shape[1])]]
            self.copies.start(None, R_YHALF, s, tail, [self.second.at[s]], self.spot.side)

    def side(self, j):
        s, cut = self.order[j], self.cut
        twin, mine = self.ready(T_Y, j)
        if self.use_x:
            first = [f.at[s] for f in self.first]
            self.copies.arrive(R_XHALF, s, first, self.spot.across)
        for i, (m, t) in enumerate(zip(mine, twin)):
            if not self.use_x:
                add_up(t, [m, t])
            elif i == 0 and self.second is not None:
                a, b = pl.ds(0, cut), pl.ds(cut, self.second.shape[1])
                add_up(t.at[a], [m.at[a], t.at[a], first[0]])
                add_up(t.at[b], [m.at[b], t.at[b]])
            else:
                add_up(t, [m, t, first[i]])
        self.start_load(T_Y, j + 2)
        self.copies.start(None, R_YALL, s, twin, [t.at[s] for t in self.near], self.spot.side)

    def over(self, j):
        s, cut = self.order[j], self.cut
        twin, mine = self.ready(T_X, j)
        if self.second is not None:
            self.copies.arrive(R_YHALF, s, [self.second.at[s]], self.spot.side)
        for i, (m, t) in enumerate(zip(mine, twin)):
            if i == 0 and self.second is not None:
                a, b = pl.ds(0, cut), pl.ds(cut, self.second.shape[1])
                add_up(t.at[a], [m.at[a], t.at[a]])
                add_up(t.at[b], [m.at[b], t.at[b], self.second.at[s]])
            else:
                add_up(t, [m, t])
        self.start_load(T_X, j + 2)
        self.copies.start(None, R_XALL, s, twin, [t.at[s] for t in self.across], self.spot.across)

    def sides(self, j):
        if 0 <= j < self.n_planes:
            self.side(j)
            if self.use_x:
                self.over(j)

    def column(self, j):
        if not 0 <= j < self.n_planes:
            return
        s, spot, copies, n = self.order[j], self.spot, self.copies, self.n
        twin, mine = self.ready(T_OWN, j)
        near = [t.at[s] for t in self.near]
        copies.arrive(R_YALL, s, near, spot.side)
        here = [[m, t, a] for m, t, a in zip(mine, twin, near)]
        if self.use_x:
            across = [t.at[s] for t in self.across]
            copies.arrive(R_XALL, s, across, spot.across)
            here = [h + [a] for h, a in zip(here, across)]
        line = [t.at[s] for t in self.line]

        def add_all(targets, *more):
            for i in range(n):
                add_up(targets[i], here[i] + [m[i] for m in more])

        if j == self.n_planes - 1:
            below = [t.at[self.n_planes] for t in self.line]
            when(spot.has_up, lambda: copies.arrive(R_DOWN, s, line, spot.up))
            when(spot.has_down, lambda: copies.arrive(R_UP, s, below, spot.down))
            when(spot.has_up & spot.has_down, lambda: add_all(self.outs, line, below))
            when(spot.z == 0, lambda: add_all(self.outs, line))
            when(spot.z == self.n_planes - 1, lambda: add_all(self.outs, below))
            return
        for goes, more, group, last, device, source in (
            (s < spot.z, spot.has_up, R_DOWN, None, spot.down, spot.up),
            (s > spot.z, spot.has_down, R_UP, s - spot.z == 1, spot.up, spot.down),
        ):

            def partial():
                copies.arrive(group, s, line, source)
                add_all(twin, line)

            when(goes & more, partial)
            when(goes & jnp.logical_not(more), lambda: add_all(twin))
            if last is None:
                copies.start(goes, group, s, twin, line, device)
            else:
                below = [t.at[self.n_planes] for t in self.line]
                copies.start(goes & last, group, s, twin, below, device)
                copies.start(goes & jnp.logical_not(last), group, s, twin, line, device)
        self.start_load(T_OWN, j + 2)

    def stage(self, step):
        self.corner(step)
        self.sides(step - 1)
        self.column(step - 2)

    def close(self):
        self.copies.close()


class WeightGradients:
    width = 256

    def __init__(self, ins, outs, scratch):
        self.sources, (self.hidden, self.shared) = ins[:4], ins[4:]
        self.outs = outs
        self.buffers, self.small_hidden, self.small_shared = scratch[:4], scratch[4], scratch[5]
        self.tall, self.flat, self.sums, self.load, self.store, self.once = scratch[6:]
        self.n_parts = self.sources[0].shape[1] // self.width

    @staticmethod
    def scratch(rows, tokens, width, shared):
        bf16, f32 = jnp.bfloat16, jnp.float32
        w = WeightGradients.width
        return [
            pltpu.VMEM((2, rows, w), bf16),
            pltpu.VMEM((2, rows, w), bf16),
            pltpu.VMEM((2, tokens, w), bf16),
            pltpu.VMEM((2, tokens, w), bf16),
            pltpu.VMEM((3, rows, width), bf16),
            pltpu.VMEM((tokens, shared), bf16),
            pltpu.VMEM((2, 2, w, width), f32),
            pltpu.VMEM((2, width, w), f32),
            pltpu.VMEM((2, shared, w), bf16),
            pltpu.SemaphoreType.DMA((2, 4)),
            pltpu.SemaphoreType.DMA((2, 4)),
            pltpu.SemaphoreType.DMA((2,)),
        ]

    def span(self, p):
        return pl.ds(p * self.width, self.width)

    def loads(self, p):
        return [
            pltpu.make_async_copy(a.at[:, self.span(p)], b.at[p % 2], self.load.at[p % 2, i])
            for i, (a, b) in enumerate(zip(self.sources, self.buffers))
        ]

    def stores(self, p):
        gate, up, down, shared = self.outs
        slot, span = p % 2, self.span(p)
        pairs = [
            (self.tall.at[slot, 0], gate.at[span]),
            (self.tall.at[slot, 1], up.at[span]),
            (self.flat.at[slot], down.at[:, span]),
            (self.sums.at[slot], shared.at[:, span]),
        ]
        return [pltpu.make_async_copy(a, b, self.store.at[slot, i]) for i, (a, b) in enumerate(pairs)]

    def resident(self):
        return [
            pltpu.make_async_copy(self.hidden, self.small_hidden, self.once.at[0]),
            pltpu.make_async_copy(self.shared, self.small_shared, self.once.at[1]),
        ]

    def begin(self):
        for c in self.resident() + self.loads(0):
            c.start()

    def part(self, p):
        if p >= self.n_parts:
            return
        if p == 0:
            for c in self.resident():
                c.wait()
        if p + 1 < self.n_parts:
            for c in self.loads(p + 1):
                c.start()
        for c in self.loads(p):
            c.wait()
        if p >= 2:
            for c in self.stores(p - 2):
                c.wait()
        slot = p % 2
        rows, grad_rows, tokens, grads = [b.at[slot] for b in self.buffers]

        def across(a, b):
            return lax.dot_general(a, b, (((0,), (0,)), ((), ())), preferred_element_type=jnp.float32)

        self.tall[slot, 0] = across(rows[...], self.small_hidden[1])
        self.tall[slot, 1] = across(rows[...], self.small_hidden[2])
        self.flat[slot] = across(self.small_hidden[0], grad_rows[...])
        n = self.small_shared.shape[1] // 3
        self.sums[slot, pl.ds(0, 2 * n)] = across(self.small_shared[:, n:], tokens[...]).astype(jnp.bfloat16)
        self.sums[slot, pl.ds(2 * n, n)] = across(self.small_shared[:, :n], grads[...]).astype(jnp.bfloat16)
        for c in self.stores(p):
            c.start()

    def end(self):
        for p in (self.n_parts - 2, self.n_parts - 1):
            for c in self.stores(p):
                c.wait()


def sum_kernel(n_planes, n, *refs):
    ins, work_ins, outs, work_outs = refs[:n], refs[n : n + 6], refs[n + 6 : 2 * n + 6], refs[2 * n + 6 : 2 * n + 10]
    scratch = refs[2 * n + 10 :]
    cut = len(scratch) - 12
    spot = Spot(n_planes)
    rows = ins[0].shape[1] // 2

    def blocks(s, yy, cc, xx):
        return [a.at[dp_of(s, yy, cc) * 2 + xx] for a in ins]

    net = Reduce(spot, blocks, outs, scratch[:cut], True, rows)
    work = WeightGradients(work_ins, work_outs, scratch[cut:])
    net.start_loads()
    spot.greet()
    net.start_twins()
    work.begin()
    done = 0
    for step in range(n_planes + 2):
        for action in (net.corner, net.sides, net.column):
            j = step - (net.corner, net.sides, net.column).index(action)
            action(j)
            if 0 <= j < n_planes and done < work.n_parts:
                work.part(done)
                done += 1
    net.close()
    work.end()


def sum_everywhere(arrays, out_dtypes, work_arrays, n_dp, collective_id):
    n, n_planes = len(arrays), n_dp // 4
    shapes = [a.shape[1:] for a in arrays]
    rows, model = work_arrays[0].shape
    tokens = work_arrays[2].shape[0]
    width = work_arrays[4].shape[2]
    shared = work_arrays[5].shape[1]
    return pl.pallas_call(
        functools.partial(sum_kernel, n_planes, n),
        out_shape=[jax.ShapeDtypeStruct(s, t) for s, t in zip(shapes, out_dtypes)]
        + [
            jax.ShapeDtypeStruct((model, width), jnp.float32),
            jax.ShapeDtypeStruct((model, width), jnp.float32),
            jax.ShapeDtypeStruct((width, model), jnp.float32),
            jax.ShapeDtypeStruct((shared, model), jnp.bfloat16),
        ],
        in_specs=[ANY] * (n + 6),
        out_specs=[pl.BlockSpec(memory_space=pltpu.VMEM)] * n + [ANY] * 4,
        scratch_shapes=Reduce.scratch(shapes, [a.dtype for a in arrays], n_planes, True, shapes[0][0] // 2)
        + WeightGradients.scratch(rows, tokens, width, shared),
        compiler_params=pltpu.CompilerParams(
            collective_id=collective_id, has_side_effects=True, vmem_limit_bytes=62 << 20
        ),
    )(*arrays, *work_arrays)


def back_kernel(n_planes, axes, *refs):
    n = len(axes)
    (
        grad_own, mixed, normed_one, query, key, value, probs, wq, wk, wv, wo, cosine, sine, tokens, grad_residual,
        gain, small, parts,
    ) = refs[:18]
    outs, grad_tokens, small_out, out_sum = refs[18 : 18 + n], *refs[18 + n : 21 + n]
    (
        grad_attn, grad_mixed, grad_query, grad_key, grad_value, gq, gk, gv, go, some_p, some_o, some_q, some_k,
        some_v, sent, received, terms, small_sum, small_in, load, x_send, x_recv,
    ) = refs[21 + n : 43 + n]
    scratch = refs[43 + n :]
    spot = Spot(n_planes)
    x = spot.x
    bf16, f32 = jnp.bfloat16, jnp.float32
    own_rows, model = tokens.shape
    grads = (gq, gk, gv, go)

    def weight_blocks(s, yy, cc, xx):
        i = dp_of(s, yy, cc)
        places = []
        for a, o, axis in zip(grads, outs, axes):
            size = o.shape[axis]
            span = pl.ds(pl.multiple_of(i * size, size), size)
            places.append(a.at[span] if axis == 0 else a.at[:, span])
        return places

    def small_blocks(s, yy, cc, xx):
        size = small_sum.shape[1]
        return [terms.at[:, pl.ds(pl.multiple_of(dp_of(s, yy, cc) * size, size), size)]]

    def token_blocks(s, yy, cc, xx):
        return [parts.at[dp_of(s, yy, cc) * 2 + xx]]

    count = 3 * n + 3
    weights = Reduce(spot, weight_blocks, outs, scratch[:count], False, direct=True)
    params = Reduce(spot, small_blocks, [small_sum], scratch[count : count + 6], False, direct=True)
    sums = Reduce(spot, token_blocks, [out_sum], scratch[count + 6 :], True, own_rows)

    def swap(i, src, dst):
        return pltpu.make_async_remote_copy(
            src_ref=src, dst_ref=dst, send_sem=x_send.at[i], recv_sem=x_recv.at[i],
            device_id=spot.across, device_id_type=MESH,
        )

    own = pltpu.make_async_copy(grad_own, grad_attn.at[x], load.at[4, 0])
    own.start()
    sums.start_loads()
    spot.greet()
    swap(0, grad_own, grad_attn.at[x]).start()
    sums.start_twins()
    terms[...] = small[...]

    heads, head_dim = probs.shape[0], cosine.shape[1]
    kv_heads = key.shape[1] // head_dim
    group = heads // kv_heads
    chunk = some_o.shape[1]
    n_chunks = wo.shape[0] // chunk
    per_chunk = chunk // head_dim

    def load_o(c):
        return pltpu.make_async_copy(wo.at[pl.ds(c * chunk, chunk)], some_o.at[c % 2], load.at[0, c % 2])

    def load_p(h):
        return pltpu.make_async_copy(probs.at[h], some_p.at[h % 2], load.at[1, h % 2])

    load_o(0).start()
    load_p(0).start()
    sums.corner(0)
    sums.sides(0)
    own.wait()
    swap(0, grad_attn.at[1 - x], grad_attn.at[1 - x]).wait_recv()
    whole = grad_attn[...].reshape(2 * own_rows, model)
    cos, sin = cosine[...], -sine[...]
    scale = head_dim ** -0.5
    for c in range(n_chunks):
        if c + 1 < n_chunks:
            load_o(c + 1).start()
        load_o(c).wait()
        span = slice(c * chunk, (c + 1) * chunk)
        grad_mixed[:, span] = plain_dot(whole, some_o[c % 2], ROWS_ROWS).astype(bf16)
        go[span, :] = plain_dot(mixed[:, span], whole, COLUMNS_COLUMNS).astype(bf16)
    sums.corner(1)
    sums.sides(1)
    for h in range(heads):
        if h + 1 < heads:
            load_p(h + 1).start()
        load_p(h).wait()
        span = slice(h * head_dim, (h + 1) * head_dim)
        shared = slice(h // group * head_dim, (h // group + 1) * head_dim)
        weight, back = some_p[h % 2], grad_mixed[:, span]
        grad_v = plain_dot(weight.astype(bf16), back, COLUMNS_COLUMNS)
        grad_p = plain_dot(back, value[:, shared], ROWS_ROWS)
        inner = jnp.sum(weight * grad_p, axis=1, keepdims=True)
        grad_s = (weight * (grad_p - inner)).astype(bf16)
        grad_q = plain_dot(grad_s, key[:, shared], ROWS_COLUMNS) * scale
        grad_query[:, span] = turn(grad_q, cos, sin).astype(bf16)
        grad_k = plain_dot(grad_s, query[:, span], COLUMNS_COLUMNS) * scale
        if h % group == 0:
            total_k, total_v = grad_k, grad_v
        else:
            total_k, total_v = total_k + grad_k, total_v + grad_v
        if h % group == group - 1:
            grad_key[:, shared] = turn(total_k, cos, sin).astype(bf16)
            grad_value[:, shared] = total_v.astype(bf16)
    for target, source in ((gk, grad_key), (gv, grad_value), (gq, grad_query)):
        target[...] = plain_dot(normed_one[...], source[...], COLUMNS_COLUMNS).astype(bf16)
    weights.start_twins()

    rows = some_q.shape[1]
    n_chunks = model // rows

    def load_w(c):
        span = pl.ds(c * rows, rows)
        return [
            pltpu.make_async_copy(w.at[span], b.at[c % 2], load.at[i, c % 2])
            for i, (w, b) in ((0, (wq, some_q)), (2, (wk, some_k)), (3, (wv, some_v)))
        ]

    for c in load_w(0):
        c.start()
    sums.column(0)
    sums.corner(2)
    sums.sides(2)
    weights.sides(0)
    other = pl.ds(pl.multiple_of((1 - x) * own_rows, own_rows), own_rows)
    mine = pl.ds(pl.multiple_of(x * own_rows, own_rows), own_rows)
    for c in range(n_chunks):
        if c + 1 < n_chunks:
            for each in load_w(c + 1):
                each.start()
        for each in load_w(c):
            each.wait()
        columns = slice(c * rows, (c + 1) * rows)
        for here, target in ((other, sent), (mine, grad_tokens)):
            total = plain_dot(grad_query[here, :], some_q[c % 2], ROWS_ROWS)
            total = total + plain_dot(grad_key[here, :], some_k[c % 2], ROWS_ROWS)
            total = total + plain_dot(grad_value[here, :], some_v[c % 2], ROWS_ROWS)
            target[:, columns] = total.astype(target.dtype)
    swap(1, sent, received).start()
    sums.column(1)
    sums.corner(3)
    sums.sides(3)
    weights.sides(1)
    swap(1, received, received).wait_recv()
    step = 32
    gain_row = gain[...].astype(f32)
    total = jnp.zeros((1, model), f32)
    for r in range(own_rows // step):
        span = pl.ds(r * step, step)
        rows_in = tokens[span, :].astype(f32)
        grad = grad_tokens[span, :] + received[span, :].astype(f32)
        size = lax.rsqrt(jnp.mean(rows_in * rows_in, axis=1, keepdims=True) + norm_eps)
        weighted = grad * gain_row
        inner = jnp.mean(rows_in * weighted, axis=1, keepdims=True)
        total = total + jnp.sum(grad * rows_in * size, axis=0, keepdims=True)
        grad_tokens[span, :] = size * weighted - rows_in * (size * size * size) * inner + grad_residual[span, :]
    place = small.shape[0] - 8
    terms[pl.ds(place, 1), :] = total
    params.start_twins()
    sums.column(2)
    weights.column(0)
    weights.sides(2)
    params.sides(0)
    sums.column(3)
    weights.column(1)
    weights.sides(3)
    for j in range(1, n_planes):
        params.sides(j)
        params.column(j - 1)
    weights.column(2)
    params.column(n_planes - 1)
    weights.column(3)
    swap(2, small_sum, small_in).start()
    swap(2, small_sum, small_in).wait()
    small_out[...] = small_sum[...] + small_in[...]
    swap(0, grad_own, grad_attn.at[x]).wait_send()
    swap(1, sent, received).wait_send()
    for each in (weights, params, sums):
        each.close()


def backward(
    grad_own, mixed, normed_one, query, key, value, probs, weights, axes, cosine, sine, tokens, grad_residual, gain,
    small, parts, n_dp, collective_id,
):
    n, n_planes = len(weights), n_dp // 4
    bf16, f32 = jnp.bfloat16, jnp.float32
    shape, vmem_ref = jax.ShapeDtypeStruct, pltpu.VMEM
    own_rows, model = tokens.shape
    seq = 2 * own_rows
    wide, narrow_ = query.shape[1], key.shape[1]

    def part(a, axis):
        some = list(a.shape)
        some[axis] //= n_dp
        return tuple(some)

    shapes = [part(a, axis) for a, axis in zip(weights, axes)]
    tile = (small.shape[0], model // n_dp)
    block = parts.shape[1:]
    vmem = pl.BlockSpec(memory_space=pltpu.VMEM)
    dma = pltpu.SemaphoreType.DMA
    chunk = 256
    return pl.pallas_call(
        functools.partial(back_kernel, n_planes, axes),
        out_shape=[shape(s, f32) for s in shapes] + [shape((own_rows, model), f32), shape(tile, f32), shape(block, f32)],
        in_specs=[ANY] + [vmem] * 5 + [ANY] * 5 + [vmem] * 6 + [ANY],
        out_specs=[vmem] * (n + 3),
        scratch_shapes=[
            vmem_ref((2, own_rows, model), bf16),
            vmem_ref((seq, wide), bf16),
            vmem_ref((seq, wide), bf16),
            vmem_ref((seq, narrow_), bf16),
            vmem_ref((seq, narrow_), bf16),
        ]
        + [vmem_ref(w.shape, bf16) for w in weights]
        + [
            vmem_ref((2,) + probs.shape[1:], f32),
            vmem_ref((2, chunk, model), bf16),
            vmem_ref((2, chunk, wide), bf16),
            vmem_ref((2, chunk, narrow_), bf16),
            vmem_ref((2, chunk, narrow_), bf16),
            vmem_ref((own_rows, model), bf16),
            vmem_ref((own_rows, model), bf16),
            vmem_ref(small.shape, f32),
            vmem_ref(tile, f32),
            vmem_ref(tile, f32),
            dma((5, 2)),
            dma((3,)),
            dma((3,)),
        ]
        + Reduce.scratch(shapes, [bf16] * n, n_planes, False, direct=True)
        + Reduce.scratch([tile], [f32], n_planes, False, direct=True)
        + Reduce.scratch([block], [parts.dtype], n_planes, True, block[0]),
        compiler_params=pltpu.CompilerParams(
            collective_id=collective_id, has_side_effects=True, vmem_limit_bytes=63 << 20
        ),
        cost_estimate=pl.CostEstimate(
            flops=12 * seq * model * wide, bytes_accessed=16 * n_dp * own_rows * model, transcendentals=0
        ),
    )(
        grad_own, mixed, normed_one, query, key, value, probs, *weights, cosine, sine, tokens, grad_residual, gain,
        small, parts,
    )
UNIT = 2


def dot_t(a, b):
    return lax.dot_general(a, b, (((1,), (1,)), ((), ())), preferred_element_type=jnp.float32)


def dot_f32(a, b):
    return lax.dot_general(a, b, (((1,), (0,)), ((), ())), preferred_element_type=jnp.float32)


class ExpertWork:
    def __init__(self, expert, weights, scratch):
        self.expert = expert
        self.w_gate, self.w_up, self.w_down, self.shared = weights
        (
            self.tokens, self.grads, self.rows, self.grad_rows, self.hidden, self.pre, self.left_out,
            self.left_grad, self.right_out, self.right_grad, self.out, self.back, self.shared_hidden,
        ) = scratch

    @staticmethod
    def scratch(model, width, capacity, own_rows):
        bf16 = jnp.bfloat16
        seq = 2 * own_rows
        return [
            pltpu.VMEM((2, 2 * UNIT, own_rows, model), bf16),
            pltpu.VMEM((2, 2 * UNIT, own_rows, model), bf16),
            pltpu.VMEM((2, UNIT * capacity, model), bf16),
            pltpu.VMEM((2, UNIT * capacity, model), bf16),
            pltpu.VMEM((2, 3, UNIT * capacity, width), bf16),
            pltpu.VMEM((3, UNIT * capacity, width), jnp.float32),
            pltpu.VMEM((UNIT, seq, capacity + 128), bf16),
            pltpu.VMEM((UNIT, seq, capacity + 256), bf16),
            pltpu.VMEM((UNIT, capacity + 128, model), bf16),
            pltpu.VMEM((UNIT, capacity + 256, model), bf16),
            pltpu.VMEM((2, 2 * UNIT, own_rows, model), bf16),
            pltpu.VMEM((2, 2 * UNIT, own_rows, model), bf16),
            pltpu.VMEM((2, UNIT * seq, 384), bf16),
        ]

    def prepare(self):
        capacity = self.rows.shape[1] // UNIT
        for q in range(UNIT):
            self.right_out[q, pl.ds(capacity, 128), :] = self.shared[pl.ds(256, 128), :]
            self.right_grad[q, pl.ds(capacity, 256), :] = self.shared[pl.ds(0, 256), :]

    def run(self, slot, unit, gates, grad_gates, hook):
        bf16, f32 = jnp.bfloat16, jnp.float32
        own_rows, model = self.tokens.shape[2:]
        seq = 2 * own_rows
        capacity = self.rows.shape[1] // UNIT
        experts = gates.shape[1]
        column = 1024
        n_columns = model // column
        first = unit * (2 * UNIT)
        before = lax.broadcasted_iota(jnp.int32, (seq, seq), 0) <= lax.broadcasted_iota(jnp.int32, (seq, seq), 1)
        before = before.astype(f32).astype(bf16)
        slots = lax.broadcasted_iota(jnp.int32, (capacity, seq), 0)
        picks, row_gates = [], []
        for q in range(UNIT):
            g = jnp.concatenate(
                [gates[first + 2 * q + h, pl.ds(self.expert, 1), :] for h in range(2)], axis=1
            )
            g = jnp.broadcast_to(g, (8, seq))
            taken = (g > 0.0).astype(f32)
            rank = dot_f32(taken.astype(bf16), before).astype(jnp.int32) - 1
            hit = (slots == rank[:1]) & (g[:1] > 0.0)
            pick = hit.astype(f32)
            picks.append(pick)
            row_gates.append(jnp.sum(pick * g[:1], axis=1, keepdims=True))
            self.left_out[q, :, pl.ds(0, capacity)] = pick.T.astype(bf16)
            self.left_grad[q, :, pl.ds(0, capacity)] = pick.T.astype(bf16)
            low = pick.astype(bf16)

            span = pl.ds(q * capacity, capacity)
            for source, target in ((self.tokens, self.rows), (self.grads, self.grad_rows)):
                whole = source[slot, pl.ds(2 * q, 2)].reshape(seq, model)
                target[slot, span] = dot_f32(low, whole).astype(bf16)
        hook(1)
        row_gate = jnp.concatenate(row_gates, axis=0)
        rows, grad_rows = self.rows.at[slot], self.grad_rows.at[slot]
        self.pre[0] = dot_f32(rows[...], self.w_gate[...])
        self.pre[1] = dot_f32(rows[...], self.w_up[...])
        self.pre[2] = dot_t(grad_rows[...], self.w_down[...])
        hook(2)
        step = 32
        parts = []
        for r in range(UNIT * capacity // step):
            span = pl.ds(r * step, step)
            gate_pre, up_pre, grad_hidden = self.pre[0, span], self.pre[1, span], self.pre[2, span]
            gate = row_gate[r * step : (r + 1) * step]
            sig = jax.nn.sigmoid(gate_pre)
            act = gate_pre * sig
            hidden = act * up_pre
            parts.append(jnp.sum(hidden * grad_hidden, axis=1, keepdims=True))
            grad_hidden = grad_hidden * gate
            self.hidden[slot, 0, span] = (hidden * gate).astype(bf16)
            slope = sig * (1.0 + gate_pre * (1.0 - sig))
            self.hidden[slot, 1, span] = (grad_hidden * up_pre * slope).astype(bf16)
            self.hidden[slot, 2, span] = (grad_hidden * act).astype(bf16)
        grad_gate_rows = jnp.concatenate(parts, axis=0)
        mine = lax.broadcasted_iota(jnp.int32, (experts, own_rows), 0) == self.expert
        for q in range(UNIT):
            per_token = jnp.sum(picks[q] * grad_gate_rows[q * capacity : (q + 1) * capacity], axis=0, keepdims=True)
            for h in range(2):
                part = jnp.broadcast_to(per_token[:, h * own_rows : (h + 1) * own_rows], (experts, own_rows))
                grad_gates[first + 2 * q + h] = jnp.where(mine, part, 0.0)

        for q in range(UNIT):
            blocks = pl.ds(2 * q, 2)
            whole = self.tokens[slot, blocks].reshape(seq, model)
            grad = self.grads[slot, blocks].reshape(seq, model)
            pre = dot_t(whole, self.shared[pl.ds(0, 256), :])
            grad_hidden = dot_t(grad, self.shared[pl.ds(256, 128), :])
            gate_pre, up_pre = pre[:, :128], pre[:, 128:]
            sig = jax.nn.sigmoid(gate_pre)
            act = gate_pre * sig
            hidden = (act * up_pre).astype(bf16)
            grad_gate = (grad_hidden * up_pre * sig * (1.0 + gate_pre * (1.0 - sig))).astype(bf16)
            grad_up = (grad_hidden * act).astype(bf16)
            span = pl.ds(q * seq, seq)
            self.shared_hidden[slot, span, pl.ds(0, 128)] = hidden
            self.shared_hidden[slot, span, pl.ds(128, 128)] = grad_gate
            self.shared_hidden[slot, span, pl.ds(256, 128)] = grad_up
            self.left_out[q, :, pl.ds(capacity, 128)] = hidden
            self.left_grad[q, :, pl.ds(capacity, 128)] = grad_gate
            self.left_grad[q, :, pl.ds(capacity + 128, 128)] = grad_up

        hook(3)

        def combine(c, carry):
            cols = pl.ds(pl.multiple_of(c * column, column), column)
            made = dot_f32(self.hidden[slot, 0], self.w_down[:, cols]).astype(bf16)
            back = dot_t(self.hidden[slot, 1], self.w_gate[cols, :])
            back = (back + dot_t(self.hidden[slot, 2], self.w_up[cols, :])).astype(bf16)
            for q in range(UNIT):
                span = slice(q * capacity, (q + 1) * capacity)
                self.right_out[q, pl.ds(0, capacity), cols] = made[span]
                self.right_grad[q, pl.ds(0, capacity), cols] = back[span]
                out = dot_f32(self.left_out[q], self.right_out[q, :, cols]).astype(bf16)
                self.out[slot, pl.ds(2 * q, 2), :, cols] = out.reshape(2, own_rows, column)
                out = dot_f32(self.left_grad[q], self.right_grad[q, :, cols]).astype(bf16)
                self.back[slot, pl.ds(2 * q, 2), :, cols] = out.reshape(2, own_rows, column)

            @pl.when(c == n_columns // 2)
            def _():
                hook(4)

            return carry

        lax.fori_loop(0, n_columns, combine, 0)


def expert_kernel(n_dp, *refs):
    own, own_gates, _, w_gate, w_up, w_down, shared = refs[:7]
    normed, grads, out_parts, back_parts, grad_gates, rows_out, grad_rows_out, hidden_out, shared_out = refs[7:16]
    scratch, (gates, load, store, local, send, recv, g_send, g_recv) = refs[16:-8], refs[-8:]
    n_planes = n_dp // 4
    spot = Spot(n_planes)
    half = own.shape[0] // 2

    def views(s, yy, cc, xx, part):
        b = dp_of(s, yy, cc) * 2 + xx
        if part == ALL:
            return [normed.at[b], gates.at[b]]
        if part == FIRST:
            return [normed.at[b, pl.ds(0, half)], gates.at[b]]
        return [normed.at[b, pl.ds(half, half)]]

    def grad_views(s, yy, cc, xx, part):
        b = dp_of(s, yy, cc) * 2 + xx
        if part == ALL:
            return [grads.at[b]]
        return [grads.at[b, pl.ds(0 if part == FIRST else half, half)]]

    kept = [
        pltpu.make_async_copy(a, v, local.at[i])
        for i, (a, v) in enumerate(zip((own, own_gates), views(spot.z, spot.y, spot.core, spot.x, ALL)))
    ]
    for c in kept:
        c.start()
    spot.greet()
    copies = Copies(n_planes, send, recv)
    net = Spread(spot, copies, [own, own_gates], views, True)
    rest = Spread(spot, Copies(n_planes, g_send, g_recv), None, grad_views, True)
    net.begin()
    work = ExpertWork(spot.dp, (w_gate, w_up, w_down, shared), scratch)
    work.prepare()
    n_units = n_dp // UNIT
    blocks = 2 * UNIT
    rows = work.rows.shape[1]
    seqs = work.shared_hidden.shape[1]
    order = net.order

    def unit_of(i):
        s = 0 * i
        for j, plane in enumerate(order):
            s = s + (i // 2 == j).astype(jnp.int32) * plane
        yy = spot.y + (i % 2) * (1 - 2 * spot.y)
        return s * 2 + yy

    def loads(u, slot):
        span = pl.ds(u * blocks, blocks)
        return [
            pltpu.make_async_copy(normed.at[span], work.tokens.at[slot], load.at[slot, 0]),
            pltpu.make_async_copy(grads.at[span], work.grads.at[slot], load.at[slot, 1]),
        ]

    def stores(u, slot):
        span = pl.ds(u * blocks, blocks)
        some = pl.ds(pl.multiple_of(u * rows, rows), rows)
        pairs = [
            (work.out.at[slot], out_parts.at[span]),
            (work.back.at[slot], back_parts.at[span]),
            (work.rows.at[slot], rows_out.at[some]),
            (work.grad_rows.at[slot], grad_rows_out.at[some]),
            (work.hidden.at[slot], hidden_out.at[:, some]),
            (work.shared_hidden.at[slot], shared_out.at[pl.ds(pl.multiple_of(u * seqs, seqs), seqs)]),
        ]
        return [pltpu.make_async_copy(a, b, store.at[slot, i]) for i, (a, b) in enumerate(pairs)]

    def load_unit(i):
        for c in loads(unit_of(jnp.int32(i)), i % 2):
            c.start()

    def near(j):
        net.twin_near(j)
        load_unit(2 * j)

    def far(j):
        net.twin_far(j)
        rest.twin_corner(j)
        if j == n_planes - 1:
            rest.twin_side(j)
        load_unit(2 * j + 1)

    def over(j):
        if j == n_planes - 1:
            rest.from_side(j)
        rest.over_x(j)
        rest.over_y(j)

    middle = spot.has_up & spot.has_down
    end = jnp.logical_not(middle)

    goes = {
        (j, c): (net.goes_down[j] & (middle if c else end), net.goes_up[j] & (middle if c else end))
        for j in range(1, n_planes)
        for c in (0, 1)
    }

    def relay(j, c):
        pl.when(middle if c else end)(functools.partial(net.relay, j, goes[j, c]))

    plan = {
        (0, 0): [(net.onward, 1)],
        (0, 1): [(net.corner, 0)],
        (0, 2): [(rest.corner, 0), (far, 0), (over, 1)],
        (0, 4): [(relay, 2, 0), (relay, 3, 1)],
        (1, 0): [(net.sides, 1)],
        (1, 1): [(net.onward, 2), (rest.onward_y, 3)],
        (1, 2): [(near, 1)],
        (1, 3): [(net.corner, 1), (rest.corner, 1)],
        (2, 0): [(far, 1), (over, 2)],
        (2, 3): [(net.sides, 2), (relay, 3, 0)],
        (2, 4): [(net.onward, 3)],
        (3, 0): [(near, 2), (over, 3)],
        (3, 1): [(net.corner, 2), (rest.corner, 2)],
        (4, 0): [(net.sides, 3), (far, 2)],
        (4, 3): [(net.corner, 3), (rest.corner, 3)],
        (5, 0): [(near, 3)],
        (6, 0): [(far, 3)],
    }

    net.relay(1)
    relay(2, 1)
    net.sides(0)
    over(0)
    for c in kept:
        c.wait()
    near(0)

    def body(i, carry):
        slot = i % 2
        u = unit_of(i)

        def hook(point):
            for (k, at), actions in plan.items():
                if at == point:

                    @pl.when(i == k)
                    def _(actions=actions):
                        for action, *values in actions:
                            action(*values)

        hook(0)

        for c in loads(u, slot):
            c.wait()

        @pl.when(i >= 2)
        def _():
            for c in stores(unit_of(i - 2), slot):
                c.wait()

        work.run(slot, u, gates, grad_gates, hook)
        for c in stores(u, slot):
            c.start()
        return carry

    lax.fori_loop(0, n_units, body, 0)
    for i in (n_units - 2, n_units - 1):
        for c in stores(unit_of(jnp.int32(i)), i % 2):
            c.wait()
    copies.close()
    rest.copies.close()


def expert_call(own, own_gates, grads, w_gate, w_up, w_down, shared, n_dp, capacity, collective_id):
    own_rows, model = own.shape
    blocks = 2 * n_dp
    width = w_gate.shape[1]
    bf16 = jnp.bfloat16
    rows = n_dp * capacity
    n_planes = n_dp // 4
    vmem = pl.BlockSpec(memory_space=pltpu.VMEM)
    everyone = jax.ShapeDtypeStruct((blocks, own_rows, model), bf16)
    all_gates = (blocks,) + own_gates.shape
    return pl.pallas_call(
        functools.partial(expert_kernel, n_dp),
        out_shape=[
            everyone,
            everyone,
            everyone,
            everyone,
            jax.ShapeDtypeStruct(all_gates, jnp.float32),
            jax.ShapeDtypeStruct((rows, model), bf16),
            jax.ShapeDtypeStruct((rows, model), bf16),
            jax.ShapeDtypeStruct((3, rows, width), bf16),
            jax.ShapeDtypeStruct((blocks * own_rows, 384), bf16),
        ],
        in_specs=[ANY, ANY, ANY, vmem, vmem, vmem, vmem],
        out_specs=[ANY, ANY, ANY, ANY, vmem, ANY, ANY, ANY, ANY],
        input_output_aliases={2: 1},
        scratch_shapes=ExpertWork.scratch(model, width, capacity, own_rows)
        + [
            pltpu.VMEM(all_gates, jnp.float32),
            pltpu.SemaphoreType.DMA((2, 2)),
            pltpu.SemaphoreType.DMA((2, 6)),
            pltpu.SemaphoreType.DMA((2,)),
            pltpu.SemaphoreType.DMA((11 * n_planes, 2)),
            pltpu.SemaphoreType.DMA((11 * n_planes, 2)),
            pltpu.SemaphoreType.DMA((11 * n_planes, 1)),
            pltpu.SemaphoreType.DMA((11 * n_planes, 1)),
        ],
        compiler_params=pltpu.CompilerParams(
            collective_id=collective_id, has_side_effects=True, vmem_limit_bytes=60 << 20
        ),
    )(own, own_gates, grads, w_gate, w_up, w_down, shared)


def gather_plan(
    tokens,
    attention_gain,
    expert_norm_gain,
    query_projection,
    key_projection,
    value_projection,
    output_projection,
    router,
    shared_gate_matrix,
    shared_up_matrix,
    shared_down_matrix,
    expert_gate_matrix,
    expert_up_matrix,
    expert_down_matrix,
    document_lengths,
    expert_indices,
    cotangent,
):
    n_dp = lax.axis_size(DP)
    x = lax.axis_index(TENSOR)
    dp = lax.axis_index(DP)
    own_rows, model_dim = tokens.shape
    sequence_length = own_rows * 2
    experts = n_dp
    top_k = expert_indices.shape[1]
    capacity = sequence_length * top_k * 4 // (3 * experts)
    bf16, f32 = jnp.bfloat16, jnp.float32

    def dot(a, b):
        return jnp.dot(a, b, preferred_element_type=f32)

    width = attention_gain.shape[0]
    lanes = 2 * width
    tile = jnp.concatenate(
        [router.T, attention_gain[None], expert_norm_gain[None], jnp.zeros((-(experts + 2) % 16, width), bf16)]
    )
    tile = lax.dynamic_update_slice(jnp.zeros((tile.shape[0], lanes), bf16), tile, (0, x * width))
    rotary_cosine, rotary_sine = rotation(sequence_length, HEAD_SIZE)
    cosine = jnp.concatenate([rotary_cosine, rotary_cosine], axis=1)
    sine = jnp.concatenate([-rotary_sine, rotary_sine], axis=1)
    doc_ends = jnp.cumsum(document_lengths[0])
    positions = jnp.arange(sequence_length, dtype=jnp.int32)
    doc_ids = jnp.sum((positions[:, None] >= doc_ends[None, :]).astype(jnp.int32), axis=-1)
    allowed = (doc_ids[:, None] == doc_ids[None, :]) & (positions[:, None] >= positions[None, :])
    own_indices = lax.dynamic_slice_in_dim(expert_indices, x * own_rows, own_rows, 0)
    chosen = jnp.any(own_indices[None] == jnp.arange(experts, dtype=jnp.int32)[:, None, None], axis=2)
    axes = (0, 0, 0, 1)
    (
        query_all, key_all, value_all, out_all, cotangent_all, params, full_one, rows_of_query, key_rows,
        rows_of_value, attn_probs, mixed_heads, residual, normed_two, gates_t,
    ) = front(
        [query_projection, key_projection, value_projection, output_projection],
        axes, tokens, tile, cotangent, chosen.astype(f32), cosine, sine, allowed.astype(f32), n_dp, 1,
    )
    router_full = params[:experts]
    first_gain = params[experts].astype(f32)
    second_gain = params[experts + 1].astype(f32)

    hidden = shared_gate_matrix.shape[1] // n_dp
    hidden_pad = -(-hidden // 16) * 16

    def slices(transposed):
        blocks = transposed.reshape(n_dp, hidden, -1)
        return jnp.pad(blocks, ((0, 0), (0, hidden_pad - hidden), (0, 0)))

    shared_out = jnp.stack(
        [slices(shared_gate_matrix.T), slices(shared_up_matrix.T), slices(shared_down_matrix)], axis=1
    )
    shared_in = lax.all_to_all(shared_out, DP, split_axis=0, concat_axis=0, tiled=True)
    shared_rows = jnp.moveaxis(shared_in, 0, 2).reshape(3, hidden_pad, model_dim)

    shared_rows = jnp.pad(shared_rows, ((0, 0), (0, 128 - hidden_pad), (0, 0))).reshape(384, model_dim)
    (
        normed_all, cotangent_all, output_parts, normed_parts, grad_gate_parts, received, grad_rows, hidden_rows,
        shared_hidden,
    ) = (
        expert_call(
            normed_two, gates_t, cotangent_all, expert_gate_matrix[0], expert_up_matrix[0], expert_down_matrix[0],
            shared_rows, n_dp, capacity, 2,
        )
    )
    (
        grad_normed_two, grad_gates_t, expert_gate_gradient, expert_up_gradient, expert_down_gradient, shared_grads,
    ) = sum_everywhere(
        [normed_parts, grad_gate_parts],
        [f32, f32],
        [
            received, grad_rows, normed_all.reshape(-1, model_dim), cotangent_all.reshape(-1, model_dim),
            hidden_rows, shared_hidden,
        ],
        n_dp, 4,
    )
    shared_grads = shared_grads.reshape(3, 128, model_dim)[:, :hidden_pad]

    gates = gates_t.T
    scale_two = lax.rsqrt(jnp.mean(residual * residual, axis=-1, keepdims=True) + norm_eps)
    grad_gates = grad_gates_t.T
    grad_logits = (
        gates * (grad_gates - jnp.sum(gates * grad_gates, axis=-1, keepdims=True))
    ).astype(bf16)
    grad_normed_two = grad_normed_two + dot(grad_logits, router_full)
    grad_router_part = dot(normed_two.T, grad_logits)
    grad_residual, grad_gain_two = rms_back(grad_normed_two, residual, scale_two, second_gain)
    grad_residual = grad_residual + cotangent.astype(f32)
    small_grads = jnp.concatenate([grad_router_part.T, jnp.zeros((8, model_dim), f32).at[1].set(grad_gain_two)])
    *weight_grads, grad_inputs, small_sums, ffn_own = backward(
        grad_residual.astype(bf16), mixed_heads, full_one, rows_of_query, key_rows, rows_of_value, attn_probs,
        [query_all, key_all, value_all, out_all], axes, cosine, sine, tokens, grad_residual, first_gain[None],
        small_grads, output_parts, n_dp, 6,
    )
    output = (residual + ffn_own).astype(bf16)
    mine = lax.dynamic_slice_in_dim(small_sums, x * width, width, 1)
    gain_one_own, gain_two_own, router_own = mine[experts], mine[experts + 1], mine[:experts].T
    returned = lax.all_to_all(
        shared_grads.reshape(3, hidden_pad, n_dp, -1).transpose(2, 0, 1, 3),
        DP, split_axis=0, concat_axis=0, tiled=True,
    )[:, :, :hidden]
    returned = returned.transpose(1, 0, 2, 3).reshape(3, n_dp * hidden, -1).astype(f32)
    return (
        output,
        grad_inputs,
        gain_one_own,
        gain_two_own,
        *weight_grads,
        router_own,
        returned[0].T,
        returned[1].T,
        returned[2],
        expert_gate_gradient[None],
        expert_up_gradient[None],
        expert_down_gradient[None],
    )


def shards(*arguments):
    tokens, expert_gate_matrix = arguments[0], arguments[11]
    n_dp, n_tensor = lax.axis_size(DP), lax.axis_size(TENSOR)
    gathered = n_dp * n_tensor * tokens.shape[0] * tokens.shape[1] * 2
    if n_tensor == 2 and n_dp % 4 == 0 and expert_gate_matrix.shape[0] == 1 and gathered <= 32 << 20:
        return gather_plan(*arguments)
    return exchange_plan(*arguments)


def solution(mesh):
    placed = (
        P((DP, TENSOR), None),
        P((DP, TENSOR)),
        P((DP, TENSOR)),
        P(DP, TENSOR),
        P(DP, TENSOR),
        P(DP, TENSOR),
        P(TENSOR, DP),
        P((DP, TENSOR), None),
        P(DP, TENSOR),
        P(DP, TENSOR),
        P(TENSOR, DP),
        P(DP, None, TENSOR),
        P(DP, None, TENSOR),
        P(DP, TENSOR, None),
        P(DP, None),
        P(DP, None),
        P((DP, TENSOR), None),
    )
    return jax.shard_map(
        shards,
        mesh=mesh,
        in_specs=placed,
        out_specs=(
            P((DP, TENSOR), None),
            P((DP, TENSOR), None),
            P((DP, TENSOR)),
            P((DP, TENSOR)),
            P(DP, TENSOR),
            P(DP, TENSOR),
            P(DP, TENSOR),
            P(TENSOR, DP),
            P((DP, TENSOR), None),
            P(DP, TENSOR),
            P(DP, TENSOR),
            P(TENSOR, DP),
            P(DP, None, TENSOR),
            P(DP, None, TENSOR),
            P(DP, TENSOR, None),
        ),
        check_vma=False,
    )
```

```python
import functools
import math

import jax
import jax.numpy as jnp
from jax import lax
from jax.experimental import pallas as pl
from jax.experimental.pallas import tpu as pltpu
from jax.sharding import PartitionSpec as P

HEAD_SIZE = 128
DP, TENSOR = ("dp", "tensor")


norm_eps = 1e-06
rope_base = 600000.0
neg_big = -1e30


def silu(argument):
    return argument * jax.nn.sigmoid(argument)


def silu_slope(argument):
    sigmoid_of = jax.nn.sigmoid(argument)
    return sigmoid_of * (1.0 + argument * (1.0 - sigmoid_of))


def rotation(sequence_length, head_dim):
    half_dim = head_dim // 2
    frequency = jnp.exp(
        jnp.arange(half_dim, dtype=jnp.float32) * (-2.0 * math.log(rope_base) / head_dim)
    )
    angles = jnp.arange(sequence_length, dtype=jnp.float32)[:, None] * frequency[None, :]
    return (jnp.cos(angles), jnp.sin(angles))


def apply_rotary(tensor, rotary_cosine, rotary_sine):
    half_dim = tensor.shape[-1] // 2
    first_half = tensor[..., :half_dim]
    second_half = tensor[..., half_dim:]
    cos_rows = rotary_cosine[:, None, :]
    sin_rows = rotary_sine[:, None, :]
    return jnp.concatenate(
        [
            first_half * cos_rows - second_half * sin_rows,
            second_half * cos_rows + first_half * sin_rows,
        ],
        axis=-1,
    )


def rotate_back(tensor, rotary_cosine, rotary_sine):
    return apply_rotary(tensor, rotary_cosine, -rotary_sine)


def rms_back(grad_normed, source, scale_rows, gain_full):
    weighted = grad_normed * gain_full
    cubed = scale_rows * scale_rows * scale_rows
    grad_source = scale_rows * weighted - source * cubed * jnp.mean(
        source * weighted, axis=-1, keepdims=True
    )
    grad_gain = jnp.sum(grad_normed * source * scale_rows, axis=0)
    return (grad_source, grad_gain)


def widen(sharded):
    return lax.all_gather(sharded, TENSOR, axis=0, tiled=True)


def narrow(partial_sum):
    return lax.psum_scatter(partial_sum, TENSOR, scatter_dimension=0, tiled=True)


def dense_fetch(
    query_projection,
    key_projection,
    value_projection,
    output_projection,
    shared_gate_matrix,
    shared_up_matrix,
    shared_down_matrix,
):
    return (
        lax.all_gather(query_projection, DP, axis=0, tiled=True),
        lax.all_gather(key_projection, DP, axis=0, tiled=True),
        lax.all_gather(value_projection, DP, axis=0, tiled=True),
        lax.all_gather(output_projection, DP, axis=1, tiled=True),
        lax.all_gather(shared_gate_matrix, DP, axis=0, tiled=True),
        lax.all_gather(shared_up_matrix, DP, axis=0, tiled=True),
        lax.all_gather(shared_down_matrix, DP, axis=1, tiled=True),
    )


def expert_up_output(received_rows, expert_gate_matrix, expert_up_matrix, expert_down_matrix):
    gate_preactivation = jnp.einsum(
        "miwy,iyh->miwh", received_rows, expert_gate_matrix, preferred_element_type=jnp.float32
    )
    up_preactivation = jnp.einsum(
        "miwy,iyh->miwh", received_rows, expert_up_matrix, preferred_element_type=jnp.float32
    )
    hidden = (silu(gate_preactivation) * up_preactivation).astype(jnp.bfloat16)
    produced_rows = jnp.einsum(
        "sxcf,xfd->sxcd", hidden, expert_down_matrix, preferred_element_type=jnp.float32
    ).astype(jnp.bfloat16)
    return (produced_rows, gate_preactivation, up_preactivation)


def expert_gradients(
    received,
    received_gradient,
    gate_preactivation,
    up_preactivation,
    expert_gate_matrix,
    expert_up_matrix,
    expert_down_matrix,
):
    hidden_expert = (silu(gate_preactivation) * up_preactivation).astype(jnp.bfloat16)
    expert_down_gradient = jnp.einsum(
        "sxcf,sxcd->xfd", hidden_expert, received_gradient, preferred_element_type=jnp.float32
    )
    grad_hidden_e = jnp.einsum(
        "sxcd,xfd->sxcf", received_gradient, expert_down_matrix, preferred_element_type=jnp.float32
    )
    grad_gate_e = (grad_hidden_e * up_preactivation * silu_slope(gate_preactivation)).astype(
        jnp.bfloat16
    )
    expert_up_hidden_gradient = (grad_hidden_e * silu(gate_preactivation)).astype(jnp.bfloat16)
    expert_gate_gradient = jnp.einsum(
        "gayi,gayr->air", received, grad_gate_e, preferred_element_type=jnp.float32
    )
    expert_up_gradient = jnp.einsum(
        "gayi,gayr->air", received, expert_up_hidden_gradient, preferred_element_type=jnp.float32
    )
    output_rows_gradient = (
        jnp.einsum(
            "zkjh,klh->zkjl", grad_gate_e, expert_gate_matrix, preferred_element_type=jnp.float32
        )
        + jnp.einsum(
            "zkjh,klh->zkjl",
            expert_up_hidden_gradient,
            expert_up_matrix,
            preferred_element_type=jnp.float32,
        )
    ).astype(jnp.bfloat16)
    return (expert_gate_gradient, expert_up_gradient, expert_down_gradient, output_rows_gradient)


def exchange_plan(
    tokens,
    attention_gain,
    expert_norm_gain,
    query_projection,
    key_projection,
    value_projection,
    output_projection,
    router,
    shared_gate_matrix,
    shared_up_matrix,
    shared_down_matrix,
    expert_gate_matrix,
    expert_up_matrix,
    expert_down_matrix,
    document_lengths,
    expert_indices,
    cotangent,
):
    n_tensor = lax.axis_size(TENSOR)
    n_dp = lax.axis_size(DP)
    tensor_pos = lax.axis_index(TENSOR)
    own_rows = tokens.shape[0]
    sequence_length = own_rows * n_tensor
    model_dim = tokens.shape[1]
    exp_dev = expert_gate_matrix.shape[0]
    experts = exp_dev * n_dp
    top_k = expert_indices.shape[1]
    capacity = max(2, sequence_length * top_k * 4 // (3 * experts))
    slot_total = experts * capacity
    router_full, gain_first, gain_second = (
        lax.all_gather(router, (DP, TENSOR), axis=0, tiled=True),
        lax.all_gather(attention_gain, (DP, TENSOR), axis=0, tiled=True),
        lax.all_gather(expert_norm_gain, (DP, TENSOR), axis=0, tiled=True),
    )
    first_gain = gain_first.astype(jnp.float32)
    second_gain = gain_second.astype(jnp.float32)
    fetched = dense_fetch(
        query_projection,
        key_projection,
        value_projection,
        output_projection,
        shared_gate_matrix,
        shared_up_matrix,
        shared_down_matrix,
    )
    query_all, key_all, value_all, out_all, sgate_all, sup_all, sdown_all = fetched
    input_values = tokens.astype(jnp.float32)
    scale_one = lax.rsqrt(jnp.mean(input_values * input_values, axis=-1, keepdims=True) + norm_eps)
    normed_one = (input_values * scale_one * first_gain).astype(jnp.bfloat16)
    full_one = widen(normed_one)
    q_heads = query_all.shape[1] // HEAD_SIZE
    kv_heads = key_all.shape[1] // HEAD_SIZE
    group_size = q_heads // kv_heads
    rotary_cosine, rotary_sine = rotation(sequence_length, HEAD_SIZE)
    query_unrotated = jnp.dot(full_one, query_all, preferred_element_type=jnp.float32).reshape(
        sequence_length, q_heads, HEAD_SIZE
    )
    key_unrotated = jnp.dot(full_one, key_all, preferred_element_type=jnp.float32).reshape(
        sequence_length, kv_heads, HEAD_SIZE
    )
    rows_of_query = (
        apply_rotary(query_unrotated, rotary_cosine, rotary_sine)
        .astype(jnp.bfloat16)
        .reshape(sequence_length, kv_heads, group_size, HEAD_SIZE)
    )
    key_rows = apply_rotary(key_unrotated, rotary_cosine, rotary_sine).astype(jnp.bfloat16)
    rows_of_value = (
        jnp.dot(full_one, value_all, preferred_element_type=jnp.float32)
        .astype(jnp.bfloat16)
        .reshape(sequence_length, kv_heads, HEAD_SIZE)
    )
    doc_ends = jnp.cumsum(document_lengths[0])
    positions = jnp.arange(sequence_length, dtype=jnp.int32)
    doc_ids = jnp.sum((positions[:, None] >= doc_ends[None, :]).astype(jnp.int32), axis=-1)
    score_scale = HEAD_SIZE ** (-0.5)

    def block_scores(start_row, end_row):
        scores = (
            jnp.einsum(
                "qkgd,skd->kgqs", rows_of_query, key_rows, preferred_element_type=jnp.float32
            )
            * score_scale
        )
        allowed = (doc_ids[start_row:end_row, None] == doc_ids[None, :end_row]) & (
            positions[start_row:end_row, None] >= positions[None, :end_row]
        )
        return (scores, allowed)

    block_index = 0
    start_row = block_index * sequence_length
    end_row = start_row + sequence_length
    scores, allowed = block_scores(start_row, end_row)
    scores = jnp.where(allowed, scores, neg_big)
    row_max = jnp.max(scores, axis=-1, keepdims=True)
    exp_scores = jnp.exp(scores - row_max)
    row_sum = jnp.sum(exp_scores, axis=-1, keepdims=True)
    lse_blocks = [row_max + jnp.log(row_sum)]
    attn_probs = (exp_scores / row_sum).astype(jnp.bfloat16)
    out_blocks = jnp.einsum(
        "kgqs,skd->qkgd", attn_probs, rows_of_value, preferred_element_type=jnp.float32
    )
    mixed_heads = out_blocks.reshape(sequence_length, q_heads * HEAD_SIZE).astype(jnp.bfloat16)
    attn_part = jnp.dot(mixed_heads, out_all, preferred_element_type=jnp.float32)
    residual = input_values + narrow(attn_part)
    scale_two = lax.rsqrt(jnp.mean(residual * residual, axis=-1, keepdims=True) + norm_eps)
    normed_two = (residual * scale_two * second_gain).astype(jnp.bfloat16)
    full_two = widen(normed_two)
    logits = jnp.dot(full_two, router_full, preferred_element_type=jnp.float32)
    chosen = expert_indices[:, :, None] == jnp.arange(experts, dtype=jnp.int32)[None, None, :]
    selected = jnp.sum(jnp.where(chosen, logits[:, None, :], 0.0), axis=-1)
    top_max = jnp.max(selected, axis=-1, keepdims=True)
    gate_exp = jnp.exp(selected - top_max)
    gate_probs = gate_exp / jnp.sum(gate_exp, axis=-1, keepdims=True)
    gate_shared = jnp.dot(full_two, sgate_all, preferred_element_type=jnp.float32)
    up_shared = jnp.dot(full_two, sup_all, preferred_element_type=jnp.float32)
    hidden_shared = (silu(gate_shared) * up_shared).astype(jnp.bfloat16)
    shared_part = jnp.dot(hidden_shared, sdown_all, preferred_element_type=jnp.float32)
    flat_ids = expert_indices.reshape(-1)
    onehot = (flat_ids[:, None] == jnp.arange(experts, dtype=jnp.int32)[None, :]).astype(jnp.int32)
    slot_rank = jnp.sum(onehot * (jnp.cumsum(onehot, axis=0) - 1), axis=-1)
    slot_index = flat_ids * capacity + slot_rank
    pair_index = jnp.arange(sequence_length * top_k, dtype=jnp.int32)
    token_of_slot = jnp.zeros((slot_total,), jnp.int32).at[slot_index].set(pair_index // top_k)
    slot_used = jnp.zeros((slot_total,), jnp.bool_).at[slot_index].set(True)
    gate_of_slot = jnp.zeros((slot_total,), jnp.float32).at[slot_index].set(gate_probs.reshape(-1))
    outgoing = jnp.where(slot_used[:, None], full_two[token_of_slot], 0).reshape(
        n_dp, exp_dev, capacity, model_dim
    )
    received_rows = lax.all_to_all(outgoing, DP, split_axis=0, concat_axis=0, tiled=True)
    produced_rows, gate_preactivation, up_preactivation = expert_up_output(
        received_rows, expert_gate_matrix, expert_up_matrix, expert_down_matrix
    )
    sent_home = lax.all_to_all(produced_rows, DP, split_axis=0, concat_axis=0, tiled=True)
    returned, received, gate_preactivation, up_preactivation = (
        sent_home,
        received_rows,
        gate_preactivation,
        up_preactivation,
    )
    picked = returned.reshape(slot_total, model_dim)[slot_index].reshape(
        sequence_length, top_k, model_dim
    )
    routed_part = jnp.einsum("sk,skd->sd", gate_probs, picked, preferred_element_type=jnp.float32)
    ffn_own = narrow(shared_part + routed_part)
    output = (residual + ffn_own).astype(jnp.bfloat16)
    weights_back = dense_fetch(
        query_projection,
        key_projection,
        value_projection,
        output_projection,
        shared_gate_matrix,
        shared_up_matrix,
        shared_down_matrix,
    )
    query_back, key_back, value_back, out_back, sgate_back, sup_back, sdown_back = weights_back
    grad_out = cotangent.astype(jnp.float32)
    grad_ffn = widen(cotangent)
    grad_hidden_sh = jnp.dot(grad_ffn, sdown_back.T, preferred_element_type=jnp.float32)
    grad_sdown = jnp.dot(hidden_shared.T, grad_ffn, preferred_element_type=jnp.float32)
    grad_gate_sh = (grad_hidden_sh * up_shared * silu_slope(gate_shared)).astype(jnp.bfloat16)
    grad_up_sh = (grad_hidden_sh * silu(gate_shared)).astype(jnp.bfloat16)
    grad_sgate = jnp.dot(full_two.T, grad_gate_sh, preferred_element_type=jnp.float32)
    grad_sup = jnp.dot(full_two.T, grad_up_sh, preferred_element_type=jnp.float32)
    grad_normed_part = jnp.dot(
        grad_gate_sh, sgate_back.T, preferred_element_type=jnp.float32
    ) + jnp.dot(grad_up_sh, sup_back.T, preferred_element_type=jnp.float32)
    grad_gates_part = jnp.einsum("sd,skd->sk", grad_ffn, picked, preferred_element_type=jnp.float32)
    grad_slot = (
        jnp.where(slot_used[:, None], grad_ffn[token_of_slot] * gate_of_slot[:, None], 0.0)
        .astype(jnp.bfloat16)
        .reshape(n_dp, exp_dev, capacity, model_dim)
    )
    received_gradient = lax.all_to_all(grad_slot, DP, split_axis=0, concat_axis=0, tiled=True)
    expert_gate_gradient, expert_up_gradient, expert_down_gradient, output_rows_gradient = (
        expert_gradients(
            received,
            received_gradient,
            gate_preactivation,
            up_preactivation,
            expert_gate_matrix,
            expert_up_matrix,
            expert_down_matrix,
        )
    )
    grad_returned = lax.all_to_all(
        output_rows_gradient, DP, split_axis=0, concat_axis=0, tiled=True
    )
    grad_picked = grad_returned.reshape(slot_total, model_dim)[slot_index].reshape(
        sequence_length, top_k, model_dim
    )
    grad_normed_part = grad_normed_part + jnp.sum(grad_picked, axis=1, dtype=jnp.float32)
    grad_normed_two, grad_gates = (
        lax.psum_scatter(
            grad_normed_part.astype(jnp.bfloat16), TENSOR, scatter_dimension=0, tiled=True
        ).astype(jnp.float32),
        lax.psum_scatter(
            grad_gates_part.astype(jnp.bfloat16), TENSOR, scatter_dimension=0, tiled=True
        ).astype(jnp.float32),
    )
    row_start = tensor_pos * own_rows
    gates_own = lax.dynamic_slice_in_dim(gate_probs, row_start, own_rows, 0)
    chosen_own = lax.dynamic_slice_in_dim(chosen, row_start, own_rows, 0)
    grad_selected = gates_own * (
        grad_gates - jnp.sum(gates_own * grad_gates, axis=-1, keepdims=True)
    )
    grad_logits = jnp.sum(jnp.where(chosen_own, grad_selected[:, :, None], 0.0), axis=1).astype(
        jnp.bfloat16
    )
    grad_normed_two = grad_normed_two + jnp.dot(
        grad_logits, router_full.T, preferred_element_type=jnp.float32
    )
    grad_router_part = jnp.dot(normed_two.T, grad_logits, preferred_element_type=jnp.float32)
    grad_residual, grad_gain_two = rms_back(grad_normed_two, residual, scale_two, second_gain)
    grad_residual = grad_residual + grad_out
    grad_attn = widen(grad_residual.astype(jnp.bfloat16))
    grad_wout = jnp.dot(mixed_heads.T, grad_attn, preferred_element_type=jnp.float32)
    grad_mixed = (
        jnp.dot(grad_attn, out_back.T, preferred_element_type=jnp.float32)
        .astype(jnp.bfloat16)
        .reshape(sequence_length, kv_heads, group_size, HEAD_SIZE)
    )
    grad_keys = jnp.zeros((sequence_length, kv_heads, HEAD_SIZE), jnp.float32)
    grad_values = jnp.zeros((sequence_length, kv_heads, HEAD_SIZE), jnp.float32)
    block_index = 0
    start_row = block_index * sequence_length
    end_row = start_row + sequence_length
    scores, allowed = block_scores(start_row, end_row)
    attn_probs = jnp.where(allowed, jnp.exp(scores - lse_blocks[block_index]), 0.0)
    probs_low = attn_probs.astype(jnp.bfloat16)
    grad_values = grad_values.at[:end_row].add(
        jnp.einsum("kgqs,qkgd->skd", probs_low, grad_mixed, preferred_element_type=jnp.float32)
    )
    grad_probs = jnp.einsum(
        "qkgd,skd->kgqs", grad_mixed, rows_of_value, preferred_element_type=jnp.float32
    )
    inner_sum = jnp.sum(attn_probs * grad_probs, axis=-1, keepdims=True)
    grad_scores = (attn_probs * (grad_probs - inner_sum)).astype(jnp.bfloat16)
    grad_query_blocks = (
        jnp.einsum("kgqs,skd->qkgd", grad_scores, key_rows, preferred_element_type=jnp.float32)
        * score_scale
    )
    grad_keys = grad_keys.at[:end_row].add(
        jnp.einsum("kgqs,qkgd->skd", grad_scores, rows_of_query, preferred_element_type=jnp.float32)
        * score_scale
    )
    grad_query = grad_query_blocks.reshape(sequence_length, q_heads, HEAD_SIZE)
    grad_q_raw = (
        rotate_back(grad_query, rotary_cosine, rotary_sine)
        .astype(jnp.bfloat16)
        .reshape(sequence_length, q_heads * HEAD_SIZE)
    )
    grad_k_raw = (
        rotate_back(grad_keys, rotary_cosine, rotary_sine)
        .astype(jnp.bfloat16)
        .reshape(sequence_length, kv_heads * HEAD_SIZE)
    )
    grad_v_low = grad_values.astype(jnp.bfloat16).reshape(sequence_length, kv_heads * HEAD_SIZE)
    grad_wquery = jnp.dot(full_one.T, grad_q_raw, preferred_element_type=jnp.float32)
    grad_wkey = jnp.dot(full_one.T, grad_k_raw, preferred_element_type=jnp.float32)
    grad_wvalue = jnp.dot(full_one.T, grad_v_low, preferred_element_type=jnp.float32)
    grad_normed_one_part = (
        jnp.dot(grad_q_raw, query_back.T, preferred_element_type=jnp.float32)
        + jnp.dot(grad_k_raw, key_back.T, preferred_element_type=jnp.float32)
        + jnp.dot(grad_v_low, value_back.T, preferred_element_type=jnp.float32)
    )
    grad_normed_one = narrow(grad_normed_one_part)
    grad_inputs, grad_gain_one = rms_back(grad_normed_one, input_values, scale_one, first_gain)
    grad_inputs = grad_inputs + grad_residual
    dense_sums = (
        lax.psum_scatter(grad_wquery, DP, scatter_dimension=0, tiled=True),
        lax.psum_scatter(grad_wkey, DP, scatter_dimension=0, tiled=True),
        lax.psum_scatter(grad_wvalue, DP, scatter_dimension=0, tiled=True),
        lax.psum_scatter(grad_wout, DP, scatter_dimension=1, tiled=True),
        lax.psum_scatter(grad_sgate, DP, scatter_dimension=0, tiled=True),
        lax.psum_scatter(grad_sup, DP, scatter_dimension=0, tiled=True),
        lax.psum_scatter(grad_sdown, DP, scatter_dimension=1, tiled=True),
    )
    small_sums = (
        lax.psum_scatter(grad_router_part, (DP, TENSOR), scatter_dimension=0, tiled=True),
        lax.psum_scatter(grad_gain_one, (DP, TENSOR), scatter_dimension=0, tiled=True),
        lax.psum_scatter(grad_gain_two, (DP, TENSOR), scatter_dimension=0, tiled=True),
    )
    return (
        output,
        grad_inputs,
        small_sums[1],
        small_sums[2],
        dense_sums[0],
        dense_sums[1],
        dense_sums[2],
        dense_sums[3],
        small_sums[0],
        dense_sums[4],
        dense_sums[5],
        dense_sums[6],
        expert_gate_gradient,
        expert_up_gradient,
        expert_down_gradient,
    )


MESH = pl.DeviceIdType.MESH
ANY = pl.BlockSpec(memory_space=pl.ANY)


def when(condition, body):
    if condition is None:
        body()
    else:
        pl.when(condition)(body)


class Spot:
    def __init__(self, n_planes):
        dp = lax.axis_index(DP)
        self.x = lax.axis_index(TENSOR)
        self.dp = dp
        self.core = dp % 2
        self.y = (dp // 2) % 2
        self.z = dp // 4
        self.n_planes = n_planes
        self.has_up = self.z < n_planes - 1
        self.has_down = self.z > 0
        self.up = (dp + 4, self.x)
        self.down = (dp - 4, self.x)
        self.side = (dp + 2 - 4 * self.y, self.x)
        self.across = (dp, 1 - self.x)
        self.twin = (dp + 1 - 2 * self.core, self.x)

    def far_first(self):
        low, high = 0 * self.z, 0 * self.z + self.n_planes - 1
        order = []
        for _ in range(self.n_planes):
            take_low = (self.z - low >= high - self.z).astype(jnp.int32)
            order.append(take_low * low + (1 - take_low) * high)
            low, high = low + take_low, high - (1 - take_low)
        return order

    def greet(self):
        barrier = pltpu.get_barrier_semaphore()
        fixed = [self.side, self.twin, self.across]
        for device in fixed:
            pl.semaphore_signal(barrier, inc=1, device_id=device, device_id_type=MESH)
        for condition, device in ((self.has_up, self.up), (self.has_down, self.down)):

            @pl.when(condition)
            def _(device=device):
                pl.semaphore_signal(barrier, inc=1, device_id=device, device_id_type=MESH)

        ends = self.has_up.astype(jnp.int32) + self.has_down.astype(jnp.int32)
        pl.semaphore_wait(barrier, len(fixed) + ends)


class Copies:
    def __init__(self, n_planes, send, recv):
        self.n_planes, self.send, self.recv = n_planes, send, recv
        self.open = []

    def copy(self, group, s, piece, src, dst, device, arrival=None):
        arrival = group if arrival is None else arrival
        return pltpu.make_async_remote_copy(
            src_ref=src,
            dst_ref=dst,
            send_sem=self.send.at[group * self.n_planes + s, piece],
            recv_sem=self.recv.at[arrival * self.n_planes + s, piece],
            device_id=device,
            device_id_type=MESH,
        )

    def start(self, condition, group, s, sources, targets, device, arrival=None):
        def body():
            for i, (src, dst) in enumerate(zip(sources, targets)):
                self.copy(group, s, i, src, dst, device, arrival).start()

        when(condition, body)
        self.open.append((condition, group, s, sources, targets, device, arrival))

    def arrive(self, group, s, targets, device):
        for i, dst in enumerate(targets):
            self.copy(group, s, i, dst, dst, device).wait_recv()

    def close(self):
        for condition, group, s, sources, targets, device, arrival in self.open:

            def body():
                for i, (src, dst) in enumerate(zip(sources, targets)):
                    self.copy(group, s, i, src, dst, device, arrival).wait_send()

            when(condition, body)


(Z_UP, Z_DOWN, Y_ALL, Y_HALF, X_ALL, X_HALF, C_OWN, C_Y, C_X, C_XH, C_YH, D_UP, D_DOWN, C_D) = range(14)
(ALL, FIRST, SECOND) = range(3)


class Spread:
    def __init__(self, spot, copies, own, views, use_x, by_z=False):
        self.spot, self.copies, self.own, self.use_x, self.by_z = spot, copies, own, use_x, by_z
        self.order = spot.far_first()[::-1]
        y, x, core = spot.y, spot.x, spot.core

        def places(s, cc):
            return (
                views(s, y, cc, x, ALL),
                views(s, 1 - y, cc, x, ALL),
                views(s, 1 - y, cc, x, FIRST),
                views(s, y, cc, 1 - x, ALL),
                views(s, y, cc, 1 - x, SECOND),
                views(s, 1 - y, cc, 1 - x, FIRST),
                views(s, 1 - y, cc, 1 - x, SECOND),
                views(s, 1 - y, cc, 1 - x, ALL),
            )

        self.mine = [places(s, core) for s in self.order]
        self.twins = [places(s, 1 - core) for s in self.order]
        self.goes_down = [(s > spot.z) & spot.has_down for s in self.order]
        self.goes_up = [(s < spot.z) & spot.has_up for s in self.order]
        middle = spot.has_up & spot.has_down
        self.among = (jnp.logical_not(middle), middle)
        self.goes = {
            (j, c): (self.goes_down[j] & self.among[c], self.goes_up[j] & self.among[c], self.among[c])
            for j in range(len(self.order))
            for c in (0, 1)
        }

    def place(self, j):
        return self.own if j == 0 else self.mine[j][0]

    def onward_y(self, j):
        self.copies.start(None, Y_ALL, self.order[j], self.place(j), self.mine[j][0], self.spot.side)

    def onward_x(self, j):
        self.copies.start(None, X_ALL, self.order[j], self.place(j), self.mine[j][0], self.spot.across)

    def onward_twin(self, j):
        self.copies.start(None, C_OWN, self.order[j], self.place(j), self.mine[j][0], self.spot.twin)

    def onward(self, j):
        self.onward_y(j)
        if self.use_x:
            self.onward_x(j)
        self.onward_twin(j)

    def begin_z(self):
        spot, here = self.spot, self.mine[0][0]
        self.copies.start(spot.has_up, Z_UP, spot.z, self.own, here, spot.up)
        self.copies.start(spot.has_down, Z_DOWN, spot.z, self.own, here, spot.down, Z_UP)

    def begin(self):
        self.begin_z()
        self.onward(0)

    def relay(self, j, goes=None):
        s, here, spot = self.order[j], self.mine[j][0], self.spot
        goes_down, goes_up, _ = goes or (self.goes_down[j], self.goes_up[j], None)
        self.copies.arrive(Z_UP, s, here, spot.up)
        self.copies.start(goes_down, Z_DOWN, s, here, here, spot.down, Z_UP)
        self.copies.start(goes_up, Z_UP, s, here, here, spot.up)

    def relay_of(self, j, c):
        pl.when(self.among[c])(functools.partial(self.relay, j, self.goes[j, c]))

    def corner_of(self, j, c):
        pl.when(self.among[c])(functools.partial(self.corner, j, self.goes[j, c]))

    def column(self, j):
        if j < len(self.order):
            self.relay(j)
            self.onward(j)

    def from_side(self, j):
        s, there, spot = self.order[j], self.mine[j][1], self.spot
        self.copies.arrive(Y_ALL, s, there, spot.side)
        self.copies.start(None, C_Y, s, there, there, spot.twin)

    def from_across(self, j):
        s, there, spot = self.order[j], self.mine[j][3], self.spot
        self.copies.arrive(X_ALL, s, there, spot.across)
        self.copies.start(None, C_X, s, there, there, spot.twin)

    def over_x(self, j):
        part = self.mine[j][2]
        self.copies.start(None, X_HALF, self.order[j], part, part, self.spot.across)

    def over_y(self, j):
        part = self.mine[j][4]
        self.copies.start(None, Y_HALF, self.order[j], part, part, self.spot.side)

    def side(self, j):
        self.from_side(j)
        if self.use_x and (j == 0 or not self.by_z):
            self.over_x(j)

    def across(self, j):
        self.from_across(j)
        if j == 0 or not self.by_z:
            self.over_y(j)

    def sides(self, j):
        if 0 <= j < len(self.order):
            self.side(j)
            if self.use_x:
                self.across(j)

    def corner(self, j, goes=None):
        if not self.use_x or not 0 <= j < len(self.order):
            return
        s, spot = self.order[j], self.spot
        first, second, whole = self.mine[j][5:]
        if self.by_z and j > 0:
            goes_down, goes_up, always = goes or (self.goes_down[j], self.goes_up[j], None)
            self.copies.arrive(D_UP, s, whole, spot.up)
            self.copies.start(goes_down, D_DOWN, s, whole, whole, spot.down, D_UP)
            self.copies.start(goes_up, D_UP, s, whole, whole, spot.up)
            self.copies.start(always, C_D, s, whole, whole, spot.twin)
            return
        self.copies.arrive(X_HALF, s, first, spot.across)
        self.copies.start(None, C_XH, s, first, first, spot.twin)
        self.copies.arrive(Y_HALF, s, second, spot.side)
        self.copies.start(None, C_YH, s, second, second, spot.twin)
        if self.by_z:
            self.copies.start(spot.has_up, D_UP, s, whole, whole, spot.up)
            self.copies.start(spot.has_down, D_DOWN, s, whole, whole, spot.down, D_UP)

    def twin_near(self, j):
        s, there, spot = self.order[j], self.twins[j], self.spot
        self.copies.arrive(C_OWN, s, there[0], spot.twin)
        if self.use_x:
            self.copies.arrive(C_X, s, there[3], spot.twin)

    def twin_side(self, j):
        self.copies.arrive(C_Y, self.order[j], self.twins[j][1], self.spot.twin)

    def twin_corner(self, j):
        if self.by_z and j > 0:
            self.copies.arrive(C_D, self.order[j], self.twins[j][7], self.spot.twin)
            return
        self.copies.arrive(C_XH, self.order[j], self.twins[j][5], self.spot.twin)
        self.copies.arrive(C_YH, self.order[j], self.twins[j][6], self.spot.twin)

    def twin_far(self, j):
        self.twin_side(j)
        if self.use_x:
            self.twin_corner(j)

    def twin_all(self):
        for j in range(len(self.order)):
            self.twin_near(j)
            self.twin_far(j)

    def stage(self, step):
        self.column(step)
        self.sides(step - 1)
        self.corner(step - 2)

    def run(self):
        self.begin()
        for step in range(1, len(self.order) + 2):
            self.stage(step)
        self.twin_all()
        self.copies.close()


def dp_of(s, yy, cc):
    return (s * 2 + yy) * 2 + cc


def plain_dot(a, b, contract):
    return lax.dot_general(a, b, (contract, ((), ())), preferred_element_type=jnp.float32)


ROWS_COLUMNS = ((1,), (0,))
ROWS_ROWS = ((1,), (1,))
COLUMNS_COLUMNS = ((0,), (0,))


def turn(heads, cosine, sine):
    return heads * cosine + pltpu.roll(heads, heads.shape[1] // 2, 1) * sine


def front_kernel(n_planes, axes, *refs):
    n = len(axes)
    shards_in, (tokens, tile, grads, chosen, cosine, sine, allowed) = refs[:n], refs[n : n + 7]
    outs = refs[n + 7 : 2 * n + 7]
    (
        all_grads, params, normed_one, query, key, value, probs, mixed, residual, normed_two, gates,
    ) = refs[2 * n + 7 : 2 * n + 18]
    (
        wq, wk, wv, wo, sequence, pair, sent, received, w_send, w_recv, p_send, p_recv, g_send, g_recv, local,
        load, x_send, x_recv,
    ) = refs[2 * n + 18 :]
    spot = Spot(n_planes)
    x = spot.x
    bf16, f32 = jnp.bfloat16, jnp.float32
    own_rows, model = tokens.shape

    def weight_views(s, yy, cc, xx, part):
        i = dp_of(s, yy, cc)
        places = []
        for o, a, axis in zip(outs, shards_in, axes):
            size = a.shape[axis]
            span = pl.ds(pl.multiple_of(i * size, size), size)
            places.append(o.at[span] if axis == 0 else o.at[:, span])
        return places

    def param_views(s, yy, cc, xx, part):
        size = tile.shape[1]
        return [params.at[:, pl.ds(pl.multiple_of(dp_of(s, yy, cc) * size, size), size)]]

    def grad_views(s, yy, cc, xx, part):
        b = dp_of(s, yy, cc) * 2 + xx
        if part == ALL:
            return [all_grads.at[b]]
        return [all_grads.at[b, pl.ds(0 if part == FIRST else own_rows // 2, own_rows // 2)]]

    def mine(views):
        return views(spot.z, spot.y, spot.core, x, ALL)

    def swap(i, src, dst):
        return pltpu.make_async_remote_copy(
            src_ref=src, dst_ref=dst, send_sem=x_send.at[i], recv_sem=x_recv.at[i],
            device_id=spot.across, device_id_type=MESH,
        )

    kept = list(zip(list(shards_in) + [tokens, grads, tile], mine(weight_views) + [sequence.at[x]] + mine(grad_views) + [pair.at[x]]))
    kept = [pltpu.make_async_copy(a, b, local.at[i]) for i, (a, b) in enumerate(kept)]
    for c in kept:
        c.start()
    spot.greet()
    swaps = [swap(0, tile, pair.at[x]), swap(1, tokens, sequence.at[x]), swap(2, sent, received)]
    swaps[0].start()
    weights = Spread(spot, Copies(n_planes, w_send, w_recv), list(shards_in), weight_views, False)
    small = Spread(spot, Copies(n_planes, p_send, p_recv), mine(param_views), param_views, False)
    net = Spread(spot, Copies(n_planes, g_send, g_recv), [grads], grad_views, True)
    weights.begin()
    swaps[1].start()
    for c in kept:
        c.wait()
    swap(0, pair.at[1 - x], pair.at[1 - x]).wait_recv()
    mine(param_views)[0][...] = pair[0] + pair[1]
    small.begin()
    net.onward_x(0)
    net.onward_twin(0)
    for step in range(1, n_planes + 1):
        weights.stage(step)
        small.stage(step)
        if step == n_planes - 1:
            net.begin_z()
    net.onward_y(0)
    net.from_across(0)

    net.relay(1)
    net.relay_of(2, 1)
    net.onward_x(1)
    net.onward_twin(1)

    small.twin_all()
    swap(1, sequence.at[1 - x], sequence.at[1 - x]).wait_recv()

    experts = chosen.shape[0]
    first_gain = params[experts : experts + 1, :].astype(f32)
    step = 32
    for h in range(2):
        for r in range(own_rows // step):
            rows = sequence[h, pl.ds(r * step, step)].astype(f32)
            scale = lax.rsqrt(jnp.mean(rows * rows, axis=1, keepdims=True) + norm_eps)
            normed_one[pl.ds(h * own_rows + r * step, step)] = (rows * scale * first_gain).astype(bf16)
    weights.twin_all()
    loads = [pltpu.make_async_copy(a, b, load.at[i]) for i, (a, b) in enumerate(zip(outs, (wq, wk, wv, wo)))]
    for c in loads:
        c.start()
    heads, head_dim = query.shape[1] // cosine.shape[1], cosine.shape[1]
    kv_heads = key.shape[1] // head_dim
    group = heads // kv_heads
    for c in loads[:3]:
        c.wait()
    cos, sin = cosine[...], sine[...]
    raw = plain_dot(normed_one[...], wk[...], ROWS_COLUMNS)
    for g in range(kv_heads):
        span = slice(g * head_dim, (g + 1) * head_dim)
        key[:, span] = turn(raw[:, span], cos, sin).astype(bf16)
    value[...] = plain_dot(normed_one[...], wv[...], ROWS_COLUMNS).astype(bf16)
    raw = plain_dot(normed_one[...], wq[...], ROWS_COLUMNS)
    for h in range(heads):
        span = slice(h * head_dim, (h + 1) * head_dim)
        query[:, span] = turn(raw[:, span], cos, sin).astype(bf16)
    net.from_side(0)
    net.onward_y(1)
    net.relay_of(2, 0)
    net.relay_of(3, 1)
    net.onward_x(2)
    net.onward_twin(2)
    net.from_across(1)
    may = allowed[...] > 0.0
    for h in range(heads):
        span = slice(h * head_dim, (h + 1) * head_dim)
        shared = slice(h // group * head_dim, (h // group + 1) * head_dim)
        scores = plain_dot(query[:, span], key[:, shared], ROWS_ROWS) * (head_dim ** -0.5)
        scores = jnp.where(may, scores, neg_big)
        weight = jnp.exp(scores - jnp.max(scores, axis=1, keepdims=True))
        weight = weight / jnp.sum(weight, axis=1, keepdims=True)
        probs[h] = weight
        mixed[:, span] = plain_dot(weight.astype(bf16), value[:, shared], ROWS_COLUMNS).astype(bf16)
    loads[3].wait()
    other = mixed[pl.ds(pl.multiple_of((1 - x) * own_rows, own_rows), own_rows), :]
    sent[...] = plain_dot(other, wo[...], ROWS_COLUMNS).astype(bf16)
    swaps[2].start()
    other = mixed[pl.ds(pl.multiple_of(x * own_rows, own_rows), own_rows), :]
    residual[...] = plain_dot(other, wo[...], ROWS_COLUMNS)
    net.from_side(1)
    net.onward_y(2)
    net.relay_of(3, 0)
    net.onward_x(3)
    net.onward_twin(3)
    net.from_across(2)
    swap(2, received, received).wait_recv()
    second_gain = params[experts + 1 : experts + 2, :].astype(f32)
    for r in range(own_rows // step):
        span = pl.ds(r * step, step)
        rows = sequence[x, span].astype(f32) + (residual[span] + received[span].astype(f32))
        residual[span] = rows
        scale = lax.rsqrt(jnp.mean(rows * rows, axis=1, keepdims=True) + norm_eps)
        normed_two[span] = (rows * scale * second_gain).astype(bf16)
    logits = plain_dot(params[:experts, :], normed_two[...], ROWS_ROWS)
    picked = chosen[...] > 0.0
    top = jnp.max(jnp.where(picked, logits, neg_big), axis=0, keepdims=True)
    weight = jnp.where(picked, jnp.exp(jnp.where(picked, logits - top, 0.0)), 0.0)
    gates[...] = weight / jnp.sum(weight, axis=0, keepdims=True)

    net.from_side(2)
    net.from_across(3)
    for j in range(n_planes):
        net.twin_near(j)
        if j < n_planes - 1:
            net.twin_side(j)
    for each in (weights, small, net):
        each.copies.close()
    for c in swaps:
        c.wait_send()


def front(arrays, axes, tokens, tile, grads, chosen, cosine, sine, allowed, n_dp, collective_id):
    n, n_planes = len(arrays), n_dp // 4
    bf16, f32 = jnp.bfloat16, jnp.float32
    shape = jax.ShapeDtypeStruct

    def whole(a, axis):
        full = list(a.shape)
        full[axis] *= n_dp
        return shape(tuple(full), a.dtype)

    own_rows, model = tokens.shape
    seq = 2 * own_rows
    experts = chosen.shape[0]
    wide, narrow_ = arrays[0].shape[1], arrays[1].shape[1]
    heads = wide // cosine.shape[1]
    gathered = [whole(a, axis) for a, axis in zip(arrays, axes)]
    vmem = pl.BlockSpec(memory_space=pltpu.VMEM)
    dma = pltpu.SemaphoreType.DMA
    return pl.pallas_call(
        functools.partial(front_kernel, n_planes, axes),
        out_shape=gathered
        + [
            shape((2 * n_dp,) + grads.shape, bf16),
            shape((tile.shape[0], tile.shape[1] * n_dp), bf16),
            shape((seq, model), bf16),
            shape((seq, wide), bf16),
            shape((seq, narrow_), bf16),
            shape((seq, narrow_), bf16),
            shape((heads, seq, seq), f32),
            shape((seq, wide), bf16),
            shape((own_rows, model), f32),
            shape((own_rows, model), bf16),
            shape((experts, own_rows), f32),
        ],
        in_specs=[ANY] * (n + 3) + [vmem] * 4,
        out_specs=[ANY] * (n + 1) + [vmem] * 10,
        scratch_shapes=[pltpu.VMEM(g.shape, bf16) for g in gathered]
        + [
            pltpu.VMEM((2, own_rows, model), bf16),
            pltpu.VMEM((2,) + tile.shape, bf16),
            pltpu.VMEM((own_rows, model), bf16),
            pltpu.VMEM((own_rows, model), bf16),
        ]
        + [dma((14 * n_planes, n))] * 2
        + [dma((14 * n_planes, 1))] * 4
        + [dma((n + 3,)), dma((n,)), dma((3,)), dma((3,))],
        compiler_params=pltpu.CompilerParams(
            collective_id=collective_id, has_side_effects=True, vmem_limit_bytes=56 << 20
        ),
        cost_estimate=pl.CostEstimate(
            flops=6 * seq * model * wide, bytes_accessed=16 * n_dp * own_rows * model, transcendentals=heads * seq * seq
        ),
    )(*arrays, tokens, tile, grads, chosen, cosine, sine, allowed)


(T_YX, T_Y, T_X, T_OWN, R_XHALF, R_YHALF, R_YALL, R_XALL, R_UP, R_DOWN, R_DUP, R_DDOWN) = range(12)


def add_up(target, sources):
    rows = target.shape[0]
    step = 16 if rows % 16 == 0 else rows

    def body(i, carry):
        span = pl.ds(pl.multiple_of(i * step, step), step)
        total = sources[0][span, :].astype(jnp.float32)
        for source in sources[1:]:
            total = total + source[span, :].astype(jnp.float32)
        target[span, :] = total.astype(target.dtype)
        return carry

    lax.fori_loop(0, rows // step, body, 0)


class Reduce:
    @staticmethod
    def scratch(shapes, dtypes, n_planes, use_x, cut=0, direct=False, by_z=False):
        kinds = 4 if use_x else 2
        out = []
        for i, (shape, dtype) in enumerate(zip(shapes, dtypes)):
            rows = cut if i == 0 else shape[0]
            out.append(pltpu.VMEM((kinds, n_planes) + shape, dtype))
            out.append(pltpu.VMEM((n_planes + 1,) + shape, dtype))
            out.append(pltpu.VMEM((n_planes,) + shape, dtype))
            if not direct:
                out.append(pltpu.VMEM((kinds, 2) + shape, dtype))
            if use_x:
                out.append(pltpu.VMEM((n_planes,) + shape, dtype))
                out.append(pltpu.VMEM((1 if by_z else n_planes, rows) + shape[1:], dtype))
                if by_z:
                    out.append(pltpu.VMEM((n_planes + 1,) + shape, dtype))
                if i == 0 and cut < shape[0]:
                    out.append(pltpu.VMEM((1 if by_z else n_planes, shape[0] - cut) + shape[1:], dtype))
        n = len(shapes)
        out.append(pltpu.SemaphoreType.DMA((12 * n_planes, n)))
        out.append(pltpu.SemaphoreType.DMA((12 * n_planes, n)))
        out.append(pltpu.SemaphoreType.DMA((kinds * n_planes, n)))
        return out

    def __init__(self, spot, blocks, outs, scratch, use_x, cut=0, direct=False, by_z=False):
        self.spot, self.outs, self.use_x, self.direct, self.by_z = spot, outs, use_x, direct, by_z
        self.slant = []
        self.n, self.n_planes, self.cut = len(outs), spot.n_planes, cut
        left = list(scratch)
        self.twin, self.line, self.near, self.ring, self.across, self.first = [], [], [], [], [], []
        self.second = None
        for i in range(self.n):
            self.twin.append(left.pop(0))
            self.line.append(left.pop(0))
            self.near.append(left.pop(0))
            if not direct:
                self.ring.append(left.pop(0))
            if use_x:
                self.across.append(left.pop(0))
                self.first.append(left.pop(0))
                if by_z:
                    self.slant.append(left.pop(0))
                if i == 0 and cut < self.near[0].shape[1]:
                    self.second = left.pop(0)
        send, recv, self.local = left
        self.copies = Copies(self.n_planes, send, recv)
        y, x, core = spot.y, spot.x, spot.core
        self.order = spot.far_first()
        places = {T_YX: (1 - y, 1 - x), T_Y: (1 - y, x), T_X: (y, 1 - x), T_OWN: (y, x)}
        self.kinds = [T_YX, T_Y, T_X, T_OWN] if use_x else [T_Y, T_OWN]
        every = [(k, j) for j in range(self.n_planes) for k in self.kinds]
        self.terms = {(k, j): blocks(self.order[j], places[k][0], core, places[k][1]) for k, j in every}
        self.others = {(k, j): blocks(self.order[j], places[k][0], 1 - core, places[k][1]) for k, j in every}

    def load(self, kind, j):
        k, s = self.kinds.index(kind), self.order[j]
        return [
            pltpu.make_async_copy(ref, self.ring[i].at[k, j % 2], self.local.at[k * self.n_planes + s, i])
            for i, ref in enumerate(self.terms[kind, j])
        ]

    def start_load(self, kind, j):
        if not self.direct and j < self.n_planes:
            for c in self.load(kind, j):
                c.start()

    def start_loads(self):
        for j in range(2):
            for kind in self.kinds:
                self.start_load(kind, j)

    def start_twins(self):
        for j in range(self.n_planes):
            s = self.order[j]
            for k, kind in enumerate(self.kinds):
                self.copies.start(None, kind, s, self.others[kind, j], [t.at[k, s] for t in self.twin], self.spot.twin)

    def ready(self, kind, j):
        k, s = self.kinds.index(kind), self.order[j]
        twin = [t.at[k, s] for t in self.twin]
        self.copies.arrive(kind, s, twin, self.spot.twin)
        if self.direct:
            return twin, self.terms[kind, j]
        for c in self.load(kind, j):
            c.wait()
        return twin, [r.at[k, j % 2] for r in self.ring]

    def along(self, j, here, line, targets, up, down):
        s, spot, copies = self.order[j], self.spot, self.copies
        some = [t.at[s] for t in line]
        below = [t.at[self.n_planes] for t in line]

        def add_all(*more):
            for i in range(self.n):
                add_up(targets[i], here[i] + [m[i] for m in more])

        if j == self.n_planes - 1:
            when(spot.has_up, lambda: copies.arrive(down, s, some, spot.up))
            when(spot.has_down, lambda: copies.arrive(up, s, below, spot.down))
            when(spot.has_up & spot.has_down, lambda: add_all(some, below))
            when(spot.z == 0, lambda: add_all(some))
            when(spot.z == self.n_planes - 1, lambda: add_all(below))
            return
        for goes, more, group, last, device, source in (
            (s < spot.z, spot.has_up, down, None, spot.down, spot.up),
            (s > spot.z, spot.has_down, up, s - spot.z == 1, spot.up, spot.down),
        ):

            def partial():
                copies.arrive(group, s, some, source)
                add_all(some)

            when(goes & more, partial)
            when(goes & jnp.logical_not(more), add_all)
            if last is None:
                copies.start(goes, group, s, targets, some, device)
            else:
                copies.start(goes & last, group, s, targets, below, device)
                copies.start(goes & jnp.logical_not(last), group, s, targets, some, device)

    def corner(self, j):
        if not self.use_x or not 0 <= j < self.n_planes:
            return
        s, cut = self.order[j], self.cut
        twin, mine = self.ready(T_YX, j)
        if self.by_z:
            self.along(j, [[m, t] for m, t in zip(mine, twin)], self.slant, twin, R_DUP, R_DDOWN)
        else:
            for m, t in zip(mine, twin):
                add_up(t, [m, t])
        self.start_load(T_YX, j + 2)
        if self.by_z and j < self.n_planes - 1:
            return
        p = 0 if self.by_z else s
        head = twin if self.second is None else [twin[0].at[pl.ds(0, cut)]] + twin[1:]
        self.copies.start(None, R_XHALF, s, head, [f.at[p] for f in self.first], self.spot.across)
        if self.second is not None:
            tail = [twin[0].at[pl.ds(cut, self.second.shape[1])]]
            self.copies.start(None, R_YHALF, s, tail, [self.second.at[p]], self.spot.side)

    def side(self, j):
        s, cut = self.order[j], self.cut
        twin, mine = self.ready(T_Y, j)
        over = self.use_x and (j == self.n_planes - 1 or not self.by_z)
        p = 0 if self.by_z else s
        if over:
            first = [f.at[p] for f in self.first]
            self.copies.arrive(R_XHALF, s, first, self.spot.across)
        for i, (m, t) in enumerate(zip(mine, twin)):
            if not over:
                add_up(t, [m, t])
            elif i == 0 and self.second is not None:
                a, b = pl.ds(0, cut), pl.ds(cut, self.second.shape[1])
                add_up(t.at[a], [m.at[a], t.at[a], first[0]])
                add_up(t.at[b], [m.at[b], t.at[b]])
            else:
                add_up(t, [m, t, first[i]])
        self.start_load(T_Y, j + 2)
        self.copies.start(None, R_YALL, s, twin, [t.at[s] for t in self.near], self.spot.side)

    def over(self, j):
        s, cut = self.order[j], self.cut
        twin, mine = self.ready(T_X, j)
        over = self.second is not None and (j == self.n_planes - 1 or not self.by_z)
        p = 0 if self.by_z else s
        if over:
            self.copies.arrive(R_YHALF, s, [self.second.at[p]], self.spot.side)
        for i, (m, t) in enumerate(zip(mine, twin)):
            if i == 0 and over:
                a, b = pl.ds(0, cut), pl.ds(cut, self.second.shape[1])
                add_up(t.at[a], [m.at[a], t.at[a]])
                add_up(t.at[b], [m.at[b], t.at[b], self.second.at[p]])
            else:
                add_up(t, [m, t])
        self.start_load(T_X, j + 2)
        self.copies.start(None, R_XALL, s, twin, [t.at[s] for t in self.across], self.spot.across)

    def sides(self, j):
        if 0 <= j < self.n_planes:
            self.side(j)
            if self.use_x:
                self.over(j)

    def column(self, j):
        if not 0 <= j < self.n_planes:
            return
        s, spot, copies = self.order[j], self.spot, self.copies
        twin, mine = self.ready(T_OWN, j)
        near = [t.at[s] for t in self.near]
        copies.arrive(R_YALL, s, near, spot.side)
        here = [[m, t, a] for m, t, a in zip(mine, twin, near)]
        if self.use_x:
            across = [t.at[s] for t in self.across]
            copies.arrive(R_XALL, s, across, spot.across)
            here = [h + [a] for h, a in zip(here, across)]
        self.along(j, here, self.line, self.outs if j == self.n_planes - 1 else twin, R_UP, R_DOWN)
        self.start_load(T_OWN, j + 2)

    def stage(self, step):
        self.corner(step)
        self.sides(step - 1)
        self.column(step - 2)

    def close(self):
        self.copies.close()


class WeightGradients:
    width = 256

    def __init__(self, ins, outs, scratch):
        self.sources, (self.hidden, self.shared) = ins[:4], ins[4:]
        self.outs = outs
        self.buffers, self.small_hidden, self.small_shared = scratch[:4], scratch[4], scratch[5]
        self.tall, self.flat, self.sums, self.load, self.store, self.once = scratch[6:]
        self.n_parts = self.sources[0].shape[1] // self.width

    @staticmethod
    def scratch(rows, tokens, width, shared):
        bf16, f32 = jnp.bfloat16, jnp.float32
        w = WeightGradients.width
        return [
            pltpu.VMEM((2, rows, w), bf16),
            pltpu.VMEM((2, rows, w), bf16),
            pltpu.VMEM((2, tokens, w), bf16),
            pltpu.VMEM((2, tokens, w), bf16),
            pltpu.VMEM((3, rows, width), bf16),
            pltpu.VMEM((tokens, shared), bf16),
            pltpu.VMEM((2, 2, w, width), f32),
            pltpu.VMEM((2, width, w), f32),
            pltpu.VMEM((2, shared, w), bf16),
            pltpu.SemaphoreType.DMA((2, 4)),
            pltpu.SemaphoreType.DMA((2, 4)),
            pltpu.SemaphoreType.DMA((2,)),
        ]

    def span(self, p):
        return pl.ds(p * self.width, self.width)

    def loads(self, p):
        return [
            pltpu.make_async_copy(a.at[:, self.span(p)], b.at[p % 2], self.load.at[p % 2, i])
            for i, (a, b) in enumerate(zip(self.sources, self.buffers))
        ]

    def stores(self, p):
        gate, up, down, shared = self.outs
        slot, span = p % 2, self.span(p)
        pairs = [
            (self.tall.at[slot, 0], gate.at[span]),
            (self.tall.at[slot, 1], up.at[span]),
            (self.flat.at[slot], down.at[:, span]),
            (self.sums.at[slot], shared.at[:, span]),
        ]
        return [pltpu.make_async_copy(a, b, self.store.at[slot, i]) for i, (a, b) in enumerate(pairs)]

    def resident(self):
        return [
            pltpu.make_async_copy(self.hidden, self.small_hidden, self.once.at[0]),
            pltpu.make_async_copy(self.shared, self.small_shared, self.once.at[1]),
        ]

    def begin(self):
        for c in self.resident() + self.loads(0):
            c.start()

    def part(self, p):
        if p >= self.n_parts:
            return
        if p == 0:
            for c in self.resident():
                c.wait()
        if p + 1 < self.n_parts:
            for c in self.loads(p + 1):
                c.start()
        for c in self.loads(p):
            c.wait()
        if p >= 2:
            for c in self.stores(p - 2):
                c.wait()
        slot = p % 2
        rows, grad_rows, tokens, grads = [b.at[slot] for b in self.buffers]

        def across(a, b):
            return lax.dot_general(a, b, (((0,), (0,)), ((), ())), preferred_element_type=jnp.float32)

        self.tall[slot, 0] = across(rows[...], self.small_hidden[1])
        self.tall[slot, 1] = across(rows[...], self.small_hidden[2])
        self.flat[slot] = across(self.small_hidden[0], grad_rows[...])
        n = self.small_shared.shape[1] // 3
        self.sums[slot, pl.ds(0, 2 * n)] = across(self.small_shared[:, n:], tokens[...]).astype(jnp.bfloat16)
        self.sums[slot, pl.ds(2 * n, n)] = across(self.small_shared[:, :n], grads[...]).astype(jnp.bfloat16)
        for c in self.stores(p):
            c.start()

    def end(self):
        for p in (self.n_parts - 2, self.n_parts - 1):
            for c in self.stores(p):
                c.wait()


def sum_kernel(n_planes, n, *refs):
    ins, work_ins, outs, work_outs = refs[:n], refs[n : n + 6], refs[n + 6 : 2 * n + 6], refs[2 * n + 6 : 2 * n + 10]
    scratch = refs[2 * n + 10 :]
    cut = len(scratch) - 12
    spot = Spot(n_planes)
    rows = ins[0].shape[1] // 2

    def blocks(s, yy, cc, xx):
        return [a.at[dp_of(s, yy, cc) * 2 + xx] for a in ins]

    net = Reduce(spot, blocks, outs, scratch[:cut], True, rows)
    work = WeightGradients(work_ins, work_outs, scratch[cut:])
    net.start_loads()
    spot.greet()
    net.start_twins()
    work.begin()
    done = 0
    for step in range(n_planes + 2):
        for action in (net.corner, net.sides, net.column):
            j = step - (net.corner, net.sides, net.column).index(action)
            action(j)
            if 0 <= j < n_planes and done < work.n_parts:
                work.part(done)
                done += 1
    net.close()
    work.end()


def sum_everywhere(arrays, out_dtypes, work_arrays, n_dp, collective_id):
    n, n_planes = len(arrays), n_dp // 4
    shapes = [a.shape[1:] for a in arrays]
    rows, model = work_arrays[0].shape
    tokens = work_arrays[2].shape[0]
    width = work_arrays[4].shape[2]
    shared = work_arrays[5].shape[1]
    return pl.pallas_call(
        functools.partial(sum_kernel, n_planes, n),
        out_shape=[jax.ShapeDtypeStruct(s, t) for s, t in zip(shapes, out_dtypes)]
        + [
            jax.ShapeDtypeStruct((model, width), jnp.float32),
            jax.ShapeDtypeStruct((model, width), jnp.float32),
            jax.ShapeDtypeStruct((width, model), jnp.float32),
            jax.ShapeDtypeStruct((shared, model), jnp.bfloat16),
        ],
        in_specs=[ANY] * (n + 6),
        out_specs=[pl.BlockSpec(memory_space=pltpu.VMEM)] * n + [ANY] * 4,
        scratch_shapes=Reduce.scratch(shapes, [a.dtype for a in arrays], n_planes, True, shapes[0][0] // 2)
        + WeightGradients.scratch(rows, tokens, width, shared),
        compiler_params=pltpu.CompilerParams(
            collective_id=collective_id, has_side_effects=True, vmem_limit_bytes=62 << 20
        ),
    )(*arrays, *work_arrays)


def back_kernel(n_planes, axes, *refs):
    n = len(axes)
    grad_own, *inputs = refs[:18]
    probs, wq, wk, wv, wo, parts = inputs[5], *inputs[6:10], inputs[16]
    inputs = inputs[:5] + inputs[10:16]
    held = refs[-len(inputs) - 1 : -1]
    mixed, normed_one, query, key, value, cosine, sine, tokens, grad_residual, gain, small = held
    held_load = refs[-1]
    outs, grad_tokens, small_out, out_sum = refs[18 : 18 + n], *refs[18 + n : 21 + n]
    (
        grad_attn, grad_mixed, grad_query, grad_key, grad_value, gq, gk, gv, go, some_p, some_o, some_q, some_k,
        some_v, sent, received, terms, small_sum, small_in, load, x_send, x_recv,
    ) = refs[21 + n : 43 + n]
    scratch = refs[43 + n : -len(inputs) - 1]
    spot = Spot(n_planes)
    x = spot.x
    bf16, f32 = jnp.bfloat16, jnp.float32
    own_rows, model = tokens.shape
    grads = (gq, gk, gv, go)

    def weight_blocks(s, yy, cc, xx):
        i = dp_of(s, yy, cc)
        places = []
        for a, o, axis in zip(grads, outs, axes):
            size = o.shape[axis]
            span = pl.ds(pl.multiple_of(i * size, size), size)
            places.append(a.at[span] if axis == 0 else a.at[:, span])
        return places

    def small_blocks(s, yy, cc, xx):
        size = small_sum.shape[1]
        return [terms.at[:, pl.ds(pl.multiple_of(dp_of(s, yy, cc) * size, size), size)]]

    def token_blocks(s, yy, cc, xx):
        return [parts.at[dp_of(s, yy, cc) * 2 + xx]]

    count = 3 * n + 3
    weights = Reduce(spot, weight_blocks, outs, scratch[:count], False, direct=True)
    params = Reduce(spot, small_blocks, [small_sum], scratch[count : count + 6], False, direct=True)
    sums = Reduce(spot, token_blocks, [out_sum], scratch[count + 6 :], True, own_rows // 2, by_z=True)

    def swap(i, src, dst):
        return pltpu.make_async_remote_copy(
            src_ref=src, dst_ref=dst, send_sem=x_send.at[i], recv_sem=x_recv.at[i],
            device_id=spot.across, device_id_type=MESH,
        )

    own = pltpu.make_async_copy(grad_own, grad_attn.at[x], load.at[4, 0])
    own.start()
    sums.start_loads()
    spot.greet()
    swap(0, grad_own, grad_attn.at[x]).start()
    sums.start_twins()
    fetched = [pltpu.make_async_copy(a, b, held_load.at[i]) for i, (a, b) in enumerate(zip(inputs, held))]
    for c in fetched:
        c.start()

    heads, head_dim = probs.shape[0], cosine.shape[1]
    kv_heads = key.shape[1] // head_dim
    group = heads // kv_heads
    chunk = some_o.shape[1]
    n_chunks = wo.shape[0] // chunk
    per_chunk = chunk // head_dim

    def load_o(c):
        return pltpu.make_async_copy(wo.at[pl.ds(c * chunk, chunk)], some_o.at[c % 2], load.at[0, c % 2])

    def load_p(h):
        return pltpu.make_async_copy(probs.at[h], some_p.at[h % 2], load.at[1, h % 2])

    load_o(0).start()
    load_p(0).start()
    sums.corner(0)
    sums.sides(0)
    sums.corner(1)
    sums.sides(1)
    for c in fetched:
        c.wait()
    terms[...] = small[...]
    own.wait()
    swap(0, grad_attn.at[1 - x], grad_attn.at[1 - x]).wait_recv()
    whole = grad_attn[...].reshape(2 * own_rows, model)
    cos, sin = cosine[...], -sine[...]
    scale = head_dim ** -0.5
    for c in range(n_chunks):
        if c + 1 < n_chunks:
            load_o(c + 1).start()
        load_o(c).wait()
        span = slice(c * chunk, (c + 1) * chunk)
        grad_mixed[:, span] = plain_dot(whole, some_o[c % 2], ROWS_ROWS).astype(bf16)
        go[span, :] = plain_dot(mixed[:, span], whole, COLUMNS_COLUMNS).astype(bf16)
    sums.corner(2)
    sums.sides(2)
    sums.column(0)
    for h in range(heads):
        if h + 1 < heads:
            load_p(h + 1).start()
        load_p(h).wait()
        span = slice(h * head_dim, (h + 1) * head_dim)
        shared = slice(h // group * head_dim, (h // group + 1) * head_dim)
        weight, back = some_p[h % 2], grad_mixed[:, span]
        grad_v = plain_dot(weight.astype(bf16), back, COLUMNS_COLUMNS)
        grad_p = plain_dot(back, value[:, shared], ROWS_ROWS)
        inner = jnp.sum(weight * grad_p, axis=1, keepdims=True)
        grad_s = (weight * (grad_p - inner)).astype(bf16)
        grad_q = plain_dot(grad_s, key[:, shared], ROWS_COLUMNS) * scale
        grad_query[:, span] = turn(grad_q, cos, sin).astype(bf16)
        grad_k = plain_dot(grad_s, query[:, span], COLUMNS_COLUMNS) * scale
        if h % group == 0:
            total_k, total_v = grad_k, grad_v
        else:
            total_k, total_v = total_k + grad_k, total_v + grad_v
        if h % group == group - 1:
            grad_key[:, shared] = turn(total_k, cos, sin).astype(bf16)
            grad_value[:, shared] = total_v.astype(bf16)
    sums.corner(3)
    sums.column(1)
    for target, source in ((gk, grad_key), (gv, grad_value), (gq, grad_query)):
        target[...] = plain_dot(normed_one[...], source[...], COLUMNS_COLUMNS).astype(bf16)
    weights.start_twins()

    rows = some_q.shape[1]
    n_chunks = model // rows

    def load_w(c):
        span = pl.ds(c * rows, rows)
        return [
            pltpu.make_async_copy(w.at[span], b.at[c % 2], load.at[i, c % 2])
            for i, (w, b) in ((0, (wq, some_q)), (2, (wk, some_k)), (3, (wv, some_v)))
        ]

    for c in load_w(0):
        c.start()
    weights.sides(0)
    sums.sides(3)
    other = pl.ds(pl.multiple_of((1 - x) * own_rows, own_rows), own_rows)
    mine = pl.ds(pl.multiple_of(x * own_rows, own_rows), own_rows)
    for c in range(n_chunks):
        if c + 1 < n_chunks:
            for each in load_w(c + 1):
                each.start()
        for each in load_w(c):
            each.wait()
        columns = slice(c * rows, (c + 1) * rows)
        for here, target in ((other, sent), (mine, grad_tokens)):
            total = plain_dot(grad_query[here, :], some_q[c % 2], ROWS_ROWS)
            total = total + plain_dot(grad_key[here, :], some_k[c % 2], ROWS_ROWS)
            total = total + plain_dot(grad_value[here, :], some_v[c % 2], ROWS_ROWS)
            target[:, columns] = total.astype(target.dtype)
    swap(1, sent, received).start()
    weights.sides(1)
    sums.column(2)
    swap(1, received, received).wait_recv()
    step = 32
    gain_row = gain[...].astype(f32)
    total = jnp.zeros((1, model), f32)
    for r in range(own_rows // step):
        span = pl.ds(r * step, step)
        rows_in = tokens[span, :].astype(f32)
        grad = grad_tokens[span, :] + received[span, :].astype(f32)
        size = lax.rsqrt(jnp.mean(rows_in * rows_in, axis=1, keepdims=True) + norm_eps)
        weighted = grad * gain_row
        inner = jnp.mean(rows_in * weighted, axis=1, keepdims=True)
        total = total + jnp.sum(grad * rows_in * size, axis=0, keepdims=True)
        grad_tokens[span, :] = size * weighted - rows_in * (size * size * size) * inner + grad_residual[span, :]
    place = small.shape[0] - 8
    terms[pl.ds(place, 1), :] = total
    params.start_twins()
    weights.column(0)
    weights.sides(2)
    params.sides(0)
    weights.column(1)
    weights.sides(3)
    sums.column(3)
    for j in range(1, n_planes):
        params.sides(j)
        params.column(j - 1)
    weights.column(2)
    params.column(n_planes - 1)
    weights.column(3)
    swap(2, small_sum, small_in).start()
    swap(2, small_sum, small_in).wait()
    small_out[...] = small_sum[...] + small_in[...]
    swap(0, grad_own, grad_attn.at[x]).wait_send()
    swap(1, sent, received).wait_send()
    for each in (weights, params, sums):
        each.close()


def backward(
    grad_own, mixed, normed_one, query, key, value, probs, weights, axes, cosine, sine, tokens, grad_residual, gain,
    small, parts, n_dp, collective_id,
):
    n, n_planes = len(weights), n_dp // 4
    bf16, f32 = jnp.bfloat16, jnp.float32
    shape, vmem_ref = jax.ShapeDtypeStruct, pltpu.VMEM
    own_rows, model = tokens.shape
    seq = 2 * own_rows
    wide, narrow_ = query.shape[1], key.shape[1]

    def part(a, axis):
        some = list(a.shape)
        some[axis] //= n_dp
        return tuple(some)

    shapes = [part(a, axis) for a, axis in zip(weights, axes)]
    tile = (small.shape[0], model // n_dp)
    block = parts.shape[1:]
    vmem = pl.BlockSpec(memory_space=pltpu.VMEM)
    dma = pltpu.SemaphoreType.DMA
    chunk = 256
    return pl.pallas_call(
        functools.partial(back_kernel, n_planes, axes),
        out_shape=[shape(s, f32) for s in shapes] + [shape((own_rows, model), f32), shape(tile, f32), shape(block, f32)],
        in_specs=[ANY] * 18,
        out_specs=[vmem] * (n + 3),
        scratch_shapes=[
            vmem_ref((2, own_rows, model), bf16),
            vmem_ref((seq, wide), bf16),
            vmem_ref((seq, wide), bf16),
            vmem_ref((seq, narrow_), bf16),
            vmem_ref((seq, narrow_), bf16),
        ]
        + [vmem_ref(w.shape, bf16) for w in weights]
        + [
            vmem_ref((2,) + probs.shape[1:], f32),
            vmem_ref((2, chunk, model), bf16),
            vmem_ref((2, chunk, wide), bf16),
            vmem_ref((2, chunk, narrow_), bf16),
            vmem_ref((2, chunk, narrow_), bf16),
            vmem_ref((own_rows, model), bf16),
            vmem_ref((own_rows, model), bf16),
            vmem_ref(small.shape, f32),
            vmem_ref(tile, f32),
            vmem_ref(tile, f32),
            dma((5, 2)),
            dma((3,)),
            dma((3,)),
        ]
        + Reduce.scratch(shapes, [bf16] * n, n_planes, False, direct=True)
        + Reduce.scratch([tile], [f32], n_planes, False, direct=True)
        + Reduce.scratch([block], [parts.dtype], n_planes, True, block[0] // 2, by_z=True)
        + [
            vmem_ref(a.shape, a.dtype)
            for a in (mixed, normed_one, query, key, value, cosine, sine, tokens, grad_residual, gain, small)
        ]
        + [dma((11,))],
        compiler_params=pltpu.CompilerParams(
            collective_id=collective_id, has_side_effects=True, vmem_limit_bytes=63 << 20
        ),
        cost_estimate=pl.CostEstimate(
            flops=12 * seq * model * wide, bytes_accessed=16 * n_dp * own_rows * model, transcendentals=0
        ),
    )(
        grad_own, mixed, normed_one, query, key, value, probs, *weights, cosine, sine, tokens, grad_residual, gain,
        small, parts,
    )
UNIT = 2


def dot_t(a, b):
    return lax.dot_general(a, b, (((1,), (1,)), ((), ())), preferred_element_type=jnp.float32)


def dot_f32(a, b):
    return lax.dot_general(a, b, (((1,), (0,)), ((), ())), preferred_element_type=jnp.float32)


class ExpertWork:
    def __init__(self, expert, weights, scratch):
        self.expert = expert
        self.w_gate, self.w_up, self.w_down, self.shared = weights
        (
            self.tokens, self.grads, self.rows, self.grad_rows, self.hidden, self.pre, self.left_out,
            self.left_grad, self.right_out, self.right_grad, self.out, self.back, self.shared_hidden,
        ) = scratch

    @staticmethod
    def scratch(model, width, capacity, own_rows):
        bf16 = jnp.bfloat16
        seq = 2 * own_rows
        return [
            pltpu.VMEM((2, 2 * UNIT, own_rows, model), bf16),
            pltpu.VMEM((2, 2 * UNIT, own_rows, model), bf16),
            pltpu.VMEM((2, UNIT * capacity, model), bf16),
            pltpu.VMEM((2, UNIT * capacity, model), bf16),
            pltpu.VMEM((2, 3, UNIT * capacity, width), bf16),
            pltpu.VMEM((3, UNIT * capacity, width), jnp.float32),
            pltpu.VMEM((UNIT, seq, capacity + 128), bf16),
            pltpu.VMEM((UNIT, seq, capacity + 256), bf16),
            pltpu.VMEM((UNIT, capacity + 128, model), bf16),
            pltpu.VMEM((UNIT, capacity + 256, model), bf16),
            pltpu.VMEM((2, 2 * UNIT, own_rows, model), bf16),
            pltpu.VMEM((2, 2 * UNIT, own_rows, model), bf16),
            pltpu.VMEM((2, UNIT * seq, 384), bf16),
        ]

    def prepare(self):
        capacity = self.rows.shape[1] // UNIT
        for q in range(UNIT):
            self.right_out[q, pl.ds(capacity, 128), :] = self.shared[pl.ds(256, 128), :]
            self.right_grad[q, pl.ds(capacity, 256), :] = self.shared[pl.ds(0, 256), :]

    def run(self, slot, unit, gates, grad_gates, hook):
        bf16, f32 = jnp.bfloat16, jnp.float32
        own_rows, model = self.tokens.shape[2:]
        seq = 2 * own_rows
        capacity = self.rows.shape[1] // UNIT
        experts = gates.shape[1]
        column = 1024
        n_columns = model // column
        first = unit * (2 * UNIT)
        before = lax.broadcasted_iota(jnp.int32, (seq, seq), 0) <= lax.broadcasted_iota(jnp.int32, (seq, seq), 1)
        before = before.astype(f32).astype(bf16)
        slots = lax.broadcasted_iota(jnp.int32, (capacity, seq), 0)
        picks, row_gates = [], []
        for q in range(UNIT):
            g = jnp.concatenate(
                [gates[first + 2 * q + h, pl.ds(self.expert, 1), :] for h in range(2)], axis=1
            )
            g = jnp.broadcast_to(g, (8, seq))
            taken = (g > 0.0).astype(f32)
            rank = dot_f32(taken.astype(bf16), before).astype(jnp.int32) - 1
            hit = (slots == rank[:1]) & (g[:1] > 0.0)
            pick = hit.astype(f32)
            picks.append(pick)
            row_gates.append(jnp.sum(pick * g[:1], axis=1, keepdims=True))
            self.left_out[q, :, pl.ds(0, capacity)] = pick.T.astype(bf16)
            self.left_grad[q, :, pl.ds(0, capacity)] = pick.T.astype(bf16)
            low = pick.astype(bf16)

            span = pl.ds(q * capacity, capacity)
            for source, target in ((self.tokens, self.rows), (self.grads, self.grad_rows)):
                whole = source[slot, pl.ds(2 * q, 2)].reshape(seq, model)
                target[slot, span] = dot_f32(low, whole).astype(bf16)
        row_gate = jnp.concatenate(row_gates, axis=0)
        rows, grad_rows = self.rows.at[slot], self.grad_rows.at[slot]
        self.pre[0] = dot_f32(rows[...], self.w_gate[...])
        self.pre[1] = dot_f32(rows[...], self.w_up[...])
        self.pre[2] = dot_t(grad_rows[...], self.w_down[...])
        hook(2)
        step = 32
        parts = []
        for r in range(UNIT * capacity // step):
            span = pl.ds(r * step, step)
            gate_pre, up_pre, grad_hidden = self.pre[0, span], self.pre[1, span], self.pre[2, span]
            gate = row_gate[r * step : (r + 1) * step]
            sig = jax.nn.sigmoid(gate_pre)
            act = gate_pre * sig
            hidden = act * up_pre
            parts.append(jnp.sum(hidden * grad_hidden, axis=1, keepdims=True))
            grad_hidden = grad_hidden * gate
            self.hidden[slot, 0, span] = (hidden * gate).astype(bf16)
            slope = sig * (1.0 + gate_pre * (1.0 - sig))
            self.hidden[slot, 1, span] = (grad_hidden * up_pre * slope).astype(bf16)
            self.hidden[slot, 2, span] = (grad_hidden * act).astype(bf16)
        grad_gate_rows = jnp.concatenate(parts, axis=0)
        mine = lax.broadcasted_iota(jnp.int32, (experts, own_rows), 0) == self.expert
        for q in range(UNIT):
            per_token = jnp.sum(picks[q] * grad_gate_rows[q * capacity : (q + 1) * capacity], axis=0, keepdims=True)
            for h in range(2):
                part = jnp.broadcast_to(per_token[:, h * own_rows : (h + 1) * own_rows], (experts, own_rows))
                grad_gates[first + 2 * q + h] = jnp.where(mine, part, 0.0)

        for q in range(UNIT):
            blocks = pl.ds(2 * q, 2)
            whole = self.tokens[slot, blocks].reshape(seq, model)
            grad = self.grads[slot, blocks].reshape(seq, model)
            pre = dot_t(whole, self.shared[pl.ds(0, 256), :])
            grad_hidden = dot_t(grad, self.shared[pl.ds(256, 128), :])
            gate_pre, up_pre = pre[:, :128], pre[:, 128:]
            sig = jax.nn.sigmoid(gate_pre)
            act = gate_pre * sig
            hidden = (act * up_pre).astype(bf16)
            grad_gate = (grad_hidden * up_pre * sig * (1.0 + gate_pre * (1.0 - sig))).astype(bf16)
            grad_up = (grad_hidden * act).astype(bf16)
            span = pl.ds(q * seq, seq)
            self.shared_hidden[slot, span, pl.ds(0, 128)] = hidden
            self.shared_hidden[slot, span, pl.ds(128, 128)] = grad_gate
            self.shared_hidden[slot, span, pl.ds(256, 128)] = grad_up
            self.left_out[q, :, pl.ds(capacity, 128)] = hidden
            self.left_grad[q, :, pl.ds(capacity, 128)] = grad_gate
            self.left_grad[q, :, pl.ds(capacity + 128, 128)] = grad_up

        hook(3)

        def combine(c, carry):
            cols = pl.ds(pl.multiple_of(c * column, column), column)
            made = dot_f32(self.hidden[slot, 0], self.w_down[:, cols]).astype(bf16)
            back = dot_t(self.hidden[slot, 1], self.w_gate[cols, :])
            back = (back + dot_t(self.hidden[slot, 2], self.w_up[cols, :])).astype(bf16)
            for q in range(UNIT):
                span = slice(q * capacity, (q + 1) * capacity)
                self.right_out[q, pl.ds(0, capacity), cols] = made[span]
                self.right_grad[q, pl.ds(0, capacity), cols] = back[span]
                out = dot_f32(self.left_out[q], self.right_out[q, :, cols]).astype(bf16)
                self.out[slot, pl.ds(2 * q, 2), :, cols] = out.reshape(2, own_rows, column)
                out = dot_f32(self.left_grad[q], self.right_grad[q, :, cols]).astype(bf16)
                self.back[slot, pl.ds(2 * q, 2), :, cols] = out.reshape(2, own_rows, column)

            return carry

        lax.fori_loop(0, n_columns, combine, 0)


def expert_kernel(n_dp, *refs):
    own, own_gates, _, *weights_in = refs[:7]
    normed, grads, out_parts, back_parts, grad_gates, rows_out, grad_rows_out, hidden_out, shared_out = refs[7:16]
    scratch, weights = refs[16:-13], refs[-13:-9]
    fetch, gates, load, store, local, send, recv, g_send, g_recv = refs[-9:]
    n_planes = n_dp // 4
    spot = Spot(n_planes)
    half = own.shape[0] // 2

    def views(s, yy, cc, xx, part):
        b = dp_of(s, yy, cc) * 2 + xx
        if part == ALL:
            return [normed.at[b], gates.at[b]]
        if part == FIRST:
            return [normed.at[b, pl.ds(0, half)], gates.at[b]]
        return [normed.at[b, pl.ds(half, half)]]

    def grad_views(s, yy, cc, xx, part):
        b = dp_of(s, yy, cc) * 2 + xx
        if part == ALL:
            return [grads.at[b]]
        return [grads.at[b, pl.ds(0 if part == FIRST else half, half)]]

    kept = [
        pltpu.make_async_copy(a, v, local.at[i])
        for i, (a, v) in enumerate(zip((own, own_gates), views(spot.z, spot.y, spot.core, spot.x, ALL)))
    ]
    for c in kept:
        c.start()
    pieces = 4
    fetched = []
    for k, (a, b) in enumerate(zip(weights_in, weights)):
        size = a.shape[0] // pieces
        for p in range(pieces):
            span = pl.ds(p * size, size)
            fetched.append(pltpu.make_async_copy(a.at[span], b.at[span], fetch.at[k, p]))
    for c in fetched:
        c.start()
    spot.greet()
    copies = Copies(n_planes, send, recv)
    net = Spread(spot, copies, [own, own_gates], views, True, by_z=True)
    rest = Spread(spot, Copies(n_planes, g_send, g_recv), None, grad_views, True)
    net.begin()
    work = ExpertWork(spot.dp, weights, scratch)
    n_units = n_dp // UNIT
    blocks = 2 * UNIT
    rows = work.rows.shape[1]
    seqs = work.shared_hidden.shape[1]
    order = net.order

    def unit_of(i):
        s = 0 * i
        for j, plane in enumerate(order):
            s = s + (i // 2 == j).astype(jnp.int32) * plane
        yy = spot.y + (i % 2) * (1 - 2 * spot.y)
        return s * 2 + yy

    def loads(u, slot):
        span = pl.ds(u * blocks, blocks)
        return [
            pltpu.make_async_copy(normed.at[span], work.tokens.at[slot], load.at[slot, 0]),
            pltpu.make_async_copy(grads.at[span], work.grads.at[slot], load.at[slot, 1]),
        ]

    def stores(u, slot):
        span = pl.ds(u * blocks, blocks)
        some = pl.ds(pl.multiple_of(u * rows, rows), rows)
        pairs = [
            (work.out.at[slot], out_parts.at[span]),
            (work.back.at[slot], back_parts.at[span]),
            (work.rows.at[slot], rows_out.at[some]),
            (work.grad_rows.at[slot], grad_rows_out.at[some]),
            (work.hidden.at[slot], hidden_out.at[:, some]),
            (work.shared_hidden.at[slot], shared_out.at[pl.ds(pl.multiple_of(u * seqs, seqs), seqs)]),
        ]
        return [pltpu.make_async_copy(a, b, store.at[slot, i]) for i, (a, b) in enumerate(pairs)]

    def load_unit(i):
        for c in loads(unit_of(jnp.int32(i)), i % 2):
            c.start()

    def near(j):
        net.twin_near(j)
        load_unit(2 * j)

    def far(j):
        net.twin_far(j)
        rest.twin_corner(j)
        if j == n_planes - 1:
            rest.twin_side(j)
        load_unit(2 * j + 1)

    def over(j):
        if j == n_planes - 1:
            rest.from_side(j)
        rest.over_x(j)
        rest.over_y(j)

    plan = {
        (0, 0): [(net.onward, 1)],
        (0, 2): [(net.corner, 0), (rest.corner, 0), (far, 0), (over, 1)],
        (0, 3): [(net.relay_of, 2, 0), (net.relay_of, 3, 1)],
        (1, 0): [(net.sides, 1), (net.onward, 2), (rest.onward_y, 3)],
        (1, 2): [(near, 1)],
        (1, 3): [(net.corner, 1), (net.corner_of, 2, 1), (rest.corner, 1)],
        (2, 0): [(far, 1), (over, 2)],
        (2, 3): [(net.sides, 2), (net.relay_of, 3, 0), (net.onward, 3), (net.corner_of, 3, 1)],
        (3, 0): [(near, 2), (over, 3)],
        (3, 2): [(net.corner_of, 2, 0), (rest.corner, 2)],
        (4, 0): [(net.sides, 3), (far, 2)],
        (4, 3): [(net.corner_of, 3, 0), (rest.corner, 3)],
        (5, 0): [(near, 3)],
        (6, 0): [(far, 3)],
    }

    net.relay(1)
    net.relay_of(2, 1)
    net.sides(0)
    over(0)
    for c in kept:
        c.wait()
    near(0)
    for c in fetched:
        c.wait()
    work.prepare()

    def body(i, carry):
        slot = i % 2
        u = unit_of(i)

        def hook(point):
            for (k, at), actions in plan.items():
                if at == point:

                    @pl.when(i == k)
                    def _(actions=actions):
                        for action, *values in actions:
                            action(*values)

        hook(0)

        for c in loads(u, slot):
            c.wait()

        @pl.when(i >= 2)
        def _():
            for c in stores(unit_of(i - 2), slot):
                c.wait()

        work.run(slot, u, gates, grad_gates, hook)
        for c in stores(u, slot):
            c.start()
        return carry

    lax.fori_loop(0, n_units, body, 0)
    for i in (n_units - 2, n_units - 1):
        for c in stores(unit_of(jnp.int32(i)), i % 2):
            c.wait()
    copies.close()
    rest.copies.close()


def expert_call(own, own_gates, grads, w_gate, w_up, w_down, shared, n_dp, capacity, collective_id):
    own_rows, model = own.shape
    blocks = 2 * n_dp
    width = w_gate.shape[1]
    bf16 = jnp.bfloat16
    rows = n_dp * capacity
    n_planes = n_dp // 4
    vmem = pl.BlockSpec(memory_space=pltpu.VMEM)
    everyone = jax.ShapeDtypeStruct((blocks, own_rows, model), bf16)
    all_gates = (blocks,) + own_gates.shape
    return pl.pallas_call(
        functools.partial(expert_kernel, n_dp),
        out_shape=[
            everyone,
            everyone,
            everyone,
            everyone,
            jax.ShapeDtypeStruct(all_gates, jnp.float32),
            jax.ShapeDtypeStruct((rows, model), bf16),
            jax.ShapeDtypeStruct((rows, model), bf16),
            jax.ShapeDtypeStruct((3, rows, width), bf16),
            jax.ShapeDtypeStruct((blocks * own_rows, 384), bf16),
        ],
        in_specs=[ANY] * 7,
        out_specs=[ANY, ANY, ANY, ANY, vmem, ANY, ANY, ANY, ANY],
        input_output_aliases={2: 1},
        scratch_shapes=ExpertWork.scratch(model, width, capacity, own_rows)
        + [pltpu.VMEM(w.shape, bf16) for w in (w_gate, w_up, w_down, shared)]
        + [
            pltpu.SemaphoreType.DMA((4, 4)),
            pltpu.VMEM(all_gates, jnp.float32),
            pltpu.SemaphoreType.DMA((2, 2)),
            pltpu.SemaphoreType.DMA((2, 6)),
            pltpu.SemaphoreType.DMA((2,)),
            pltpu.SemaphoreType.DMA((14 * n_planes, 2)),
            pltpu.SemaphoreType.DMA((14 * n_planes, 2)),
            pltpu.SemaphoreType.DMA((14 * n_planes, 1)),
            pltpu.SemaphoreType.DMA((14 * n_planes, 1)),
        ],
        compiler_params=pltpu.CompilerParams(
            collective_id=collective_id, has_side_effects=True, vmem_limit_bytes=60 << 20
        ),
    )(own, own_gates, grads, w_gate, w_up, w_down, shared)


def gather_plan(
    tokens,
    attention_gain,
    expert_norm_gain,
    query_projection,
    key_projection,
    value_projection,
    output_projection,
    router,
    shared_gate_matrix,
    shared_up_matrix,
    shared_down_matrix,
    expert_gate_matrix,
    expert_up_matrix,
    expert_down_matrix,
    document_lengths,
    expert_indices,
    cotangent,
):
    n_dp = lax.axis_size(DP)
    x = lax.axis_index(TENSOR)
    dp = lax.axis_index(DP)
    own_rows, model_dim = tokens.shape
    sequence_length = own_rows * 2
    experts = n_dp
    top_k = expert_indices.shape[1]
    capacity = sequence_length * top_k * 4 // (3 * experts)
    bf16, f32 = jnp.bfloat16, jnp.float32

    def dot(a, b):
        return jnp.dot(a, b, preferred_element_type=f32)

    width = attention_gain.shape[0]
    lanes = 2 * width
    tile = jnp.concatenate(
        [router.T, attention_gain[None], expert_norm_gain[None], jnp.zeros((-(experts + 2) % 16, width), bf16)]
    )
    tile = lax.dynamic_update_slice(jnp.zeros((tile.shape[0], lanes), bf16), tile, (0, x * width))
    rotary_cosine, rotary_sine = rotation(sequence_length, HEAD_SIZE)
    cosine = jnp.concatenate([rotary_cosine, rotary_cosine], axis=1)
    sine = jnp.concatenate([-rotary_sine, rotary_sine], axis=1)
    doc_ends = jnp.cumsum(document_lengths[0])
    positions = jnp.arange(sequence_length, dtype=jnp.int32)
    doc_ids = jnp.sum((positions[:, None] >= doc_ends[None, :]).astype(jnp.int32), axis=-1)
    allowed = (doc_ids[:, None] == doc_ids[None, :]) & (positions[:, None] >= positions[None, :])
    own_indices = lax.dynamic_slice_in_dim(expert_indices, x * own_rows, own_rows, 0)
    chosen = jnp.any(own_indices[None] == jnp.arange(experts, dtype=jnp.int32)[:, None, None], axis=2)
    axes = (0, 0, 0, 1)
    (
        query_all, key_all, value_all, out_all, cotangent_all, params, full_one, rows_of_query, key_rows,
        rows_of_value, attn_probs, mixed_heads, residual, normed_two, gates_t,
    ) = front(
        [query_projection, key_projection, value_projection, output_projection],
        axes, tokens, tile, cotangent, chosen.astype(f32), cosine, sine, allowed.astype(f32), n_dp, 1,
    )
    router_full = params[:experts]
    first_gain = params[experts].astype(f32)
    second_gain = params[experts + 1].astype(f32)

    hidden = shared_gate_matrix.shape[1] // n_dp
    hidden_pad = -(-hidden // 16) * 16

    def slices(transposed):
        blocks = transposed.reshape(n_dp, hidden, -1)
        return jnp.pad(blocks, ((0, 0), (0, hidden_pad - hidden), (0, 0)))

    shared_out = jnp.stack(
        [slices(shared_gate_matrix.T), slices(shared_up_matrix.T), slices(shared_down_matrix)], axis=1
    )
    shared_in = lax.all_to_all(shared_out, DP, split_axis=0, concat_axis=0, tiled=True)
    shared_rows = jnp.moveaxis(shared_in, 0, 2).reshape(3, hidden_pad, model_dim)

    shared_rows = jnp.pad(shared_rows, ((0, 0), (0, 128 - hidden_pad), (0, 0))).reshape(384, model_dim)
    (
        normed_all, cotangent_all, output_parts, normed_parts, grad_gate_parts, received, grad_rows, hidden_rows,
        shared_hidden,
    ) = (
        expert_call(
            normed_two, gates_t, cotangent_all, expert_gate_matrix[0], expert_up_matrix[0], expert_down_matrix[0],
            shared_rows, n_dp, capacity, 2,
        )
    )
    (
        grad_normed_two, grad_gates_t, expert_gate_gradient, expert_up_gradient, expert_down_gradient, shared_grads,
    ) = sum_everywhere(
        [normed_parts, grad_gate_parts],
        [f32, f32],
        [
            received, grad_rows, normed_all.reshape(-1, model_dim), cotangent_all.reshape(-1, model_dim),
            hidden_rows, shared_hidden,
        ],
        n_dp, 4,
    )
    shared_grads = shared_grads.reshape(3, 128, model_dim)[:, :hidden_pad]

    gates = gates_t.T
    scale_two = lax.rsqrt(jnp.mean(residual * residual, axis=-1, keepdims=True) + norm_eps)
    grad_gates = grad_gates_t.T
    grad_logits = (
        gates * (grad_gates - jnp.sum(gates * grad_gates, axis=-1, keepdims=True))
    ).astype(bf16)
    grad_normed_two = grad_normed_two + dot(grad_logits, router_full)
    grad_router_part = dot(normed_two.T, grad_logits)
    grad_residual, grad_gain_two = rms_back(grad_normed_two, residual, scale_two, second_gain)
    grad_residual = grad_residual + cotangent.astype(f32)
    small_grads = jnp.concatenate([grad_router_part.T, jnp.zeros((8, model_dim), f32).at[1].set(grad_gain_two)])
    *weight_grads, grad_inputs, small_sums, ffn_own = backward(
        grad_residual.astype(bf16), mixed_heads, full_one, rows_of_query, key_rows, rows_of_value, attn_probs,
        [query_all, key_all, value_all, out_all], axes, cosine, sine, tokens, grad_residual, first_gain[None],
        small_grads, output_parts, n_dp, 6,
    )
    output = (residual + ffn_own).astype(bf16)
    mine = lax.dynamic_slice_in_dim(small_sums, x * width, width, 1)
    gain_one_own, gain_two_own, router_own = mine[experts], mine[experts + 1], mine[:experts].T
    returned = lax.all_to_all(
        shared_grads.reshape(3, hidden_pad, n_dp, -1).transpose(2, 0, 1, 3),
        DP, split_axis=0, concat_axis=0, tiled=True,
    )[:, :, :hidden]
    returned = returned.transpose(1, 0, 2, 3).reshape(3, n_dp * hidden, -1).astype(f32)
    return (
        output,
        grad_inputs,
        gain_one_own,
        gain_two_own,
        *weight_grads,
        router_own,
        returned[0].T,
        returned[1].T,
        returned[2],
        expert_gate_gradient[None],
        expert_up_gradient[None],
        expert_down_gradient[None],
    )


def shards(*arguments):
    tokens, expert_gate_matrix = arguments[0], arguments[11]
    n_dp, n_tensor = lax.axis_size(DP), lax.axis_size(TENSOR)
    gathered = n_dp * n_tensor * tokens.shape[0] * tokens.shape[1] * 2
    if n_tensor == 2 and n_dp % 4 == 0 and expert_gate_matrix.shape[0] == 1 and gathered <= 32 << 20:
        return gather_plan(*arguments)
    return exchange_plan(*arguments)


def solution(mesh):
    placed = (
        P((DP, TENSOR), None),
        P((DP, TENSOR)),
        P((DP, TENSOR)),
        P(DP, TENSOR),
        P(DP, TENSOR),
        P(DP, TENSOR),
        P(TENSOR, DP),
        P((DP, TENSOR), None),
        P(DP, TENSOR),
        P(DP, TENSOR),
        P(TENSOR, DP),
        P(DP, None, TENSOR),
        P(DP, None, TENSOR),
        P(DP, TENSOR, None),
        P(DP, None),
        P(DP, None),
        P((DP, TENSOR), None),
    )
    return jax.shard_map(
        shards,
        mesh=mesh,
        in_specs=placed,
        out_specs=(
            P((DP, TENSOR), None),
            P((DP, TENSOR), None),
            P((DP, TENSOR)),
            P((DP, TENSOR)),
            P(DP, TENSOR),
            P(DP, TENSOR),
            P(DP, TENSOR),
            P(TENSOR, DP),
            P((DP, TENSOR), None),
            P(DP, TENSOR),
            P(DP, TENSOR),
            P(TENSOR, DP),
            P(DP, None, TENSOR),
            P(DP, None, TENSOR),
            P(DP, TENSOR, None),
        ),
        check_vma=False,
    )
```

```python
import functools
import math

import jax
import jax.numpy as jnp
from jax import lax
from jax.experimental import pallas as pl
from jax.experimental.pallas import tpu as pltpu
from jax.sharding import PartitionSpec as P

HEAD_SIZE = 128
DP, TENSOR = ("dp", "tensor")


norm_eps = 1e-06
rope_base = 600000.0
neg_big = -1e30


def silu(argument):
    return argument * jax.nn.sigmoid(argument)


def silu_slope(argument):
    sigmoid_of = jax.nn.sigmoid(argument)
    return sigmoid_of * (1.0 + argument * (1.0 - sigmoid_of))


def rotation(sequence_length, head_dim):
    half_dim = head_dim // 2
    frequency = jnp.exp(
        jnp.arange(half_dim, dtype=jnp.float32) * (-2.0 * math.log(rope_base) / head_dim)
    )
    angles = jnp.arange(sequence_length, dtype=jnp.float32)[:, None] * frequency[None, :]
    return (jnp.cos(angles), jnp.sin(angles))


def apply_rotary(tensor, rotary_cosine, rotary_sine):
    half_dim = tensor.shape[-1] // 2
    first_half = tensor[..., :half_dim]
    second_half = tensor[..., half_dim:]
    cos_rows = rotary_cosine[:, None, :]
    sin_rows = rotary_sine[:, None, :]
    return jnp.concatenate(
        [
            first_half * cos_rows - second_half * sin_rows,
            second_half * cos_rows + first_half * sin_rows,
        ],
        axis=-1,
    )


def rotate_back(tensor, rotary_cosine, rotary_sine):
    return apply_rotary(tensor, rotary_cosine, -rotary_sine)


def rms_back(grad_normed, source, scale_rows, gain_full):
    weighted = grad_normed * gain_full
    cubed = scale_rows * scale_rows * scale_rows
    grad_source = scale_rows * weighted - source * cubed * jnp.mean(
        source * weighted, axis=-1, keepdims=True
    )
    grad_gain = jnp.sum(grad_normed * source * scale_rows, axis=0)
    return (grad_source, grad_gain)


def widen(sharded):
    return lax.all_gather(sharded, TENSOR, axis=0, tiled=True)


def narrow(partial_sum):
    return lax.psum_scatter(partial_sum, TENSOR, scatter_dimension=0, tiled=True)


def dense_fetch(
    query_projection,
    key_projection,
    value_projection,
    output_projection,
    shared_gate_matrix,
    shared_up_matrix,
    shared_down_matrix,
):
    return (
        lax.all_gather(query_projection, DP, axis=0, tiled=True),
        lax.all_gather(key_projection, DP, axis=0, tiled=True),
        lax.all_gather(value_projection, DP, axis=0, tiled=True),
        lax.all_gather(output_projection, DP, axis=1, tiled=True),
        lax.all_gather(shared_gate_matrix, DP, axis=0, tiled=True),
        lax.all_gather(shared_up_matrix, DP, axis=0, tiled=True),
        lax.all_gather(shared_down_matrix, DP, axis=1, tiled=True),
    )


def expert_up_output(received_rows, expert_gate_matrix, expert_up_matrix, expert_down_matrix):
    gate_preactivation = jnp.einsum(
        "miwy,iyh->miwh", received_rows, expert_gate_matrix, preferred_element_type=jnp.float32
    )
    up_preactivation = jnp.einsum(
        "miwy,iyh->miwh", received_rows, expert_up_matrix, preferred_element_type=jnp.float32
    )
    hidden = (silu(gate_preactivation) * up_preactivation).astype(jnp.bfloat16)
    produced_rows = jnp.einsum(
        "sxcf,xfd->sxcd", hidden, expert_down_matrix, preferred_element_type=jnp.float32
    ).astype(jnp.bfloat16)
    return (produced_rows, gate_preactivation, up_preactivation)


def expert_gradients(
    received,
    received_gradient,
    gate_preactivation,
    up_preactivation,
    expert_gate_matrix,
    expert_up_matrix,
    expert_down_matrix,
):
    hidden_expert = (silu(gate_preactivation) * up_preactivation).astype(jnp.bfloat16)
    expert_down_gradient = jnp.einsum(
        "sxcf,sxcd->xfd", hidden_expert, received_gradient, preferred_element_type=jnp.float32
    )
    grad_hidden_e = jnp.einsum(
        "sxcd,xfd->sxcf", received_gradient, expert_down_matrix, preferred_element_type=jnp.float32
    )
    grad_gate_e = (grad_hidden_e * up_preactivation * silu_slope(gate_preactivation)).astype(
        jnp.bfloat16
    )
    expert_up_hidden_gradient = (grad_hidden_e * silu(gate_preactivation)).astype(jnp.bfloat16)
    expert_gate_gradient = jnp.einsum(
        "gayi,gayr->air", received, grad_gate_e, preferred_element_type=jnp.float32
    )
    expert_up_gradient = jnp.einsum(
        "gayi,gayr->air", received, expert_up_hidden_gradient, preferred_element_type=jnp.float32
    )
    output_rows_gradient = (
        jnp.einsum(
            "zkjh,klh->zkjl", grad_gate_e, expert_gate_matrix, preferred_element_type=jnp.float32
        )
        + jnp.einsum(
            "zkjh,klh->zkjl",
            expert_up_hidden_gradient,
            expert_up_matrix,
            preferred_element_type=jnp.float32,
        )
    ).astype(jnp.bfloat16)
    return (expert_gate_gradient, expert_up_gradient, expert_down_gradient, output_rows_gradient)


def exchange_plan(
    tokens,
    attention_gain,
    expert_norm_gain,
    query_projection,
    key_projection,
    value_projection,
    output_projection,
    router,
    shared_gate_matrix,
    shared_up_matrix,
    shared_down_matrix,
    expert_gate_matrix,
    expert_up_matrix,
    expert_down_matrix,
    document_lengths,
    expert_indices,
    cotangent,
):
    n_tensor = lax.axis_size(TENSOR)
    n_dp = lax.axis_size(DP)
    tensor_pos = lax.axis_index(TENSOR)
    own_rows = tokens.shape[0]
    sequence_length = own_rows * n_tensor
    model_dim = tokens.shape[1]
    exp_dev = expert_gate_matrix.shape[0]
    experts = exp_dev * n_dp
    top_k = expert_indices.shape[1]
    capacity = max(2, sequence_length * top_k * 4 // (3 * experts))
    slot_total = experts * capacity
    router_full, gain_first, gain_second = (
        lax.all_gather(router, (DP, TENSOR), axis=0, tiled=True),
        lax.all_gather(attention_gain, (DP, TENSOR), axis=0, tiled=True),
        lax.all_gather(expert_norm_gain, (DP, TENSOR), axis=0, tiled=True),
    )
    first_gain = gain_first.astype(jnp.float32)
    second_gain = gain_second.astype(jnp.float32)
    fetched = dense_fetch(
        query_projection,
        key_projection,
        value_projection,
        output_projection,
        shared_gate_matrix,
        shared_up_matrix,
        shared_down_matrix,
    )
    query_all, key_all, value_all, out_all, sgate_all, sup_all, sdown_all = fetched
    input_values = tokens.astype(jnp.float32)
    scale_one = lax.rsqrt(jnp.mean(input_values * input_values, axis=-1, keepdims=True) + norm_eps)
    normed_one = (input_values * scale_one * first_gain).astype(jnp.bfloat16)
    full_one = widen(normed_one)
    q_heads = query_all.shape[1] // HEAD_SIZE
    kv_heads = key_all.shape[1] // HEAD_SIZE
    group_size = q_heads // kv_heads
    rotary_cosine, rotary_sine = rotation(sequence_length, HEAD_SIZE)
    query_unrotated = jnp.dot(full_one, query_all, preferred_element_type=jnp.float32).reshape(
        sequence_length, q_heads, HEAD_SIZE
    )
    key_unrotated = jnp.dot(full_one, key_all, preferred_element_type=jnp.float32).reshape(
        sequence_length, kv_heads, HEAD_SIZE
    )
    rows_of_query = (
        apply_rotary(query_unrotated, rotary_cosine, rotary_sine)
        .astype(jnp.bfloat16)
        .reshape(sequence_length, kv_heads, group_size, HEAD_SIZE)
    )
    key_rows = apply_rotary(key_unrotated, rotary_cosine, rotary_sine).astype(jnp.bfloat16)
    rows_of_value = (
        jnp.dot(full_one, value_all, preferred_element_type=jnp.float32)
        .astype(jnp.bfloat16)
        .reshape(sequence_length, kv_heads, HEAD_SIZE)
    )
    doc_ends = jnp.cumsum(document_lengths[0])
    positions = jnp.arange(sequence_length, dtype=jnp.int32)
    doc_ids = jnp.sum((positions[:, None] >= doc_ends[None, :]).astype(jnp.int32), axis=-1)
    score_scale = HEAD_SIZE ** (-0.5)

    def block_scores(start_row, end_row):
        scores = (
            jnp.einsum(
                "qkgd,skd->kgqs", rows_of_query, key_rows, preferred_element_type=jnp.float32
            )
            * score_scale
        )
        allowed = (doc_ids[start_row:end_row, None] == doc_ids[None, :end_row]) & (
            positions[start_row:end_row, None] >= positions[None, :end_row]
        )
        return (scores, allowed)

    block_index = 0
    start_row = block_index * sequence_length
    end_row = start_row + sequence_length
    scores, allowed = block_scores(start_row, end_row)
    scores = jnp.where(allowed, scores, neg_big)
    row_max = jnp.max(scores, axis=-1, keepdims=True)
    exp_scores = jnp.exp(scores - row_max)
    row_sum = jnp.sum(exp_scores, axis=-1, keepdims=True)
    lse_blocks = [row_max + jnp.log(row_sum)]
    attn_probs = (exp_scores / row_sum).astype(jnp.bfloat16)
    out_blocks = jnp.einsum(
        "kgqs,skd->qkgd", attn_probs, rows_of_value, preferred_element_type=jnp.float32
    )
    mixed_heads = out_blocks.reshape(sequence_length, q_heads * HEAD_SIZE).astype(jnp.bfloat16)
    attn_part = jnp.dot(mixed_heads, out_all, preferred_element_type=jnp.float32)
    residual = input_values + narrow(attn_part)
    scale_two = lax.rsqrt(jnp.mean(residual * residual, axis=-1, keepdims=True) + norm_eps)
    normed_two = (residual * scale_two * second_gain).astype(jnp.bfloat16)
    full_two = widen(normed_two)
    logits = jnp.dot(full_two, router_full, preferred_element_type=jnp.float32)
    chosen = expert_indices[:, :, None] == jnp.arange(experts, dtype=jnp.int32)[None, None, :]
    selected = jnp.sum(jnp.where(chosen, logits[:, None, :], 0.0), axis=-1)
    top_max = jnp.max(selected, axis=-1, keepdims=True)
    gate_exp = jnp.exp(selected - top_max)
    gate_probs = gate_exp / jnp.sum(gate_exp, axis=-1, keepdims=True)
    gate_shared = jnp.dot(full_two, sgate_all, preferred_element_type=jnp.float32)
    up_shared = jnp.dot(full_two, sup_all, preferred_element_type=jnp.float32)
    hidden_shared = (silu(gate_shared) * up_shared).astype(jnp.bfloat16)
    shared_part = jnp.dot(hidden_shared, sdown_all, preferred_element_type=jnp.float32)
    flat_ids = expert_indices.reshape(-1)
    onehot = (flat_ids[:, None] == jnp.arange(experts, dtype=jnp.int32)[None, :]).astype(jnp.int32)
    slot_rank = jnp.sum(onehot * (jnp.cumsum(onehot, axis=0) - 1), axis=-1)
    slot_index = flat_ids * capacity + slot_rank
    pair_index = jnp.arange(sequence_length * top_k, dtype=jnp.int32)
    token_of_slot = jnp.zeros((slot_total,), jnp.int32).at[slot_index].set(pair_index // top_k)
    slot_used = jnp.zeros((slot_total,), jnp.bool_).at[slot_index].set(True)
    gate_of_slot = jnp.zeros((slot_total,), jnp.float32).at[slot_index].set(gate_probs.reshape(-1))
    outgoing = jnp.where(slot_used[:, None], full_two[token_of_slot], 0).reshape(
        n_dp, exp_dev, capacity, model_dim
    )
    received_rows = lax.all_to_all(outgoing, DP, split_axis=0, concat_axis=0, tiled=True)
    produced_rows, gate_preactivation, up_preactivation = expert_up_output(
        received_rows, expert_gate_matrix, expert_up_matrix, expert_down_matrix
    )
    sent_home = lax.all_to_all(produced_rows, DP, split_axis=0, concat_axis=0, tiled=True)
    returned, received, gate_preactivation, up_preactivation = (
        sent_home,
        received_rows,
        gate_preactivation,
        up_preactivation,
    )
    picked = returned.reshape(slot_total, model_dim)[slot_index].reshape(
        sequence_length, top_k, model_dim
    )
    routed_part = jnp.einsum("sk,skd->sd", gate_probs, picked, preferred_element_type=jnp.float32)
    ffn_own = narrow(shared_part + routed_part)
    output = (residual + ffn_own).astype(jnp.bfloat16)
    weights_back = dense_fetch(
        query_projection,
        key_projection,
        value_projection,
        output_projection,
        shared_gate_matrix,
        shared_up_matrix,
        shared_down_matrix,
    )
    query_back, key_back, value_back, out_back, sgate_back, sup_back, sdown_back = weights_back
    grad_out = cotangent.astype(jnp.float32)
    grad_ffn = widen(cotangent)
    grad_hidden_sh = jnp.dot(grad_ffn, sdown_back.T, preferred_element_type=jnp.float32)
    grad_sdown = jnp.dot(hidden_shared.T, grad_ffn, preferred_element_type=jnp.float32)
    grad_gate_sh = (grad_hidden_sh * up_shared * silu_slope(gate_shared)).astype(jnp.bfloat16)
    grad_up_sh = (grad_hidden_sh * silu(gate_shared)).astype(jnp.bfloat16)
    grad_sgate = jnp.dot(full_two.T, grad_gate_sh, preferred_element_type=jnp.float32)
    grad_sup = jnp.dot(full_two.T, grad_up_sh, preferred_element_type=jnp.float32)
    grad_normed_part = jnp.dot(
        grad_gate_sh, sgate_back.T, preferred_element_type=jnp.float32
    ) + jnp.dot(grad_up_sh, sup_back.T, preferred_element_type=jnp.float32)
    grad_gates_part = jnp.einsum("sd,skd->sk", grad_ffn, picked, preferred_element_type=jnp.float32)
    grad_slot = (
        jnp.where(slot_used[:, None], grad_ffn[token_of_slot] * gate_of_slot[:, None], 0.0)
        .astype(jnp.bfloat16)
        .reshape(n_dp, exp_dev, capacity, model_dim)
    )
    received_gradient = lax.all_to_all(grad_slot, DP, split_axis=0, concat_axis=0, tiled=True)
    expert_gate_gradient, expert_up_gradient, expert_down_gradient, output_rows_gradient = (
        expert_gradients(
            received,
            received_gradient,
            gate_preactivation,
            up_preactivation,
            expert_gate_matrix,
            expert_up_matrix,
            expert_down_matrix,
        )
    )
    grad_returned = lax.all_to_all(
        output_rows_gradient, DP, split_axis=0, concat_axis=0, tiled=True
    )
    grad_picked = grad_returned.reshape(slot_total, model_dim)[slot_index].reshape(
        sequence_length, top_k, model_dim
    )
    grad_normed_part = grad_normed_part + jnp.sum(grad_picked, axis=1, dtype=jnp.float32)
    grad_normed_two, grad_gates = (
        lax.psum_scatter(
            grad_normed_part.astype(jnp.bfloat16), TENSOR, scatter_dimension=0, tiled=True
        ).astype(jnp.float32),
        lax.psum_scatter(
            grad_gates_part.astype(jnp.bfloat16), TENSOR, scatter_dimension=0, tiled=True
        ).astype(jnp.float32),
    )
    row_start = tensor_pos * own_rows
    gates_own = lax.dynamic_slice_in_dim(gate_probs, row_start, own_rows, 0)
    chosen_own = lax.dynamic_slice_in_dim(chosen, row_start, own_rows, 0)
    grad_selected = gates_own * (
        grad_gates - jnp.sum(gates_own * grad_gates, axis=-1, keepdims=True)
    )
    grad_logits = jnp.sum(jnp.where(chosen_own, grad_selected[:, :, None], 0.0), axis=1).astype(
        jnp.bfloat16
    )
    grad_normed_two = grad_normed_two + jnp.dot(
        grad_logits, router_full.T, preferred_element_type=jnp.float32
    )
    grad_router_part = jnp.dot(normed_two.T, grad_logits, preferred_element_type=jnp.float32)
    grad_residual, grad_gain_two = rms_back(grad_normed_two, residual, scale_two, second_gain)
    grad_residual = grad_residual + grad_out
    grad_attn = widen(grad_residual.astype(jnp.bfloat16))
    grad_wout = jnp.dot(mixed_heads.T, grad_attn, preferred_element_type=jnp.float32)
    grad_mixed = (
        jnp.dot(grad_attn, out_back.T, preferred_element_type=jnp.float32)
        .astype(jnp.bfloat16)
        .reshape(sequence_length, kv_heads, group_size, HEAD_SIZE)
    )
    grad_keys = jnp.zeros((sequence_length, kv_heads, HEAD_SIZE), jnp.float32)
    grad_values = jnp.zeros((sequence_length, kv_heads, HEAD_SIZE), jnp.float32)
    block_index = 0
    start_row = block_index * sequence_length
    end_row = start_row + sequence_length
    scores, allowed = block_scores(start_row, end_row)
    attn_probs = jnp.where(allowed, jnp.exp(scores - lse_blocks[block_index]), 0.0)
    probs_low = attn_probs.astype(jnp.bfloat16)
    grad_values = grad_values.at[:end_row].add(
        jnp.einsum("kgqs,qkgd->skd", probs_low, grad_mixed, preferred_element_type=jnp.float32)
    )
    grad_probs = jnp.einsum(
        "qkgd,skd->kgqs", grad_mixed, rows_of_value, preferred_element_type=jnp.float32
    )
    inner_sum = jnp.sum(attn_probs * grad_probs, axis=-1, keepdims=True)
    grad_scores = (attn_probs * (grad_probs - inner_sum)).astype(jnp.bfloat16)
    grad_query_blocks = (
        jnp.einsum("kgqs,skd->qkgd", grad_scores, key_rows, preferred_element_type=jnp.float32)
        * score_scale
    )
    grad_keys = grad_keys.at[:end_row].add(
        jnp.einsum("kgqs,qkgd->skd", grad_scores, rows_of_query, preferred_element_type=jnp.float32)
        * score_scale
    )
    grad_query = grad_query_blocks.reshape(sequence_length, q_heads, HEAD_SIZE)
    grad_q_raw = (
        rotate_back(grad_query, rotary_cosine, rotary_sine)
        .astype(jnp.bfloat16)
        .reshape(sequence_length, q_heads * HEAD_SIZE)
    )
    grad_k_raw = (
        rotate_back(grad_keys, rotary_cosine, rotary_sine)
        .astype(jnp.bfloat16)
        .reshape(sequence_length, kv_heads * HEAD_SIZE)
    )
    grad_v_low = grad_values.astype(jnp.bfloat16).reshape(sequence_length, kv_heads * HEAD_SIZE)
    grad_wquery = jnp.dot(full_one.T, grad_q_raw, preferred_element_type=jnp.float32)
    grad_wkey = jnp.dot(full_one.T, grad_k_raw, preferred_element_type=jnp.float32)
    grad_wvalue = jnp.dot(full_one.T, grad_v_low, preferred_element_type=jnp.float32)
    grad_normed_one_part = (
        jnp.dot(grad_q_raw, query_back.T, preferred_element_type=jnp.float32)
        + jnp.dot(grad_k_raw, key_back.T, preferred_element_type=jnp.float32)
        + jnp.dot(grad_v_low, value_back.T, preferred_element_type=jnp.float32)
    )
    grad_normed_one = narrow(grad_normed_one_part)
    grad_inputs, grad_gain_one = rms_back(grad_normed_one, input_values, scale_one, first_gain)
    grad_inputs = grad_inputs + grad_residual
    dense_sums = (
        lax.psum_scatter(grad_wquery, DP, scatter_dimension=0, tiled=True),
        lax.psum_scatter(grad_wkey, DP, scatter_dimension=0, tiled=True),
        lax.psum_scatter(grad_wvalue, DP, scatter_dimension=0, tiled=True),
        lax.psum_scatter(grad_wout, DP, scatter_dimension=1, tiled=True),
        lax.psum_scatter(grad_sgate, DP, scatter_dimension=0, tiled=True),
        lax.psum_scatter(grad_sup, DP, scatter_dimension=0, tiled=True),
        lax.psum_scatter(grad_sdown, DP, scatter_dimension=1, tiled=True),
    )
    small_sums = (
        lax.psum_scatter(grad_router_part, (DP, TENSOR), scatter_dimension=0, tiled=True),
        lax.psum_scatter(grad_gain_one, (DP, TENSOR), scatter_dimension=0, tiled=True),
        lax.psum_scatter(grad_gain_two, (DP, TENSOR), scatter_dimension=0, tiled=True),
    )
    return (
        output,
        grad_inputs,
        small_sums[1],
        small_sums[2],
        dense_sums[0],
        dense_sums[1],
        dense_sums[2],
        dense_sums[3],
        small_sums[0],
        dense_sums[4],
        dense_sums[5],
        dense_sums[6],
        expert_gate_gradient,
        expert_up_gradient,
        expert_down_gradient,
    )


MESH = pl.DeviceIdType.MESH
ANY = pl.BlockSpec(memory_space=pl.ANY)


def when(condition, body):
    if condition is None:
        body()
    else:
        pl.when(condition)(body)


class Spot:
    def __init__(self, n_planes):
        dp = lax.axis_index(DP)
        self.x = lax.axis_index(TENSOR)
        self.dp = dp
        self.core = dp % 2
        self.y = (dp // 2) % 2
        self.z = dp // 4
        self.n_planes = n_planes
        self.has_up = self.z < n_planes - 1
        self.has_down = self.z > 0
        self.up = (dp + 4, self.x)
        self.down = (dp - 4, self.x)
        self.side = (dp + 2 - 4 * self.y, self.x)
        self.across = (dp, 1 - self.x)
        self.twin = (dp + 1 - 2 * self.core, self.x)

    def far_first(self):
        low, high = 0 * self.z, 0 * self.z + self.n_planes - 1
        order = []
        for _ in range(self.n_planes):
            take_low = (self.z - low >= high - self.z).astype(jnp.int32)
            order.append(take_low * low + (1 - take_low) * high)
            low, high = low + take_low, high - (1 - take_low)
        return order

    def greet(self):
        barrier = pltpu.get_barrier_semaphore()
        fixed = [self.side, self.twin, self.across]
        for device in fixed:
            pl.semaphore_signal(barrier, inc=1, device_id=device, device_id_type=MESH)
        for condition, device in ((self.has_up, self.up), (self.has_down, self.down)):

            @pl.when(condition)
            def _(device=device):
                pl.semaphore_signal(barrier, inc=1, device_id=device, device_id_type=MESH)

        ends = self.has_up.astype(jnp.int32) + self.has_down.astype(jnp.int32)
        pl.semaphore_wait(barrier, len(fixed) + ends)


class Copies:
    def __init__(self, n_planes, send, recv):
        self.n_planes, self.send, self.recv = n_planes, send, recv
        self.open = []

    def copy(self, group, s, piece, src, dst, device, arrival=None):
        arrival = group if arrival is None else arrival
        return pltpu.make_async_remote_copy(
            src_ref=src,
            dst_ref=dst,
            send_sem=self.send.at[group * self.n_planes + s, piece],
            recv_sem=self.recv.at[arrival * self.n_planes + s, piece],
            device_id=device,
            device_id_type=MESH,
        )

    def start(self, condition, group, s, sources, targets, device, arrival=None):
        def body():
            for i, (src, dst) in enumerate(zip(sources, targets)):
                self.copy(group, s, i, src, dst, device, arrival).start()

        when(condition, body)
        self.open.append((condition, group, s, sources, targets, device, arrival))

    def arrive(self, group, s, targets, device):
        for i, dst in enumerate(targets):
            self.copy(group, s, i, dst, dst, device).wait_recv()

    def close(self):
        for condition, group, s, sources, targets, device, arrival in self.open:

            def body():
                for i, (src, dst) in enumerate(zip(sources, targets)):
                    self.copy(group, s, i, src, dst, device, arrival).wait_send()

            when(condition, body)


(Z_UP, Z_DOWN, Y_ALL, Y_HALF, X_ALL, X_HALF, C_OWN, C_Y, C_X, C_XH, C_YH, D_UP, D_DOWN, C_D) = range(14)
(ALL, FIRST, SECOND) = range(3)


class Spread:
    def __init__(self, spot, copies, own, views, use_x, by_z=False):
        self.spot, self.copies, self.own, self.use_x, self.by_z = spot, copies, own, use_x, by_z
        self.order = spot.far_first()[::-1]
        y, x, core = spot.y, spot.x, spot.core

        def places(s, cc):
            return (
                views(s, y, cc, x, ALL),
                views(s, 1 - y, cc, x, ALL),
                views(s, 1 - y, cc, x, FIRST),
                views(s, y, cc, 1 - x, ALL),
                views(s, y, cc, 1 - x, SECOND),
                views(s, 1 - y, cc, 1 - x, FIRST),
                views(s, 1 - y, cc, 1 - x, SECOND),
                views(s, 1 - y, cc, 1 - x, ALL),
            )

        self.mine = [places(s, core) for s in self.order]
        self.twins = [places(s, 1 - core) for s in self.order]
        self.goes_down = [(s > spot.z) & spot.has_down for s in self.order]
        self.goes_up = [(s < spot.z) & spot.has_up for s in self.order]
        middle = spot.has_up & spot.has_down
        self.among = (jnp.logical_not(middle), middle)
        self.goes = {
            (j, c): (self.goes_down[j] & self.among[c], self.goes_up[j] & self.among[c], self.among[c])
            for j in range(len(self.order))
            for c in (0, 1)
        }

    def place(self, j):
        return self.own if j == 0 else self.mine[j][0]

    def onward_y(self, j):
        self.copies.start(None, Y_ALL, self.order[j], self.place(j), self.mine[j][0], self.spot.side)

    def onward_x(self, j):
        self.copies.start(None, X_ALL, self.order[j], self.place(j), self.mine[j][0], self.spot.across)

    def onward_twin(self, j):
        self.copies.start(None, C_OWN, self.order[j], self.place(j), self.mine[j][0], self.spot.twin)

    def onward(self, j):
        self.onward_y(j)
        if self.use_x:
            self.onward_x(j)
        self.onward_twin(j)

    def begin_z(self):
        spot, here = self.spot, self.mine[0][0]
        self.copies.start(spot.has_up, Z_UP, spot.z, self.own, here, spot.up)
        self.copies.start(spot.has_down, Z_DOWN, spot.z, self.own, here, spot.down, Z_UP)

    def begin(self):
        self.begin_z()
        self.onward(0)

    def relay(self, j, goes=None):
        s, here, spot = self.order[j], self.mine[j][0], self.spot
        goes_down, goes_up, _ = goes or (self.goes_down[j], self.goes_up[j], None)
        self.copies.arrive(Z_UP, s, here, spot.up)
        self.copies.start(goes_down, Z_DOWN, s, here, here, spot.down, Z_UP)
        self.copies.start(goes_up, Z_UP, s, here, here, spot.up)

    def relay_of(self, j, c):
        pl.when(self.among[c])(functools.partial(self.relay, j, self.goes[j, c]))

    def corner_of(self, j, c):
        pl.when(self.among[c])(functools.partial(self.corner, j, self.goes[j, c]))

    def column(self, j):
        if j < len(self.order):
            self.relay(j)
            self.onward(j)

    def from_side(self, j):
        s, there, spot = self.order[j], self.mine[j][1], self.spot
        self.copies.arrive(Y_ALL, s, there, spot.side)
        self.copies.start(None, C_Y, s, there, there, spot.twin)

    def from_across(self, j):
        s, there, spot = self.order[j], self.mine[j][3], self.spot
        self.copies.arrive(X_ALL, s, there, spot.across)
        self.copies.start(None, C_X, s, there, there, spot.twin)

    def over_x(self, j):
        part = self.mine[j][2]
        self.copies.start(None, X_HALF, self.order[j], part, part, self.spot.across)

    def over_y(self, j):
        part = self.mine[j][4]
        self.copies.start(None, Y_HALF, self.order[j], part, part, self.spot.side)

    def side(self, j):
        self.from_side(j)
        if self.use_x and (j == 0 or not self.by_z):
            self.over_x(j)

    def across(self, j):
        self.from_across(j)
        if j == 0 or not self.by_z:
            self.over_y(j)

    def sides(self, j):
        if 0 <= j < len(self.order):
            self.side(j)
            if self.use_x:
                self.across(j)

    def corner(self, j, goes=None):
        if not self.use_x or not 0 <= j < len(self.order):
            return
        s, spot = self.order[j], self.spot
        first, second, whole = self.mine[j][5:]
        if self.by_z and j > 0:
            goes_down, goes_up, always = goes or (self.goes_down[j], self.goes_up[j], None)
            self.copies.arrive(D_UP, s, whole, spot.up)
            self.copies.start(goes_down, D_DOWN, s, whole, whole, spot.down, D_UP)
            self.copies.start(goes_up, D_UP, s, whole, whole, spot.up)
            self.copies.start(always, C_D, s, whole, whole, spot.twin)
            return
        self.copies.arrive(X_HALF, s, first, spot.across)
        self.copies.start(None, C_XH, s, first, first, spot.twin)
        self.copies.arrive(Y_HALF, s, second, spot.side)
        self.copies.start(None, C_YH, s, second, second, spot.twin)
        if self.by_z:
            self.copies.start(spot.has_up, D_UP, s, whole, whole, spot.up)
            self.copies.start(spot.has_down, D_DOWN, s, whole, whole, spot.down, D_UP)

    def twin_own(self, j):
        self.copies.arrive(C_OWN, self.order[j], self.twins[j][0], self.spot.twin)

    def twin_across(self, j):
        self.copies.arrive(C_X, self.order[j], self.twins[j][3], self.spot.twin)

    def twin_near(self, j):
        self.twin_own(j)
        if self.use_x:
            self.twin_across(j)

    def twin_side(self, j):
        self.copies.arrive(C_Y, self.order[j], self.twins[j][1], self.spot.twin)

    def twin_corner(self, j):
        if self.by_z and j > 0:
            self.copies.arrive(C_D, self.order[j], self.twins[j][7], self.spot.twin)
            return
        self.copies.arrive(C_XH, self.order[j], self.twins[j][5], self.spot.twin)
        self.copies.arrive(C_YH, self.order[j], self.twins[j][6], self.spot.twin)

    def twin_far(self, j):
        self.twin_side(j)
        if self.use_x:
            self.twin_corner(j)

    def twin_all(self):
        for j in range(len(self.order)):
            self.twin_near(j)
            self.twin_far(j)

    def stage(self, step):
        self.column(step)
        self.sides(step - 1)
        self.corner(step - 2)

    def run(self):
        self.begin()
        for step in range(1, len(self.order) + 2):
            self.stage(step)
        self.twin_all()
        self.copies.close()


def dp_of(s, yy, cc):
    return (s * 2 + yy) * 2 + cc


def plain_dot(a, b, contract):
    return lax.dot_general(a, b, (contract, ((), ())), preferred_element_type=jnp.float32)


ROWS_COLUMNS = ((1,), (0,))
ROWS_ROWS = ((1,), (1,))
COLUMNS_COLUMNS = ((0,), (0,))


def turn(heads, cosine, sine):
    return heads * cosine + pltpu.roll(heads, heads.shape[1] // 2, 1) * sine


def front_kernel(n_planes, axes, *refs):
    n = len(axes)
    shards_in, (tokens, tile, grads, chosen, cosine, sine, allowed) = refs[:n], refs[n : n + 7]
    outs = refs[n + 7 : 2 * n + 7]
    all_grads, params, *kept_out, residual, normed_two, gates = refs[2 * n + 7 : 2 * n + 18]
    normed_one, query, key, value, probs, mixed = refs[-7:-1]
    out_sems = refs[-1]
    (
        wq, wk, wv, wo, sequence, pair, sent, received, w_send, w_recv, p_send, p_recv, g_send, g_recv, local,
        x_send, x_recv,
    ) = refs[2 * n + 18 : -7]
    spot = Spot(n_planes)
    x = spot.x
    bf16, f32 = jnp.bfloat16, jnp.float32
    own_rows, model = tokens.shape

    def weight_views(s, yy, cc, xx, part):
        i = dp_of(s, yy, cc)
        places = []
        for o, a, axis in zip((wq, wk, wv, wo), shards_in, axes):
            size = a.shape[axis]
            span = pl.ds(pl.multiple_of(i * size, size), size)
            places.append(o.at[span] if axis == 0 else o.at[:, span])
        return places

    def param_views(s, yy, cc, xx, part):
        size = tile.shape[1]
        return [params.at[:, pl.ds(pl.multiple_of(dp_of(s, yy, cc) * size, size), size)]]

    def grad_views(s, yy, cc, xx, part):
        b = dp_of(s, yy, cc) * 2 + xx
        if part == ALL:
            return [all_grads.at[b]]
        return [all_grads.at[b, pl.ds(0 if part == FIRST else own_rows // 2, own_rows // 2)]]

    def mine(views):
        return views(spot.z, spot.y, spot.core, x, ALL)

    def swap(i, src, dst):
        return pltpu.make_async_remote_copy(
            src_ref=src, dst_ref=dst, send_sem=x_send.at[i], recv_sem=x_recv.at[i],
            device_id=spot.across, device_id_type=MESH,
        )

    kept = list(zip(list(shards_in) + [tokens, grads, tile], mine(weight_views) + [sequence.at[x]] + mine(grad_views) + [pair.at[x]]))
    kept = [pltpu.make_async_copy(a, b, local.at[i]) for i, (a, b) in enumerate(kept)]
    for c in kept:
        c.start()
    spot.greet()
    swaps = [swap(0, tile, pair.at[x]), swap(1, tokens, sequence.at[x]), swap(2, sent, received)]
    swaps[0].start()
    weights = Spread(spot, Copies(n_planes, w_send, w_recv), list(shards_in), weight_views, False)
    small = Spread(spot, Copies(n_planes, p_send, p_recv), mine(param_views), param_views, False)
    net = Spread(spot, Copies(n_planes, g_send, g_recv), [grads], grad_views, True)
    weights.begin()
    swaps[1].start()
    for c in kept:
        c.wait()
    swap(0, pair.at[1 - x], pair.at[1 - x]).wait_recv()
    mine(param_views)[0][...] = pair[0] + pair[1]
    small.begin()
    net.onward_x(0)
    net.onward_twin(0)
    for step in range(1, n_planes + 1):
        weights.stage(step)
        small.stage(step)
        if step == n_planes - 1:
            net.begin_z()
    net.onward_y(0)
    net.from_across(0)

    net.relay(1)
    net.relay_of(2, 1)
    net.onward_x(1)
    net.onward_twin(1)

    small.twin_all()
    swap(1, sequence.at[1 - x], sequence.at[1 - x]).wait_recv()

    experts = chosen.shape[0]
    first_gain = params[experts : experts + 1, :].astype(f32)
    step = 32
    for h in range(2):
        for r in range(own_rows // step):
            rows = sequence[h, pl.ds(r * step, step)].astype(f32)
            scale = lax.rsqrt(jnp.mean(rows * rows, axis=1, keepdims=True) + norm_eps)
            normed_one[pl.ds(h * own_rows + r * step, step)] = (rows * scale * first_gain).astype(bf16)
    weights.twin_all()
    pairs = list(zip((wq, wk, wv, wo), outs)) + list(zip((normed_one, query, key, value, probs, mixed), kept_out))
    written = [pltpu.make_async_copy(a, b, out_sems.at[i]) for i, (a, b) in enumerate(pairs)]
    for c in written[: n + 1]:
        c.start()
    heads, head_dim = query.shape[1] // cosine.shape[1], cosine.shape[1]
    kv_heads = key.shape[1] // head_dim
    group = heads // kv_heads
    cos, sin = cosine[...], sine[...]
    raw = plain_dot(normed_one[...], wk[...], ROWS_COLUMNS)
    for g in range(kv_heads):
        span = slice(g * head_dim, (g + 1) * head_dim)
        key[:, span] = turn(raw[:, span], cos, sin).astype(bf16)
    value[...] = plain_dot(normed_one[...], wv[...], ROWS_COLUMNS).astype(bf16)
    raw = plain_dot(normed_one[...], wq[...], ROWS_COLUMNS)
    for h in range(heads):
        span = slice(h * head_dim, (h + 1) * head_dim)
        query[:, span] = turn(raw[:, span], cos, sin).astype(bf16)
    net.from_side(0)
    net.onward_y(1)
    net.relay_of(2, 0)
    net.relay_of(3, 1)
    net.onward_x(2)
    net.onward_twin(2)
    net.from_across(1)
    may = allowed[...] > 0.0
    for h in range(heads):
        span = slice(h * head_dim, (h + 1) * head_dim)
        shared = slice(h // group * head_dim, (h // group + 1) * head_dim)
        scores = plain_dot(query[:, span], key[:, shared], ROWS_ROWS) * (head_dim ** -0.5)
        scores = jnp.where(may, scores, neg_big)
        weight = jnp.exp(scores - jnp.max(scores, axis=1, keepdims=True))
        weight = weight / jnp.sum(weight, axis=1, keepdims=True)
        probs[h] = weight
        mixed[:, span] = plain_dot(weight.astype(bf16), value[:, shared], ROWS_COLUMNS).astype(bf16)
    for c in written[n + 1 :]:
        c.start()
    other = mixed[pl.ds(pl.multiple_of((1 - x) * own_rows, own_rows), own_rows), :]
    sent[...] = plain_dot(other, wo[...], ROWS_COLUMNS).astype(bf16)
    swaps[2].start()
    other = mixed[pl.ds(pl.multiple_of(x * own_rows, own_rows), own_rows), :]
    residual[...] = plain_dot(other, wo[...], ROWS_COLUMNS)
    net.relay_of(3, 0)
    net.onward_twin(3)
    net.from_side(1)
    net.from_across(2)
    swap(2, received, received).wait_recv()
    second_gain = params[experts + 1 : experts + 2, :].astype(f32)
    for r in range(own_rows // step):
        span = pl.ds(r * step, step)
        rows = sequence[x, span].astype(f32) + (residual[span] + received[span].astype(f32))
        residual[span] = rows
        scale = lax.rsqrt(jnp.mean(rows * rows, axis=1, keepdims=True) + norm_eps)
        normed_two[span] = (rows * scale * second_gain).astype(bf16)
    logits = plain_dot(params[:experts, :], normed_two[...], ROWS_ROWS)
    picked = chosen[...] > 0.0
    top = jnp.max(jnp.where(picked, logits, neg_big), axis=0, keepdims=True)
    weight = jnp.where(picked, jnp.exp(jnp.where(picked, logits - top, 0.0)), 0.0)
    gates[...] = weight / jnp.sum(weight, axis=0, keepdims=True)

    for j in range(n_planes):
        net.twin_own(j)
        if j < n_planes - 1:
            net.twin_across(j)
        if j < n_planes - 2:
            net.twin_side(j)
    for each in (weights, small, net):
        each.copies.close()
    for c in swaps:
        c.wait_send()
    for c in written:
        c.wait()


def front(arrays, axes, tokens, tile, grads, chosen, cosine, sine, allowed, n_dp, collective_id):
    n, n_planes = len(arrays), n_dp // 4
    bf16, f32 = jnp.bfloat16, jnp.float32
    shape = jax.ShapeDtypeStruct

    def whole(a, axis):
        full = list(a.shape)
        full[axis] *= n_dp
        return shape(tuple(full), a.dtype)

    own_rows, model = tokens.shape
    seq = 2 * own_rows
    experts = chosen.shape[0]
    wide, narrow_ = arrays[0].shape[1], arrays[1].shape[1]
    heads = wide // cosine.shape[1]
    gathered = [whole(a, axis) for a, axis in zip(arrays, axes)]
    vmem = pl.BlockSpec(memory_space=pltpu.VMEM)
    dma = pltpu.SemaphoreType.DMA
    return pl.pallas_call(
        functools.partial(front_kernel, n_planes, axes),
        out_shape=gathered
        + [
            shape((2 * n_dp,) + grads.shape, bf16),
            shape((tile.shape[0], tile.shape[1] * n_dp), bf16),
            shape((seq, model), bf16),
            shape((seq, wide), bf16),
            shape((seq, narrow_), bf16),
            shape((seq, narrow_), bf16),
            shape((heads, seq, seq), f32),
            shape((seq, wide), bf16),
            shape((own_rows, model), f32),
            shape((own_rows, model), bf16),
            shape((experts, own_rows), f32),
        ],
        in_specs=[ANY] * (n + 3) + [vmem] * 4,
        out_specs=[ANY] * (n + 1) + [vmem] + [ANY] * 6 + [vmem] * 3,
        scratch_shapes=[pltpu.VMEM(g.shape, bf16) for g in gathered]
        + [
            pltpu.VMEM((2, own_rows, model), bf16),
            pltpu.VMEM((2,) + tile.shape, bf16),
            pltpu.VMEM((own_rows, model), bf16),
            pltpu.VMEM((own_rows, model), bf16),
        ]
        + [dma((14 * n_planes, n))] * 2
        + [dma((14 * n_planes, 1))] * 4
        + [dma((n + 3,)), dma((3,)), dma((3,))]
        + [
            pltpu.VMEM((seq, model), bf16),
            pltpu.VMEM((seq, wide), bf16),
            pltpu.VMEM((seq, narrow_), bf16),
            pltpu.VMEM((seq, narrow_), bf16),
            pltpu.VMEM((heads, seq, seq), f32),
            pltpu.VMEM((seq, wide), bf16),
            dma((n + 6,)),
        ],
        compiler_params=pltpu.CompilerParams(
            collective_id=collective_id, has_side_effects=True, vmem_limit_bytes=56 << 20
        ),
        cost_estimate=pl.CostEstimate(
            flops=6 * seq * model * wide, bytes_accessed=16 * n_dp * own_rows * model, transcendentals=heads * seq * seq
        ),
    )(*arrays, tokens, tile, grads, chosen, cosine, sine, allowed)


(T_YX, T_Y, T_X, T_OWN, R_XHALF, R_YHALF, R_YALL, R_XALL, R_UP, R_DOWN, R_DUP, R_DDOWN) = range(12)


def add_up(target, sources):
    rows = target.shape[0]
    step = 16 if rows % 16 == 0 else rows

    def body(i, carry):
        span = pl.ds(pl.multiple_of(i * step, step), step)
        total = sources[0][span, :].astype(jnp.float32)
        for source in sources[1:]:
            total = total + source[span, :].astype(jnp.float32)
        target[span, :] = total.astype(target.dtype)
        return carry

    lax.fori_loop(0, rows // step, body, 0)


class Reduce:
    @staticmethod
    def scratch(shapes, dtypes, n_planes, use_x, cut=0, direct=False, by_z=False):
        kinds = 4 if use_x else 2
        out = []
        for i, (shape, dtype) in enumerate(zip(shapes, dtypes)):
            rows = cut if i == 0 else shape[0]
            out.append(pltpu.VMEM((kinds, n_planes) + shape, dtype))
            out.append(pltpu.VMEM((n_planes + 1,) + shape, dtype))
            out.append(pltpu.VMEM((n_planes,) + shape, dtype))
            if not direct:
                out.append(pltpu.VMEM((kinds, 2) + shape, dtype))
            if use_x:
                out.append(pltpu.VMEM((n_planes,) + shape, dtype))
                out.append(pltpu.VMEM((1 if by_z else n_planes, rows) + shape[1:], dtype))
                if by_z:
                    out.append(pltpu.VMEM((n_planes + 1,) + shape, dtype))
                if i == 0 and cut < shape[0]:
                    out.append(pltpu.VMEM((1 if by_z else n_planes, shape[0] - cut) + shape[1:], dtype))
        n = len(shapes)
        out.append(pltpu.SemaphoreType.DMA((12 * n_planes, n)))
        out.append(pltpu.SemaphoreType.DMA((12 * n_planes, n)))
        out.append(pltpu.SemaphoreType.DMA((kinds * n_planes, n)))
        return out

    def __init__(self, spot, blocks, outs, scratch, use_x, cut=0, direct=False, by_z=False):
        self.spot, self.outs, self.use_x, self.direct, self.by_z = spot, outs, use_x, direct, by_z
        self.slant = []
        self.n, self.n_planes, self.cut = len(outs), spot.n_planes, cut
        left = list(scratch)
        self.twin, self.line, self.near, self.ring, self.across, self.first = [], [], [], [], [], []
        self.second = None
        for i in range(self.n):
            self.twin.append(left.pop(0))
            self.line.append(left.pop(0))
            self.near.append(left.pop(0))
            if not direct:
                self.ring.append(left.pop(0))
            if use_x:
                self.across.append(left.pop(0))
                self.first.append(left.pop(0))
                if by_z:
                    self.slant.append(left.pop(0))
                if i == 0 and cut < self.near[0].shape[1]:
                    self.second = left.pop(0)
        send, recv, self.local = left
        self.copies = Copies(self.n_planes, send, recv)
        y, x, core = spot.y, spot.x, spot.core
        self.order = spot.far_first()
        places = {T_YX: (1 - y, 1 - x), T_Y: (1 - y, x), T_X: (y, 1 - x), T_OWN: (y, x)}
        self.kinds = [T_YX, T_Y, T_X, T_OWN] if use_x else [T_Y, T_OWN]
        every = [(k, j) for j in range(self.n_planes) for k in self.kinds]
        self.terms = {(k, j): blocks(self.order[j], places[k][0], core, places[k][1]) for k, j in every}
        self.others = {(k, j): blocks(self.order[j], places[k][0], 1 - core, places[k][1]) for k, j in every}

    def load(self, kind, j):
        k, s = self.kinds.index(kind), self.order[j]
        return [
            pltpu.make_async_copy(ref, self.ring[i].at[k, j % 2], self.local.at[k * self.n_planes + s, i])
            for i, ref in enumerate(self.terms[kind, j])
        ]

    def start_load(self, kind, j):
        if not self.direct and j < self.n_planes:
            for c in self.load(kind, j):
                c.start()

    def start_loads(self):
        for j in range(2):
            for kind in self.kinds:
                self.start_load(kind, j)

    def start_twins(self):
        for j in range(self.n_planes):
            s = self.order[j]
            for k, kind in enumerate(self.kinds):
                self.copies.start(None, kind, s, self.others[kind, j], [t.at[k, s] for t in self.twin], self.spot.twin)

    def ready(self, kind, j):
        k, s = self.kinds.index(kind), self.order[j]
        twin = [t.at[k, s] for t in self.twin]
        self.copies.arrive(kind, s, twin, self.spot.twin)
        if self.direct:
            return twin, self.terms[kind, j]
        for c in self.load(kind, j):
            c.wait()
        return twin, [r.at[k, j % 2] for r in self.ring]

    def along(self, j, here, line, targets, up, down):
        s, spot, copies = self.order[j], self.spot, self.copies
        some = [t.at[s] for t in line]
        below = [t.at[self.n_planes] for t in line]

        def add_all(*more):
            for i in range(self.n):
                add_up(targets[i], here[i] + [m[i] for m in more])

        if j == self.n_planes - 1:
            when(spot.has_up, lambda: copies.arrive(down, s, some, spot.up))
            when(spot.has_down, lambda: copies.arrive(up, s, below, spot.down))
            when(spot.has_up & spot.has_down, lambda: add_all(some, below))
            when(spot.z == 0, lambda: add_all(some))
            when(spot.z == self.n_planes - 1, lambda: add_all(below))
            return
        for goes, more, group, last, device, source in (
            (s < spot.z, spot.has_up, down, None, spot.down, spot.up),
            (s > spot.z, spot.has_down, up, s - spot.z == 1, spot.up, spot.down),
        ):

            def partial():
                copies.arrive(group, s, some, source)
                add_all(some)

            when(goes & more, partial)
            when(goes & jnp.logical_not(more), add_all)
            if last is None:
                copies.start(goes, group, s, targets, some, device)
            else:
                copies.start(goes & last, group, s, targets, below, device)
                copies.start(goes & jnp.logical_not(last), group, s, targets, some, device)

    def corner(self, j):
        if not self.use_x or not 0 <= j < self.n_planes:
            return
        s, cut = self.order[j], self.cut
        twin, mine = self.ready(T_YX, j)
        if self.by_z:
            self.along(j, [[m, t] for m, t in zip(mine, twin)], self.slant, twin, R_DUP, R_DDOWN)
        else:
            for m, t in zip(mine, twin):
                add_up(t, [m, t])
        self.start_load(T_YX, j + 2)
        if self.by_z and j < self.n_planes - 1:
            return
        p = 0 if self.by_z else s
        head = twin if self.second is None else [twin[0].at[pl.ds(0, cut)]] + twin[1:]
        self.copies.start(None, R_XHALF, s, head, [f.at[p] for f in self.first], self.spot.across)
        if self.second is not None:
            tail = [twin[0].at[pl.ds(cut, self.second.shape[1])]]
            self.copies.start(None, R_YHALF, s, tail, [self.second.at[p]], self.spot.side)

    def side(self, j):
        s, cut = self.order[j], self.cut
        twin, mine = self.ready(T_Y, j)
        over = self.use_x and (j == self.n_planes - 1 or not self.by_z)
        p = 0 if self.by_z else s
        if over:
            first = [f.at[p] for f in self.first]
            self.copies.arrive(R_XHALF, s, first, self.spot.across)
        for i, (m, t) in enumerate(zip(mine, twin)):
            if not over:
                add_up(t, [m, t])
            elif i == 0 and self.second is not None:
                a, b = pl.ds(0, cut), pl.ds(cut, self.second.shape[1])
                add_up(t.at[a], [m.at[a], t.at[a], first[0]])
                add_up(t.at[b], [m.at[b], t.at[b]])
            else:
                add_up(t, [m, t, first[i]])
        self.start_load(T_Y, j + 2)
        self.copies.start(None, R_YALL, s, twin, [t.at[s] for t in self.near], self.spot.side)

    def over(self, j):
        s, cut = self.order[j], self.cut
        twin, mine = self.ready(T_X, j)
        over = self.second is not None and (j == self.n_planes - 1 or not self.by_z)
        p = 0 if self.by_z else s
        if over:
            self.copies.arrive(R_YHALF, s, [self.second.at[p]], self.spot.side)
        for i, (m, t) in enumerate(zip(mine, twin)):
            if i == 0 and over:
                a, b = pl.ds(0, cut), pl.ds(cut, self.second.shape[1])
                add_up(t.at[a], [m.at[a], t.at[a]])
                add_up(t.at[b], [m.at[b], t.at[b], self.second.at[p]])
            else:
                add_up(t, [m, t])
        self.start_load(T_X, j + 2)
        self.copies.start(None, R_XALL, s, twin, [t.at[s] for t in self.across], self.spot.across)

    def sides(self, j):
        if 0 <= j < self.n_planes:
            self.side(j)
            if self.use_x:
                self.over(j)

    def column(self, j):
        if not 0 <= j < self.n_planes:
            return
        s, spot, copies = self.order[j], self.spot, self.copies
        twin, mine = self.ready(T_OWN, j)
        near = [t.at[s] for t in self.near]
        copies.arrive(R_YALL, s, near, spot.side)
        here = [[m, t, a] for m, t, a in zip(mine, twin, near)]
        if self.use_x:
            across = [t.at[s] for t in self.across]
            copies.arrive(R_XALL, s, across, spot.across)
            here = [h + [a] for h, a in zip(here, across)]
        self.along(j, here, self.line, self.outs if j == self.n_planes - 1 else twin, R_UP, R_DOWN)
        self.start_load(T_OWN, j + 2)

    def stage(self, step):
        self.corner(step)
        self.sides(step - 1)
        self.column(step - 2)

    def close(self):
        self.copies.close()


class WeightGradients:
    width = 256

    def __init__(self, ins, outs, scratch):
        self.sources, (self.hidden, self.shared) = ins[:4], ins[4:]
        self.outs = outs
        self.buffers, self.small_hidden, self.small_shared = scratch[:4], scratch[4], scratch[5]
        self.flat, self.sums, self.load, self.store, self.once = scratch[6:]
        self.n_parts = self.sources[0].shape[1] // self.width

    @staticmethod
    def scratch(rows, tokens, width, shared):
        bf16, f32 = jnp.bfloat16, jnp.float32
        w = WeightGradients.width
        return [
            pltpu.VMEM((2, rows, w), bf16),
            pltpu.VMEM((2, rows, w), bf16),
            pltpu.VMEM((2, tokens, w), bf16),
            pltpu.VMEM((2, tokens, w), bf16),
            pltpu.VMEM((3, rows, width), bf16),
            pltpu.VMEM((tokens, shared), bf16),
            pltpu.VMEM((2, 3, width, w), f32),
            pltpu.VMEM((2, shared, w), bf16),
            pltpu.SemaphoreType.DMA((2, 4)),
            pltpu.SemaphoreType.DMA((2, 4)),
            pltpu.SemaphoreType.DMA((2,)),
        ]

    def span(self, p):
        return pl.ds(p * self.width, self.width)

    def loads(self, p):
        return [
            pltpu.make_async_copy(a.at[:, self.span(p)], b.at[p % 2], self.load.at[p % 2, i])
            for i, (a, b) in enumerate(zip(self.sources, self.buffers))
        ]

    def stores(self, p):
        gate_t, up_t, down, shared = self.outs
        slot, span = p % 2, self.span(p)
        pairs = [
            (self.flat.at[slot, 0], gate_t.at[:, span]),
            (self.flat.at[slot, 1], up_t.at[:, span]),
            (self.flat.at[slot, 2], down.at[:, span]),
            (self.sums.at[slot], shared.at[:, span]),
        ]
        return [pltpu.make_async_copy(a, b, self.store.at[slot, i]) for i, (a, b) in enumerate(pairs)]

    def resident(self):
        return [
            pltpu.make_async_copy(self.hidden, self.small_hidden, self.once.at[0]),
            pltpu.make_async_copy(self.shared, self.small_shared, self.once.at[1]),
        ]

    def begin(self):
        for c in self.resident() + self.loads(0):
            c.start()

    def part(self, p):
        if p >= self.n_parts:
            return
        if p == 0:
            for c in self.resident():
                c.wait()
        if p + 1 < self.n_parts:
            for c in self.loads(p + 1):
                c.start()
        for c in self.loads(p):
            c.wait()
        if p >= 2:
            for c in self.stores(p - 2):
                c.wait()
        slot = p % 2
        rows, grad_rows, tokens, grads = [b.at[slot] for b in self.buffers]

        def across(a, b):
            return lax.dot_general(a, b, (((0,), (0,)), ((), ())), preferred_element_type=jnp.float32)

        self.flat[slot, 0] = across(self.small_hidden[1], rows[...])
        self.flat[slot, 1] = across(self.small_hidden[2], rows[...])
        self.flat[slot, 2] = across(self.small_hidden[0], grad_rows[...])
        n = self.small_shared.shape[1] // 3
        self.sums[slot, pl.ds(0, 2 * n)] = across(self.small_shared[:, n:], tokens[...]).astype(jnp.bfloat16)
        self.sums[slot, pl.ds(2 * n, n)] = across(self.small_shared[:, :n], grads[...]).astype(jnp.bfloat16)
        for c in self.stores(p):
            c.start()

    def end(self):
        for p in (self.n_parts - 2, self.n_parts - 1):
            for c in self.stores(p):
                c.wait()


def sum_kernel(n_planes, n, *refs):
    ins, work_ins, outs, work_outs = refs[:n], refs[n : n + 6], refs[n + 6 : 2 * n + 6], refs[2 * n + 6 : 2 * n + 10]
    scratch = refs[2 * n + 10 :]
    cut = len(scratch) - 11
    spot = Spot(n_planes)
    rows = ins[0].shape[1] // 2

    def blocks(s, yy, cc, xx):
        return [a.at[dp_of(s, yy, cc) * 2 + xx] for a in ins]

    net = Reduce(spot, blocks, outs, scratch[:cut], True, rows)
    work = WeightGradients(work_ins, work_outs, scratch[cut:])
    net.start_loads()
    spot.greet()
    net.start_twins()
    work.begin()
    done = 0
    for step in range(n_planes + 2):
        for action in (net.corner, net.sides, net.column):
            j = step - (net.corner, net.sides, net.column).index(action)
            action(j)
            if 0 <= j < n_planes and done < work.n_parts:
                work.part(done)
                done += 1
    net.close()
    work.end()


def sum_everywhere(arrays, out_dtypes, work_arrays, n_dp, collective_id):
    n, n_planes = len(arrays), n_dp // 4
    shapes = [a.shape[1:] for a in arrays]
    rows, model = work_arrays[0].shape
    tokens = work_arrays[2].shape[0]
    width = work_arrays[4].shape[2]
    shared = work_arrays[5].shape[1]
    return pl.pallas_call(
        functools.partial(sum_kernel, n_planes, n),
        out_shape=[jax.ShapeDtypeStruct(s, t) for s, t in zip(shapes, out_dtypes)]
        + [
            jax.ShapeDtypeStruct((width, model), jnp.float32),
            jax.ShapeDtypeStruct((width, model), jnp.float32),
            jax.ShapeDtypeStruct((width, model), jnp.float32),
            jax.ShapeDtypeStruct((shared, model), jnp.bfloat16),
        ],
        in_specs=[ANY] * (n + 6),
        out_specs=[pl.BlockSpec(memory_space=pltpu.VMEM)] * n + [ANY] * 4,
        scratch_shapes=Reduce.scratch(shapes, [a.dtype for a in arrays], n_planes, True, shapes[0][0] // 2)
        + WeightGradients.scratch(rows, tokens, width, shared),
        compiler_params=pltpu.CompilerParams(
            collective_id=collective_id, has_side_effects=True, vmem_limit_bytes=62 << 20
        ),
    )(*arrays, *work_arrays)


def back_kernel(n_planes, axes, *refs):
    n = len(axes)
    grad_own, *inputs = refs[:18]
    probs, wq, wk, wv, wo, parts = inputs[5], *inputs[6:10], inputs[16]
    inputs = inputs[:5] + inputs[10:16]
    held = refs[-len(inputs) - 1 : -1]
    mixed, normed_one, query, key, value, cosine, sine, tokens, grad_residual, gain, small = held
    held_load = refs[-1]
    outs, grad_tokens, small_out, out_sum = refs[18 : 18 + n], *refs[18 + n : 21 + n]
    (
        grad_attn, grad_mixed, grad_query, grad_key, grad_value, gq, gk, gv, go, some_p, some_o, some_q, some_k,
        some_v, sent, received, terms, small_sum, small_in, load, x_send, x_recv,
    ) = refs[21 + n : 43 + n]
    scratch = refs[43 + n : -len(inputs) - 1]
    spot = Spot(n_planes)
    x = spot.x
    bf16, f32 = jnp.bfloat16, jnp.float32
    own_rows, model = tokens.shape
    grads = (gq, gk, gv, go)

    def weight_blocks(s, yy, cc, xx):
        i = dp_of(s, yy, cc)
        places = []
        for a, o, axis in zip(grads, outs, axes):
            size = o.shape[axis]
            span = pl.ds(pl.multiple_of(i * size, size), size)
            places.append(a.at[span] if axis == 0 else a.at[:, span])
        return places

    def small_blocks(s, yy, cc, xx):
        size = small_sum.shape[1]
        return [terms.at[:, pl.ds(pl.multiple_of(dp_of(s, yy, cc) * size, size), size)]]

    def token_blocks(s, yy, cc, xx):
        return [parts.at[dp_of(s, yy, cc) * 2 + xx]]

    count = 3 * n + 3
    weights = Reduce(spot, weight_blocks, outs, scratch[:count], False, direct=True)
    params = Reduce(spot, small_blocks, [small_sum], scratch[count : count + 6], False, direct=True)
    sums = Reduce(spot, token_blocks, [out_sum], scratch[count + 6 :], True, own_rows // 2, by_z=True)

    def swap(i, src, dst):
        return pltpu.make_async_remote_copy(
            src_ref=src, dst_ref=dst, send_sem=x_send.at[i], recv_sem=x_recv.at[i],
            device_id=spot.across, device_id_type=MESH,
        )

    own = pltpu.make_async_copy(grad_own, grad_attn.at[x], load.at[4, 0])
    own.start()
    sums.start_loads()
    spot.greet()
    swap(0, grad_own, grad_attn.at[x]).start()
    sums.start_twins()
    fetched = [pltpu.make_async_copy(a, b, held_load.at[i]) for i, (a, b) in enumerate(zip(inputs, held))]
    for c in fetched:
        c.start()

    heads, head_dim = probs.shape[0], cosine.shape[1]
    kv_heads = key.shape[1] // head_dim
    group = heads // kv_heads
    chunk = some_o.shape[1]
    n_chunks = wo.shape[0] // chunk
    per_chunk = chunk // head_dim

    def load_o(c):
        return pltpu.make_async_copy(wo.at[pl.ds(c * chunk, chunk)], some_o.at[c % 2], load.at[0, c % 2])

    def load_p(h):
        return pltpu.make_async_copy(probs.at[h], some_p.at[h % 2], load.at[1, h % 2])

    load_o(0).start()
    load_p(0).start()
    sums.corner(0)
    for j in range(n_planes - 1):
        sums.sides(j)
    for c in fetched:
        c.wait()
    terms[...] = small[...]
    own.wait()
    swap(0, grad_attn.at[1 - x], grad_attn.at[1 - x]).wait_recv()
    whole = grad_attn[...].reshape(2 * own_rows, model)
    sums.corner(1)
    cos, sin = cosine[...], -sine[...]
    scale = head_dim ** -0.5
    for c in range(n_chunks):
        if c + 1 < n_chunks:
            load_o(c + 1).start()
        load_o(c).wait()
        span = slice(c * chunk, (c + 1) * chunk)
        grad_mixed[:, span] = plain_dot(whole, some_o[c % 2], ROWS_ROWS).astype(bf16)
        go[span, :] = plain_dot(mixed[:, span], whole, COLUMNS_COLUMNS).astype(bf16)
    sums.corner(2)
    for h in range(heads):
        if h + 1 < heads:
            load_p(h + 1).start()
        load_p(h).wait()
        span = slice(h * head_dim, (h + 1) * head_dim)
        shared = slice(h // group * head_dim, (h // group + 1) * head_dim)
        weight, back = some_p[h % 2], grad_mixed[:, span]
        grad_v = plain_dot(weight.astype(bf16), back, COLUMNS_COLUMNS)
        grad_p = plain_dot(back, value[:, shared], ROWS_ROWS)
        inner = jnp.sum(weight * grad_p, axis=1, keepdims=True)
        grad_s = (weight * (grad_p - inner)).astype(bf16)
        grad_q = plain_dot(grad_s, key[:, shared], ROWS_COLUMNS) * scale
        grad_query[:, span] = turn(grad_q, cos, sin).astype(bf16)
        grad_k = plain_dot(grad_s, query[:, span], COLUMNS_COLUMNS) * scale
        if h % group == 0:
            total_k, total_v = grad_k, grad_v
        else:
            total_k, total_v = total_k + grad_k, total_v + grad_v
        if h % group == group - 1:
            grad_key[:, shared] = turn(total_k, cos, sin).astype(bf16)
            grad_value[:, shared] = total_v.astype(bf16)
    sums.corner(3)
    for target, source in ((gk, grad_key), (gv, grad_value), (gq, grad_query)):
        target[...] = plain_dot(normed_one[...], source[...], COLUMNS_COLUMNS).astype(bf16)
    weights.start_twins()

    rows = some_q.shape[1]
    n_chunks = model // rows

    def load_w(c):
        span = pl.ds(c * rows, rows)
        return [
            pltpu.make_async_copy(w.at[span], b.at[c % 2], load.at[i, c % 2])
            for i, (w, b) in ((0, (wq, some_q)), (2, (wk, some_k)), (3, (wv, some_v)))
        ]

    for c in load_w(0):
        c.start()
    sums.column(0)
    sums.sides(3)
    weights.sides(0)
    other = pl.ds(pl.multiple_of((1 - x) * own_rows, own_rows), own_rows)
    mine = pl.ds(pl.multiple_of(x * own_rows, own_rows), own_rows)
    for c in range(n_chunks):
        if c + 1 < n_chunks:
            for each in load_w(c + 1):
                each.start()
        for each in load_w(c):
            each.wait()
        columns = slice(c * rows, (c + 1) * rows)
        for here, target in ((other, sent), (mine, grad_tokens)):
            total = plain_dot(grad_query[here, :], some_q[c % 2], ROWS_ROWS)
            total = total + plain_dot(grad_key[here, :], some_k[c % 2], ROWS_ROWS)
            total = total + plain_dot(grad_value[here, :], some_v[c % 2], ROWS_ROWS)
            target[:, columns] = total.astype(target.dtype)
    swap(1, sent, received).start()
    sums.column(1)
    weights.sides(1)
    sums.column(2)
    swap(1, received, received).wait_recv()
    step = 32
    gain_row = gain[...].astype(f32)
    total = jnp.zeros((1, model), f32)
    for r in range(own_rows // step):
        span = pl.ds(r * step, step)
        rows_in = tokens[span, :].astype(f32)
        grad = grad_tokens[span, :] + received[span, :].astype(f32)
        size = lax.rsqrt(jnp.mean(rows_in * rows_in, axis=1, keepdims=True) + norm_eps)
        weighted = grad * gain_row
        inner = jnp.mean(rows_in * weighted, axis=1, keepdims=True)
        total = total + jnp.sum(grad * rows_in * size, axis=0, keepdims=True)
        grad_tokens[span, :] = size * weighted - rows_in * (size * size * size) * inner + grad_residual[span, :]
    place = small.shape[0] - 8
    terms[pl.ds(place, 1), :] = total
    params.start_twins()
    weights.column(0)
    weights.sides(2)
    params.sides(0)
    weights.column(1)
    weights.sides(3)
    sums.column(3)
    for j in range(1, n_planes):
        params.sides(j)
        params.column(j - 1)
    weights.column(2)
    params.column(n_planes - 1)
    weights.column(3)
    swap(2, small_sum, small_in).start()
    swap(2, small_sum, small_in).wait()
    small_out[...] = small_sum[...] + small_in[...]
    swap(0, grad_own, grad_attn.at[x]).wait_send()
    swap(1, sent, received).wait_send()
    for each in (weights, params, sums):
        each.close()


def backward(
    grad_own, mixed, normed_one, query, key, value, probs, weights, axes, cosine, sine, tokens, grad_residual, gain,
    small, parts, n_dp, collective_id,
):
    n, n_planes = len(weights), n_dp // 4
    bf16, f32 = jnp.bfloat16, jnp.float32
    shape, vmem_ref = jax.ShapeDtypeStruct, pltpu.VMEM
    own_rows, model = tokens.shape
    seq = 2 * own_rows
    wide, narrow_ = query.shape[1], key.shape[1]

    def part(a, axis):
        some = list(a.shape)
        some[axis] //= n_dp
        return tuple(some)

    shapes = [part(a, axis) for a, axis in zip(weights, axes)]
    tile = (small.shape[0], model // n_dp)
    block = parts.shape[1:]
    vmem = pl.BlockSpec(memory_space=pltpu.VMEM)
    dma = pltpu.SemaphoreType.DMA
    chunk = 256
    return pl.pallas_call(
        functools.partial(back_kernel, n_planes, axes),
        out_shape=[shape(s, f32) for s in shapes] + [shape((own_rows, model), f32), shape(tile, f32), shape(block, f32)],
        in_specs=[ANY] * 18,
        out_specs=[vmem] * (n + 3),
        scratch_shapes=[
            vmem_ref((2, own_rows, model), bf16),
            vmem_ref((seq, wide), bf16),
            vmem_ref((seq, wide), bf16),
            vmem_ref((seq, narrow_), bf16),
            vmem_ref((seq, narrow_), bf16),
        ]
        + [vmem_ref(w.shape, bf16) for w in weights]
        + [
            vmem_ref((2,) + probs.shape[1:], f32),
            vmem_ref((2, chunk, model), bf16),
            vmem_ref((2, chunk, wide), bf16),
            vmem_ref((2, chunk, narrow_), bf16),
            vmem_ref((2, chunk, narrow_), bf16),
            vmem_ref((own_rows, model), bf16),
            vmem_ref((own_rows, model), bf16),
            vmem_ref(small.shape, f32),
            vmem_ref(tile, f32),
            vmem_ref(tile, f32),
            dma((5, 2)),
            dma((3,)),
            dma((3,)),
        ]
        + Reduce.scratch(shapes, [bf16] * n, n_planes, False, direct=True)
        + Reduce.scratch([tile], [f32], n_planes, False, direct=True)
        + Reduce.scratch([block], [parts.dtype], n_planes, True, block[0] // 2, by_z=True)
        + [
            vmem_ref(a.shape, a.dtype)
            for a in (mixed, normed_one, query, key, value, cosine, sine, tokens, grad_residual, gain, small)
        ]
        + [dma((11,))],
        compiler_params=pltpu.CompilerParams(
            collective_id=collective_id, has_side_effects=True, vmem_limit_bytes=63 << 20
        ),
        cost_estimate=pl.CostEstimate(
            flops=12 * seq * model * wide, bytes_accessed=16 * n_dp * own_rows * model, transcendentals=0
        ),
    )(
        grad_own, mixed, normed_one, query, key, value, probs, *weights, cosine, sine, tokens, grad_residual, gain,
        small, parts,
    )
UNIT = 2


def dot_t(a, b):
    return lax.dot_general(a, b, (((1,), (1,)), ((), ())), preferred_element_type=jnp.float32)


def dot_f32(a, b):
    return lax.dot_general(a, b, (((1,), (0,)), ((), ())), preferred_element_type=jnp.float32)


class ExpertWork:
    def __init__(self, expert, weights, scratch):
        self.expert = expert
        self.w_gate, self.w_up, self.w_down, self.shared = weights
        (
            self.tokens, self.grads, self.rows, self.grad_rows, self.hidden, self.pre, self.left_out,
            self.left_grad, self.right_out, self.right_grad, self.out, self.back, self.shared_hidden,
        ) = scratch

    @staticmethod
    def scratch(model, width, capacity, own_rows):
        bf16 = jnp.bfloat16
        seq = 2 * own_rows
        return [
            pltpu.VMEM((2, 2 * UNIT, own_rows, model), bf16),
            pltpu.VMEM((2, 2 * UNIT, own_rows, model), bf16),
            pltpu.VMEM((2, UNIT * capacity, model), bf16),
            pltpu.VMEM((2, UNIT * capacity, model), bf16),
            pltpu.VMEM((2, 3, UNIT * capacity, width), bf16),
            pltpu.VMEM((3, UNIT * capacity, width), jnp.float32),
            pltpu.VMEM((UNIT, seq, capacity + 128), bf16),
            pltpu.VMEM((UNIT, seq, capacity + 256), bf16),
            pltpu.VMEM((UNIT, capacity + 128, model), bf16),
            pltpu.VMEM((UNIT, capacity + 256, model), bf16),
            pltpu.VMEM((2, 2 * UNIT, own_rows, model), bf16),
            pltpu.VMEM((2, 2 * UNIT, own_rows, model), bf16),
            pltpu.VMEM((2, UNIT * seq, 384), bf16),
        ]

    def prepare(self):
        capacity = self.rows.shape[1] // UNIT
        for q in range(UNIT):
            self.right_out[q, pl.ds(capacity, 128), :] = self.shared[pl.ds(256, 128), :]
            self.right_grad[q, pl.ds(capacity, 256), :] = self.shared[pl.ds(0, 256), :]

    def run(self, slot, unit, gates, grad_gates, hook):
        bf16, f32 = jnp.bfloat16, jnp.float32
        own_rows, model = self.tokens.shape[2:]
        seq = 2 * own_rows
        capacity = self.rows.shape[1] // UNIT
        experts = gates.shape[1]
        column = 1024
        n_columns = model // column
        first = unit * (2 * UNIT)
        before = lax.broadcasted_iota(jnp.int32, (seq, seq), 0) <= lax.broadcasted_iota(jnp.int32, (seq, seq), 1)
        before = before.astype(f32).astype(bf16)
        slots = lax.broadcasted_iota(jnp.int32, (capacity, seq), 0)
        picks, row_gates = [], []
        for q in range(UNIT):
            g = jnp.concatenate(
                [gates[first + 2 * q + h, pl.ds(self.expert, 1), :] for h in range(2)], axis=1
            )
            g = jnp.broadcast_to(g, (8, seq))
            taken = (g > 0.0).astype(f32)
            rank = dot_f32(taken.astype(bf16), before).astype(jnp.int32) - 1
            hit = (slots == rank[:1]) & (g[:1] > 0.0)
            pick = hit.astype(f32)
            picks.append(pick)
            row_gates.append(jnp.sum(pick * g[:1], axis=1, keepdims=True))
            self.left_out[q, :, pl.ds(0, capacity)] = pick.T.astype(bf16)
            self.left_grad[q, :, pl.ds(0, capacity)] = pick.T.astype(bf16)
            low = pick.astype(bf16)

            span = pl.ds(q * capacity, capacity)
            for source, target in ((self.tokens, self.rows), (self.grads, self.grad_rows)):
                whole = source[slot, pl.ds(2 * q, 2)].reshape(seq, model)
                target[slot, span] = dot_f32(low, whole).astype(bf16)
        row_gate = jnp.concatenate(row_gates, axis=0)
        rows, grad_rows = self.rows.at[slot], self.grad_rows.at[slot]
        self.pre[0] = dot_t(rows[...], self.w_gate[...])
        self.pre[1] = dot_t(rows[...], self.w_up[...])
        self.pre[2] = dot_t(grad_rows[...], self.w_down[...])
        hook(2)
        step = 32
        parts = []
        for r in range(UNIT * capacity // step):
            span = pl.ds(r * step, step)
            gate_pre, up_pre, grad_hidden = self.pre[0, span], self.pre[1, span], self.pre[2, span]
            gate = row_gate[r * step : (r + 1) * step]
            sig = jax.nn.sigmoid(gate_pre)
            act = gate_pre * sig
            hidden = act * up_pre
            parts.append(jnp.sum(hidden * grad_hidden, axis=1, keepdims=True))
            grad_hidden = grad_hidden * gate
            self.hidden[slot, 0, span] = (hidden * gate).astype(bf16)
            slope = sig * (1.0 + gate_pre * (1.0 - sig))
            self.hidden[slot, 1, span] = (grad_hidden * up_pre * slope).astype(bf16)
            self.hidden[slot, 2, span] = (grad_hidden * act).astype(bf16)
        grad_gate_rows = jnp.concatenate(parts, axis=0)
        mine = lax.broadcasted_iota(jnp.int32, (experts, own_rows), 0) == self.expert
        for q in range(UNIT):
            per_token = jnp.sum(picks[q] * grad_gate_rows[q * capacity : (q + 1) * capacity], axis=0, keepdims=True)
            for h in range(2):
                part = jnp.broadcast_to(per_token[:, h * own_rows : (h + 1) * own_rows], (experts, own_rows))
                grad_gates[first + 2 * q + h] = jnp.where(mine, part, 0.0)

        for q in range(UNIT):
            blocks = pl.ds(2 * q, 2)
            whole = self.tokens[slot, blocks].reshape(seq, model)
            grad = self.grads[slot, blocks].reshape(seq, model)
            pre = dot_t(whole, self.shared[pl.ds(0, 256), :])
            grad_hidden = dot_t(grad, self.shared[pl.ds(256, 128), :])
            gate_pre, up_pre = pre[:, :128], pre[:, 128:]
            sig = jax.nn.sigmoid(gate_pre)
            act = gate_pre * sig
            hidden = (act * up_pre).astype(bf16)
            grad_gate = (grad_hidden * up_pre * sig * (1.0 + gate_pre * (1.0 - sig))).astype(bf16)
            grad_up = (grad_hidden * act).astype(bf16)
            span = pl.ds(q * seq, seq)
            self.shared_hidden[slot, span, pl.ds(0, 128)] = hidden
            self.shared_hidden[slot, span, pl.ds(128, 128)] = grad_gate
            self.shared_hidden[slot, span, pl.ds(256, 128)] = grad_up
            self.left_out[q, :, pl.ds(capacity, 128)] = hidden
            self.left_grad[q, :, pl.ds(capacity, 128)] = grad_gate
            self.left_grad[q, :, pl.ds(capacity + 128, 128)] = grad_up

        hook(3)

        def combine(c, carry):
            cols = pl.ds(pl.multiple_of(c * column, column), column)
            made = dot_f32(self.hidden[slot, 0], self.w_down[:, cols]).astype(bf16)
            back = dot_f32(self.hidden[slot, 1], self.w_gate[:, cols])
            back = (back + dot_f32(self.hidden[slot, 2], self.w_up[:, cols])).astype(bf16)
            for q in range(UNIT):
                span = slice(q * capacity, (q + 1) * capacity)
                self.right_out[q, pl.ds(0, capacity), cols] = made[span]
                self.right_grad[q, pl.ds(0, capacity), cols] = back[span]
                out = dot_f32(self.left_out[q], self.right_out[q, :, cols]).astype(bf16)
                self.out[slot, pl.ds(2 * q, 2), :, cols] = out.reshape(2, own_rows, column)
                out = dot_f32(self.left_grad[q], self.right_grad[q, :, cols]).astype(bf16)
                self.back[slot, pl.ds(2 * q, 2), :, cols] = out.reshape(2, own_rows, column)

            return carry

        lax.fori_loop(0, n_columns, combine, 0)


def expert_kernel(n_dp, *refs):
    own, own_gates, _, *weights_in = refs[:7]
    normed, grads, out_parts, back_parts, grad_gates, rows_out, grad_rows_out, hidden_out, shared_out = refs[7:16]
    scratch, weights = refs[16:-13], refs[-13:-9]
    fetch, gates, load, store, local, send, recv, g_send, g_recv = refs[-9:]
    n_planes = n_dp // 4
    spot = Spot(n_planes)
    half = own.shape[0] // 2

    def views(s, yy, cc, xx, part):
        b = dp_of(s, yy, cc) * 2 + xx
        if part == ALL:
            return [normed.at[b], gates.at[b]]
        if part == FIRST:
            return [normed.at[b, pl.ds(0, half)], gates.at[b]]
        return [normed.at[b, pl.ds(half, half)]]

    def grad_views(s, yy, cc, xx, part):
        b = dp_of(s, yy, cc) * 2 + xx
        if part == ALL:
            return [grads.at[b]]
        return [grads.at[b, pl.ds(0 if part == FIRST else half, half)]]

    kept = [
        pltpu.make_async_copy(a, v, local.at[i])
        for i, (a, v) in enumerate(zip((own, own_gates), views(spot.z, spot.y, spot.core, spot.x, ALL)))
    ]
    for c in kept:
        c.start()
    pieces = 4
    fetched = []
    for k, (a, b) in enumerate(zip(weights_in, weights)):
        size = a.shape[0] // pieces
        for p in range(pieces):
            span = pl.ds(p * size, size)
            fetched.append(pltpu.make_async_copy(a.at[span], b.at[span], fetch.at[k, p]))
    for c in fetched:
        c.start()
    spot.greet()
    copies = Copies(n_planes, send, recv)
    net = Spread(spot, copies, [own, own_gates], views, True, by_z=True)
    rest = Spread(spot, Copies(n_planes, g_send, g_recv), None, grad_views, True)
    net.begin()
    work = ExpertWork(spot.dp, weights, scratch)
    n_units = n_dp // UNIT
    blocks = 2 * UNIT
    rows = work.rows.shape[1]
    seqs = work.shared_hidden.shape[1]
    order = net.order

    def unit_of(i):
        s = 0 * i
        for j, plane in enumerate(order):
            s = s + (i // 2 == j).astype(jnp.int32) * plane
        yy = spot.y + (i % 2) * (1 - 2 * spot.y)
        return s * 2 + yy

    def loads(u, slot):
        span = pl.ds(u * blocks, blocks)
        return [
            pltpu.make_async_copy(normed.at[span], work.tokens.at[slot], load.at[slot, 0]),
            pltpu.make_async_copy(grads.at[span], work.grads.at[slot], load.at[slot, 1]),
        ]

    def stores(u, slot):
        span = pl.ds(u * blocks, blocks)
        some = pl.ds(pl.multiple_of(u * rows, rows), rows)
        pairs = [
            (work.out.at[slot], out_parts.at[span]),
            (work.back.at[slot], back_parts.at[span]),
            (work.rows.at[slot], rows_out.at[some]),
            (work.grad_rows.at[slot], grad_rows_out.at[some]),
            (work.hidden.at[slot], hidden_out.at[:, some]),
            (work.shared_hidden.at[slot], shared_out.at[pl.ds(pl.multiple_of(u * seqs, seqs), seqs)]),
        ]
        return [pltpu.make_async_copy(a, b, store.at[slot, i]) for i, (a, b) in enumerate(pairs)]

    def load_unit(i):
        for c in loads(unit_of(jnp.int32(i)), i % 2):
            c.start()

    def near(j):
        net.twin_near(j)
        if j == n_planes - 1:
            rest.twin_across(j)
        load_unit(2 * j)

    def far(j):
        net.twin_far(j)
        rest.twin_corner(j)
        if j >= n_planes - 2:
            rest.twin_side(j)
        load_unit(2 * j + 1)

    def over(j):
        if j >= n_planes - 2:
            rest.from_side(j)
        if j == n_planes - 1:
            rest.from_across(j)
        rest.over_x(j)
        rest.over_y(j)

    plan = {
        (0, 0): [(net.onward, 1)],
        (0, 2): [(net.corner, 0), (rest.corner, 0), (far, 0), (over, 1)],
        (0, 3): [(net.relay_of, 2, 0), (net.relay_of, 3, 1), (rest.onward_y, 2), (rest.onward_x, 3)],
        (1, 0): [(net.sides, 1), (net.onward, 2)],
        (1, 2): [(near, 1)],
        (1, 3): [(net.corner, 1), (net.corner_of, 2, 1), (rest.corner, 1)],
        (2, 0): [(far, 1), (over, 2), (rest.onward_y, 3)],
        (2, 3): [(net.sides, 2), (net.relay_of, 3, 0), (net.onward, 3), (net.corner_of, 3, 1)],
        (3, 0): [(near, 2)],
        (3, 2): [(net.corner_of, 2, 0), (rest.corner, 2), (over, 3)],
        (4, 0): [(net.sides, 3), (far, 2)],
        (4, 3): [(net.corner_of, 3, 0), (rest.corner, 3)],
        (5, 0): [(near, 3)],
        (6, 0): [(far, 3)],
    }

    net.relay(1)
    net.relay_of(2, 1)
    net.sides(0)
    over(0)
    for c in kept:
        c.wait()
    near(0)
    for c in fetched:
        c.wait()
    work.prepare()

    def body(i, carry):
        slot = i % 2
        u = unit_of(i)

        def hook(point):
            for (k, at), actions in plan.items():
                if at == point:

                    @pl.when(i == k)
                    def _(actions=actions):
                        for action, *values in actions:
                            action(*values)

        hook(0)

        for c in loads(u, slot):
            c.wait()

        @pl.when(i >= 2)
        def _():
            for c in stores(unit_of(i - 2), slot):
                c.wait()

        work.run(slot, u, gates, grad_gates, hook)
        for c in stores(u, slot):
            c.start()
        return carry

    lax.fori_loop(0, n_units, body, 0)
    for i in (n_units - 2, n_units - 1):
        for c in stores(unit_of(jnp.int32(i)), i % 2):
            c.wait()
    copies.close()
    rest.copies.close()


def expert_call(own, own_gates, grads, w_gate, w_up, w_down, shared, n_dp, capacity, collective_id):
    own_rows, model = own.shape
    blocks = 2 * n_dp
    width = w_down.shape[0]
    bf16 = jnp.bfloat16
    rows = n_dp * capacity
    n_planes = n_dp // 4
    vmem = pl.BlockSpec(memory_space=pltpu.VMEM)
    everyone = jax.ShapeDtypeStruct((blocks, own_rows, model), bf16)
    all_gates = (blocks,) + own_gates.shape
    return pl.pallas_call(
        functools.partial(expert_kernel, n_dp),
        out_shape=[
            everyone,
            everyone,
            everyone,
            everyone,
            jax.ShapeDtypeStruct(all_gates, jnp.float32),
            jax.ShapeDtypeStruct((rows, model), bf16),
            jax.ShapeDtypeStruct((rows, model), bf16),
            jax.ShapeDtypeStruct((3, rows, width), bf16),
            jax.ShapeDtypeStruct((blocks * own_rows, 384), bf16),
        ],
        in_specs=[ANY] * 7,
        out_specs=[ANY, ANY, ANY, ANY, vmem, ANY, ANY, ANY, ANY],
        input_output_aliases={2: 1},
        scratch_shapes=ExpertWork.scratch(model, width, capacity, own_rows)
        + [pltpu.VMEM(w.shape, bf16) for w in (w_gate, w_up, w_down, shared)]
        + [
            pltpu.SemaphoreType.DMA((4, 4)),
            pltpu.VMEM(all_gates, jnp.float32),
            pltpu.SemaphoreType.DMA((2, 2)),
            pltpu.SemaphoreType.DMA((2, 6)),
            pltpu.SemaphoreType.DMA((2,)),
            pltpu.SemaphoreType.DMA((14 * n_planes, 2)),
            pltpu.SemaphoreType.DMA((14 * n_planes, 2)),
            pltpu.SemaphoreType.DMA((14 * n_planes, 1)),
            pltpu.SemaphoreType.DMA((14 * n_planes, 1)),
        ],
        compiler_params=pltpu.CompilerParams(
            collective_id=collective_id, has_side_effects=True, vmem_limit_bytes=60 << 20
        ),
    )(own, own_gates, grads, w_gate, w_up, w_down, shared)


def gather_plan(
    tokens,
    attention_gain,
    expert_norm_gain,
    query_projection,
    key_projection,
    value_projection,
    output_projection,
    router,
    shared_gate_matrix,
    shared_up_matrix,
    shared_down_matrix,
    expert_gate_matrix,
    expert_up_matrix,
    expert_down_matrix,
    document_lengths,
    expert_indices,
    cotangent,
):
    n_dp = lax.axis_size(DP)
    x = lax.axis_index(TENSOR)
    dp = lax.axis_index(DP)
    own_rows, model_dim = tokens.shape
    sequence_length = own_rows * 2
    experts = n_dp
    top_k = expert_indices.shape[1]
    capacity = sequence_length * top_k * 4 // (3 * experts)
    bf16, f32 = jnp.bfloat16, jnp.float32

    def dot(a, b):
        return jnp.dot(a, b, preferred_element_type=f32)

    width = attention_gain.shape[0]
    lanes = 2 * width
    tile = jnp.concatenate(
        [router.T, attention_gain[None], expert_norm_gain[None], jnp.zeros((-(experts + 2) % 16, width), bf16)]
    )
    tile = lax.dynamic_update_slice(jnp.zeros((tile.shape[0], lanes), bf16), tile, (0, x * width))
    rotary_cosine, rotary_sine = rotation(sequence_length, HEAD_SIZE)
    cosine = jnp.concatenate([rotary_cosine, rotary_cosine], axis=1)
    sine = jnp.concatenate([-rotary_sine, rotary_sine], axis=1)
    doc_ends = jnp.cumsum(document_lengths[0])
    positions = jnp.arange(sequence_length, dtype=jnp.int32)
    doc_ids = jnp.sum((positions[:, None] >= doc_ends[None, :]).astype(jnp.int32), axis=-1)
    allowed = (doc_ids[:, None] == doc_ids[None, :]) & (positions[:, None] >= positions[None, :])
    own_indices = lax.dynamic_slice_in_dim(expert_indices, x * own_rows, own_rows, 0)
    chosen = jnp.any(own_indices[None] == jnp.arange(experts, dtype=jnp.int32)[:, None, None], axis=2)
    axes = (0, 0, 0, 1)
    (
        query_all, key_all, value_all, out_all, cotangent_all, params, full_one, rows_of_query, key_rows,
        rows_of_value, attn_probs, mixed_heads, residual, normed_two, gates_t,
    ) = front(
        [query_projection, key_projection, value_projection, output_projection],
        axes, tokens, tile, cotangent, chosen.astype(f32), cosine, sine, allowed.astype(f32), n_dp, 1,
    )
    router_full = params[:experts]
    first_gain = params[experts].astype(f32)
    second_gain = params[experts + 1].astype(f32)

    hidden = shared_gate_matrix.shape[1] // n_dp
    hidden_pad = -(-hidden // 16) * 16

    def slices(transposed):
        blocks = transposed.reshape(n_dp, hidden, -1)
        return jnp.pad(blocks, ((0, 0), (0, hidden_pad - hidden), (0, 0)))

    shared_out = jnp.stack(
        [slices(shared_gate_matrix.T), slices(shared_up_matrix.T), slices(shared_down_matrix)], axis=1
    )
    shared_in = lax.all_to_all(shared_out, DP, split_axis=0, concat_axis=0, tiled=True)
    shared_rows = jnp.moveaxis(shared_in, 0, 2).reshape(3, hidden_pad, model_dim)

    shared_rows = jnp.pad(shared_rows, ((0, 0), (0, 128 - hidden_pad), (0, 0))).reshape(384, model_dim)
    (
        normed_all, cotangent_all, output_parts, normed_parts, grad_gate_parts, received, grad_rows, hidden_rows,
        shared_hidden,
    ) = (
        expert_call(
            normed_two, gates_t, cotangent_all, expert_gate_matrix[0].T, expert_up_matrix[0].T, expert_down_matrix[0],
            shared_rows, n_dp, capacity, 2,
        )
    )
    (
        grad_normed_two, grad_gates_t, expert_gate_gradient, expert_up_gradient, expert_down_gradient, shared_grads,
    ) = sum_everywhere(
        [normed_parts, grad_gate_parts],
        [f32, f32],
        [
            received, grad_rows, normed_all.reshape(-1, model_dim), cotangent_all.reshape(-1, model_dim),
            hidden_rows, shared_hidden,
        ],
        n_dp, 4,
    )
    shared_grads = shared_grads.reshape(3, 128, model_dim)[:, :hidden_pad]

    gates = gates_t.T
    scale_two = lax.rsqrt(jnp.mean(residual * residual, axis=-1, keepdims=True) + norm_eps)
    grad_gates = grad_gates_t.T
    grad_logits = (
        gates * (grad_gates - jnp.sum(gates * grad_gates, axis=-1, keepdims=True))
    ).astype(bf16)
    grad_normed_two = grad_normed_two + dot(grad_logits, router_full)
    grad_router_part = dot(normed_two.T, grad_logits)
    grad_residual, grad_gain_two = rms_back(grad_normed_two, residual, scale_two, second_gain)
    grad_residual = grad_residual + cotangent.astype(f32)
    small_grads = jnp.concatenate([grad_router_part.T, jnp.zeros((8, model_dim), f32).at[1].set(grad_gain_two)])
    *weight_grads, grad_inputs, small_sums, ffn_own = backward(
        grad_residual.astype(bf16), mixed_heads, full_one, rows_of_query, key_rows, rows_of_value, attn_probs,
        [query_all, key_all, value_all, out_all], axes, cosine, sine, tokens, grad_residual, first_gain[None],
        small_grads, output_parts, n_dp, 6,
    )
    output = (residual + ffn_own).astype(bf16)
    mine = lax.dynamic_slice_in_dim(small_sums, x * width, width, 1)
    gain_one_own, gain_two_own, router_own = mine[experts], mine[experts + 1], mine[:experts].T
    returned = lax.all_to_all(
        shared_grads.reshape(3, hidden_pad, n_dp, -1).transpose(2, 0, 1, 3),
        DP, split_axis=0, concat_axis=0, tiled=True,
    )[:, :, :hidden]
    returned = returned.transpose(1, 0, 2, 3).reshape(3, n_dp * hidden, -1).astype(f32)
    return (
        output,
        grad_inputs,
        gain_one_own,
        gain_two_own,
        *weight_grads,
        router_own,
        returned[0].T,
        returned[1].T,
        returned[2],
        expert_gate_gradient.T[None],
        expert_up_gradient.T[None],
        expert_down_gradient[None],
    )


def shards(*arguments):
    tokens, expert_gate_matrix = arguments[0], arguments[11]
    n_dp, n_tensor = lax.axis_size(DP), lax.axis_size(TENSOR)
    gathered = n_dp * n_tensor * tokens.shape[0] * tokens.shape[1] * 2
    if n_tensor == 2 and n_dp % 4 == 0 and expert_gate_matrix.shape[0] == 1 and gathered <= 32 << 20:
        return gather_plan(*arguments)
    return exchange_plan(*arguments)


def solution(mesh):
    placed = (
        P((DP, TENSOR), None),
        P((DP, TENSOR)),
        P((DP, TENSOR)),
        P(DP, TENSOR),
        P(DP, TENSOR),
        P(DP, TENSOR),
        P(TENSOR, DP),
        P((DP, TENSOR), None),
        P(DP, TENSOR),
        P(DP, TENSOR),
        P(TENSOR, DP),
        P(DP, None, TENSOR),
        P(DP, None, TENSOR),
        P(DP, TENSOR, None),
        P(DP, None),
        P(DP, None),
        P((DP, TENSOR), None),
    )
    return jax.shard_map(
        shards,
        mesh=mesh,
        in_specs=placed,
        out_specs=(
            P((DP, TENSOR), None),
            P((DP, TENSOR), None),
            P((DP, TENSOR)),
            P((DP, TENSOR)),
            P(DP, TENSOR),
            P(DP, TENSOR),
            P(DP, TENSOR),
            P(TENSOR, DP),
            P((DP, TENSOR), None),
            P(DP, TENSOR),
            P(DP, TENSOR),
            P(TENSOR, DP),
            P(DP, None, TENSOR),
            P(DP, None, TENSOR),
            P(DP, TENSOR, None),
        ),
        check_vma=False,
    )
```

```python
import functools
import math

import jax
import jax.numpy as jnp
from jax import lax
from jax.experimental import pallas as pl
from jax.experimental.pallas import tpu as pltpu
from jax.sharding import PartitionSpec as P

HEAD_SIZE = 128
DP, TENSOR = ("dp", "tensor")


norm_eps = 1e-06
rope_base = 600000.0
neg_big = -1e30


def silu(argument):
    return argument * jax.nn.sigmoid(argument)


def silu_slope(argument):
    sigmoid_of = jax.nn.sigmoid(argument)
    return sigmoid_of * (1.0 + argument * (1.0 - sigmoid_of))


def rotation(sequence_length, head_dim):
    half_dim = head_dim // 2
    frequency = jnp.exp(
        jnp.arange(half_dim, dtype=jnp.float32) * (-2.0 * math.log(rope_base) / head_dim)
    )
    angles = jnp.arange(sequence_length, dtype=jnp.float32)[:, None] * frequency[None, :]
    return (jnp.cos(angles), jnp.sin(angles))


def apply_rotary(tensor, rotary_cosine, rotary_sine):
    half_dim = tensor.shape[-1] // 2
    first_half = tensor[..., :half_dim]
    second_half = tensor[..., half_dim:]
    cos_rows = rotary_cosine[:, None, :]
    sin_rows = rotary_sine[:, None, :]
    return jnp.concatenate(
        [
            first_half * cos_rows - second_half * sin_rows,
            second_half * cos_rows + first_half * sin_rows,
        ],
        axis=-1,
    )


def rotate_back(tensor, rotary_cosine, rotary_sine):
    return apply_rotary(tensor, rotary_cosine, -rotary_sine)


def rms_back(grad_normed, source, scale_rows, gain_full):
    weighted = grad_normed * gain_full
    cubed = scale_rows * scale_rows * scale_rows
    grad_source = scale_rows * weighted - source * cubed * jnp.mean(
        source * weighted, axis=-1, keepdims=True
    )
    grad_gain = jnp.sum(grad_normed * source * scale_rows, axis=0)
    return (grad_source, grad_gain)


def widen(sharded):
    return lax.all_gather(sharded, TENSOR, axis=0, tiled=True)


def narrow(partial_sum):
    return lax.psum_scatter(partial_sum, TENSOR, scatter_dimension=0, tiled=True)


def dense_fetch(
    query_projection,
    key_projection,
    value_projection,
    output_projection,
    shared_gate_matrix,
    shared_up_matrix,
    shared_down_matrix,
):
    return (
        lax.all_gather(query_projection, DP, axis=0, tiled=True),
        lax.all_gather(key_projection, DP, axis=0, tiled=True),
        lax.all_gather(value_projection, DP, axis=0, tiled=True),
        lax.all_gather(output_projection, DP, axis=1, tiled=True),
        lax.all_gather(shared_gate_matrix, DP, axis=0, tiled=True),
        lax.all_gather(shared_up_matrix, DP, axis=0, tiled=True),
        lax.all_gather(shared_down_matrix, DP, axis=1, tiled=True),
    )


def expert_up_output(received_rows, expert_gate_matrix, expert_up_matrix, expert_down_matrix):
    gate_preactivation = jnp.einsum(
        "miwy,iyh->miwh", received_rows, expert_gate_matrix, preferred_element_type=jnp.float32
    )
    up_preactivation = jnp.einsum(
        "miwy,iyh->miwh", received_rows, expert_up_matrix, preferred_element_type=jnp.float32
    )
    hidden = (silu(gate_preactivation) * up_preactivation).astype(jnp.bfloat16)
    produced_rows = jnp.einsum(
        "sxcf,xfd->sxcd", hidden, expert_down_matrix, preferred_element_type=jnp.float32
    ).astype(jnp.bfloat16)
    return (produced_rows, gate_preactivation, up_preactivation)


def expert_gradients(
    received,
    received_gradient,
    gate_preactivation,
    up_preactivation,
    expert_gate_matrix,
    expert_up_matrix,
    expert_down_matrix,
):
    hidden_expert = (silu(gate_preactivation) * up_preactivation).astype(jnp.bfloat16)
    expert_down_gradient = jnp.einsum(
        "sxcf,sxcd->xfd", hidden_expert, received_gradient, preferred_element_type=jnp.float32
    )
    grad_hidden_e = jnp.einsum(
        "sxcd,xfd->sxcf", received_gradient, expert_down_matrix, preferred_element_type=jnp.float32
    )
    grad_gate_e = (grad_hidden_e * up_preactivation * silu_slope(gate_preactivation)).astype(
        jnp.bfloat16
    )
    expert_up_hidden_gradient = (grad_hidden_e * silu(gate_preactivation)).astype(jnp.bfloat16)
    expert_gate_gradient = jnp.einsum(
        "gayi,gayr->air", received, grad_gate_e, preferred_element_type=jnp.float32
    )
    expert_up_gradient = jnp.einsum(
        "gayi,gayr->air", received, expert_up_hidden_gradient, preferred_element_type=jnp.float32
    )
    output_rows_gradient = (
        jnp.einsum(
            "zkjh,klh->zkjl", grad_gate_e, expert_gate_matrix, preferred_element_type=jnp.float32
        )
        + jnp.einsum(
            "zkjh,klh->zkjl",
            expert_up_hidden_gradient,
            expert_up_matrix,
            preferred_element_type=jnp.float32,
        )
    ).astype(jnp.bfloat16)
    return (expert_gate_gradient, expert_up_gradient, expert_down_gradient, output_rows_gradient)


def exchange_plan(
    tokens,
    attention_gain,
    expert_norm_gain,
    query_projection,
    key_projection,
    value_projection,
    output_projection,
    router,
    shared_gate_matrix,
    shared_up_matrix,
    shared_down_matrix,
    expert_gate_matrix,
    expert_up_matrix,
    expert_down_matrix,
    document_lengths,
    expert_indices,
    cotangent,
):
    n_tensor = lax.axis_size(TENSOR)
    n_dp = lax.axis_size(DP)
    tensor_pos = lax.axis_index(TENSOR)
    own_rows = tokens.shape[0]
    sequence_length = own_rows * n_tensor
    model_dim = tokens.shape[1]
    exp_dev = expert_gate_matrix.shape[0]
    experts = exp_dev * n_dp
    top_k = expert_indices.shape[1]
    capacity = max(2, sequence_length * top_k * 4 // (3 * experts))
    slot_total = experts * capacity
    router_full, gain_first, gain_second = (
        lax.all_gather(router, (DP, TENSOR), axis=0, tiled=True),
        lax.all_gather(attention_gain, (DP, TENSOR), axis=0, tiled=True),
        lax.all_gather(expert_norm_gain, (DP, TENSOR), axis=0, tiled=True),
    )
    first_gain = gain_first.astype(jnp.float32)
    second_gain = gain_second.astype(jnp.float32)
    fetched = dense_fetch(
        query_projection,
        key_projection,
        value_projection,
        output_projection,
        shared_gate_matrix,
        shared_up_matrix,
        shared_down_matrix,
    )
    query_all, key_all, value_all, out_all, sgate_all, sup_all, sdown_all = fetched
    input_values = tokens.astype(jnp.float32)
    scale_one = lax.rsqrt(jnp.mean(input_values * input_values, axis=-1, keepdims=True) + norm_eps)
    normed_one = (input_values * scale_one * first_gain).astype(jnp.bfloat16)
    full_one = widen(normed_one)
    q_heads = query_all.shape[1] // HEAD_SIZE
    kv_heads = key_all.shape[1] // HEAD_SIZE
    group_size = q_heads // kv_heads
    rotary_cosine, rotary_sine = rotation(sequence_length, HEAD_SIZE)
    query_unrotated = jnp.dot(full_one, query_all, preferred_element_type=jnp.float32).reshape(
        sequence_length, q_heads, HEAD_SIZE
    )
    key_unrotated = jnp.dot(full_one, key_all, preferred_element_type=jnp.float32).reshape(
        sequence_length, kv_heads, HEAD_SIZE
    )
    rows_of_query = (
        apply_rotary(query_unrotated, rotary_cosine, rotary_sine)
        .astype(jnp.bfloat16)
        .reshape(sequence_length, kv_heads, group_size, HEAD_SIZE)
    )
    key_rows = apply_rotary(key_unrotated, rotary_cosine, rotary_sine).astype(jnp.bfloat16)
    rows_of_value = (
        jnp.dot(full_one, value_all, preferred_element_type=jnp.float32)
        .astype(jnp.bfloat16)
        .reshape(sequence_length, kv_heads, HEAD_SIZE)
    )
    doc_ends = jnp.cumsum(document_lengths[0])
    positions = jnp.arange(sequence_length, dtype=jnp.int32)
    doc_ids = jnp.sum((positions[:, None] >= doc_ends[None, :]).astype(jnp.int32), axis=-1)
    score_scale = HEAD_SIZE ** (-0.5)

    def block_scores(start_row, end_row):
        scores = (
            jnp.einsum(
                "qkgd,skd->kgqs", rows_of_query, key_rows, preferred_element_type=jnp.float32
            )
            * score_scale
        )
        allowed = (doc_ids[start_row:end_row, None] == doc_ids[None, :end_row]) & (
            positions[start_row:end_row, None] >= positions[None, :end_row]
        )
        return (scores, allowed)

    block_index = 0
    start_row = block_index * sequence_length
    end_row = start_row + sequence_length
    scores, allowed = block_scores(start_row, end_row)
    scores = jnp.where(allowed, scores, neg_big)
    row_max = jnp.max(scores, axis=-1, keepdims=True)
    exp_scores = jnp.exp(scores - row_max)
    row_sum = jnp.sum(exp_scores, axis=-1, keepdims=True)
    lse_blocks = [row_max + jnp.log(row_sum)]
    attn_probs = (exp_scores / row_sum).astype(jnp.bfloat16)
    out_blocks = jnp.einsum(
        "kgqs,skd->qkgd", attn_probs, rows_of_value, preferred_element_type=jnp.float32
    )
    mixed_heads = out_blocks.reshape(sequence_length, q_heads * HEAD_SIZE).astype(jnp.bfloat16)
    attn_part = jnp.dot(mixed_heads, out_all, preferred_element_type=jnp.float32)
    residual = input_values + narrow(attn_part)
    scale_two = lax.rsqrt(jnp.mean(residual * residual, axis=-1, keepdims=True) + norm_eps)
    normed_two = (residual * scale_two * second_gain).astype(jnp.bfloat16)
    full_two = widen(normed_two)
    logits = jnp.dot(full_two, router_full, preferred_element_type=jnp.float32)
    chosen = expert_indices[:, :, None] == jnp.arange(experts, dtype=jnp.int32)[None, None, :]
    selected = jnp.sum(jnp.where(chosen, logits[:, None, :], 0.0), axis=-1)
    top_max = jnp.max(selected, axis=-1, keepdims=True)
    gate_exp = jnp.exp(selected - top_max)
    gate_probs = gate_exp / jnp.sum(gate_exp, axis=-1, keepdims=True)
    gate_shared = jnp.dot(full_two, sgate_all, preferred_element_type=jnp.float32)
    up_shared = jnp.dot(full_two, sup_all, preferred_element_type=jnp.float32)
    hidden_shared = (silu(gate_shared) * up_shared).astype(jnp.bfloat16)
    shared_part = jnp.dot(hidden_shared, sdown_all, preferred_element_type=jnp.float32)
    flat_ids = expert_indices.reshape(-1)
    onehot = (flat_ids[:, None] == jnp.arange(experts, dtype=jnp.int32)[None, :]).astype(jnp.int32)
    slot_rank = jnp.sum(onehot * (jnp.cumsum(onehot, axis=0) - 1), axis=-1)
    slot_index = flat_ids * capacity + slot_rank
    pair_index = jnp.arange(sequence_length * top_k, dtype=jnp.int32)
    token_of_slot = jnp.zeros((slot_total,), jnp.int32).at[slot_index].set(pair_index // top_k)
    slot_used = jnp.zeros((slot_total,), jnp.bool_).at[slot_index].set(True)
    gate_of_slot = jnp.zeros((slot_total,), jnp.float32).at[slot_index].set(gate_probs.reshape(-1))
    outgoing = jnp.where(slot_used[:, None], full_two[token_of_slot], 0).reshape(
        n_dp, exp_dev, capacity, model_dim
    )
    received_rows = lax.all_to_all(outgoing, DP, split_axis=0, concat_axis=0, tiled=True)
    produced_rows, gate_preactivation, up_preactivation = expert_up_output(
        received_rows, expert_gate_matrix, expert_up_matrix, expert_down_matrix
    )
    sent_home = lax.all_to_all(produced_rows, DP, split_axis=0, concat_axis=0, tiled=True)
    returned, received, gate_preactivation, up_preactivation = (
        sent_home,
        received_rows,
        gate_preactivation,
        up_preactivation,
    )
    picked = returned.reshape(slot_total, model_dim)[slot_index].reshape(
        sequence_length, top_k, model_dim
    )
    routed_part = jnp.einsum("sk,skd->sd", gate_probs, picked, preferred_element_type=jnp.float32)
    ffn_own = narrow(shared_part + routed_part)
    output = (residual + ffn_own).astype(jnp.bfloat16)
    weights_back = dense_fetch(
        query_projection,
        key_projection,
        value_projection,
        output_projection,
        shared_gate_matrix,
        shared_up_matrix,
        shared_down_matrix,
    )
    query_back, key_back, value_back, out_back, sgate_back, sup_back, sdown_back = weights_back
    grad_out = cotangent.astype(jnp.float32)
    grad_ffn = widen(cotangent)
    grad_hidden_sh = jnp.dot(grad_ffn, sdown_back.T, preferred_element_type=jnp.float32)
    grad_sdown = jnp.dot(hidden_shared.T, grad_ffn, preferred_element_type=jnp.float32)
    grad_gate_sh = (grad_hidden_sh * up_shared * silu_slope(gate_shared)).astype(jnp.bfloat16)
    grad_up_sh = (grad_hidden_sh * silu(gate_shared)).astype(jnp.bfloat16)
    grad_sgate = jnp.dot(full_two.T, grad_gate_sh, preferred_element_type=jnp.float32)
    grad_sup = jnp.dot(full_two.T, grad_up_sh, preferred_element_type=jnp.float32)
    grad_normed_part = jnp.dot(
        grad_gate_sh, sgate_back.T, preferred_element_type=jnp.float32
    ) + jnp.dot(grad_up_sh, sup_back.T, preferred_element_type=jnp.float32)
    grad_gates_part = jnp.einsum("sd,skd->sk", grad_ffn, picked, preferred_element_type=jnp.float32)
    grad_slot = (
        jnp.where(slot_used[:, None], grad_ffn[token_of_slot] * gate_of_slot[:, None], 0.0)
        .astype(jnp.bfloat16)
        .reshape(n_dp, exp_dev, capacity, model_dim)
    )
    received_gradient = lax.all_to_all(grad_slot, DP, split_axis=0, concat_axis=0, tiled=True)
    expert_gate_gradient, expert_up_gradient, expert_down_gradient, output_rows_gradient = (
        expert_gradients(
            received,
            received_gradient,
            gate_preactivation,
            up_preactivation,
            expert_gate_matrix,
            expert_up_matrix,
            expert_down_matrix,
        )
    )
    grad_returned = lax.all_to_all(
        output_rows_gradient, DP, split_axis=0, concat_axis=0, tiled=True
    )
    grad_picked = grad_returned.reshape(slot_total, model_dim)[slot_index].reshape(
        sequence_length, top_k, model_dim
    )
    grad_normed_part = grad_normed_part + jnp.sum(grad_picked, axis=1, dtype=jnp.float32)
    grad_normed_two, grad_gates = (
        lax.psum_scatter(
            grad_normed_part.astype(jnp.bfloat16), TENSOR, scatter_dimension=0, tiled=True
        ).astype(jnp.float32),
        lax.psum_scatter(
            grad_gates_part.astype(jnp.bfloat16), TENSOR, scatter_dimension=0, tiled=True
        ).astype(jnp.float32),
    )
    row_start = tensor_pos * own_rows
    gates_own = lax.dynamic_slice_in_dim(gate_probs, row_start, own_rows, 0)
    chosen_own = lax.dynamic_slice_in_dim(chosen, row_start, own_rows, 0)
    grad_selected = gates_own * (
        grad_gates - jnp.sum(gates_own * grad_gates, axis=-1, keepdims=True)
    )
    grad_logits = jnp.sum(jnp.where(chosen_own, grad_selected[:, :, None], 0.0), axis=1).astype(
        jnp.bfloat16
    )
    grad_normed_two = grad_normed_two + jnp.dot(
        grad_logits, router_full.T, preferred_element_type=jnp.float32
    )
    grad_router_part = jnp.dot(normed_two.T, grad_logits, preferred_element_type=jnp.float32)
    grad_residual, grad_gain_two = rms_back(grad_normed_two, residual, scale_two, second_gain)
    grad_residual = grad_residual + grad_out
    grad_attn = widen(grad_residual.astype(jnp.bfloat16))
    grad_wout = jnp.dot(mixed_heads.T, grad_attn, preferred_element_type=jnp.float32)
    grad_mixed = (
        jnp.dot(grad_attn, out_back.T, preferred_element_type=jnp.float32)
        .astype(jnp.bfloat16)
        .reshape(sequence_length, kv_heads, group_size, HEAD_SIZE)
    )
    grad_keys = jnp.zeros((sequence_length, kv_heads, HEAD_SIZE), jnp.float32)
    grad_values = jnp.zeros((sequence_length, kv_heads, HEAD_SIZE), jnp.float32)
    block_index = 0
    start_row = block_index * sequence_length
    end_row = start_row + sequence_length
    scores, allowed = block_scores(start_row, end_row)
    attn_probs = jnp.where(allowed, jnp.exp(scores - lse_blocks[block_index]), 0.0)
    probs_low = attn_probs.astype(jnp.bfloat16)
    grad_values = grad_values.at[:end_row].add(
        jnp.einsum("kgqs,qkgd->skd", probs_low, grad_mixed, preferred_element_type=jnp.float32)
    )
    grad_probs = jnp.einsum(
        "qkgd,skd->kgqs", grad_mixed, rows_of_value, preferred_element_type=jnp.float32
    )
    inner_sum = jnp.sum(attn_probs * grad_probs, axis=-1, keepdims=True)
    grad_scores = (attn_probs * (grad_probs - inner_sum)).astype(jnp.bfloat16)
    grad_query_blocks = (
        jnp.einsum("kgqs,skd->qkgd", grad_scores, key_rows, preferred_element_type=jnp.float32)
        * score_scale
    )
    grad_keys = grad_keys.at[:end_row].add(
        jnp.einsum("kgqs,qkgd->skd", grad_scores, rows_of_query, preferred_element_type=jnp.float32)
        * score_scale
    )
    grad_query = grad_query_blocks.reshape(sequence_length, q_heads, HEAD_SIZE)
    grad_q_raw = (
        rotate_back(grad_query, rotary_cosine, rotary_sine)
        .astype(jnp.bfloat16)
        .reshape(sequence_length, q_heads * HEAD_SIZE)
    )
    grad_k_raw = (
        rotate_back(grad_keys, rotary_cosine, rotary_sine)
        .astype(jnp.bfloat16)
        .reshape(sequence_length, kv_heads * HEAD_SIZE)
    )
    grad_v_low = grad_values.astype(jnp.bfloat16).reshape(sequence_length, kv_heads * HEAD_SIZE)
    grad_wquery = jnp.dot(full_one.T, grad_q_raw, preferred_element_type=jnp.float32)
    grad_wkey = jnp.dot(full_one.T, grad_k_raw, preferred_element_type=jnp.float32)
    grad_wvalue = jnp.dot(full_one.T, grad_v_low, preferred_element_type=jnp.float32)
    grad_normed_one_part = (
        jnp.dot(grad_q_raw, query_back.T, preferred_element_type=jnp.float32)
        + jnp.dot(grad_k_raw, key_back.T, preferred_element_type=jnp.float32)
        + jnp.dot(grad_v_low, value_back.T, preferred_element_type=jnp.float32)
    )
    grad_normed_one = narrow(grad_normed_one_part)
    grad_inputs, grad_gain_one = rms_back(grad_normed_one, input_values, scale_one, first_gain)
    grad_inputs = grad_inputs + grad_residual
    dense_sums = (
        lax.psum_scatter(grad_wquery, DP, scatter_dimension=0, tiled=True),
        lax.psum_scatter(grad_wkey, DP, scatter_dimension=0, tiled=True),
        lax.psum_scatter(grad_wvalue, DP, scatter_dimension=0, tiled=True),
        lax.psum_scatter(grad_wout, DP, scatter_dimension=1, tiled=True),
        lax.psum_scatter(grad_sgate, DP, scatter_dimension=0, tiled=True),
        lax.psum_scatter(grad_sup, DP, scatter_dimension=0, tiled=True),
        lax.psum_scatter(grad_sdown, DP, scatter_dimension=1, tiled=True),
    )
    small_sums = (
        lax.psum_scatter(grad_router_part, (DP, TENSOR), scatter_dimension=0, tiled=True),
        lax.psum_scatter(grad_gain_one, (DP, TENSOR), scatter_dimension=0, tiled=True),
        lax.psum_scatter(grad_gain_two, (DP, TENSOR), scatter_dimension=0, tiled=True),
    )
    return (
        output,
        grad_inputs,
        small_sums[1],
        small_sums[2],
        dense_sums[0],
        dense_sums[1],
        dense_sums[2],
        dense_sums[3],
        small_sums[0],
        dense_sums[4],
        dense_sums[5],
        dense_sums[6],
        expert_gate_gradient,
        expert_up_gradient,
        expert_down_gradient,
    )


MESH = pl.DeviceIdType.MESH
ANY = pl.BlockSpec(memory_space=pl.ANY)


def when(condition, body):
    if condition is None:
        body()
    else:
        pl.when(condition)(body)


class Spot:
    def __init__(self, n_planes):
        dp = lax.axis_index(DP)
        self.x = lax.axis_index(TENSOR)
        self.dp = dp
        self.core = dp % 2
        self.y = (dp // 2) % 2
        self.z = dp // 4
        self.n_planes = n_planes
        self.has_up = self.z < n_planes - 1
        self.has_down = self.z > 0
        self.up = (dp + 4, self.x)
        self.down = (dp - 4, self.x)
        self.side = (dp + 2 - 4 * self.y, self.x)
        self.across = (dp, 1 - self.x)
        self.twin = (dp + 1 - 2 * self.core, self.x)

    def far_first(self):
        low, high = 0 * self.z, 0 * self.z + self.n_planes - 1
        order = []
        for _ in range(self.n_planes):
            take_low = (self.z - low >= high - self.z).astype(jnp.int32)
            order.append(take_low * low + (1 - take_low) * high)
            low, high = low + take_low, high - (1 - take_low)
        return order

    def plane(self, k):
        s = (self.z + k) % self.n_planes
        return s, (s * 4 + self.dp % 4, self.x)

    def greet(self, all_planes=False):
        barrier = pltpu.get_barrier_semaphore()
        if all_planes:
            peers = [self.side, self.twin, self.across] + [self.plane(k)[1] for k in range(1, self.n_planes)]
            for device in peers:
                pl.semaphore_signal(barrier, inc=1, device_id=device, device_id_type=MESH)
            pl.semaphore_wait(barrier, len(peers))
            return
        fixed = [self.side, self.twin, self.across]
        for device in fixed:
            pl.semaphore_signal(barrier, inc=1, device_id=device, device_id_type=MESH)
        for condition, device in ((self.has_up, self.up), (self.has_down, self.down)):

            @pl.when(condition)
            def _(device=device):
                pl.semaphore_signal(barrier, inc=1, device_id=device, device_id_type=MESH)

        ends = self.has_up.astype(jnp.int32) + self.has_down.astype(jnp.int32)
        pl.semaphore_wait(barrier, len(fixed) + ends)


class Copies:
    def __init__(self, n_planes, send, recv):
        self.n_planes, self.send, self.recv = n_planes, send, recv
        self.open = []

    def copy(self, group, s, piece, src, dst, device, arrival=None):
        arrival = group if arrival is None else arrival
        return pltpu.make_async_remote_copy(
            src_ref=src,
            dst_ref=dst,
            send_sem=self.send.at[group * self.n_planes + s, piece],
            recv_sem=self.recv.at[arrival * self.n_planes + s, piece],
            device_id=device,
            device_id_type=MESH,
        )

    def start(self, condition, group, s, sources, targets, device, arrival=None):
        def body():
            for i, (src, dst) in enumerate(zip(sources, targets)):
                self.copy(group, s, i, src, dst, device, arrival).start()

        when(condition, body)
        self.open.append((condition, group, s, sources, targets, device, arrival))

    def arrive(self, group, s, targets, device):
        for i, dst in enumerate(targets):
            self.copy(group, s, i, dst, dst, device).wait_recv()

    def close(self):
        for condition, group, s, sources, targets, device, arrival in self.open:

            def body():
                for i, (src, dst) in enumerate(zip(sources, targets)):
                    self.copy(group, s, i, src, dst, device, arrival).wait_send()

            when(condition, body)


(Z_UP, Z_DOWN, Y_ALL, Y_HALF, X_ALL, X_HALF, C_OWN, C_Y, C_X, C_XH, C_YH, D_UP, D_DOWN, C_D) = range(14)
(ALL, FIRST, SECOND) = range(3)


class Spread:
    def __init__(self, spot, copies, own, views, use_x, by_z=False):
        self.spot, self.copies, self.own, self.use_x, self.by_z = spot, copies, own, use_x, by_z
        self.order = spot.far_first()[::-1]
        y, x, core = spot.y, spot.x, spot.core

        def places(s, cc):
            return (
                views(s, y, cc, x, ALL),
                views(s, 1 - y, cc, x, ALL),
                views(s, 1 - y, cc, x, FIRST),
                views(s, y, cc, 1 - x, ALL),
                views(s, y, cc, 1 - x, SECOND),
                views(s, 1 - y, cc, 1 - x, FIRST),
                views(s, 1 - y, cc, 1 - x, SECOND),
                views(s, 1 - y, cc, 1 - x, ALL),
            )

        self.mine = [places(s, core) for s in self.order]
        self.twins = [places(s, 1 - core) for s in self.order]
        self.goes_down = [(s > spot.z) & spot.has_down for s in self.order]
        self.goes_up = [(s < spot.z) & spot.has_up for s in self.order]
        middle = spot.has_up & spot.has_down
        self.among = (jnp.logical_not(middle), middle)
        self.goes = {
            (j, c): (self.goes_down[j] & self.among[c], self.goes_up[j] & self.among[c], self.among[c])
            for j in range(len(self.order))
            for c in (0, 1)
        }

    def place(self, j):
        return self.own if j == 0 else self.mine[j][0]

    def onward_y(self, j):
        self.copies.start(None, Y_ALL, self.order[j], self.place(j), self.mine[j][0], self.spot.side)

    def onward_x(self, j):
        self.copies.start(None, X_ALL, self.order[j], self.place(j), self.mine[j][0], self.spot.across)

    def onward_twin(self, j):
        self.copies.start(None, C_OWN, self.order[j], self.place(j), self.mine[j][0], self.spot.twin)

    def onward(self, j):
        self.onward_y(j)
        if self.use_x:
            self.onward_x(j)
        self.onward_twin(j)

    def begin_z(self):
        spot, here = self.spot, self.mine[0][0]
        self.copies.start(spot.has_up, Z_UP, spot.z, self.own, here, spot.up)
        self.copies.start(spot.has_down, Z_DOWN, spot.z, self.own, here, spot.down, Z_UP)

    def begin(self):
        self.begin_z()
        self.onward(0)

    def relay(self, j, goes=None):
        s, here, spot = self.order[j], self.mine[j][0], self.spot
        goes_down, goes_up, _ = goes or (self.goes_down[j], self.goes_up[j], None)
        self.copies.arrive(Z_UP, s, here, spot.up)
        self.copies.start(goes_down, Z_DOWN, s, here, here, spot.down, Z_UP)
        self.copies.start(goes_up, Z_UP, s, here, here, spot.up)

    def relay_of(self, j, c):
        pl.when(self.among[c])(functools.partial(self.relay, j, self.goes[j, c]))

    def corner_of(self, j, c):
        pl.when(self.among[c])(functools.partial(self.corner, j, self.goes[j, c]))

    def column(self, j):
        if j < len(self.order):
            self.relay(j)
            self.onward(j)

    def from_side(self, j):
        s, there, spot = self.order[j], self.mine[j][1], self.spot
        self.copies.arrive(Y_ALL, s, there, spot.side)
        self.copies.start(None, C_Y, s, there, there, spot.twin)

    def from_across(self, j):
        s, there, spot = self.order[j], self.mine[j][3], self.spot
        self.copies.arrive(X_ALL, s, there, spot.across)
        self.copies.start(None, C_X, s, there, there, spot.twin)

    def over_x(self, j):
        part = self.mine[j][2]
        self.copies.start(None, X_HALF, self.order[j], part, part, self.spot.across)

    def over_y(self, j):
        part = self.mine[j][4]
        self.copies.start(None, Y_HALF, self.order[j], part, part, self.spot.side)

    def side(self, j):
        self.from_side(j)
        if self.use_x and (j == 0 or not self.by_z):
            self.over_x(j)

    def across(self, j):
        self.from_across(j)
        if j == 0 or not self.by_z:
            self.over_y(j)

    def sides(self, j):
        if 0 <= j < len(self.order):
            self.side(j)
            if self.use_x:
                self.across(j)

    def corner(self, j, goes=None):
        if not self.use_x or not 0 <= j < len(self.order):
            return
        s, spot = self.order[j], self.spot
        first, second, whole = self.mine[j][5:]
        if self.by_z and j > 0:
            goes_down, goes_up, always = goes or (self.goes_down[j], self.goes_up[j], None)
            self.copies.arrive(D_UP, s, whole, spot.up)
            self.copies.start(goes_down, D_DOWN, s, whole, whole, spot.down, D_UP)
            self.copies.start(goes_up, D_UP, s, whole, whole, spot.up)
            self.copies.start(always, C_D, s, whole, whole, spot.twin)
            return
        self.copies.arrive(X_HALF, s, first, spot.across)
        self.copies.start(None, C_XH, s, first, first, spot.twin)
        self.copies.arrive(Y_HALF, s, second, spot.side)
        self.copies.start(None, C_YH, s, second, second, spot.twin)
        if self.by_z:
            self.copies.start(spot.has_up, D_UP, s, whole, whole, spot.up)
            self.copies.start(spot.has_down, D_DOWN, s, whole, whole, spot.down, D_UP)

    def twin_own(self, j):
        self.copies.arrive(C_OWN, self.order[j], self.twins[j][0], self.spot.twin)

    def twin_across(self, j):
        self.copies.arrive(C_X, self.order[j], self.twins[j][3], self.spot.twin)

    def twin_near(self, j):
        self.twin_own(j)
        if self.use_x:
            self.twin_across(j)

    def twin_side(self, j):
        self.copies.arrive(C_Y, self.order[j], self.twins[j][1], self.spot.twin)

    def twin_corner(self, j):
        if self.by_z and j > 0:
            self.copies.arrive(C_D, self.order[j], self.twins[j][7], self.spot.twin)
            return
        self.copies.arrive(C_XH, self.order[j], self.twins[j][5], self.spot.twin)
        self.copies.arrive(C_YH, self.order[j], self.twins[j][6], self.spot.twin)

    def twin_far(self, j):
        self.twin_side(j)
        if self.use_x:
            self.twin_corner(j)

    def twin_all(self):
        for j in range(len(self.order)):
            self.twin_near(j)
            self.twin_far(j)

    def stage(self, step):
        self.column(step)
        self.sides(step - 1)
        self.corner(step - 2)

    def run(self):
        self.begin()
        for step in range(1, len(self.order) + 2):
            self.stage(step)
        self.twin_all()
        self.copies.close()


def dp_of(s, yy, cc):
    return (s * 2 + yy) * 2 + cc


def plain_dot(a, b, contract):
    return lax.dot_general(a, b, (contract, ((), ())), preferred_element_type=jnp.float32)


ROWS_COLUMNS = ((1,), (0,))
ROWS_ROWS = ((1,), (1,))
COLUMNS_COLUMNS = ((0,), (0,))


def turn(heads, cosine, sine):
    return heads * cosine + pltpu.roll(heads, heads.shape[1] // 2, 1) * sine


def front_kernel(n_planes, axes, *refs):
    n = len(axes)
    shards_in, (tokens, tile, grads, chosen, cosine, sine, allowed) = refs[:n], refs[n : n + 7]
    outs = refs[n + 7 : 2 * n + 7]
    all_grads, params, *kept_out, residual, normed_two, gates = refs[2 * n + 7 : 2 * n + 18]
    normed_one, query, key, value, probs, mixed = refs[-7:-1]
    out_sems = refs[-1]
    (
        wq, wk, wv, wo, sequence, pair, sent, received, w_send, w_recv, p_send, p_recv, g_send, g_recv, local,
        x_send, x_recv,
    ) = refs[2 * n + 18 : -7]
    spot = Spot(n_planes)
    x = spot.x
    bf16, f32 = jnp.bfloat16, jnp.float32
    own_rows, model = tokens.shape

    def weight_views(s, yy, cc, xx, part):
        i = dp_of(s, yy, cc)
        places = []
        for o, a, axis in zip((wq, wk, wv, wo), shards_in, axes):
            size = a.shape[axis]
            span = pl.ds(pl.multiple_of(i * size, size), size)
            places.append(o.at[span] if axis == 0 else o.at[:, span])
        return places

    def param_views(s, yy, cc, xx, part):
        size = tile.shape[1]
        return [params.at[:, pl.ds(pl.multiple_of(dp_of(s, yy, cc) * size, size), size)]]

    def grad_views(s, yy, cc, xx, part):
        b = dp_of(s, yy, cc) * 2 + xx
        if part == ALL:
            return [all_grads.at[b]]
        return [all_grads.at[b, pl.ds(0 if part == FIRST else own_rows // 2, own_rows // 2)]]

    def mine(views):
        return views(spot.z, spot.y, spot.core, x, ALL)

    def swap(i, src, dst):
        return pltpu.make_async_remote_copy(
            src_ref=src, dst_ref=dst, send_sem=x_send.at[i], recv_sem=x_recv.at[i],
            device_id=spot.across, device_id_type=MESH,
        )

    kept = list(zip(list(shards_in) + [tokens, grads, tile], mine(weight_views) + [sequence.at[x]] + mine(grad_views) + [pair.at[x]]))
    kept = [pltpu.make_async_copy(a, b, local.at[i]) for i, (a, b) in enumerate(kept)]
    for c in kept:
        c.start()
    spot.greet()
    swaps = [swap(0, tile, pair.at[x]), swap(1, tokens, sequence.at[x]), swap(2, sent, received)]
    swaps[0].start()
    weights = Spread(spot, Copies(n_planes, w_send, w_recv), list(shards_in), weight_views, False)
    small = Spread(spot, Copies(n_planes, p_send, p_recv), mine(param_views), param_views, False)
    net = Spread(spot, Copies(n_planes, g_send, g_recv), [grads], grad_views, True)
    weights.begin()
    swaps[1].start()
    for c in kept:
        c.wait()
    swap(0, pair.at[1 - x], pair.at[1 - x]).wait_recv()
    mine(param_views)[0][...] = pair[0] + pair[1]
    small.begin()
    net.onward_x(0)
    net.onward_twin(0)
    for step in range(1, n_planes + 1):
        weights.stage(step)
        small.stage(step)
        if step == n_planes - 1:
            net.begin_z()
    net.onward_y(0)
    net.from_across(0)

    net.relay(1)
    net.relay_of(2, 1)
    net.onward_x(1)
    net.onward_twin(1)

    small.twin_all()
    swap(1, sequence.at[1 - x], sequence.at[1 - x]).wait_recv()

    experts = chosen.shape[0]
    first_gain = params[experts : experts + 1, :].astype(f32)
    step = 32
    for h in range(2):
        for r in range(own_rows // step):
            rows = sequence[h, pl.ds(r * step, step)].astype(f32)
            scale = lax.rsqrt(jnp.mean(rows * rows, axis=1, keepdims=True) + norm_eps)
            normed_one[pl.ds(h * own_rows + r * step, step)] = (rows * scale * first_gain).astype(bf16)
    weights.twin_all()
    pairs = list(zip((wq, wk, wv, wo), outs)) + list(zip((normed_one, query, key, value, probs, mixed), kept_out))
    written = [pltpu.make_async_copy(a, b, out_sems.at[i]) for i, (a, b) in enumerate(pairs)]
    for c in written[: n + 1]:
        c.start()
    heads, head_dim = query.shape[1] // cosine.shape[1], cosine.shape[1]
    kv_heads = key.shape[1] // head_dim
    group = heads // kv_heads
    cos, sin = cosine[...], sine[...]
    raw = plain_dot(normed_one[...], wk[...], ROWS_COLUMNS)
    for g in range(kv_heads):
        span = slice(g * head_dim, (g + 1) * head_dim)
        key[:, span] = turn(raw[:, span], cos, sin).astype(bf16)
    value[...] = plain_dot(normed_one[...], wv[...], ROWS_COLUMNS).astype(bf16)
    raw = plain_dot(normed_one[...], wq[...], ROWS_COLUMNS)
    for h in range(heads):
        span = slice(h * head_dim, (h + 1) * head_dim)
        query[:, span] = turn(raw[:, span], cos, sin).astype(bf16)
    net.from_side(0)
    net.onward_y(1)
    net.relay_of(2, 0)
    net.relay_of(3, 1)
    net.onward_x(2)
    net.onward_twin(2)
    net.from_across(1)
    may = allowed[...] > 0.0
    for h in range(heads):
        span = slice(h * head_dim, (h + 1) * head_dim)
        shared = slice(h // group * head_dim, (h // group + 1) * head_dim)
        scores = plain_dot(query[:, span], key[:, shared], ROWS_ROWS) * (head_dim ** -0.5)
        scores = jnp.where(may, scores, neg_big)
        weight = jnp.exp(scores - jnp.max(scores, axis=1, keepdims=True))
        weight = weight / jnp.sum(weight, axis=1, keepdims=True)
        probs[h] = weight
        mixed[:, span] = plain_dot(weight.astype(bf16), value[:, shared], ROWS_COLUMNS).astype(bf16)
    for c in written[n + 1 :]:
        c.start()
    other = mixed[pl.ds(pl.multiple_of((1 - x) * own_rows, own_rows), own_rows), :]
    sent[...] = plain_dot(other, wo[...], ROWS_COLUMNS).astype(bf16)
    swaps[2].start()
    other = mixed[pl.ds(pl.multiple_of(x * own_rows, own_rows), own_rows), :]
    residual[...] = plain_dot(other, wo[...], ROWS_COLUMNS)
    net.relay_of(3, 0)
    net.onward_twin(3)
    net.from_side(1)
    net.from_across(2)
    swap(2, received, received).wait_recv()
    second_gain = params[experts + 1 : experts + 2, :].astype(f32)
    for r in range(own_rows // step):
        span = pl.ds(r * step, step)
        rows = sequence[x, span].astype(f32) + (residual[span] + received[span].astype(f32))
        residual[span] = rows
        scale = lax.rsqrt(jnp.mean(rows * rows, axis=1, keepdims=True) + norm_eps)
        normed_two[span] = (rows * scale * second_gain).astype(bf16)
    logits = plain_dot(params[:experts, :], normed_two[...], ROWS_ROWS)
    picked = chosen[...] > 0.0
    top = jnp.max(jnp.where(picked, logits, neg_big), axis=0, keepdims=True)
    weight = jnp.where(picked, jnp.exp(jnp.where(picked, logits - top, 0.0)), 0.0)
    gates[...] = weight / jnp.sum(weight, axis=0, keepdims=True)

    for j in range(n_planes):
        net.twin_own(j)
        if j < n_planes - 1:
            net.twin_across(j)
        if j < n_planes - 2:
            net.twin_side(j)
    for each in (weights, small, net):
        each.copies.close()
    for c in swaps:
        c.wait_send()
    for c in written:
        c.wait()


def front(arrays, axes, tokens, tile, grads, chosen, cosine, sine, allowed, n_dp, collective_id):
    n, n_planes = len(arrays), n_dp // 4
    bf16, f32 = jnp.bfloat16, jnp.float32
    shape = jax.ShapeDtypeStruct

    def whole(a, axis):
        full = list(a.shape)
        full[axis] *= n_dp
        return shape(tuple(full), a.dtype)

    own_rows, model = tokens.shape
    seq = 2 * own_rows
    experts = chosen.shape[0]
    wide, narrow_ = arrays[0].shape[1], arrays[1].shape[1]
    heads = wide // cosine.shape[1]
    gathered = [whole(a, axis) for a, axis in zip(arrays, axes)]
    vmem = pl.BlockSpec(memory_space=pltpu.VMEM)
    dma = pltpu.SemaphoreType.DMA
    return pl.pallas_call(
        functools.partial(front_kernel, n_planes, axes),
        out_shape=gathered
        + [
            shape((2 * n_dp,) + grads.shape, bf16),
            shape((tile.shape[0], tile.shape[1] * n_dp), bf16),
            shape((seq, model), bf16),
            shape((seq, wide), bf16),
            shape((seq, narrow_), bf16),
            shape((seq, narrow_), bf16),
            shape((heads, seq, seq), f32),
            shape((seq, wide), bf16),
            shape((own_rows, model), f32),
            shape((own_rows, model), bf16),
            shape((experts, own_rows), f32),
        ],
        in_specs=[ANY] * (n + 3) + [vmem] * 4,
        out_specs=[ANY] * (n + 1) + [vmem] + [ANY] * 6 + [vmem] * 3,
        scratch_shapes=[pltpu.VMEM(g.shape, bf16) for g in gathered]
        + [
            pltpu.VMEM((2, own_rows, model), bf16),
            pltpu.VMEM((2,) + tile.shape, bf16),
            pltpu.VMEM((own_rows, model), bf16),
            pltpu.VMEM((own_rows, model), bf16),
        ]
        + [dma((14 * n_planes, n))] * 2
        + [dma((14 * n_planes, 1))] * 4
        + [dma((n + 3,)), dma((3,)), dma((3,))]
        + [
            pltpu.VMEM((seq, model), bf16),
            pltpu.VMEM((seq, wide), bf16),
            pltpu.VMEM((seq, narrow_), bf16),
            pltpu.VMEM((seq, narrow_), bf16),
            pltpu.VMEM((heads, seq, seq), f32),
            pltpu.VMEM((seq, wide), bf16),
            dma((n + 6,)),
        ],
        compiler_params=pltpu.CompilerParams(
            collective_id=collective_id, has_side_effects=True, vmem_limit_bytes=56 << 20
        ),
        cost_estimate=pl.CostEstimate(
            flops=6 * seq * model * wide, bytes_accessed=16 * n_dp * own_rows * model, transcendentals=heads * seq * seq
        ),
    )(*arrays, tokens, tile, grads, chosen, cosine, sine, allowed)


(T_YX, T_Y, T_X, T_OWN, R_XHALF, R_YHALF, R_YALL, R_XALL, R_UP, R_DOWN, R_DUP, R_DDOWN) = range(12)


def add_up(target, sources):
    rows = target.shape[0]
    step = 16 if rows % 16 == 0 else rows

    def body(i, carry):
        span = pl.ds(pl.multiple_of(i * step, step), step)
        total = sources[0][span, :].astype(jnp.float32)
        for source in sources[1:]:
            total = total + source[span, :].astype(jnp.float32)
        target[span, :] = total.astype(target.dtype)
        return carry

    lax.fori_loop(0, rows // step, body, 0)


class Reduce:
    @staticmethod
    def scratch(shapes, dtypes, n_planes, use_x, cut=0, direct=False, by_z=False):
        kinds = 4 if use_x else 2
        out = []
        for i, (shape, dtype) in enumerate(zip(shapes, dtypes)):
            rows = cut if i == 0 else shape[0]
            out.append(pltpu.VMEM((kinds, n_planes) + shape, dtype))
            out.append(pltpu.VMEM((n_planes + 1,) + shape, dtype))
            out.append(pltpu.VMEM((n_planes,) + shape, dtype))
            if not direct:
                out.append(pltpu.VMEM((kinds, 2) + shape, dtype))
            if use_x:
                out.append(pltpu.VMEM((n_planes,) + shape, dtype))
                out.append(pltpu.VMEM((1 if by_z else n_planes, rows) + shape[1:], dtype))
                if by_z:
                    out.append(pltpu.VMEM((n_planes + 1,) + shape, dtype))
                if i == 0 and cut < shape[0]:
                    out.append(pltpu.VMEM((1 if by_z else n_planes, shape[0] - cut) + shape[1:], dtype))
        n = len(shapes)
        out.append(pltpu.SemaphoreType.DMA((12 * n_planes, n)))
        out.append(pltpu.SemaphoreType.DMA((12 * n_planes, n)))
        out.append(pltpu.SemaphoreType.DMA((kinds * n_planes, n)))
        return out

    def __init__(self, spot, blocks, outs, scratch, use_x, cut=0, direct=False, by_z=False):
        self.spot, self.outs, self.use_x, self.direct, self.by_z = spot, outs, use_x, direct, by_z
        self.slant = []
        self.n, self.n_planes, self.cut = len(outs), spot.n_planes, cut
        left = list(scratch)
        self.twin, self.line, self.near, self.ring, self.across, self.first = [], [], [], [], [], []
        self.second = None
        for i in range(self.n):
            self.twin.append(left.pop(0))
            self.line.append(left.pop(0))
            self.near.append(left.pop(0))
            if not direct:
                self.ring.append(left.pop(0))
            if use_x:
                self.across.append(left.pop(0))
                self.first.append(left.pop(0))
                if by_z:
                    self.slant.append(left.pop(0))
                if i == 0 and cut < self.near[0].shape[1]:
                    self.second = left.pop(0)
        send, recv, self.local = left
        self.copies = Copies(self.n_planes, send, recv)
        y, x, core = spot.y, spot.x, spot.core
        self.order = spot.far_first()
        places = {T_YX: (1 - y, 1 - x), T_Y: (1 - y, x), T_X: (y, 1 - x), T_OWN: (y, x)}
        self.kinds = [T_YX, T_Y, T_X, T_OWN] if use_x else [T_Y, T_OWN]
        every = [(k, j) for j in range(self.n_planes) for k in self.kinds]
        self.terms = {(k, j): blocks(self.order[j], places[k][0], core, places[k][1]) for k, j in every}
        self.others = {(k, j): blocks(self.order[j], places[k][0], 1 - core, places[k][1]) for k, j in every}

    def load(self, kind, j):
        k, s = self.kinds.index(kind), self.order[j]
        return [
            pltpu.make_async_copy(ref, self.ring[i].at[k, j % 2], self.local.at[k * self.n_planes + s, i])
            for i, ref in enumerate(self.terms[kind, j])
        ]

    def start_load(self, kind, j):
        if not self.direct and j < self.n_planes:
            for c in self.load(kind, j):
                c.start()

    def start_loads(self):
        for j in range(2):
            for kind in self.kinds:
                self.start_load(kind, j)

    def start_twins(self):
        for j in range(self.n_planes):
            s = self.order[j]
            for k, kind in enumerate(self.kinds):
                self.copies.start(None, kind, s, self.others[kind, j], [t.at[k, s] for t in self.twin], self.spot.twin)

    def ready(self, kind, j):
        k, s = self.kinds.index(kind), self.order[j]
        twin = [t.at[k, s] for t in self.twin]
        self.copies.arrive(kind, s, twin, self.spot.twin)
        if self.direct:
            return twin, self.terms[kind, j]
        for c in self.load(kind, j):
            c.wait()
        return twin, [r.at[k, j % 2] for r in self.ring]

    def along(self, j, here, line, targets, up, down):
        s, spot, copies = self.order[j], self.spot, self.copies
        some = [t.at[s] for t in line]
        below = [t.at[self.n_planes] for t in line]

        def add_all(*more):
            for i in range(self.n):
                add_up(targets[i], here[i] + [m[i] for m in more])

        if j == self.n_planes - 1:
            when(spot.has_up, lambda: copies.arrive(down, s, some, spot.up))
            when(spot.has_down, lambda: copies.arrive(up, s, below, spot.down))
            when(spot.has_up & spot.has_down, lambda: add_all(some, below))
            when(spot.z == 0, lambda: add_all(some))
            when(spot.z == self.n_planes - 1, lambda: add_all(below))
            return
        for goes, more, group, last, device, source in (
            (s < spot.z, spot.has_up, down, None, spot.down, spot.up),
            (s > spot.z, spot.has_down, up, s - spot.z == 1, spot.up, spot.down),
        ):

            def partial():
                copies.arrive(group, s, some, source)
                add_all(some)

            when(goes & more, partial)
            when(goes & jnp.logical_not(more), add_all)
            if last is None:
                copies.start(goes, group, s, targets, some, device)
            else:
                copies.start(goes & last, group, s, targets, below, device)
                copies.start(goes & jnp.logical_not(last), group, s, targets, some, device)

    def corner(self, j):
        if not self.use_x or not 0 <= j < self.n_planes:
            return
        s, cut = self.order[j], self.cut
        twin, mine = self.ready(T_YX, j)
        if self.by_z:
            self.along(j, [[m, t] for m, t in zip(mine, twin)], self.slant, twin, R_DUP, R_DDOWN)
        else:
            for m, t in zip(mine, twin):
                add_up(t, [m, t])
        self.start_load(T_YX, j + 2)
        if self.by_z and j < self.n_planes - 1:
            return
        p = 0 if self.by_z else s
        head = twin if self.second is None else [twin[0].at[pl.ds(0, cut)]] + twin[1:]
        self.copies.start(None, R_XHALF, s, head, [f.at[p] for f in self.first], self.spot.across)
        if self.second is not None:
            tail = [twin[0].at[pl.ds(cut, self.second.shape[1])]]
            self.copies.start(None, R_YHALF, s, tail, [self.second.at[p]], self.spot.side)

    def side(self, j):
        s, cut = self.order[j], self.cut
        twin, mine = self.ready(T_Y, j)
        over = self.use_x and (j == self.n_planes - 1 or not self.by_z)
        p = 0 if self.by_z else s
        if over:
            first = [f.at[p] for f in self.first]
            self.copies.arrive(R_XHALF, s, first, self.spot.across)
        for i, (m, t) in enumerate(zip(mine, twin)):
            if not over:
                add_up(t, [m, t])
            elif i == 0 and self.second is not None:
                a, b = pl.ds(0, cut), pl.ds(cut, self.second.shape[1])
                add_up(t.at[a], [m.at[a], t.at[a], first[0]])
                add_up(t.at[b], [m.at[b], t.at[b]])
            else:
                add_up(t, [m, t, first[i]])
        self.start_load(T_Y, j + 2)
        self.copies.start(None, R_YALL, s, twin, [t.at[s] for t in self.near], self.spot.side)

    def over(self, j):
        s, cut = self.order[j], self.cut
        twin, mine = self.ready(T_X, j)
        over = self.second is not None and (j == self.n_planes - 1 or not self.by_z)
        p = 0 if self.by_z else s
        if over:
            self.copies.arrive(R_YHALF, s, [self.second.at[p]], self.spot.side)
        for i, (m, t) in enumerate(zip(mine, twin)):
            if i == 0 and over:
                a, b = pl.ds(0, cut), pl.ds(cut, self.second.shape[1])
                add_up(t.at[a], [m.at[a], t.at[a]])
                add_up(t.at[b], [m.at[b], t.at[b], self.second.at[p]])
            else:
                add_up(t, [m, t])
        self.start_load(T_X, j + 2)
        self.copies.start(None, R_XALL, s, twin, [t.at[s] for t in self.across], self.spot.across)

    def sides(self, j):
        if 0 <= j < self.n_planes:
            self.side(j)
            if self.use_x:
                self.over(j)

    def column(self, j):
        if not 0 <= j < self.n_planes:
            return
        s, spot, copies = self.order[j], self.spot, self.copies
        twin, mine = self.ready(T_OWN, j)
        near = [t.at[s] for t in self.near]
        copies.arrive(R_YALL, s, near, spot.side)
        here = [[m, t, a] for m, t, a in zip(mine, twin, near)]
        if self.use_x:
            across = [t.at[s] for t in self.across]
            copies.arrive(R_XALL, s, across, spot.across)
            here = [h + [a] for h, a in zip(here, across)]
        self.along(j, here, self.line, self.outs if j == self.n_planes - 1 else twin, R_UP, R_DOWN)
        self.start_load(T_OWN, j + 2)

    def stage(self, step):
        self.corner(step)
        self.sides(step - 1)
        self.column(step - 2)

    def close(self):
        self.copies.close()


class WeightGradients:
    width = 256

    def __init__(self, ins, outs, scratch):
        self.sources, (self.hidden, self.shared) = ins[:4], ins[4:]
        self.outs = outs
        self.buffers, self.small_hidden, self.small_shared = scratch[:4], scratch[4], scratch[5]
        self.flat, self.sums, self.load, self.store, self.once = scratch[6:]
        self.n_parts = self.sources[0].shape[1] // self.width

    @staticmethod
    def scratch(rows, tokens, width, shared):
        bf16, f32 = jnp.bfloat16, jnp.float32
        w = WeightGradients.width
        return [
            pltpu.VMEM((2, rows, w), bf16),
            pltpu.VMEM((2, rows, w), bf16),
            pltpu.VMEM((2, tokens, w), bf16),
            pltpu.VMEM((2, tokens, w), bf16),
            pltpu.VMEM((3, rows, width), bf16),
            pltpu.VMEM((tokens, shared), bf16),
            pltpu.VMEM((2, 3, width, w), f32),
            pltpu.VMEM((2, shared, w), bf16),
            pltpu.SemaphoreType.DMA((2, 4)),
            pltpu.SemaphoreType.DMA((2, 4)),
            pltpu.SemaphoreType.DMA((2,)),
        ]

    def span(self, p):
        return pl.ds(p * self.width, self.width)

    def loads(self, p):
        return [
            pltpu.make_async_copy(a.at[:, self.span(p)], b.at[p % 2], self.load.at[p % 2, i])
            for i, (a, b) in enumerate(zip(self.sources, self.buffers))
        ]

    def stores(self, p):
        gate_t, up_t, down, shared = self.outs
        slot, span = p % 2, self.span(p)
        pairs = [
            (self.flat.at[slot, 0], gate_t.at[:, span]),
            (self.flat.at[slot, 1], up_t.at[:, span]),
            (self.flat.at[slot, 2], down.at[:, span]),
            (self.sums.at[slot], shared.at[:, span]),
        ]
        return [pltpu.make_async_copy(a, b, self.store.at[slot, i]) for i, (a, b) in enumerate(pairs)]

    def resident(self):
        return [
            pltpu.make_async_copy(self.hidden, self.small_hidden, self.once.at[0]),
            pltpu.make_async_copy(self.shared, self.small_shared, self.once.at[1]),
        ]

    def begin(self):
        for c in self.resident() + self.loads(0):
            c.start()

    def part(self, p):
        if p >= self.n_parts:
            return
        if p == 0:
            for c in self.resident():
                c.wait()
        if p + 1 < self.n_parts:
            for c in self.loads(p + 1):
                c.start()
        for c in self.loads(p):
            c.wait()
        if p >= 2:
            for c in self.stores(p - 2):
                c.wait()
        slot = p % 2
        rows, grad_rows, tokens, grads = [b.at[slot] for b in self.buffers]

        def across(a, b):
            return lax.dot_general(a, b, (((0,), (0,)), ((), ())), preferred_element_type=jnp.float32)

        self.flat[slot, 0] = across(self.small_hidden[1], rows[...])
        self.flat[slot, 1] = across(self.small_hidden[2], rows[...])
        self.flat[slot, 2] = across(self.small_hidden[0], grad_rows[...])
        n = self.small_shared.shape[1] // 3
        self.sums[slot, pl.ds(0, 2 * n)] = across(self.small_shared[:, n:], tokens[...]).astype(jnp.bfloat16)
        self.sums[slot, pl.ds(2 * n, n)] = across(self.small_shared[:, :n], grads[...]).astype(jnp.bfloat16)
        for c in self.stores(p):
            c.start()

    def end(self):
        for p in (self.n_parts - 2, self.n_parts - 1):
            for c in self.stores(p):
                c.wait()


def sum_kernel(n_planes, n, *refs):
    ins, work_ins, outs, work_outs = refs[:n], refs[n : n + 6], refs[n + 6 : 2 * n + 6], refs[2 * n + 6 : 2 * n + 10]
    scratch = refs[2 * n + 10 :]
    cut = len(scratch) - 11
    spot = Spot(n_planes)
    rows = ins[0].shape[1] // 2

    def blocks(s, yy, cc, xx):
        return [a.at[dp_of(s, yy, cc) * 2 + xx] for a in ins]

    net = Reduce(spot, blocks, outs, scratch[:cut], True, rows)
    work = WeightGradients(work_ins, work_outs, scratch[cut:])
    net.start_loads()
    spot.greet()
    net.start_twins()
    work.begin()
    done = 0
    for step in range(n_planes + 2):
        for action in (net.corner, net.sides, net.column):
            j = step - (net.corner, net.sides, net.column).index(action)
            action(j)
            if 0 <= j < n_planes and done < work.n_parts:
                work.part(done)
                done += 1
    net.close()
    work.end()


def sum_everywhere(arrays, out_dtypes, work_arrays, n_dp, collective_id):
    n, n_planes = len(arrays), n_dp // 4
    shapes = [a.shape[1:] for a in arrays]
    rows, model = work_arrays[0].shape
    tokens = work_arrays[2].shape[0]
    width = work_arrays[4].shape[2]
    shared = work_arrays[5].shape[1]
    return pl.pallas_call(
        functools.partial(sum_kernel, n_planes, n),
        out_shape=[jax.ShapeDtypeStruct(s, t) for s, t in zip(shapes, out_dtypes)]
        + [
            jax.ShapeDtypeStruct((width, model), jnp.float32),
            jax.ShapeDtypeStruct((width, model), jnp.float32),
            jax.ShapeDtypeStruct((width, model), jnp.float32),
            jax.ShapeDtypeStruct((shared, model), jnp.bfloat16),
        ],
        in_specs=[ANY] * (n + 6),
        out_specs=[pl.BlockSpec(memory_space=pltpu.VMEM)] * n + [ANY] * 4,
        scratch_shapes=Reduce.scratch(shapes, [a.dtype for a in arrays], n_planes, True, shapes[0][0] // 2)
        + WeightGradients.scratch(rows, tokens, width, shared),
        compiler_params=pltpu.CompilerParams(
            collective_id=collective_id, has_side_effects=True, vmem_limit_bytes=62 << 20
        ),
    )(*arrays, *work_arrays)


def back_kernel(n_planes, axes, *refs):
    n = len(axes)
    grad_own, *inputs = refs[:18]
    probs, wq, wk, wv, wo, parts = inputs[5], *inputs[6:10], inputs[16]
    inputs = inputs[:5] + inputs[10:16]
    held = refs[-len(inputs) - 1 : -1]
    mixed, normed_one, query, key, value, cosine, sine, tokens, grad_residual, gain, small = held
    held_load = refs[-1]
    outs, grad_tokens, small_out, out_sum = refs[18 : 18 + n], *refs[18 + n : 21 + n]
    (
        grad_attn, grad_mixed, grad_query, grad_key, grad_value, gq, gk, gv, go, some_p, some_o, some_q, some_k,
        some_v, sent, received, terms, from_twin, from_side, from_across, quarter, from_planes, load, x_send, x_recv,
        p_send, p_recv,
    ) = refs[21 + n : 48 + n]
    scratch = refs[48 + n : -len(inputs) - 1]
    spot = Spot(n_planes)
    x = spot.x
    bf16, f32 = jnp.bfloat16, jnp.float32
    own_rows, model = tokens.shape
    grads = (gq, gk, gv, go)

    def weight_blocks(s, yy, cc, xx):
        i = dp_of(s, yy, cc)
        places = []
        for a, o, axis in zip(grads, outs, axes):
            size = o.shape[axis]
            span = pl.ds(pl.multiple_of(i * size, size), size)
            places.append(a.at[span] if axis == 0 else a.at[:, span])
        return places

    def token_blocks(s, yy, cc, xx):
        return [parts.at[dp_of(s, yy, cc) * 2 + xx]]

    count = 3 * n + 3
    weights = Reduce(spot, weight_blocks, outs, scratch[:count], False, direct=True)
    sums = Reduce(spot, token_blocks, [out_sum], scratch[count:], True, own_rows // 2, by_z=True)

    def swap(i, src, dst):
        return pltpu.make_async_remote_copy(
            src_ref=src, dst_ref=dst, send_sem=x_send.at[i], recv_sem=x_recv.at[i],
            device_id=spot.across, device_id_type=MESH,
        )

    def hop(i, src, dst, device):
        return pltpu.make_async_remote_copy(
            src_ref=src, dst_ref=dst, send_sem=p_send.at[i], recv_sem=p_recv.at[i],
            device_id=device, device_id_type=MESH,
        )

    lanes = terms.shape[1]

    def of_core(c):
        return terms.at[:, pl.ds(pl.multiple_of(c * (lanes // 2), lanes // 2), lanes // 2)]

    def of_side(y):
        start = spot.core * (lanes // 2) + y * (lanes // 4)
        return terms.at[:, pl.ds(pl.multiple_of(start, lanes // 4), lanes // 4)]

    def of_plane(s):
        size = lanes // 4 // n_planes
        return quarter.at[:, pl.ds(pl.multiple_of(s * size, size), size)]

    hops = [
        hop(0, of_core(1 - spot.core), from_twin, spot.twin),
        hop(1, of_side(1 - spot.y), from_side, spot.side),
        hop(2, of_side(spot.y), from_across, spot.across),
    ]
    for k in range(1, n_planes):
        s, device = spot.plane(k)
        hops.append(hop(2 + k, of_plane(s), from_planes.at[k - 1], device))

    def small_step(i):
        if i > 0:
            for h in hops[i - 1 : i] if i < 4 else hops[3:]:
                h.wait_recv()
        if i == 1:
            mine = of_core(spot.core)
            mine[...] = mine[...] + from_twin[...]
        if i == 2:
            mine = of_side(spot.y)
            mine[...] = mine[...] + from_side[...]
        if i == 3:
            quarter[...] = of_side(spot.y)[...] + from_across[...]
        if i == 4:
            total = of_plane(spot.z)[...]
            for k in range(n_planes - 1):
                total = total + from_planes[k]
            small_out[...] = total
            return
        for h in hops[i : i + 1] if i < 3 else hops[3:]:
            h.start()

    own = pltpu.make_async_copy(grad_own, grad_attn.at[x], load.at[4, 0])
    own.start()
    sums.start_loads()
    spot.greet(True)
    swap(0, grad_own, grad_attn.at[x]).start()
    sums.start_twins()
    fetched = [pltpu.make_async_copy(a, b, held_load.at[i]) for i, (a, b) in enumerate(zip(inputs, held))]
    for c in fetched:
        c.start()

    heads, head_dim = probs.shape[0], cosine.shape[1]
    kv_heads = key.shape[1] // head_dim
    group = heads // kv_heads
    chunk = some_o.shape[1]
    n_chunks = wo.shape[0] // chunk
    per_chunk = chunk // head_dim

    def load_o(c):
        return pltpu.make_async_copy(wo.at[pl.ds(c * chunk, chunk)], some_o.at[c % 2], load.at[0, c % 2])

    def load_p(h):
        return pltpu.make_async_copy(probs.at[h], some_p.at[h % 2], load.at[1, h % 2])

    load_o(0).start()
    load_p(0).start()
    sums.corner(0)
    for j in range(n_planes - 1):
        sums.sides(j)
    for c in fetched:
        c.wait()
    terms[...] = small[...]
    own.wait()
    swap(0, grad_attn.at[1 - x], grad_attn.at[1 - x]).wait_recv()
    whole = grad_attn[...].reshape(2 * own_rows, model)
    sums.corner(1)
    cos, sin = cosine[...], -sine[...]
    scale = head_dim ** -0.5
    for c in range(n_chunks):
        if c + 1 < n_chunks:
            load_o(c + 1).start()
        load_o(c).wait()
        span = slice(c * chunk, (c + 1) * chunk)
        grad_mixed[:, span] = plain_dot(whole, some_o[c % 2], ROWS_ROWS).astype(bf16)
        go[span, :] = plain_dot(mixed[:, span], whole, COLUMNS_COLUMNS).astype(bf16)
    sums.corner(2)
    for h in range(heads):
        if h + 1 < heads:
            load_p(h + 1).start()
        load_p(h).wait()
        span = slice(h * head_dim, (h + 1) * head_dim)
        shared = slice(h // group * head_dim, (h // group + 1) * head_dim)
        weight, back = some_p[h % 2], grad_mixed[:, span]
        grad_v = plain_dot(weight.astype(bf16), back, COLUMNS_COLUMNS)
        grad_p = plain_dot(back, value[:, shared], ROWS_ROWS)
        inner = jnp.sum(weight * grad_p, axis=1, keepdims=True)
        grad_s = (weight * (grad_p - inner)).astype(bf16)
        grad_q = plain_dot(grad_s, key[:, shared], ROWS_COLUMNS) * scale
        grad_query[:, span] = turn(grad_q, cos, sin).astype(bf16)
        grad_k = plain_dot(grad_s, query[:, span], COLUMNS_COLUMNS) * scale
        if h % group == 0:
            total_k, total_v = grad_k, grad_v
        else:
            total_k, total_v = total_k + grad_k, total_v + grad_v
        if h % group == group - 1:
            grad_key[:, shared] = turn(total_k, cos, sin).astype(bf16)
            grad_value[:, shared] = total_v.astype(bf16)
    sums.corner(3)
    for target, source in ((gk, grad_key), (gv, grad_value), (gq, grad_query)):
        target[...] = plain_dot(normed_one[...], source[...], COLUMNS_COLUMNS).astype(bf16)
    weights.start_twins()

    rows = some_q.shape[1]
    n_chunks = model // rows

    def load_w(c):
        span = pl.ds(c * rows, rows)
        return [
            pltpu.make_async_copy(w.at[span], b.at[c % 2], load.at[i, c % 2])
            for i, (w, b) in ((0, (wq, some_q)), (2, (wk, some_k)), (3, (wv, some_v)))
        ]

    for c in load_w(0):
        c.start()
    sums.column(0)
    sums.sides(3)
    weights.sides(0)
    other = pl.ds(pl.multiple_of((1 - x) * own_rows, own_rows), own_rows)
    mine = pl.ds(pl.multiple_of(x * own_rows, own_rows), own_rows)
    for c in range(n_chunks):
        if c + 1 < n_chunks:
            for each in load_w(c + 1):
                each.start()
        for each in load_w(c):
            each.wait()
        columns = slice(c * rows, (c + 1) * rows)
        for here, target in ((other, sent), (mine, grad_tokens)):
            total = plain_dot(grad_query[here, :], some_q[c % 2], ROWS_ROWS)
            total = total + plain_dot(grad_key[here, :], some_k[c % 2], ROWS_ROWS)
            total = total + plain_dot(grad_value[here, :], some_v[c % 2], ROWS_ROWS)
            target[:, columns] = total.astype(target.dtype)
    swap(1, sent, received).start()
    sums.column(1)
    weights.sides(1)
    sums.column(2)
    swap(1, received, received).wait_recv()
    step = 32
    gain_row = gain[...].astype(f32)
    total = jnp.zeros((1, model), f32)
    for r in range(own_rows // step):
        span = pl.ds(r * step, step)
        rows_in = tokens[span, :].astype(f32)
        grad = grad_tokens[span, :] + received[span, :].astype(f32)
        size = lax.rsqrt(jnp.mean(rows_in * rows_in, axis=1, keepdims=True) + norm_eps)
        weighted = grad * gain_row
        inner = jnp.mean(rows_in * weighted, axis=1, keepdims=True)
        total = total + jnp.sum(grad * rows_in * size, axis=0, keepdims=True)
        grad_tokens[span, :] = size * weighted - rows_in * (size * size * size) * inner + grad_residual[span, :]
    place = small.shape[0] - 8
    size = lanes // 4 // n_planes
    for i in range(4 * n_planes):
        at = (i % 2 * 2 + i // 2 % 2) * n_planes + i // 4
        terms[pl.ds(place, 1), pl.ds(at * size, size)] = total[:, i * size : (i + 1) * size]
    small_step(0)
    weights.column(0)
    small_step(1)
    weights.sides(2)
    small_step(2)
    weights.column(1)
    small_step(3)
    weights.sides(3)
    sums.column(3)
    weights.column(2)
    small_step(4)
    weights.column(3)
    for h in hops:
        h.wait_send()
    swap(0, grad_own, grad_attn.at[x]).wait_send()
    swap(1, sent, received).wait_send()
    for each in (weights, sums):
        each.close()


def backward(
    grad_own, mixed, normed_one, query, key, value, probs, weights, axes, cosine, sine, tokens, grad_residual, gain,
    small, parts, n_dp, collective_id,
):
    n, n_planes = len(weights), n_dp // 4
    bf16, f32 = jnp.bfloat16, jnp.float32
    shape, vmem_ref = jax.ShapeDtypeStruct, pltpu.VMEM
    own_rows, model = tokens.shape
    seq = 2 * own_rows
    wide, narrow_ = query.shape[1], key.shape[1]

    def part(a, axis):
        some = list(a.shape)
        some[axis] //= n_dp
        return tuple(some)

    shapes = [part(a, axis) for a, axis in zip(weights, axes)]
    tile = (small.shape[0], model // n_dp)
    block = parts.shape[1:]
    vmem = pl.BlockSpec(memory_space=pltpu.VMEM)
    dma = pltpu.SemaphoreType.DMA
    chunk = 256
    return pl.pallas_call(
        functools.partial(back_kernel, n_planes, axes),
        out_shape=[shape(s, f32) for s in shapes] + [shape((own_rows, model), f32), shape(tile, f32), shape(block, f32)],
        in_specs=[ANY] * 18,
        out_specs=[vmem] * (n + 3),
        scratch_shapes=[
            vmem_ref((2, own_rows, model), bf16),
            vmem_ref((seq, wide), bf16),
            vmem_ref((seq, wide), bf16),
            vmem_ref((seq, narrow_), bf16),
            vmem_ref((seq, narrow_), bf16),
        ]
        + [vmem_ref(w.shape, bf16) for w in weights]
        + [
            vmem_ref((2,) + probs.shape[1:], f32),
            vmem_ref((2, chunk, model), bf16),
            vmem_ref((2, chunk, wide), bf16),
            vmem_ref((2, chunk, narrow_), bf16),
            vmem_ref((2, chunk, narrow_), bf16),
            vmem_ref((own_rows, model), bf16),
            vmem_ref((own_rows, model), bf16),
            vmem_ref(small.shape, f32),
            vmem_ref((small.shape[0], model // 2), f32),
            vmem_ref((small.shape[0], model // 4), f32),
            vmem_ref((small.shape[0], model // 4), f32),
            vmem_ref((small.shape[0], model // 4), f32),
            vmem_ref((n_planes - 1,) + tile, f32),
            dma((5, 2)),
            dma((3,)),
            dma((3,)),
            dma((2 + n_planes,)),
            dma((2 + n_planes,)),
        ]
        + Reduce.scratch(shapes, [bf16] * n, n_planes, False, direct=True)
        + Reduce.scratch([block], [parts.dtype], n_planes, True, block[0] // 2, by_z=True)
        + [
            vmem_ref(a.shape, a.dtype)
            for a in (mixed, normed_one, query, key, value, cosine, sine, tokens, grad_residual, gain, small)
        ]
        + [dma((11,))],
        compiler_params=pltpu.CompilerParams(
            collective_id=collective_id, has_side_effects=True, vmem_limit_bytes=63 << 20
        ),
        cost_estimate=pl.CostEstimate(
            flops=12 * seq * model * wide, bytes_accessed=16 * n_dp * own_rows * model, transcendentals=0
        ),
    )(
        grad_own, mixed, normed_one, query, key, value, probs, *weights, cosine, sine, tokens, grad_residual, gain,
        small, parts,
    )
UNIT = 2


def dot_t(a, b):
    return lax.dot_general(a, b, (((1,), (1,)), ((), ())), preferred_element_type=jnp.float32)


def dot_f32(a, b):
    return lax.dot_general(a, b, (((1,), (0,)), ((), ())), preferred_element_type=jnp.float32)


class ExpertWork:
    def __init__(self, expert, weights, scratch):
        self.expert = expert
        self.w_gate, self.w_up, self.w_down, self.shared = weights
        (
            self.tokens, self.grads, self.rows, self.grad_rows, self.hidden, self.pre, self.left_out,
            self.left_grad, self.right_out, self.right_grad, self.out, self.back, self.shared_hidden,
        ) = scratch

    @staticmethod
    def scratch(model, width, capacity, own_rows):
        bf16 = jnp.bfloat16
        seq = 2 * own_rows
        return [
            pltpu.VMEM((2, 2 * UNIT, own_rows, model), bf16),
            pltpu.VMEM((2, 2 * UNIT, own_rows, model), bf16),
            pltpu.VMEM((2, UNIT * capacity, model), bf16),
            pltpu.VMEM((2, UNIT * capacity, model), bf16),
            pltpu.VMEM((2, 3, UNIT * capacity, width), bf16),
            pltpu.VMEM((3, UNIT * capacity, width), jnp.float32),
            pltpu.VMEM((UNIT, seq, capacity + 128), bf16),
            pltpu.VMEM((UNIT, seq, capacity + 256), bf16),
            pltpu.VMEM((UNIT, capacity + 128, model), bf16),
            pltpu.VMEM((UNIT, capacity + 256, model), bf16),
            pltpu.VMEM((2, 2 * UNIT, own_rows, model), bf16),
            pltpu.VMEM((2, 2 * UNIT, own_rows, model), bf16),
            pltpu.VMEM((2, UNIT * seq, 384), bf16),
        ]

    def prepare(self):
        capacity = self.rows.shape[1] // UNIT
        for q in range(UNIT):
            self.right_out[q, pl.ds(capacity, 128), :] = self.shared[pl.ds(256, 128), :]
            self.right_grad[q, pl.ds(capacity, 256), :] = self.shared[pl.ds(0, 256), :]

    def run(self, slot, unit, gates, grad_gates, hook):
        bf16, f32 = jnp.bfloat16, jnp.float32
        own_rows, model = self.tokens.shape[2:]
        seq = 2 * own_rows
        capacity = self.rows.shape[1] // UNIT
        experts = gates.shape[1]
        column = 1024
        n_columns = model // column
        first = unit * (2 * UNIT)
        before = lax.broadcasted_iota(jnp.int32, (seq, seq), 0) <= lax.broadcasted_iota(jnp.int32, (seq, seq), 1)
        before = before.astype(f32).astype(bf16)
        slots = lax.broadcasted_iota(jnp.int32, (capacity, seq), 0)
        picks, row_gates = [], []
        for q in range(UNIT):
            g = jnp.concatenate(
                [gates[first + 2 * q + h, pl.ds(self.expert, 1), :] for h in range(2)], axis=1
            )
            g = jnp.broadcast_to(g, (8, seq))
            taken = (g > 0.0).astype(f32)
            rank = dot_f32(taken.astype(bf16), before).astype(jnp.int32) - 1
            hit = (slots == rank[:1]) & (g[:1] > 0.0)
            pick = hit.astype(f32)
            picks.append(pick)
            row_gates.append(jnp.sum(pick * g[:1], axis=1, keepdims=True))
            self.left_out[q, :, pl.ds(0, capacity)] = pick.T.astype(bf16)
            self.left_grad[q, :, pl.ds(0, capacity)] = pick.T.astype(bf16)
            low = pick.astype(bf16)

            span = pl.ds(q * capacity, capacity)
            for source, target in ((self.tokens, self.rows), (self.grads, self.grad_rows)):
                whole = source[slot, pl.ds(2 * q, 2)].reshape(seq, model)
                target[slot, span] = dot_f32(low, whole).astype(bf16)
        row_gate = jnp.concatenate(row_gates, axis=0)
        rows, grad_rows = self.rows.at[slot], self.grad_rows.at[slot]
        self.pre[0] = dot_t(rows[...], self.w_gate[...])
        self.pre[1] = dot_t(rows[...], self.w_up[...])
        self.pre[2] = dot_t(grad_rows[...], self.w_down[...])
        hook(2)
        step = 32
        parts = []
        for r in range(UNIT * capacity // step):
            span = pl.ds(r * step, step)
            gate_pre, up_pre, grad_hidden = self.pre[0, span], self.pre[1, span], self.pre[2, span]
            gate = row_gate[r * step : (r + 1) * step]
            sig = jax.nn.sigmoid(gate_pre)
            act = gate_pre * sig
            hidden = act * up_pre
            parts.append(jnp.sum(hidden * grad_hidden, axis=1, keepdims=True))
            grad_hidden = grad_hidden * gate
            self.hidden[slot, 0, span] = (hidden * gate).astype(bf16)
            slope = sig * (1.0 + gate_pre * (1.0 - sig))
            self.hidden[slot, 1, span] = (grad_hidden * up_pre * slope).astype(bf16)
            self.hidden[slot, 2, span] = (grad_hidden * act).astype(bf16)
        grad_gate_rows = jnp.concatenate(parts, axis=0)
        mine = lax.broadcasted_iota(jnp.int32, (experts, own_rows), 0) == self.expert
        for q in range(UNIT):
            per_token = jnp.sum(picks[q] * grad_gate_rows[q * capacity : (q + 1) * capacity], axis=0, keepdims=True)
            for h in range(2):
                part = jnp.broadcast_to(per_token[:, h * own_rows : (h + 1) * own_rows], (experts, own_rows))
                grad_gates[first + 2 * q + h] = jnp.where(mine, part, 0.0)

        for q in range(UNIT):
            blocks = pl.ds(2 * q, 2)
            whole = self.tokens[slot, blocks].reshape(seq, model)
            grad = self.grads[slot, blocks].reshape(seq, model)
            pre = dot_t(whole, self.shared[pl.ds(0, 256), :])
            grad_hidden = dot_t(grad, self.shared[pl.ds(256, 128), :])
            gate_pre, up_pre = pre[:, :128], pre[:, 128:]
            sig = jax.nn.sigmoid(gate_pre)
            act = gate_pre * sig
            hidden = (act * up_pre).astype(bf16)
            grad_gate = (grad_hidden * up_pre * sig * (1.0 + gate_pre * (1.0 - sig))).astype(bf16)
            grad_up = (grad_hidden * act).astype(bf16)
            span = pl.ds(q * seq, seq)
            self.shared_hidden[slot, span, pl.ds(0, 128)] = hidden
            self.shared_hidden[slot, span, pl.ds(128, 128)] = grad_gate
            self.shared_hidden[slot, span, pl.ds(256, 128)] = grad_up
            self.left_out[q, :, pl.ds(capacity, 128)] = hidden
            self.left_grad[q, :, pl.ds(capacity, 128)] = grad_gate
            self.left_grad[q, :, pl.ds(capacity + 128, 128)] = grad_up

        hook(3)

        def combine(c, carry):
            cols = pl.ds(pl.multiple_of(c * column, column), column)
            made = dot_f32(self.hidden[slot, 0], self.w_down[:, cols]).astype(bf16)
            back = dot_f32(self.hidden[slot, 1], self.w_gate[:, cols])
            back = (back + dot_f32(self.hidden[slot, 2], self.w_up[:, cols])).astype(bf16)
            for q in range(UNIT):
                span = slice(q * capacity, (q + 1) * capacity)
                self.right_out[q, pl.ds(0, capacity), cols] = made[span]
                self.right_grad[q, pl.ds(0, capacity), cols] = back[span]
                out = dot_f32(self.left_out[q], self.right_out[q, :, cols]).astype(bf16)
                self.out[slot, pl.ds(2 * q, 2), :, cols] = out.reshape(2, own_rows, column)
                out = dot_f32(self.left_grad[q], self.right_grad[q, :, cols]).astype(bf16)
                self.back[slot, pl.ds(2 * q, 2), :, cols] = out.reshape(2, own_rows, column)

            return carry

        lax.fori_loop(0, n_columns, combine, 0)


def expert_kernel(n_dp, *refs):
    own, own_gates, _, *weights_in = refs[:7]
    normed, grads, out_parts, back_parts, grad_gates, rows_out, grad_rows_out, hidden_out, shared_out = refs[7:16]
    scratch, weights = refs[16:-13], refs[-13:-9]
    fetch, gates, load, store, local, send, recv, g_send, g_recv = refs[-9:]
    n_planes = n_dp // 4
    spot = Spot(n_planes)
    half = own.shape[0] // 2

    def views(s, yy, cc, xx, part):
        b = dp_of(s, yy, cc) * 2 + xx
        if part == ALL:
            return [normed.at[b], gates.at[b]]
        if part == FIRST:
            return [normed.at[b, pl.ds(0, half)], gates.at[b]]
        return [normed.at[b, pl.ds(half, half)]]

    def grad_views(s, yy, cc, xx, part):
        b = dp_of(s, yy, cc) * 2 + xx
        if part == ALL:
            return [grads.at[b]]
        some = 5 * own.shape[0] // 8
        if part == FIRST:
            return [grads.at[b, pl.ds(0, some)]]
        return [grads.at[b, pl.ds(some, own.shape[0] - some)]]

    kept = [
        pltpu.make_async_copy(a, v, local.at[i])
        for i, (a, v) in enumerate(zip((own, own_gates), views(spot.z, spot.y, spot.core, spot.x, ALL)))
    ]
    for c in kept:
        c.start()
    pieces = 4
    fetched = []
    for k, (a, b) in enumerate(zip(weights_in, weights)):
        size = a.shape[0] // pieces
        for p in range(pieces):
            span = pl.ds(p * size, size)
            fetched.append(pltpu.make_async_copy(a.at[span], b.at[span], fetch.at[k, p]))
    for c in fetched:
        c.start()
    spot.greet()
    copies = Copies(n_planes, send, recv)
    net = Spread(spot, copies, [own, own_gates], views, True, by_z=True)
    rest = Spread(spot, Copies(n_planes, g_send, g_recv), None, grad_views, True)
    net.begin()
    work = ExpertWork(spot.dp, weights, scratch)
    n_units = n_dp // UNIT
    blocks = 2 * UNIT
    rows = work.rows.shape[1]
    seqs = work.shared_hidden.shape[1]
    order = net.order

    def unit_of(i):
        s = 0 * i
        for j, plane in enumerate(order):
            s = s + (i // 2 == j).astype(jnp.int32) * plane
        yy = spot.y + (i % 2) * (1 - 2 * spot.y)
        return s * 2 + yy

    def loads(u, slot):
        span = pl.ds(u * blocks, blocks)
        return [
            pltpu.make_async_copy(normed.at[span], work.tokens.at[slot], load.at[slot, 0]),
            pltpu.make_async_copy(grads.at[span], work.grads.at[slot], load.at[slot, 1]),
        ]

    def stores(u, slot):
        span = pl.ds(u * blocks, blocks)
        some = pl.ds(pl.multiple_of(u * rows, rows), rows)
        pairs = [
            (work.out.at[slot], out_parts.at[span]),
            (work.back.at[slot], back_parts.at[span]),
            (work.rows.at[slot], rows_out.at[some]),
            (work.grad_rows.at[slot], grad_rows_out.at[some]),
            (work.hidden.at[slot], hidden_out.at[:, some]),
            (work.shared_hidden.at[slot], shared_out.at[pl.ds(pl.multiple_of(u * seqs, seqs), seqs)]),
        ]
        return [pltpu.make_async_copy(a, b, store.at[slot, i]) for i, (a, b) in enumerate(pairs)]

    def load_unit(i):
        for c in loads(unit_of(jnp.int32(i)), i % 2):
            c.start()

    def near(j):
        net.twin_near(j)
        if j == n_planes - 1:
            rest.twin_across(j)
        load_unit(2 * j)

    def far(j):
        net.twin_far(j)
        rest.twin_corner(j)
        if j >= n_planes - 2:
            rest.twin_side(j)
        load_unit(2 * j + 1)

    def over(j):
        if j >= n_planes - 2:
            rest.from_side(j)
        if j == n_planes - 1:
            rest.from_across(j)
        rest.over_x(j)
        rest.over_y(j)

    plan = {
        (0, 0): [(net.onward, 1)],
        (0, 2): [(net.corner, 0), (rest.corner, 0), (far, 0), (over, 1)],
        (0, 3): [(net.relay_of, 2, 0), (net.relay_of, 3, 1), (rest.onward_y, 2), (rest.onward_x, 3)],
        (1, 0): [(net.sides, 1), (net.onward, 2)],
        (1, 2): [(near, 1)],
        (1, 3): [(net.corner, 1), (net.corner_of, 2, 1), (rest.corner, 1)],
        (2, 0): [(far, 1), (over, 2), (rest.onward_y, 3)],
        (2, 3): [(net.sides, 2), (net.relay_of, 3, 0), (net.onward, 3), (net.corner_of, 3, 1)],
        (3, 0): [(near, 2)],
        (3, 2): [(net.corner_of, 2, 0), (rest.corner, 2), (over, 3)],
        (4, 0): [(net.sides, 3), (far, 2)],
        (4, 3): [(net.corner_of, 3, 0), (rest.corner, 3)],
        (5, 0): [(near, 3)],
        (6, 0): [(far, 3)],
    }

    net.relay(1)
    net.relay_of(2, 1)
    net.sides(0)
    over(0)
    for c in kept:
        c.wait()
    near(0)
    for c in fetched:
        c.wait()
    work.prepare()

    def body(i, carry):
        slot = i % 2
        u = unit_of(i)

        def hook(point):
            for (k, at), actions in plan.items():
                if at == point:

                    @pl.when(i == k)
                    def _(actions=actions):
                        for action, *values in actions:
                            action(*values)

        hook(0)

        for c in loads(u, slot):
            c.wait()

        @pl.when(i >= 2)
        def _():
            for c in stores(unit_of(i - 2), slot):
                c.wait()

        work.run(slot, u, gates, grad_gates, hook)
        for c in stores(u, slot):
            c.start()
        return carry

    lax.fori_loop(0, n_units, body, 0)
    for i in (n_units - 2, n_units - 1):
        for c in stores(unit_of(jnp.int32(i)), i % 2):
            c.wait()
    copies.close()
    rest.copies.close()


def expert_call(own, own_gates, grads, w_gate, w_up, w_down, shared, n_dp, capacity, collective_id):
    own_rows, model = own.shape
    blocks = 2 * n_dp
    width = w_down.shape[0]
    bf16 = jnp.bfloat16
    rows = n_dp * capacity
    n_planes = n_dp // 4
    vmem = pl.BlockSpec(memory_space=pltpu.VMEM)
    everyone = jax.ShapeDtypeStruct((blocks, own_rows, model), bf16)
    all_gates = (blocks,) + own_gates.shape
    return pl.pallas_call(
        functools.partial(expert_kernel, n_dp),
        out_shape=[
            everyone,
            everyone,
            everyone,
            everyone,
            jax.ShapeDtypeStruct(all_gates, jnp.float32),
            jax.ShapeDtypeStruct((rows, model), bf16),
            jax.ShapeDtypeStruct((rows, model), bf16),
            jax.ShapeDtypeStruct((3, rows, width), bf16),
            jax.ShapeDtypeStruct((blocks * own_rows, 384), bf16),
        ],
        in_specs=[ANY] * 7,
        out_specs=[ANY, ANY, ANY, ANY, vmem, ANY, ANY, ANY, ANY],
        input_output_aliases={2: 1},
        scratch_shapes=ExpertWork.scratch(model, width, capacity, own_rows)
        + [pltpu.VMEM(w.shape, bf16) for w in (w_gate, w_up, w_down, shared)]
        + [
            pltpu.SemaphoreType.DMA((4, 4)),
            pltpu.VMEM(all_gates, jnp.float32),
            pltpu.SemaphoreType.DMA((2, 2)),
            pltpu.SemaphoreType.DMA((2, 6)),
            pltpu.SemaphoreType.DMA((2,)),
            pltpu.SemaphoreType.DMA((14 * n_planes, 2)),
            pltpu.SemaphoreType.DMA((14 * n_planes, 2)),
            pltpu.SemaphoreType.DMA((14 * n_planes, 1)),
            pltpu.SemaphoreType.DMA((14 * n_planes, 1)),
        ],
        compiler_params=pltpu.CompilerParams(
            collective_id=collective_id, has_side_effects=True, vmem_limit_bytes=60 << 20
        ),
    )(own, own_gates, grads, w_gate, w_up, w_down, shared)


def gather_plan(
    tokens,
    attention_gain,
    expert_norm_gain,
    query_projection,
    key_projection,
    value_projection,
    output_projection,
    router,
    shared_gate_matrix,
    shared_up_matrix,
    shared_down_matrix,
    expert_gate_matrix,
    expert_up_matrix,
    expert_down_matrix,
    document_lengths,
    expert_indices,
    cotangent,
):
    n_dp = lax.axis_size(DP)
    x = lax.axis_index(TENSOR)
    dp = lax.axis_index(DP)
    own_rows, model_dim = tokens.shape
    sequence_length = own_rows * 2
    experts = n_dp
    top_k = expert_indices.shape[1]
    capacity = sequence_length * top_k * 4 // (3 * experts)
    bf16, f32 = jnp.bfloat16, jnp.float32

    def dot(a, b):
        return jnp.dot(a, b, preferred_element_type=f32)

    width = attention_gain.shape[0]
    lanes = 2 * width
    tile = jnp.concatenate(
        [router.T, attention_gain[None], expert_norm_gain[None], jnp.zeros((-(experts + 2) % 16, width), bf16)]
    )
    tile = lax.dynamic_update_slice(jnp.zeros((tile.shape[0], lanes), bf16), tile, (0, x * width))
    rotary_cosine, rotary_sine = rotation(sequence_length, HEAD_SIZE)
    cosine = jnp.concatenate([rotary_cosine, rotary_cosine], axis=1)
    sine = jnp.concatenate([-rotary_sine, rotary_sine], axis=1)
    doc_ends = jnp.cumsum(document_lengths[0])
    positions = jnp.arange(sequence_length, dtype=jnp.int32)
    doc_ids = jnp.sum((positions[:, None] >= doc_ends[None, :]).astype(jnp.int32), axis=-1)
    allowed = (doc_ids[:, None] == doc_ids[None, :]) & (positions[:, None] >= positions[None, :])
    own_indices = lax.dynamic_slice_in_dim(expert_indices, x * own_rows, own_rows, 0)
    chosen = jnp.any(own_indices[None] == jnp.arange(experts, dtype=jnp.int32)[:, None, None], axis=2)
    axes = (0, 0, 0, 1)
    (
        query_all, key_all, value_all, out_all, cotangent_all, params, full_one, rows_of_query, key_rows,
        rows_of_value, attn_probs, mixed_heads, residual, normed_two, gates_t,
    ) = front(
        [query_projection, key_projection, value_projection, output_projection],
        axes, tokens, tile, cotangent, chosen.astype(f32), cosine, sine, allowed.astype(f32), n_dp, 1,
    )
    router_full = params[:experts]
    first_gain = params[experts].astype(f32)
    second_gain = params[experts + 1].astype(f32)

    hidden = shared_gate_matrix.shape[1] // n_dp
    hidden_pad = -(-hidden // 16) * 16

    def slices(transposed):
        blocks = transposed.reshape(n_dp, hidden, -1)
        return jnp.pad(blocks, ((0, 0), (0, hidden_pad - hidden), (0, 0)))

    shared_out = jnp.stack(
        [slices(shared_gate_matrix.T), slices(shared_up_matrix.T), slices(shared_down_matrix)], axis=1
    )
    shared_in = lax.all_to_all(shared_out, DP, split_axis=0, concat_axis=0, tiled=True)
    shared_rows = jnp.moveaxis(shared_in, 0, 2).reshape(3, hidden_pad, model_dim)

    shared_rows = jnp.pad(shared_rows, ((0, 0), (0, 128 - hidden_pad), (0, 0))).reshape(384, model_dim)
    (
        normed_all, cotangent_all, output_parts, normed_parts, grad_gate_parts, received, grad_rows, hidden_rows,
        shared_hidden,
    ) = (
        expert_call(
            normed_two, gates_t, cotangent_all, expert_gate_matrix[0].T, expert_up_matrix[0].T, expert_down_matrix[0],
            shared_rows, n_dp, capacity, 2,
        )
    )
    (
        grad_normed_two, grad_gates_t, expert_gate_gradient, expert_up_gradient, expert_down_gradient, shared_grads,
    ) = sum_everywhere(
        [normed_parts, grad_gate_parts],
        [f32, f32],
        [
            received, grad_rows, normed_all.reshape(-1, model_dim), cotangent_all.reshape(-1, model_dim),
            hidden_rows, shared_hidden,
        ],
        n_dp, 4,
    )
    shared_grads = shared_grads.reshape(3, 128, model_dim)[:, :hidden_pad]

    gates = gates_t.T
    scale_two = lax.rsqrt(jnp.mean(residual * residual, axis=-1, keepdims=True) + norm_eps)
    grad_gates = grad_gates_t.T
    grad_logits = (
        gates * (grad_gates - jnp.sum(gates * grad_gates, axis=-1, keepdims=True))
    ).astype(bf16)
    grad_normed_two = grad_normed_two + dot(grad_logits, router_full)
    grad_router_part = dot(normed_two.T, grad_logits)
    grad_residual, grad_gain_two = rms_back(grad_normed_two, residual, scale_two, second_gain)
    grad_residual = grad_residual + cotangent.astype(f32)
    small_grads = jnp.concatenate([grad_router_part.T, jnp.zeros((8, model_dim), f32).at[1].set(grad_gain_two)])
    by_place = small_grads.reshape(-1, n_dp // 4, 2, 2, 2 * width).transpose(0, 3, 2, 1, 4)
    small_grads = by_place.reshape(small_grads.shape)
    *weight_grads, grad_inputs, small_sums, ffn_own = backward(
        grad_residual.astype(bf16), mixed_heads, full_one, rows_of_query, key_rows, rows_of_value, attn_probs,
        [query_all, key_all, value_all, out_all], axes, cosine, sine, tokens, grad_residual, first_gain[None],
        small_grads, output_parts, n_dp, 6,
    )
    output = (residual + ffn_own).astype(bf16)
    mine = lax.dynamic_slice_in_dim(small_sums, x * width, width, 1)
    gain_one_own, gain_two_own, router_own = mine[experts], mine[experts + 1], mine[:experts].T
    returned = lax.all_to_all(
        shared_grads.reshape(3, hidden_pad, n_dp, -1).transpose(2, 0, 1, 3),
        DP, split_axis=0, concat_axis=0, tiled=True,
    )[:, :, :hidden]
    returned = returned.transpose(1, 0, 2, 3).reshape(3, n_dp * hidden, -1).astype(f32)
    return (
        output,
        grad_inputs,
        gain_one_own,
        gain_two_own,
        *weight_grads,
        router_own,
        returned[0].T,
        returned[1].T,
        returned[2],
        expert_gate_gradient.T[None],
        expert_up_gradient.T[None],
        expert_down_gradient[None],
    )


def shards(*arguments):
    tokens, expert_gate_matrix = arguments[0], arguments[11]
    n_dp, n_tensor = lax.axis_size(DP), lax.axis_size(TENSOR)
    gathered = n_dp * n_tensor * tokens.shape[0] * tokens.shape[1] * 2
    if n_tensor == 2 and n_dp % 4 == 0 and expert_gate_matrix.shape[0] == 1 and gathered <= 32 << 20:
        return gather_plan(*arguments)
    return exchange_plan(*arguments)


def solution(mesh):
    placed = (
        P((DP, TENSOR), None),
        P((DP, TENSOR)),
        P((DP, TENSOR)),
        P(DP, TENSOR),
        P(DP, TENSOR),
        P(DP, TENSOR),
        P(TENSOR, DP),
        P((DP, TENSOR), None),
        P(DP, TENSOR),
        P(DP, TENSOR),
        P(TENSOR, DP),
        P(DP, None, TENSOR),
        P(DP, None, TENSOR),
        P(DP, TENSOR, None),
        P(DP, None),
        P(DP, None),
        P((DP, TENSOR), None),
    )
    return jax.shard_map(
        shards,
        mesh=mesh,
        in_specs=placed,
        out_specs=(
            P((DP, TENSOR), None),
            P((DP, TENSOR), None),
            P((DP, TENSOR)),
            P((DP, TENSOR)),
            P(DP, TENSOR),
            P(DP, TENSOR),
            P(DP, TENSOR),
            P(TENSOR, DP),
            P((DP, TENSOR), None),
            P(DP, TENSOR),
            P(DP, TENSOR),
            P(TENSOR, DP),
            P(DP, None, TENSOR),
            P(DP, None, TENSOR),
            P(DP, TENSOR, None),
        ),
        check_vma=False,
    )
```

```python
import functools
import math

import jax
import jax.numpy as jnp
from jax import lax
from jax.experimental import pallas as pl
from jax.experimental.pallas import tpu as pltpu
from jax.sharding import PartitionSpec as P

HEAD_SIZE = 128
DP, TENSOR = ("dp", "tensor")


norm_eps = 1e-06
rope_base = 600000.0
neg_big = -1e30


def silu(argument):
    return argument * jax.nn.sigmoid(argument)


def silu_slope(argument):
    sigmoid_of = jax.nn.sigmoid(argument)
    return sigmoid_of * (1.0 + argument * (1.0 - sigmoid_of))


def rotation(sequence_length, head_dim):
    half_dim = head_dim // 2
    frequency = jnp.exp(
        jnp.arange(half_dim, dtype=jnp.float32) * (-2.0 * math.log(rope_base) / head_dim)
    )
    angles = jnp.arange(sequence_length, dtype=jnp.float32)[:, None] * frequency[None, :]
    return (jnp.cos(angles), jnp.sin(angles))


def apply_rotary(tensor, rotary_cosine, rotary_sine):
    half_dim = tensor.shape[-1] // 2
    first_half = tensor[..., :half_dim]
    second_half = tensor[..., half_dim:]
    cos_rows = rotary_cosine[:, None, :]
    sin_rows = rotary_sine[:, None, :]
    return jnp.concatenate(
        [
            first_half * cos_rows - second_half * sin_rows,
            second_half * cos_rows + first_half * sin_rows,
        ],
        axis=-1,
    )


def rotate_back(tensor, rotary_cosine, rotary_sine):
    return apply_rotary(tensor, rotary_cosine, -rotary_sine)


def rms_back(grad_normed, source, scale_rows, gain_full):
    weighted = grad_normed * gain_full
    cubed = scale_rows * scale_rows * scale_rows
    grad_source = scale_rows * weighted - source * cubed * jnp.mean(
        source * weighted, axis=-1, keepdims=True
    )
    grad_gain = jnp.sum(grad_normed * source * scale_rows, axis=0)
    return (grad_source, grad_gain)


def widen(sharded):
    return lax.all_gather(sharded, TENSOR, axis=0, tiled=True)


def narrow(partial_sum):
    return lax.psum_scatter(partial_sum, TENSOR, scatter_dimension=0, tiled=True)


def dense_fetch(
    query_projection,
    key_projection,
    value_projection,
    output_projection,
    shared_gate_matrix,
    shared_up_matrix,
    shared_down_matrix,
):
    return (
        lax.all_gather(query_projection, DP, axis=0, tiled=True),
        lax.all_gather(key_projection, DP, axis=0, tiled=True),
        lax.all_gather(value_projection, DP, axis=0, tiled=True),
        lax.all_gather(output_projection, DP, axis=1, tiled=True),
        lax.all_gather(shared_gate_matrix, DP, axis=0, tiled=True),
        lax.all_gather(shared_up_matrix, DP, axis=0, tiled=True),
        lax.all_gather(shared_down_matrix, DP, axis=1, tiled=True),
    )


def expert_up_output(received_rows, expert_gate_matrix, expert_up_matrix, expert_down_matrix):
    gate_preactivation = jnp.einsum(
        "miwy,iyh->miwh", received_rows, expert_gate_matrix, preferred_element_type=jnp.float32
    )
    up_preactivation = jnp.einsum(
        "miwy,iyh->miwh", received_rows, expert_up_matrix, preferred_element_type=jnp.float32
    )
    hidden = (silu(gate_preactivation) * up_preactivation).astype(jnp.bfloat16)
    produced_rows = jnp.einsum(
        "sxcf,xfd->sxcd", hidden, expert_down_matrix, preferred_element_type=jnp.float32
    ).astype(jnp.bfloat16)
    return (produced_rows, gate_preactivation, up_preactivation)


def expert_gradients(
    received,
    received_gradient,
    gate_preactivation,
    up_preactivation,
    expert_gate_matrix,
    expert_up_matrix,
    expert_down_matrix,
):
    hidden_expert = (silu(gate_preactivation) * up_preactivation).astype(jnp.bfloat16)
    expert_down_gradient = jnp.einsum(
        "sxcf,sxcd->xfd", hidden_expert, received_gradient, preferred_element_type=jnp.float32
    )
    grad_hidden_e = jnp.einsum(
        "sxcd,xfd->sxcf", received_gradient, expert_down_matrix, preferred_element_type=jnp.float32
    )
    grad_gate_e = (grad_hidden_e * up_preactivation * silu_slope(gate_preactivation)).astype(
        jnp.bfloat16
    )
    expert_up_hidden_gradient = (grad_hidden_e * silu(gate_preactivation)).astype(jnp.bfloat16)
    expert_gate_gradient = jnp.einsum(
        "gayi,gayr->air", received, grad_gate_e, preferred_element_type=jnp.float32
    )
    expert_up_gradient = jnp.einsum(
        "gayi,gayr->air", received, expert_up_hidden_gradient, preferred_element_type=jnp.float32
    )
    output_rows_gradient = (
        jnp.einsum(
            "zkjh,klh->zkjl", grad_gate_e, expert_gate_matrix, preferred_element_type=jnp.float32
        )
        + jnp.einsum(
            "zkjh,klh->zkjl",
            expert_up_hidden_gradient,
            expert_up_matrix,
            preferred_element_type=jnp.float32,
        )
    ).astype(jnp.bfloat16)
    return (expert_gate_gradient, expert_up_gradient, expert_down_gradient, output_rows_gradient)


def exchange_plan(
    tokens,
    attention_gain,
    expert_norm_gain,
    query_projection,
    key_projection,
    value_projection,
    output_projection,
    router,
    shared_gate_matrix,
    shared_up_matrix,
    shared_down_matrix,
    expert_gate_matrix,
    expert_up_matrix,
    expert_down_matrix,
    document_lengths,
    expert_indices,
    cotangent,
):
    n_tensor = lax.axis_size(TENSOR)
    n_dp = lax.axis_size(DP)
    tensor_pos = lax.axis_index(TENSOR)
    own_rows = tokens.shape[0]
    sequence_length = own_rows * n_tensor
    model_dim = tokens.shape[1]
    exp_dev = expert_gate_matrix.shape[0]
    experts = exp_dev * n_dp
    top_k = expert_indices.shape[1]
    capacity = max(2, sequence_length * top_k * 4 // (3 * experts))
    slot_total = experts * capacity
    router_full, gain_first, gain_second = (
        lax.all_gather(router, (DP, TENSOR), axis=0, tiled=True),
        lax.all_gather(attention_gain, (DP, TENSOR), axis=0, tiled=True),
        lax.all_gather(expert_norm_gain, (DP, TENSOR), axis=0, tiled=True),
    )
    first_gain = gain_first.astype(jnp.float32)
    second_gain = gain_second.astype(jnp.float32)
    fetched = dense_fetch(
        query_projection,
        key_projection,
        value_projection,
        output_projection,
        shared_gate_matrix,
        shared_up_matrix,
        shared_down_matrix,
    )
    query_all, key_all, value_all, out_all, sgate_all, sup_all, sdown_all = fetched
    input_values = tokens.astype(jnp.float32)
    scale_one = lax.rsqrt(jnp.mean(input_values * input_values, axis=-1, keepdims=True) + norm_eps)
    normed_one = (input_values * scale_one * first_gain).astype(jnp.bfloat16)
    full_one = widen(normed_one)
    q_heads = query_all.shape[1] // HEAD_SIZE
    kv_heads = key_all.shape[1] // HEAD_SIZE
    group_size = q_heads // kv_heads
    rotary_cosine, rotary_sine = rotation(sequence_length, HEAD_SIZE)
    query_unrotated = jnp.dot(full_one, query_all, preferred_element_type=jnp.float32).reshape(
        sequence_length, q_heads, HEAD_SIZE
    )
    key_unrotated = jnp.dot(full_one, key_all, preferred_element_type=jnp.float32).reshape(
        sequence_length, kv_heads, HEAD_SIZE
    )
    rows_of_query = (
        apply_rotary(query_unrotated, rotary_cosine, rotary_sine)
        .astype(jnp.bfloat16)
        .reshape(sequence_length, kv_heads, group_size, HEAD_SIZE)
    )
    key_rows = apply_rotary(key_unrotated, rotary_cosine, rotary_sine).astype(jnp.bfloat16)
    rows_of_value = (
        jnp.dot(full_one, value_all, preferred_element_type=jnp.float32)
        .astype(jnp.bfloat16)
        .reshape(sequence_length, kv_heads, HEAD_SIZE)
    )
    doc_ends = jnp.cumsum(document_lengths[0])
    positions = jnp.arange(sequence_length, dtype=jnp.int32)
    doc_ids = jnp.sum((positions[:, None] >= doc_ends[None, :]).astype(jnp.int32), axis=-1)
    score_scale = HEAD_SIZE ** (-0.5)

    def block_scores(start_row, end_row):
        scores = (
            jnp.einsum(
                "qkgd,skd->kgqs", rows_of_query, key_rows, preferred_element_type=jnp.float32
            )
            * score_scale
        )
        allowed = (doc_ids[start_row:end_row, None] == doc_ids[None, :end_row]) & (
            positions[start_row:end_row, None] >= positions[None, :end_row]
        )
        return (scores, allowed)

    block_index = 0
    start_row = block_index * sequence_length
    end_row = start_row + sequence_length
    scores, allowed = block_scores(start_row, end_row)
    scores = jnp.where(allowed, scores, neg_big)
    row_max = jnp.max(scores, axis=-1, keepdims=True)
    exp_scores = jnp.exp(scores - row_max)
    row_sum = jnp.sum(exp_scores, axis=-1, keepdims=True)
    lse_blocks = [row_max + jnp.log(row_sum)]
    attn_probs = (exp_scores / row_sum).astype(jnp.bfloat16)
    out_blocks = jnp.einsum(
        "kgqs,skd->qkgd", attn_probs, rows_of_value, preferred_element_type=jnp.float32
    )
    mixed_heads = out_blocks.reshape(sequence_length, q_heads * HEAD_SIZE).astype(jnp.bfloat16)
    attn_part = jnp.dot(mixed_heads, out_all, preferred_element_type=jnp.float32)
    residual = input_values + narrow(attn_part)
    scale_two = lax.rsqrt(jnp.mean(residual * residual, axis=-1, keepdims=True) + norm_eps)
    normed_two = (residual * scale_two * second_gain).astype(jnp.bfloat16)
    full_two = widen(normed_two)
    logits = jnp.dot(full_two, router_full, preferred_element_type=jnp.float32)
    chosen = expert_indices[:, :, None] == jnp.arange(experts, dtype=jnp.int32)[None, None, :]
    selected = jnp.sum(jnp.where(chosen, logits[:, None, :], 0.0), axis=-1)
    top_max = jnp.max(selected, axis=-1, keepdims=True)
    gate_exp = jnp.exp(selected - top_max)
    gate_probs = gate_exp / jnp.sum(gate_exp, axis=-1, keepdims=True)
    gate_shared = jnp.dot(full_two, sgate_all, preferred_element_type=jnp.float32)
    up_shared = jnp.dot(full_two, sup_all, preferred_element_type=jnp.float32)
    hidden_shared = (silu(gate_shared) * up_shared).astype(jnp.bfloat16)
    shared_part = jnp.dot(hidden_shared, sdown_all, preferred_element_type=jnp.float32)
    flat_ids = expert_indices.reshape(-1)
    onehot = (flat_ids[:, None] == jnp.arange(experts, dtype=jnp.int32)[None, :]).astype(jnp.int32)
    slot_rank = jnp.sum(onehot * (jnp.cumsum(onehot, axis=0) - 1), axis=-1)
    slot_index = flat_ids * capacity + slot_rank
    pair_index = jnp.arange(sequence_length * top_k, dtype=jnp.int32)
    token_of_slot = jnp.zeros((slot_total,), jnp.int32).at[slot_index].set(pair_index // top_k)
    slot_used = jnp.zeros((slot_total,), jnp.bool_).at[slot_index].set(True)
    gate_of_slot = jnp.zeros((slot_total,), jnp.float32).at[slot_index].set(gate_probs.reshape(-1))
    outgoing = jnp.where(slot_used[:, None], full_two[token_of_slot], 0).reshape(
        n_dp, exp_dev, capacity, model_dim
    )
    received_rows = lax.all_to_all(outgoing, DP, split_axis=0, concat_axis=0, tiled=True)
    produced_rows, gate_preactivation, up_preactivation = expert_up_output(
        received_rows, expert_gate_matrix, expert_up_matrix, expert_down_matrix
    )
    sent_home = lax.all_to_all(produced_rows, DP, split_axis=0, concat_axis=0, tiled=True)
    returned, received, gate_preactivation, up_preactivation = (
        sent_home,
        received_rows,
        gate_preactivation,
        up_preactivation,
    )
    picked = returned.reshape(slot_total, model_dim)[slot_index].reshape(
        sequence_length, top_k, model_dim
    )
    routed_part = jnp.einsum("sk,skd->sd", gate_probs, picked, preferred_element_type=jnp.float32)
    ffn_own = narrow(shared_part + routed_part)
    output = (residual + ffn_own).astype(jnp.bfloat16)
    weights_back = dense_fetch(
        query_projection,
        key_projection,
        value_projection,
        output_projection,
        shared_gate_matrix,
        shared_up_matrix,
        shared_down_matrix,
    )
    query_back, key_back, value_back, out_back, sgate_back, sup_back, sdown_back = weights_back
    grad_out = cotangent.astype(jnp.float32)
    grad_ffn = widen(cotangent)
    grad_hidden_sh = jnp.dot(grad_ffn, sdown_back.T, preferred_element_type=jnp.float32)
    grad_sdown = jnp.dot(hidden_shared.T, grad_ffn, preferred_element_type=jnp.float32)
    grad_gate_sh = (grad_hidden_sh * up_shared * silu_slope(gate_shared)).astype(jnp.bfloat16)
    grad_up_sh = (grad_hidden_sh * silu(gate_shared)).astype(jnp.bfloat16)
    grad_sgate = jnp.dot(full_two.T, grad_gate_sh, preferred_element_type=jnp.float32)
    grad_sup = jnp.dot(full_two.T, grad_up_sh, preferred_element_type=jnp.float32)
    grad_normed_part = jnp.dot(
        grad_gate_sh, sgate_back.T, preferred_element_type=jnp.float32
    ) + jnp.dot(grad_up_sh, sup_back.T, preferred_element_type=jnp.float32)
    grad_gates_part = jnp.einsum("sd,skd->sk", grad_ffn, picked, preferred_element_type=jnp.float32)
    grad_slot = (
        jnp.where(slot_used[:, None], grad_ffn[token_of_slot] * gate_of_slot[:, None], 0.0)
        .astype(jnp.bfloat16)
        .reshape(n_dp, exp_dev, capacity, model_dim)
    )
    received_gradient = lax.all_to_all(grad_slot, DP, split_axis=0, concat_axis=0, tiled=True)
    expert_gate_gradient, expert_up_gradient, expert_down_gradient, output_rows_gradient = (
        expert_gradients(
            received,
            received_gradient,
            gate_preactivation,
            up_preactivation,
            expert_gate_matrix,
            expert_up_matrix,
            expert_down_matrix,
        )
    )
    grad_returned = lax.all_to_all(
        output_rows_gradient, DP, split_axis=0, concat_axis=0, tiled=True
    )
    grad_picked = grad_returned.reshape(slot_total, model_dim)[slot_index].reshape(
        sequence_length, top_k, model_dim
    )
    grad_normed_part = grad_normed_part + jnp.sum(grad_picked, axis=1, dtype=jnp.float32)
    grad_normed_two, grad_gates = (
        lax.psum_scatter(
            grad_normed_part.astype(jnp.bfloat16), TENSOR, scatter_dimension=0, tiled=True
        ).astype(jnp.float32),
        lax.psum_scatter(
            grad_gates_part.astype(jnp.bfloat16), TENSOR, scatter_dimension=0, tiled=True
        ).astype(jnp.float32),
    )
    row_start = tensor_pos * own_rows
    gates_own = lax.dynamic_slice_in_dim(gate_probs, row_start, own_rows, 0)
    chosen_own = lax.dynamic_slice_in_dim(chosen, row_start, own_rows, 0)
    grad_selected = gates_own * (
        grad_gates - jnp.sum(gates_own * grad_gates, axis=-1, keepdims=True)
    )
    grad_logits = jnp.sum(jnp.where(chosen_own, grad_selected[:, :, None], 0.0), axis=1).astype(
        jnp.bfloat16
    )
    grad_normed_two = grad_normed_two + jnp.dot(
        grad_logits, router_full.T, preferred_element_type=jnp.float32
    )
    grad_router_part = jnp.dot(normed_two.T, grad_logits, preferred_element_type=jnp.float32)
    grad_residual, grad_gain_two = rms_back(grad_normed_two, residual, scale_two, second_gain)
    grad_residual = grad_residual + grad_out
    grad_attn = widen(grad_residual.astype(jnp.bfloat16))
    grad_wout = jnp.dot(mixed_heads.T, grad_attn, preferred_element_type=jnp.float32)
    grad_mixed = (
        jnp.dot(grad_attn, out_back.T, preferred_element_type=jnp.float32)
        .astype(jnp.bfloat16)
        .reshape(sequence_length, kv_heads, group_size, HEAD_SIZE)
    )
    grad_keys = jnp.zeros((sequence_length, kv_heads, HEAD_SIZE), jnp.float32)
    grad_values = jnp.zeros((sequence_length, kv_heads, HEAD_SIZE), jnp.float32)
    block_index = 0
    start_row = block_index * sequence_length
    end_row = start_row + sequence_length
    scores, allowed = block_scores(start_row, end_row)
    attn_probs = jnp.where(allowed, jnp.exp(scores - lse_blocks[block_index]), 0.0)
    probs_low = attn_probs.astype(jnp.bfloat16)
    grad_values = grad_values.at[:end_row].add(
        jnp.einsum("kgqs,qkgd->skd", probs_low, grad_mixed, preferred_element_type=jnp.float32)
    )
    grad_probs = jnp.einsum(
        "qkgd,skd->kgqs", grad_mixed, rows_of_value, preferred_element_type=jnp.float32
    )
    inner_sum = jnp.sum(attn_probs * grad_probs, axis=-1, keepdims=True)
    grad_scores = (attn_probs * (grad_probs - inner_sum)).astype(jnp.bfloat16)
    grad_query_blocks = (
        jnp.einsum("kgqs,skd->qkgd", grad_scores, key_rows, preferred_element_type=jnp.float32)
        * score_scale
    )
    grad_keys = grad_keys.at[:end_row].add(
        jnp.einsum("kgqs,qkgd->skd", grad_scores, rows_of_query, preferred_element_type=jnp.float32)
        * score_scale
    )
    grad_query = grad_query_blocks.reshape(sequence_length, q_heads, HEAD_SIZE)
    grad_q_raw = (
        rotate_back(grad_query, rotary_cosine, rotary_sine)
        .astype(jnp.bfloat16)
        .reshape(sequence_length, q_heads * HEAD_SIZE)
    )
    grad_k_raw = (
        rotate_back(grad_keys, rotary_cosine, rotary_sine)
        .astype(jnp.bfloat16)
        .reshape(sequence_length, kv_heads * HEAD_SIZE)
    )
    grad_v_low = grad_values.astype(jnp.bfloat16).reshape(sequence_length, kv_heads * HEAD_SIZE)
    grad_wquery = jnp.dot(full_one.T, grad_q_raw, preferred_element_type=jnp.float32)
    grad_wkey = jnp.dot(full_one.T, grad_k_raw, preferred_element_type=jnp.float32)
    grad_wvalue = jnp.dot(full_one.T, grad_v_low, preferred_element_type=jnp.float32)
    grad_normed_one_part = (
        jnp.dot(grad_q_raw, query_back.T, preferred_element_type=jnp.float32)
        + jnp.dot(grad_k_raw, key_back.T, preferred_element_type=jnp.float32)
        + jnp.dot(grad_v_low, value_back.T, preferred_element_type=jnp.float32)
    )
    grad_normed_one = narrow(grad_normed_one_part)
    grad_inputs, grad_gain_one = rms_back(grad_normed_one, input_values, scale_one, first_gain)
    grad_inputs = grad_inputs + grad_residual
    dense_sums = (
        lax.psum_scatter(grad_wquery, DP, scatter_dimension=0, tiled=True),
        lax.psum_scatter(grad_wkey, DP, scatter_dimension=0, tiled=True),
        lax.psum_scatter(grad_wvalue, DP, scatter_dimension=0, tiled=True),
        lax.psum_scatter(grad_wout, DP, scatter_dimension=1, tiled=True),
        lax.psum_scatter(grad_sgate, DP, scatter_dimension=0, tiled=True),
        lax.psum_scatter(grad_sup, DP, scatter_dimension=0, tiled=True),
        lax.psum_scatter(grad_sdown, DP, scatter_dimension=1, tiled=True),
    )
    small_sums = (
        lax.psum_scatter(grad_router_part, (DP, TENSOR), scatter_dimension=0, tiled=True),
        lax.psum_scatter(grad_gain_one, (DP, TENSOR), scatter_dimension=0, tiled=True),
        lax.psum_scatter(grad_gain_two, (DP, TENSOR), scatter_dimension=0, tiled=True),
    )
    return (
        output,
        grad_inputs,
        small_sums[1],
        small_sums[2],
        dense_sums[0],
        dense_sums[1],
        dense_sums[2],
        dense_sums[3],
        small_sums[0],
        dense_sums[4],
        dense_sums[5],
        dense_sums[6],
        expert_gate_gradient,
        expert_up_gradient,
        expert_down_gradient,
    )


MESH = pl.DeviceIdType.MESH
ANY = pl.BlockSpec(memory_space=pl.ANY)


def when(condition, body):
    if condition is None:
        body()
    else:
        pl.when(condition)(body)


class Spot:
    def __init__(self, n_planes):
        dp = lax.axis_index(DP)
        self.x = lax.axis_index(TENSOR)
        self.dp = dp
        self.core = dp % 2
        self.y = (dp // 2) % 2
        self.z = dp // 4
        self.n_planes = n_planes
        self.has_up = self.z < n_planes - 1
        self.has_down = self.z > 0
        self.up = (dp + 4, self.x)
        self.down = (dp - 4, self.x)
        self.side = (dp + 2 - 4 * self.y, self.x)
        self.across = (dp, 1 - self.x)
        self.twin = (dp + 1 - 2 * self.core, self.x)

    def far_first(self):
        low, high = 0 * self.z, 0 * self.z + self.n_planes - 1
        order = []
        for _ in range(self.n_planes):
            take_low = (self.z - low >= high - self.z).astype(jnp.int32)
            order.append(take_low * low + (1 - take_low) * high)
            low, high = low + take_low, high - (1 - take_low)
        return order

    def plane(self, k):
        s = (self.z + k) % self.n_planes
        return s, (s * 4 + self.dp % 4, self.x)

    def greet(self, all_planes=False):
        barrier = pltpu.get_barrier_semaphore()
        if all_planes:
            peers = [self.side, self.twin, self.across] + [self.plane(k)[1] for k in range(1, self.n_planes)]
            for device in peers:
                pl.semaphore_signal(barrier, inc=1, device_id=device, device_id_type=MESH)
            pl.semaphore_wait(barrier, len(peers))
            return
        fixed = [self.side, self.twin, self.across]
        for device in fixed:
            pl.semaphore_signal(barrier, inc=1, device_id=device, device_id_type=MESH)
        for condition, device in ((self.has_up, self.up), (self.has_down, self.down)):

            @pl.when(condition)
            def _(device=device):
                pl.semaphore_signal(barrier, inc=1, device_id=device, device_id_type=MESH)

        ends = self.has_up.astype(jnp.int32) + self.has_down.astype(jnp.int32)
        pl.semaphore_wait(barrier, len(fixed) + ends)


class Copies:
    def __init__(self, n_planes, send, recv):
        self.n_planes, self.send, self.recv = n_planes, send, recv
        self.open = []

    def copy(self, group, s, piece, src, dst, device, arrival=None):
        arrival = group if arrival is None else arrival
        return pltpu.make_async_remote_copy(
            src_ref=src,
            dst_ref=dst,
            send_sem=self.send.at[group * self.n_planes + s, piece],
            recv_sem=self.recv.at[arrival * self.n_planes + s, piece],
            device_id=device,
            device_id_type=MESH,
        )

    def start(self, condition, group, s, sources, targets, device, arrival=None):
        def body():
            for i, (src, dst) in enumerate(zip(sources, targets)):
                self.copy(group, s, i, src, dst, device, arrival).start()

        when(condition, body)
        self.open.append((condition, group, s, sources, targets, device, arrival))

    def arrive(self, group, s, targets, device):
        for i, dst in enumerate(targets):
            self.copy(group, s, i, dst, dst, device).wait_recv()

    def close(self):
        for condition, group, s, sources, targets, device, arrival in self.open:

            def body():
                for i, (src, dst) in enumerate(zip(sources, targets)):
                    self.copy(group, s, i, src, dst, device, arrival).wait_send()

            when(condition, body)


(Z_UP, Z_DOWN, Y_ALL, Y_HALF, X_ALL, X_HALF, C_OWN, C_Y, C_X, C_XH, C_YH, D_UP, D_DOWN, C_D) = range(14)
(ALL, FIRST, SECOND) = range(3)


class Spread:
    def __init__(self, spot, copies, own, views, use_x, by_z=False):
        self.spot, self.copies, self.own, self.use_x, self.by_z = spot, copies, own, use_x, by_z
        self.order = spot.far_first()[::-1]
        y, x, core = spot.y, spot.x, spot.core

        def places(s, cc):
            return (
                views(s, y, cc, x, ALL),
                views(s, 1 - y, cc, x, ALL),
                views(s, 1 - y, cc, x, FIRST),
                views(s, y, cc, 1 - x, ALL),
                views(s, y, cc, 1 - x, SECOND),
                views(s, 1 - y, cc, 1 - x, FIRST),
                views(s, 1 - y, cc, 1 - x, SECOND),
                views(s, 1 - y, cc, 1 - x, ALL),
            )

        self.mine = [places(s, core) for s in self.order]
        self.twins = [places(s, 1 - core) for s in self.order]
        self.goes_down = [(s > spot.z) & spot.has_down for s in self.order]
        self.goes_up = [(s < spot.z) & spot.has_up for s in self.order]
        middle = spot.has_up & spot.has_down
        self.among = (jnp.logical_not(middle), middle)
        self.goes = {
            (j, c): (self.goes_down[j] & self.among[c], self.goes_up[j] & self.among[c], self.among[c])
            for j in range(len(self.order))
            for c in (0, 1)
        }

    def place(self, j):
        return self.own if j == 0 else self.mine[j][0]

    def onward_y(self, j):
        self.copies.start(None, Y_ALL, self.order[j], self.place(j), self.mine[j][0], self.spot.side)

    def onward_x(self, j):
        self.copies.start(None, X_ALL, self.order[j], self.place(j), self.mine[j][0], self.spot.across)

    def onward_twin(self, j):
        self.copies.start(None, C_OWN, self.order[j], self.place(j), self.mine[j][0], self.spot.twin)

    def onward(self, j):
        self.onward_y(j)
        if self.use_x:
            self.onward_x(j)
        self.onward_twin(j)

    def begin_z(self):
        spot, here = self.spot, self.mine[0][0]
        self.copies.start(spot.has_up, Z_UP, spot.z, self.own, here, spot.up)
        self.copies.start(spot.has_down, Z_DOWN, spot.z, self.own, here, spot.down, Z_UP)

    def begin(self):
        self.begin_z()
        self.onward(0)

    def relay(self, j, goes=None):
        s, here, spot = self.order[j], self.mine[j][0], self.spot
        goes_down, goes_up, _ = goes or (self.goes_down[j], self.goes_up[j], None)
        self.copies.arrive(Z_UP, s, here, spot.up)
        self.copies.start(goes_down, Z_DOWN, s, here, here, spot.down, Z_UP)
        self.copies.start(goes_up, Z_UP, s, here, here, spot.up)

    def relay_of(self, j, c):
        pl.when(self.among[c])(functools.partial(self.relay, j, self.goes[j, c]))

    def corner_of(self, j, c):
        pl.when(self.among[c])(functools.partial(self.corner, j, self.goes[j, c]))

    def column(self, j):
        if j < len(self.order):
            self.relay(j)
            self.onward(j)

    def from_side(self, j):
        s, there, spot = self.order[j], self.mine[j][1], self.spot
        self.copies.arrive(Y_ALL, s, there, spot.side)
        self.copies.start(None, C_Y, s, there, there, spot.twin)

    def from_across(self, j):
        s, there, spot = self.order[j], self.mine[j][3], self.spot
        self.copies.arrive(X_ALL, s, there, spot.across)
        self.copies.start(None, C_X, s, there, there, spot.twin)

    def over_x(self, j):
        part = self.mine[j][2]
        self.copies.start(None, X_HALF, self.order[j], part, part, self.spot.across)

    def over_y(self, j):
        part = self.mine[j][4]
        self.copies.start(None, Y_HALF, self.order[j], part, part, self.spot.side)

    def side(self, j):
        self.from_side(j)
        if self.use_x and (j == 0 or not self.by_z):
            self.over_x(j)

    def across(self, j):
        self.from_across(j)
        if j == 0 or not self.by_z:
            self.over_y(j)

    def sides(self, j):
        if 0 <= j < len(self.order):
            self.side(j)
            if self.use_x:
                self.across(j)

    def corner(self, j, goes=None):
        if not self.use_x or not 0 <= j < len(self.order):
            return
        s, spot = self.order[j], self.spot
        first, second, whole = self.mine[j][5:]
        if self.by_z and j > 0:
            goes_down, goes_up, always = goes or (self.goes_down[j], self.goes_up[j], None)
            self.copies.arrive(D_UP, s, whole, spot.up)
            self.copies.start(goes_down, D_DOWN, s, whole, whole, spot.down, D_UP)
            self.copies.start(goes_up, D_UP, s, whole, whole, spot.up)
            self.copies.start(always, C_D, s, whole, whole, spot.twin)
            return
        self.copies.arrive(X_HALF, s, first, spot.across)
        self.copies.start(None, C_XH, s, first, first, spot.twin)
        self.copies.arrive(Y_HALF, s, second, spot.side)
        self.copies.start(None, C_YH, s, second, second, spot.twin)
        if self.by_z:
            self.copies.start(spot.has_up, D_UP, s, whole, whole, spot.up)
            self.copies.start(spot.has_down, D_DOWN, s, whole, whole, spot.down, D_UP)

    def twin_own(self, j):
        self.copies.arrive(C_OWN, self.order[j], self.twins[j][0], self.spot.twin)

    def twin_across(self, j):
        self.copies.arrive(C_X, self.order[j], self.twins[j][3], self.spot.twin)

    def twin_near(self, j):
        self.twin_own(j)
        if self.use_x:
            self.twin_across(j)

    def twin_side(self, j):
        self.copies.arrive(C_Y, self.order[j], self.twins[j][1], self.spot.twin)

    def twin_corner(self, j):
        if self.by_z and j > 0:
            self.copies.arrive(C_D, self.order[j], self.twins[j][7], self.spot.twin)
            return
        self.copies.arrive(C_XH, self.order[j], self.twins[j][5], self.spot.twin)
        self.copies.arrive(C_YH, self.order[j], self.twins[j][6], self.spot.twin)

    def twin_far(self, j):
        self.twin_side(j)
        if self.use_x:
            self.twin_corner(j)

    def twin_all(self):
        for j in range(len(self.order)):
            self.twin_near(j)
            self.twin_far(j)

    def stage(self, step):
        self.column(step)
        self.sides(step - 1)
        self.corner(step - 2)

    def run(self):
        self.begin()
        for step in range(1, len(self.order) + 2):
            self.stage(step)
        self.twin_all()
        self.copies.close()


def dp_of(s, yy, cc):
    return (s * 2 + yy) * 2 + cc


def plain_dot(a, b, contract):
    return lax.dot_general(a, b, (contract, ((), ())), preferred_element_type=jnp.float32)


ROWS_COLUMNS = ((1,), (0,))
ROWS_ROWS = ((1,), (1,))
COLUMNS_COLUMNS = ((0,), (0,))


def turn(heads, cosine, sine):
    return heads * cosine + pltpu.roll(heads, heads.shape[1] // 2, 1) * sine


def front_kernel(n_planes, axes, *refs):
    n = len(axes)
    shards_in, (tokens, tile, grads, chosen, cosine, sine, allowed) = refs[:n], refs[n : n + 7]
    outs = refs[n + 7 : 2 * n + 7]
    all_grads, params, *kept_out, residual, normed_two, gates = refs[2 * n + 7 : 2 * n + 18]
    normed_one, query, key, value, probs, mixed = refs[-7:-1]
    out_sems = refs[-1]
    (
        wq, wk, wv, wo, sequence, pair, sent, received, w_send, w_recv, p_send, p_recv, g_send, g_recv, local,
        x_send, x_recv,
    ) = refs[2 * n + 18 : -7]
    spot = Spot(n_planes)
    x = spot.x
    bf16, f32 = jnp.bfloat16, jnp.float32
    own_rows, model = tokens.shape

    def weight_views(s, yy, cc, xx, part):
        i = dp_of(s, yy, cc)
        places = []
        for o, a, axis in zip((wq, wk, wv, wo), shards_in, axes):
            size = a.shape[axis]
            span = pl.ds(pl.multiple_of(i * size, size), size)
            places.append(o.at[span] if axis == 0 else o.at[:, span])
        return places

    def param_views(s, yy, cc, xx, part):
        size = tile.shape[1]
        return [params.at[:, pl.ds(pl.multiple_of(dp_of(s, yy, cc) * size, size), size)]]

    def grad_views(s, yy, cc, xx, part):
        b = dp_of(s, yy, cc) * 2 + xx
        if part == ALL:
            return [all_grads.at[b]]
        return [all_grads.at[b, pl.ds(0 if part == FIRST else own_rows // 2, own_rows // 2)]]

    def mine(views):
        return views(spot.z, spot.y, spot.core, x, ALL)

    def swap(i, src, dst):
        return pltpu.make_async_remote_copy(
            src_ref=src, dst_ref=dst, send_sem=x_send.at[i], recv_sem=x_recv.at[i],
            device_id=spot.across, device_id_type=MESH,
        )

    kept = list(zip(list(shards_in) + [tokens, grads, tile], mine(weight_views) + [sequence.at[x]] + mine(grad_views) + [pair.at[x]]))
    kept = [pltpu.make_async_copy(a, b, local.at[i]) for i, (a, b) in enumerate(kept)]
    for c in kept:
        c.start()
    spot.greet()
    swaps = [swap(0, tile, pair.at[x]), swap(1, tokens, sequence.at[x]), swap(2, sent, received)]
    swaps[0].start()
    weights = Spread(spot, Copies(n_planes, w_send, w_recv), list(shards_in), weight_views, False)
    small = Spread(spot, Copies(n_planes, p_send, p_recv), mine(param_views), param_views, False)
    net = Spread(spot, Copies(n_planes, g_send, g_recv), [grads], grad_views, True)
    weights.begin()
    swaps[1].start()
    for c in kept:
        c.wait()
    swap(0, pair.at[1 - x], pair.at[1 - x]).wait_recv()
    mine(param_views)[0][...] = pair[0] + pair[1]
    small.begin()
    net.onward_x(0)
    net.onward_twin(0)
    for step in range(1, n_planes + 1):
        weights.stage(step)
        small.stage(step)
        if step == n_planes - 1:
            net.begin_z()
    net.onward_y(0)
    net.from_across(0)

    net.relay(1)
    net.relay_of(2, 1)
    net.onward_x(1)
    net.onward_twin(1)

    small.twin_all()
    swap(1, sequence.at[1 - x], sequence.at[1 - x]).wait_recv()

    experts = chosen.shape[0]
    first_gain = params[experts : experts + 1, :].astype(f32)
    step = 32
    for h in range(2):
        for r in range(own_rows // step):
            rows = sequence[h, pl.ds(r * step, step)].astype(f32)
            scale = lax.rsqrt(jnp.mean(rows * rows, axis=1, keepdims=True) + norm_eps)
            normed_one[pl.ds(h * own_rows + r * step, step)] = (rows * scale * first_gain).astype(bf16)
    weights.twin_all()
    pairs = list(zip((wq, wk, wv, wo), outs)) + list(zip((normed_one, query, key, value, probs, mixed), kept_out))
    written = [pltpu.make_async_copy(a, b, out_sems.at[i]) for i, (a, b) in enumerate(pairs)]
    for c in written[: n + 1]:
        c.start()
    heads, head_dim = query.shape[1] // cosine.shape[1], cosine.shape[1]
    kv_heads = key.shape[1] // head_dim
    group = heads // kv_heads
    cos, sin = cosine[...], sine[...]
    raw = plain_dot(normed_one[...], wk[...], ROWS_COLUMNS)
    for g in range(kv_heads):
        span = slice(g * head_dim, (g + 1) * head_dim)
        key[:, span] = turn(raw[:, span], cos, sin).astype(bf16)
    value[...] = plain_dot(normed_one[...], wv[...], ROWS_COLUMNS).astype(bf16)
    raw = plain_dot(normed_one[...], wq[...], ROWS_COLUMNS)
    for h in range(heads):
        span = slice(h * head_dim, (h + 1) * head_dim)
        query[:, span] = turn(raw[:, span], cos, sin).astype(bf16)
    net.from_side(0)
    net.onward_y(1)
    net.relay_of(2, 0)
    net.relay_of(3, 1)
    net.onward_twin(2)
    net.from_across(1)
    may = allowed[...] > 0.0
    for h in range(heads):
        span = slice(h * head_dim, (h + 1) * head_dim)
        shared = slice(h // group * head_dim, (h // group + 1) * head_dim)
        scores = plain_dot(query[:, span], key[:, shared], ROWS_ROWS) * (head_dim ** -0.5)
        scores = jnp.where(may, scores, neg_big)
        weight = jnp.exp(scores - jnp.max(scores, axis=1, keepdims=True))
        weight = weight / jnp.sum(weight, axis=1, keepdims=True)
        probs[h] = weight
        mixed[:, span] = plain_dot(weight.astype(bf16), value[:, shared], ROWS_COLUMNS).astype(bf16)
    for c in written[n + 1 :]:
        c.start()
    other = mixed[pl.ds(pl.multiple_of((1 - x) * own_rows, own_rows), own_rows), :]
    sent[...] = plain_dot(other, wo[...], ROWS_COLUMNS).astype(bf16)
    swaps[2].start()
    other = mixed[pl.ds(pl.multiple_of(x * own_rows, own_rows), own_rows), :]
    residual[...] = plain_dot(other, wo[...], ROWS_COLUMNS)
    net.relay_of(3, 0)
    net.onward_twin(3)
    net.from_side(1)
    swap(2, received, received).wait_recv()
    second_gain = params[experts + 1 : experts + 2, :].astype(f32)
    for r in range(own_rows // step):
        span = pl.ds(r * step, step)
        rows = sequence[x, span].astype(f32) + (residual[span] + received[span].astype(f32))
        residual[span] = rows
        scale = lax.rsqrt(jnp.mean(rows * rows, axis=1, keepdims=True) + norm_eps)
        normed_two[span] = (rows * scale * second_gain).astype(bf16)
    logits = plain_dot(params[:experts, :], normed_two[...], ROWS_ROWS)
    picked = chosen[...] > 0.0
    top = jnp.max(jnp.where(picked, logits, neg_big), axis=0, keepdims=True)
    weight = jnp.where(picked, jnp.exp(jnp.where(picked, logits - top, 0.0)), 0.0)
    gates[...] = weight / jnp.sum(weight, axis=0, keepdims=True)

    for j in range(n_planes):
        net.twin_own(j)
        if j < n_planes - 2:
            net.twin_across(j)
        if j < n_planes - 2:
            net.twin_side(j)
    for each in (weights, small, net):
        each.copies.close()
    for c in swaps:
        c.wait_send()
    for c in written:
        c.wait()


def front(arrays, axes, tokens, tile, grads, chosen, cosine, sine, allowed, n_dp, collective_id):
    n, n_planes = len(arrays), n_dp // 4
    bf16, f32 = jnp.bfloat16, jnp.float32
    shape = jax.ShapeDtypeStruct

    def whole(a, axis):
        full = list(a.shape)
        full[axis] *= n_dp
        return shape(tuple(full), a.dtype)

    own_rows, model = tokens.shape
    seq = 2 * own_rows
    experts = chosen.shape[0]
    wide, narrow_ = arrays[0].shape[1], arrays[1].shape[1]
    heads = wide // cosine.shape[1]
    gathered = [whole(a, axis) for a, axis in zip(arrays, axes)]
    vmem = pl.BlockSpec(memory_space=pltpu.VMEM)
    dma = pltpu.SemaphoreType.DMA
    return pl.pallas_call(
        functools.partial(front_kernel, n_planes, axes),
        out_shape=gathered
        + [
            shape((2 * n_dp,) + grads.shape, bf16),
            shape((tile.shape[0], tile.shape[1] * n_dp), bf16),
            shape((seq, model), bf16),
            shape((seq, wide), bf16),
            shape((seq, narrow_), bf16),
            shape((seq, narrow_), bf16),
            shape((heads, seq, seq), f32),
            shape((seq, wide), bf16),
            shape((own_rows, model), f32),
            shape((own_rows, model), bf16),
            shape((experts, own_rows), f32),
        ],
        in_specs=[ANY] * (n + 3) + [vmem] * 4,
        out_specs=[ANY] * (n + 1) + [vmem] + [ANY] * 6 + [vmem] * 3,
        scratch_shapes=[pltpu.VMEM(g.shape, bf16) for g in gathered]
        + [
            pltpu.VMEM((2, own_rows, model), bf16),
            pltpu.VMEM((2,) + tile.shape, bf16),
            pltpu.VMEM((own_rows, model), bf16),
            pltpu.VMEM((own_rows, model), bf16),
        ]
        + [dma((14 * n_planes, n))] * 2
        + [dma((14 * n_planes, 1))] * 4
        + [dma((n + 3,)), dma((3,)), dma((3,))]
        + [
            pltpu.VMEM((seq, model), bf16),
            pltpu.VMEM((seq, wide), bf16),
            pltpu.VMEM((seq, narrow_), bf16),
            pltpu.VMEM((seq, narrow_), bf16),
            pltpu.VMEM((heads, seq, seq), f32),
            pltpu.VMEM((seq, wide), bf16),
            dma((n + 6,)),
        ],
        compiler_params=pltpu.CompilerParams(
            collective_id=collective_id, has_side_effects=True, vmem_limit_bytes=56 << 20
        ),
        cost_estimate=pl.CostEstimate(
            flops=6 * seq * model * wide, bytes_accessed=16 * n_dp * own_rows * model, transcendentals=heads * seq * seq
        ),
    )(*arrays, tokens, tile, grads, chosen, cosine, sine, allowed)


(T_YX, T_Y, T_X, T_OWN, R_XHALF, R_YHALF, R_YALL, R_XALL, R_UP, R_DOWN, R_DUP, R_DDOWN) = range(12)


def add_up(target, sources):
    rows = target.shape[0]
    step = 16 if rows % 16 == 0 else rows

    def body(i, carry):
        span = pl.ds(pl.multiple_of(i * step, step), step)
        total = sources[0][span, :].astype(jnp.float32)
        for source in sources[1:]:
            total = total + source[span, :].astype(jnp.float32)
        target[span, :] = total.astype(target.dtype)
        return carry

    lax.fori_loop(0, rows // step, body, 0)


class Reduce:
    @staticmethod
    def scratch(shapes, dtypes, n_planes, use_x, cut=0, direct=False, by_z=False):
        kinds = 4 if use_x else 2
        out = []
        for i, (shape, dtype) in enumerate(zip(shapes, dtypes)):
            rows = cut if i == 0 else shape[0]
            out.append(pltpu.VMEM((kinds, n_planes) + shape, dtype))
            out.append(pltpu.VMEM((n_planes + 1,) + shape, dtype))
            out.append(pltpu.VMEM((n_planes,) + shape, dtype))
            if not direct:
                out.append(pltpu.VMEM((kinds, 2) + shape, dtype))
            if use_x:
                out.append(pltpu.VMEM((n_planes,) + shape, dtype))
                out.append(pltpu.VMEM((1 if by_z else n_planes, rows) + shape[1:], dtype))
                if by_z:
                    out.append(pltpu.VMEM((n_planes + 1,) + shape, dtype))
                if i == 0 and cut < shape[0]:
                    out.append(pltpu.VMEM((1 if by_z else n_planes, shape[0] - cut) + shape[1:], dtype))
        n = len(shapes)
        out.append(pltpu.SemaphoreType.DMA((12 * n_planes, n)))
        out.append(pltpu.SemaphoreType.DMA((12 * n_planes, n)))
        out.append(pltpu.SemaphoreType.DMA((kinds * n_planes, n)))
        return out

    def __init__(self, spot, blocks, outs, scratch, use_x, cut=0, direct=False, by_z=False):
        self.spot, self.outs, self.use_x, self.direct, self.by_z = spot, outs, use_x, direct, by_z
        self.slant = []
        self.n, self.n_planes, self.cut = len(outs), spot.n_planes, cut
        left = list(scratch)
        self.twin, self.line, self.near, self.ring, self.across, self.first = [], [], [], [], [], []
        self.second = None
        for i in range(self.n):
            self.twin.append(left.pop(0))
            self.line.append(left.pop(0))
            self.near.append(left.pop(0))
            if not direct:
                self.ring.append(left.pop(0))
            if use_x:
                self.across.append(left.pop(0))
                self.first.append(left.pop(0))
                if by_z:
                    self.slant.append(left.pop(0))
                if i == 0 and cut < self.near[0].shape[1]:
                    self.second = left.pop(0)
        send, recv, self.local = left
        self.copies = Copies(self.n_planes, send, recv)
        y, x, core = spot.y, spot.x, spot.core
        self.order = spot.far_first()
        places = {T_YX: (1 - y, 1 - x), T_Y: (1 - y, x), T_X: (y, 1 - x), T_OWN: (y, x)}
        self.kinds = [T_YX, T_Y, T_X, T_OWN] if use_x else [T_Y, T_OWN]
        every = [(k, j) for j in range(self.n_planes) for k in self.kinds]
        self.terms = {(k, j): blocks(self.order[j], places[k][0], core, places[k][1]) for k, j in every}
        self.others = {(k, j): blocks(self.order[j], places[k][0], 1 - core, places[k][1]) for k, j in every}

    def load(self, kind, j):
        k, s = self.kinds.index(kind), self.order[j]
        return [
            pltpu.make_async_copy(ref, self.ring[i].at[k, j % 2], self.local.at[k * self.n_planes + s, i])
            for i, ref in enumerate(self.terms[kind, j])
        ]

    def start_load(self, kind, j):
        if not self.direct and j < self.n_planes:
            for c in self.load(kind, j):
                c.start()

    def start_loads(self):
        for j in range(2):
            for kind in self.kinds:
                self.start_load(kind, j)

    def start_twins(self):
        for j in range(self.n_planes):
            s = self.order[j]
            for k, kind in enumerate(self.kinds):
                self.copies.start(None, kind, s, self.others[kind, j], [t.at[k, s] for t in self.twin], self.spot.twin)

    def ready(self, kind, j):
        k, s = self.kinds.index(kind), self.order[j]
        twin = [t.at[k, s] for t in self.twin]
        self.copies.arrive(kind, s, twin, self.spot.twin)
        if self.direct:
            return twin, self.terms[kind, j]
        for c in self.load(kind, j):
            c.wait()
        return twin, [r.at[k, j % 2] for r in self.ring]

    def along(self, j, here, line, targets, up, down):
        s, spot, copies = self.order[j], self.spot, self.copies
        some = [t.at[s] for t in line]
        below = [t.at[self.n_planes] for t in line]

        def add_all(*more):
            for i in range(self.n):
                add_up(targets[i], here[i] + [m[i] for m in more])

        if j == self.n_planes - 1:
            when(spot.has_up, lambda: copies.arrive(down, s, some, spot.up))
            when(spot.has_down, lambda: copies.arrive(up, s, below, spot.down))
            when(spot.has_up & spot.has_down, lambda: add_all(some, below))
            when(spot.z == 0, lambda: add_all(some))
            when(spot.z == self.n_planes - 1, lambda: add_all(below))
            return
        for goes, more, group, last, device, source in (
            (s < spot.z, spot.has_up, down, None, spot.down, spot.up),
            (s > spot.z, spot.has_down, up, s - spot.z == 1, spot.up, spot.down),
        ):

            def partial():
                copies.arrive(group, s, some, source)
                add_all(some)

            when(goes & more, partial)
            when(goes & jnp.logical_not(more), add_all)
            if last is None:
                copies.start(goes, group, s, targets, some, device)
            else:
                copies.start(goes & last, group, s, targets, below, device)
                copies.start(goes & jnp.logical_not(last), group, s, targets, some, device)

    def corner(self, j):
        if not self.use_x or not 0 <= j < self.n_planes:
            return
        s, cut = self.order[j], self.cut
        twin, mine = self.ready(T_YX, j)
        if self.by_z:
            self.along(j, [[m, t] for m, t in zip(mine, twin)], self.slant, twin, R_DUP, R_DDOWN)
        else:
            for m, t in zip(mine, twin):
                add_up(t, [m, t])
        self.start_load(T_YX, j + 2)
        if self.by_z and j < self.n_planes - 1:
            return
        p = 0 if self.by_z else s
        head = twin if self.second is None else [twin[0].at[pl.ds(0, cut)]] + twin[1:]
        self.copies.start(None, R_XHALF, s, head, [f.at[p] for f in self.first], self.spot.across)
        if self.second is not None:
            tail = [twin[0].at[pl.ds(cut, self.second.shape[1])]]
            self.copies.start(None, R_YHALF, s, tail, [self.second.at[p]], self.spot.side)

    def side(self, j):
        s, cut = self.order[j], self.cut
        twin, mine = self.ready(T_Y, j)
        over = self.use_x and (j == self.n_planes - 1 or not self.by_z)
        p = 0 if self.by_z else s
        if over:
            first = [f.at[p] for f in self.first]
            self.copies.arrive(R_XHALF, s, first, self.spot.across)
        for i, (m, t) in enumerate(zip(mine, twin)):
            if not over:
                add_up(t, [m, t])
            elif i == 0 and self.second is not None:
                a, b = pl.ds(0, cut), pl.ds(cut, self.second.shape[1])
                add_up(t.at[a], [m.at[a], t.at[a], first[0]])
                add_up(t.at[b], [m.at[b], t.at[b]])
            else:
                add_up(t, [m, t, first[i]])
        self.start_load(T_Y, j + 2)
        self.copies.start(None, R_YALL, s, twin, [t.at[s] for t in self.near], self.spot.side)

    def over(self, j):
        s, cut = self.order[j], self.cut
        twin, mine = self.ready(T_X, j)
        over = self.second is not None and (j == self.n_planes - 1 or not self.by_z)
        p = 0 if self.by_z else s
        if over:
            self.copies.arrive(R_YHALF, s, [self.second.at[p]], self.spot.side)
        for i, (m, t) in enumerate(zip(mine, twin)):
            if i == 0 and over:
                a, b = pl.ds(0, cut), pl.ds(cut, self.second.shape[1])
                add_up(t.at[a], [m.at[a], t.at[a]])
                add_up(t.at[b], [m.at[b], t.at[b], self.second.at[p]])
            else:
                add_up(t, [m, t])
        self.start_load(T_X, j + 2)
        self.copies.start(None, R_XALL, s, twin, [t.at[s] for t in self.across], self.spot.across)

    def sides(self, j):
        if 0 <= j < self.n_planes:
            self.side(j)
            if self.use_x:
                self.over(j)

    def column(self, j):
        if not 0 <= j < self.n_planes:
            return
        s, spot, copies = self.order[j], self.spot, self.copies
        twin, mine = self.ready(T_OWN, j)
        near = [t.at[s] for t in self.near]
        copies.arrive(R_YALL, s, near, spot.side)
        here = [[m, t, a] for m, t, a in zip(mine, twin, near)]
        if self.use_x:
            across = [t.at[s] for t in self.across]
            copies.arrive(R_XALL, s, across, spot.across)
            here = [h + [a] for h, a in zip(here, across)]
        self.along(j, here, self.line, self.outs if j == self.n_planes - 1 else twin, R_UP, R_DOWN)
        self.start_load(T_OWN, j + 2)

    def stage(self, step):
        self.corner(step)
        self.sides(step - 1)
        self.column(step - 2)

    def close(self):
        self.copies.close()


class WeightGradients:
    width = 256

    def __init__(self, ins, outs, scratch):
        self.sources, (self.hidden, self.shared) = ins[:4], ins[4:]
        self.outs = outs
        self.buffers, self.small_hidden, self.small_shared = scratch[:4], scratch[4], scratch[5]
        self.flat, self.sums, self.load, self.store, self.once = scratch[6:]
        self.n_parts = self.sources[0].shape[1] // self.width

    @staticmethod
    def scratch(rows, tokens, width, shared):
        bf16, f32 = jnp.bfloat16, jnp.float32
        w = WeightGradients.width
        return [
            pltpu.VMEM((2, rows, w), bf16),
            pltpu.VMEM((2, rows, w), bf16),
            pltpu.VMEM((2, tokens, w), bf16),
            pltpu.VMEM((2, tokens, w), bf16),
            pltpu.VMEM((3, rows, width), bf16),
            pltpu.VMEM((tokens, shared), bf16),
            pltpu.VMEM((2, 3, width, w), f32),
            pltpu.VMEM((2, shared, w), bf16),
            pltpu.SemaphoreType.DMA((2, 4)),
            pltpu.SemaphoreType.DMA((2, 4)),
            pltpu.SemaphoreType.DMA((2,)),
        ]

    def span(self, p):
        return pl.ds(p * self.width, self.width)

    def loads(self, p):
        return [
            pltpu.make_async_copy(a.at[:, self.span(p)], b.at[p % 2], self.load.at[p % 2, i])
            for i, (a, b) in enumerate(zip(self.sources, self.buffers))
        ]

    def stores(self, p):
        gate_t, up_t, down, shared = self.outs
        slot, span = p % 2, self.span(p)
        pairs = [
            (self.flat.at[slot, 0], gate_t.at[:, span]),
            (self.flat.at[slot, 1], up_t.at[:, span]),
            (self.flat.at[slot, 2], down.at[:, span]),
            (self.sums.at[slot], shared.at[:, span]),
        ]
        return [pltpu.make_async_copy(a, b, self.store.at[slot, i]) for i, (a, b) in enumerate(pairs)]

    def resident(self):
        return [
            pltpu.make_async_copy(self.hidden, self.small_hidden, self.once.at[0]),
            pltpu.make_async_copy(self.shared, self.small_shared, self.once.at[1]),
        ]

    def begin(self):
        for c in self.resident() + self.loads(0):
            c.start()

    def part(self, p):
        if p >= self.n_parts:
            return
        if p == 0:
            for c in self.resident():
                c.wait()
        if p + 1 < self.n_parts:
            for c in self.loads(p + 1):
                c.start()
        for c in self.loads(p):
            c.wait()
        if p >= 2:
            for c in self.stores(p - 2):
                c.wait()
        slot = p % 2
        rows, grad_rows, tokens, grads = [b.at[slot] for b in self.buffers]

        def across(a, b):
            return lax.dot_general(a, b, (((0,), (0,)), ((), ())), preferred_element_type=jnp.float32)

        self.flat[slot, 0] = across(self.small_hidden[1], rows[...])
        self.flat[slot, 1] = across(self.small_hidden[2], rows[...])
        self.flat[slot, 2] = across(self.small_hidden[0], grad_rows[...])
        n = self.small_shared.shape[1] // 3
        self.sums[slot, pl.ds(0, 2 * n)] = across(self.small_shared[:, n:], tokens[...]).astype(jnp.bfloat16)
        self.sums[slot, pl.ds(2 * n, n)] = across(self.small_shared[:, :n], grads[...]).astype(jnp.bfloat16)
        for c in self.stores(p):
            c.start()

    def end(self):
        for p in (self.n_parts - 2, self.n_parts - 1):
            for c in self.stores(p):
                c.wait()


def sum_kernel(n_planes, n, *refs):
    ins, work_ins, outs, work_outs = refs[:n], refs[n : n + 6], refs[n + 6 : 2 * n + 6], refs[2 * n + 6 : 2 * n + 10]
    scratch = refs[2 * n + 10 :]
    cut = len(scratch) - 11
    spot = Spot(n_planes)
    rows = ins[0].shape[1] // 2

    def blocks(s, yy, cc, xx):
        return [a.at[dp_of(s, yy, cc) * 2 + xx] for a in ins]

    net = Reduce(spot, blocks, outs, scratch[:cut], True, rows)
    work = WeightGradients(work_ins, work_outs, scratch[cut:])
    net.start_loads()
    spot.greet()
    net.start_twins()
    work.begin()
    done = 0
    for step in range(n_planes + 2):
        for action in (net.corner, net.sides, net.column):
            j = step - (net.corner, net.sides, net.column).index(action)
            action(j)
            if 0 <= j < n_planes and done < work.n_parts:
                work.part(done)
                done += 1
    net.close()
    work.end()


def sum_everywhere(arrays, out_dtypes, work_arrays, n_dp, collective_id):
    n, n_planes = len(arrays), n_dp // 4
    shapes = [a.shape[1:] for a in arrays]
    rows, model = work_arrays[0].shape
    tokens = work_arrays[2].shape[0]
    width = work_arrays[4].shape[2]
    shared = work_arrays[5].shape[1]
    return pl.pallas_call(
        functools.partial(sum_kernel, n_planes, n),
        out_shape=[jax.ShapeDtypeStruct(s, t) for s, t in zip(shapes, out_dtypes)]
        + [
            jax.ShapeDtypeStruct((width, model), jnp.float32),
            jax.ShapeDtypeStruct((width, model), jnp.float32),
            jax.ShapeDtypeStruct((width, model), jnp.float32),
            jax.ShapeDtypeStruct((shared, model), jnp.bfloat16),
        ],
        in_specs=[ANY] * (n + 6),
        out_specs=[pl.BlockSpec(memory_space=pltpu.VMEM)] * n + [ANY] * 4,
        scratch_shapes=Reduce.scratch(shapes, [a.dtype for a in arrays], n_planes, True, shapes[0][0] // 2)
        + WeightGradients.scratch(rows, tokens, width, shared),
        compiler_params=pltpu.CompilerParams(
            collective_id=collective_id, has_side_effects=True, vmem_limit_bytes=62 << 20
        ),
    )(*arrays, *work_arrays)


def back_kernel(n_planes, axes, *refs):
    n = len(axes)
    grad_own, *inputs = refs[:18]
    probs, wq, wk, wv, wo, parts = inputs[5], *inputs[6:10], inputs[16]
    inputs = inputs[:5] + inputs[10:16]
    held = refs[-len(inputs) - 1 : -1]
    mixed, normed_one, query, key, value, cosine, sine, tokens, grad_residual, gain, small = held
    held_load = refs[-1]
    outs, grad_tokens, small_out, out_sum = refs[18 : 18 + n], *refs[18 + n : 21 + n]
    (
        grad_attn, grad_mixed, grad_query, grad_key, grad_value, gq, gk, gv, go, some_p, some_o, some_q, some_k,
        some_v, sent, received, terms, from_twin, from_side, from_across, quarter, from_planes, load, x_send, x_recv,
        p_send, p_recv,
    ) = refs[21 + n : 48 + n]
    scratch = refs[48 + n : -len(inputs) - 1]
    spot = Spot(n_planes)
    x = spot.x
    bf16, f32 = jnp.bfloat16, jnp.float32
    own_rows, model = tokens.shape
    grads = (gq, gk, gv, go)

    def weight_blocks(s, yy, cc, xx):
        i = dp_of(s, yy, cc)
        places = []
        for a, o, axis in zip(grads, outs, axes):
            size = o.shape[axis]
            span = pl.ds(pl.multiple_of(i * size, size), size)
            places.append(a.at[span] if axis == 0 else a.at[:, span])
        return places

    def token_blocks(s, yy, cc, xx):
        return [parts.at[dp_of(s, yy, cc) * 2 + xx]]

    count = 3 * n + 3
    weights = Reduce(spot, weight_blocks, outs, scratch[:count], False, direct=True)
    sums = Reduce(spot, token_blocks, [out_sum], scratch[count:], True, own_rows // 2, by_z=True)

    def swap(i, src, dst):
        return pltpu.make_async_remote_copy(
            src_ref=src, dst_ref=dst, send_sem=x_send.at[i], recv_sem=x_recv.at[i],
            device_id=spot.across, device_id_type=MESH,
        )

    def hop(i, src, dst, device):
        return pltpu.make_async_remote_copy(
            src_ref=src, dst_ref=dst, send_sem=p_send.at[i], recv_sem=p_recv.at[i],
            device_id=device, device_id_type=MESH,
        )

    lanes = terms.shape[1]

    def of_core(c):
        return terms.at[:, pl.ds(pl.multiple_of(c * (lanes // 2), lanes // 2), lanes // 2)]

    def of_side(y):
        start = spot.core * (lanes // 2) + y * (lanes // 4)
        return terms.at[:, pl.ds(pl.multiple_of(start, lanes // 4), lanes // 4)]

    def of_plane(s):
        size = lanes // 4 // n_planes
        return quarter.at[:, pl.ds(pl.multiple_of(s * size, size), size)]

    hops = [
        hop(0, of_core(1 - spot.core), from_twin, spot.twin),
        hop(1, of_side(1 - spot.y), from_side, spot.side),
        hop(2, of_side(spot.y), from_across, spot.across),
    ]
    for k in range(1, n_planes):
        s, device = spot.plane(k)
        hops.append(hop(2 + k, of_plane(s), from_planes.at[k - 1], device))

    def small_step(i):
        if i > 0:
            for h in hops[i - 1 : i] if i < 4 else hops[3:]:
                h.wait_recv()
        if i == 1:
            mine = of_core(spot.core)
            mine[...] = mine[...] + from_twin[...]
        if i == 2:
            mine = of_side(spot.y)
            mine[...] = mine[...] + from_side[...]
        if i == 3:
            quarter[...] = of_side(spot.y)[...] + from_across[...]
        if i == 4:
            total = of_plane(spot.z)[...]
            for k in range(n_planes - 1):
                total = total + from_planes[k]
            small_out[...] = total
            return
        for h in hops[i : i + 1] if i < 3 else hops[3:]:
            h.start()

    own = pltpu.make_async_copy(grad_own, grad_attn.at[x], load.at[4, 0])
    own.start()
    sums.start_loads()
    spot.greet(True)
    swap(0, grad_own, grad_attn.at[x]).start()
    sums.start_twins()
    fetched = [pltpu.make_async_copy(a, b, held_load.at[i]) for i, (a, b) in enumerate(zip(inputs, held))]
    for c in fetched:
        c.start()

    heads, head_dim = probs.shape[0], cosine.shape[1]
    kv_heads = key.shape[1] // head_dim
    group = heads // kv_heads
    chunk = some_o.shape[1]
    n_chunks = wo.shape[0] // chunk
    per_chunk = chunk // head_dim

    def load_o(c):
        return pltpu.make_async_copy(wo.at[pl.ds(c * chunk, chunk)], some_o.at[c % 2], load.at[0, c % 2])

    def load_p(h):
        return pltpu.make_async_copy(probs.at[h], some_p.at[h % 2], load.at[1, h % 2])

    load_o(0).start()
    load_p(0).start()
    sums.corner(0)
    for j in range(n_planes - 1):
        sums.sides(j)
    for c in fetched:
        c.wait()
    terms[...] = small[...]
    own.wait()
    swap(0, grad_attn.at[1 - x], grad_attn.at[1 - x]).wait_recv()
    whole = grad_attn[...].reshape(2 * own_rows, model)
    sums.corner(1)
    cos, sin = cosine[...], -sine[...]
    scale = head_dim ** -0.5
    for c in range(n_chunks):
        if c + 1 < n_chunks:
            load_o(c + 1).start()
        load_o(c).wait()
        span = slice(c * chunk, (c + 1) * chunk)
        grad_mixed[:, span] = plain_dot(whole, some_o[c % 2], ROWS_ROWS).astype(bf16)
        go[span, :] = plain_dot(mixed[:, span], whole, COLUMNS_COLUMNS).astype(bf16)
    sums.corner(2)
    for h in range(heads):
        if h + 1 < heads:
            load_p(h + 1).start()
        load_p(h).wait()
        span = slice(h * head_dim, (h + 1) * head_dim)
        shared = slice(h // group * head_dim, (h // group + 1) * head_dim)
        weight, back = some_p[h % 2], grad_mixed[:, span]
        grad_v = plain_dot(weight.astype(bf16), back, COLUMNS_COLUMNS)
        grad_p = plain_dot(back, value[:, shared], ROWS_ROWS)
        inner = jnp.sum(weight * grad_p, axis=1, keepdims=True)
        grad_s = (weight * (grad_p - inner)).astype(bf16)
        grad_q = plain_dot(grad_s, key[:, shared], ROWS_COLUMNS) * scale
        grad_query[:, span] = turn(grad_q, cos, sin).astype(bf16)
        grad_k = plain_dot(grad_s, query[:, span], COLUMNS_COLUMNS) * scale
        if h % group == 0:
            total_k, total_v = grad_k, grad_v
        else:
            total_k, total_v = total_k + grad_k, total_v + grad_v
        if h % group == group - 1:
            grad_key[:, shared] = turn(total_k, cos, sin).astype(bf16)
            grad_value[:, shared] = total_v.astype(bf16)
    sums.corner(3)
    for target, source in ((gk, grad_key), (gv, grad_value), (gq, grad_query)):
        target[...] = plain_dot(normed_one[...], source[...], COLUMNS_COLUMNS).astype(bf16)
    weights.start_twins()

    rows = some_q.shape[1]
    n_chunks = model // rows

    def load_w(c):
        span = pl.ds(c * rows, rows)
        return [
            pltpu.make_async_copy(w.at[span], b.at[c % 2], load.at[i, c % 2])
            for i, (w, b) in ((0, (wq, some_q)), (2, (wk, some_k)), (3, (wv, some_v)))
        ]

    for c in load_w(0):
        c.start()
    sums.column(0)
    sums.sides(3)
    weights.sides(0)
    other = pl.ds(pl.multiple_of((1 - x) * own_rows, own_rows), own_rows)
    mine = pl.ds(pl.multiple_of(x * own_rows, own_rows), own_rows)
    for c in range(n_chunks):
        if c + 1 < n_chunks:
            for each in load_w(c + 1):
                each.start()
        for each in load_w(c):
            each.wait()
        columns = slice(c * rows, (c + 1) * rows)
        for here, target in ((other, sent), (mine, grad_tokens)):
            total = plain_dot(grad_query[here, :], some_q[c % 2], ROWS_ROWS)
            total = total + plain_dot(grad_key[here, :], some_k[c % 2], ROWS_ROWS)
            total = total + plain_dot(grad_value[here, :], some_v[c % 2], ROWS_ROWS)
            target[:, columns] = total.astype(target.dtype)
    swap(1, sent, received).start()
    sums.column(1)
    weights.sides(1)
    sums.column(2)
    swap(1, received, received).wait_recv()
    step = 32
    gain_row = gain[...].astype(f32)
    total = jnp.zeros((1, model), f32)
    for r in range(own_rows // step):
        span = pl.ds(r * step, step)
        rows_in = tokens[span, :].astype(f32)
        grad = grad_tokens[span, :] + received[span, :].astype(f32)
        size = lax.rsqrt(jnp.mean(rows_in * rows_in, axis=1, keepdims=True) + norm_eps)
        weighted = grad * gain_row
        inner = jnp.mean(rows_in * weighted, axis=1, keepdims=True)
        total = total + jnp.sum(grad * rows_in * size, axis=0, keepdims=True)
        grad_tokens[span, :] = size * weighted - rows_in * (size * size * size) * inner + grad_residual[span, :]
    place = small.shape[0] - 8
    size = lanes // 4 // n_planes
    for i in range(4 * n_planes):
        at = (i % 2 * 2 + i // 2 % 2) * n_planes + i // 4
        terms[pl.ds(place, 1), pl.ds(at * size, size)] = total[:, i * size : (i + 1) * size]
    small_step(0)
    weights.column(0)
    small_step(1)
    weights.sides(2)
    small_step(2)
    weights.column(1)
    small_step(3)
    weights.sides(3)
    sums.column(3)
    weights.column(2)
    small_step(4)
    weights.column(3)
    for h in hops:
        h.wait_send()
    swap(0, grad_own, grad_attn.at[x]).wait_send()
    swap(1, sent, received).wait_send()
    for each in (weights, sums):
        each.close()


def backward(
    grad_own, mixed, normed_one, query, key, value, probs, weights, axes, cosine, sine, tokens, grad_residual, gain,
    small, parts, n_dp, collective_id,
):
    n, n_planes = len(weights), n_dp // 4
    bf16, f32 = jnp.bfloat16, jnp.float32
    shape, vmem_ref = jax.ShapeDtypeStruct, pltpu.VMEM
    own_rows, model = tokens.shape
    seq = 2 * own_rows
    wide, narrow_ = query.shape[1], key.shape[1]

    def part(a, axis):
        some = list(a.shape)
        some[axis] //= n_dp
        return tuple(some)

    shapes = [part(a, axis) for a, axis in zip(weights, axes)]
    tile = (small.shape[0], model // n_dp)
    block = parts.shape[1:]
    vmem = pl.BlockSpec(memory_space=pltpu.VMEM)
    dma = pltpu.SemaphoreType.DMA
    chunk = 256
    return pl.pallas_call(
        functools.partial(back_kernel, n_planes, axes),
        out_shape=[shape(s, f32) for s in shapes] + [shape((own_rows, model), f32), shape(tile, f32), shape(block, f32)],
        in_specs=[ANY] * 18,
        out_specs=[vmem] * (n + 3),
        scratch_shapes=[
            vmem_ref((2, own_rows, model), bf16),
            vmem_ref((seq, wide), bf16),
            vmem_ref((seq, wide), bf16),
            vmem_ref((seq, narrow_), bf16),
            vmem_ref((seq, narrow_), bf16),
        ]
        + [vmem_ref(w.shape, bf16) for w in weights]
        + [
            vmem_ref((2,) + probs.shape[1:], f32),
            vmem_ref((2, chunk, model), bf16),
            vmem_ref((2, chunk, wide), bf16),
            vmem_ref((2, chunk, narrow_), bf16),
            vmem_ref((2, chunk, narrow_), bf16),
            vmem_ref((own_rows, model), bf16),
            vmem_ref((own_rows, model), bf16),
            vmem_ref(small.shape, f32),
            vmem_ref((small.shape[0], model // 2), f32),
            vmem_ref((small.shape[0], model // 4), f32),
            vmem_ref((small.shape[0], model // 4), f32),
            vmem_ref((small.shape[0], model // 4), f32),
            vmem_ref((n_planes - 1,) + tile, f32),
            dma((5, 2)),
            dma((3,)),
            dma((3,)),
            dma((2 + n_planes,)),
            dma((2 + n_planes,)),
        ]
        + Reduce.scratch(shapes, [bf16] * n, n_planes, False, direct=True)
        + Reduce.scratch([block], [parts.dtype], n_planes, True, block[0] // 2, by_z=True)
        + [
            vmem_ref(a.shape, a.dtype)
            for a in (mixed, normed_one, query, key, value, cosine, sine, tokens, grad_residual, gain, small)
        ]
        + [dma((11,))],
        compiler_params=pltpu.CompilerParams(
            collective_id=collective_id, has_side_effects=True, vmem_limit_bytes=63 << 20
        ),
        cost_estimate=pl.CostEstimate(
            flops=12 * seq * model * wide, bytes_accessed=16 * n_dp * own_rows * model, transcendentals=0
        ),
    )(
        grad_own, mixed, normed_one, query, key, value, probs, *weights, cosine, sine, tokens, grad_residual, gain,
        small, parts,
    )
UNIT = 2


def dot_t(a, b):
    return lax.dot_general(a, b, (((1,), (1,)), ((), ())), preferred_element_type=jnp.float32)


def dot_f32(a, b):
    return lax.dot_general(a, b, (((1,), (0,)), ((), ())), preferred_element_type=jnp.float32)


class ExpertWork:
    def __init__(self, expert, weights, scratch):
        self.expert = expert
        self.w_gate, self.w_up, self.w_down, self.shared = weights
        (
            self.tokens, self.grads, self.rows, self.grad_rows, self.hidden, self.pre, self.left_out,
            self.left_grad, self.right_out, self.right_grad, self.out, self.back, self.shared_hidden,
        ) = scratch

    @staticmethod
    def scratch(model, width, capacity, own_rows):
        bf16 = jnp.bfloat16
        seq = 2 * own_rows
        return [
            pltpu.VMEM((2, 2 * UNIT, own_rows, model), bf16),
            pltpu.VMEM((2, 2 * UNIT, own_rows, model), bf16),
            pltpu.VMEM((2, UNIT * capacity, model), bf16),
            pltpu.VMEM((2, UNIT * capacity, model), bf16),
            pltpu.VMEM((2, 3, UNIT * capacity, width), bf16),
            pltpu.VMEM((3, UNIT * capacity, width), jnp.float32),
            pltpu.VMEM((UNIT, seq, capacity + 128), bf16),
            pltpu.VMEM((UNIT, seq, capacity + 256), bf16),
            pltpu.VMEM((UNIT, capacity + 128, model), bf16),
            pltpu.VMEM((UNIT, capacity + 256, model), bf16),
            pltpu.VMEM((2, 2 * UNIT, own_rows, model), bf16),
            pltpu.VMEM((2, 2 * UNIT, own_rows, model), bf16),
            pltpu.VMEM((2, UNIT * seq, 384), bf16),
        ]

    def prepare(self):
        capacity = self.rows.shape[1] // UNIT
        for q in range(UNIT):
            self.right_out[q, pl.ds(capacity, 128), :] = self.shared[pl.ds(256, 128), :]
            self.right_grad[q, pl.ds(capacity, 256), :] = self.shared[pl.ds(0, 256), :]

    def run(self, slot, unit, gates, grad_gates, hook):
        bf16, f32 = jnp.bfloat16, jnp.float32
        own_rows, model = self.tokens.shape[2:]
        seq = 2 * own_rows
        capacity = self.rows.shape[1] // UNIT
        experts = gates.shape[1]
        column = 1024
        n_columns = model // column
        first = unit * (2 * UNIT)
        before = lax.broadcasted_iota(jnp.int32, (seq, seq), 0) <= lax.broadcasted_iota(jnp.int32, (seq, seq), 1)
        before = before.astype(f32).astype(bf16)
        slots = lax.broadcasted_iota(jnp.int32, (capacity, seq), 0)
        picks, row_gates = [], []
        for q in range(UNIT):
            g = jnp.concatenate(
                [gates[first + 2 * q + h, pl.ds(self.expert, 1), :] for h in range(2)], axis=1
            )
            g = jnp.broadcast_to(g, (8, seq))
            taken = (g > 0.0).astype(f32)
            rank = dot_f32(taken.astype(bf16), before).astype(jnp.int32) - 1
            hit = (slots == rank[:1]) & (g[:1] > 0.0)
            pick = hit.astype(f32)
            picks.append(pick)
            row_gates.append(jnp.sum(pick * g[:1], axis=1, keepdims=True))
            self.left_out[q, :, pl.ds(0, capacity)] = pick.T.astype(bf16)
            self.left_grad[q, :, pl.ds(0, capacity)] = pick.T.astype(bf16)
            low = pick.astype(bf16)

            span = pl.ds(q * capacity, capacity)
            for source, target in ((self.tokens, self.rows), (self.grads, self.grad_rows)):
                whole = source[slot, pl.ds(2 * q, 2)].reshape(seq, model)
                target[slot, span] = dot_f32(low, whole).astype(bf16)
        row_gate = jnp.concatenate(row_gates, axis=0)
        rows, grad_rows = self.rows.at[slot], self.grad_rows.at[slot]
        self.pre[0] = dot_t(rows[...], self.w_gate[...])
        self.pre[1] = dot_t(rows[...], self.w_up[...])
        self.pre[2] = dot_t(grad_rows[...], self.w_down[...])
        hook(2)
        step = 32
        parts = []
        for r in range(UNIT * capacity // step):
            span = pl.ds(r * step, step)
            gate_pre, up_pre, grad_hidden = self.pre[0, span], self.pre[1, span], self.pre[2, span]
            gate = row_gate[r * step : (r + 1) * step]
            sig = jax.nn.sigmoid(gate_pre)
            act = gate_pre * sig
            hidden = act * up_pre
            parts.append(jnp.sum(hidden * grad_hidden, axis=1, keepdims=True))
            grad_hidden = grad_hidden * gate
            self.hidden[slot, 0, span] = (hidden * gate).astype(bf16)
            slope = sig * (1.0 + gate_pre * (1.0 - sig))
            self.hidden[slot, 1, span] = (grad_hidden * up_pre * slope).astype(bf16)
            self.hidden[slot, 2, span] = (grad_hidden * act).astype(bf16)
        grad_gate_rows = jnp.concatenate(parts, axis=0)
        mine = lax.broadcasted_iota(jnp.int32, (experts, own_rows), 0) == self.expert
        for q in range(UNIT):
            per_token = jnp.sum(picks[q] * grad_gate_rows[q * capacity : (q + 1) * capacity], axis=0, keepdims=True)
            for h in range(2):
                part = jnp.broadcast_to(per_token[:, h * own_rows : (h + 1) * own_rows], (experts, own_rows))
                grad_gates[first + 2 * q + h] = jnp.where(mine, part, 0.0)

        for q in range(UNIT):
            blocks = pl.ds(2 * q, 2)
            whole = self.tokens[slot, blocks].reshape(seq, model)
            grad = self.grads[slot, blocks].reshape(seq, model)
            pre = dot_t(whole, self.shared[pl.ds(0, 256), :])
            grad_hidden = dot_t(grad, self.shared[pl.ds(256, 128), :])
            gate_pre, up_pre = pre[:, :128], pre[:, 128:]
            sig = jax.nn.sigmoid(gate_pre)
            act = gate_pre * sig
            hidden = (act * up_pre).astype(bf16)
            grad_gate = (grad_hidden * up_pre * sig * (1.0 + gate_pre * (1.0 - sig))).astype(bf16)
            grad_up = (grad_hidden * act).astype(bf16)
            span = pl.ds(q * seq, seq)
            self.shared_hidden[slot, span, pl.ds(0, 128)] = hidden
            self.shared_hidden[slot, span, pl.ds(128, 128)] = grad_gate
            self.shared_hidden[slot, span, pl.ds(256, 128)] = grad_up
            self.left_out[q, :, pl.ds(capacity, 128)] = hidden
            self.left_grad[q, :, pl.ds(capacity, 128)] = grad_gate
            self.left_grad[q, :, pl.ds(capacity + 128, 128)] = grad_up

        hook(3)

        def combine(c, carry):
            cols = pl.ds(pl.multiple_of(c * column, column), column)
            made = dot_f32(self.hidden[slot, 0], self.w_down[:, cols]).astype(bf16)
            back = dot_f32(self.hidden[slot, 1], self.w_gate[:, cols])
            back = (back + dot_f32(self.hidden[slot, 2], self.w_up[:, cols])).astype(bf16)
            for q in range(UNIT):
                span = slice(q * capacity, (q + 1) * capacity)
                self.right_out[q, pl.ds(0, capacity), cols] = made[span]
                self.right_grad[q, pl.ds(0, capacity), cols] = back[span]
                out = dot_f32(self.left_out[q], self.right_out[q, :, cols]).astype(bf16)
                self.out[slot, pl.ds(2 * q, 2), :, cols] = out.reshape(2, own_rows, column)
                out = dot_f32(self.left_grad[q], self.right_grad[q, :, cols]).astype(bf16)
                self.back[slot, pl.ds(2 * q, 2), :, cols] = out.reshape(2, own_rows, column)

            return carry

        lax.fori_loop(0, n_columns, combine, 0)


def expert_kernel(n_dp, *refs):
    own, own_gates, _, *weights_in = refs[:7]
    normed, grads, out_parts, back_parts, grad_gates, rows_out, grad_rows_out, hidden_out, shared_out = refs[7:16]
    scratch, weights = refs[16:-13], refs[-13:-9]
    fetch, gates, load, store, local, send, recv, g_send, g_recv = refs[-9:]
    n_planes = n_dp // 4
    spot = Spot(n_planes)
    half = own.shape[0] // 2

    def views(s, yy, cc, xx, part):
        b = dp_of(s, yy, cc) * 2 + xx
        if part == ALL:
            return [normed.at[b], gates.at[b]]
        if part == FIRST:
            return [normed.at[b, pl.ds(0, half)], gates.at[b]]
        return [normed.at[b, pl.ds(half, half)]]

    def grad_views(s, yy, cc, xx, part):
        b = dp_of(s, yy, cc) * 2 + xx
        if part == ALL:
            return [grads.at[b]]
        some = own.shape[0] // 2
        if part == FIRST:
            return [grads.at[b, pl.ds(0, some)]]
        return [grads.at[b, pl.ds(some, own.shape[0] - some)]]

    kept = [
        pltpu.make_async_copy(a, v, local.at[i])
        for i, (a, v) in enumerate(zip((own, own_gates), views(spot.z, spot.y, spot.core, spot.x, ALL)))
    ]
    for c in kept:
        c.start()
    pieces = 4
    fetched = []
    for k, (a, b) in enumerate(zip(weights_in, weights)):
        size = a.shape[0] // pieces
        for p in range(pieces):
            span = pl.ds(p * size, size)
            fetched.append(pltpu.make_async_copy(a.at[span], b.at[span], fetch.at[k, p]))
    for c in fetched:
        c.start()
    spot.greet()
    copies = Copies(n_planes, send, recv)
    net = Spread(spot, copies, [own, own_gates], views, True, by_z=True)
    rest = Spread(spot, Copies(n_planes, g_send, g_recv), None, grad_views, True)
    net.begin()
    work = ExpertWork(spot.dp, weights, scratch)
    n_units = n_dp // UNIT
    blocks = 2 * UNIT
    rows = work.rows.shape[1]
    seqs = work.shared_hidden.shape[1]
    order = net.order

    def unit_of(i):
        s = 0 * i
        for j, plane in enumerate(order):
            s = s + (i // 2 == j).astype(jnp.int32) * plane
        yy = spot.y + (i % 2) * (1 - 2 * spot.y)
        return s * 2 + yy

    def loads(u, slot):
        span = pl.ds(u * blocks, blocks)
        return [
            pltpu.make_async_copy(normed.at[span], work.tokens.at[slot], load.at[slot, 0]),
            pltpu.make_async_copy(grads.at[span], work.grads.at[slot], load.at[slot, 1]),
        ]

    def stores(u, slot):
        span = pl.ds(u * blocks, blocks)
        some = pl.ds(pl.multiple_of(u * rows, rows), rows)
        pairs = [
            (work.out.at[slot], out_parts.at[span]),
            (work.back.at[slot], back_parts.at[span]),
            (work.rows.at[slot], rows_out.at[some]),
            (work.grad_rows.at[slot], grad_rows_out.at[some]),
            (work.hidden.at[slot], hidden_out.at[:, some]),
            (work.shared_hidden.at[slot], shared_out.at[pl.ds(pl.multiple_of(u * seqs, seqs), seqs)]),
        ]
        return [pltpu.make_async_copy(a, b, store.at[slot, i]) for i, (a, b) in enumerate(pairs)]

    def load_unit(i):
        for c in loads(unit_of(jnp.int32(i)), i % 2):
            c.start()

    def near(j):
        net.twin_near(j)
        if j >= n_planes - 2:
            rest.twin_across(j)
        load_unit(2 * j)

    def far(j):
        net.twin_far(j)
        rest.twin_corner(j)
        if j >= n_planes - 2:
            rest.twin_side(j)
        load_unit(2 * j + 1)

    def over(j):
        if j >= n_planes - 2:
            rest.from_side(j)
            rest.from_across(j)
        rest.over_x(j)
        rest.over_y(j)

    plan = {
        (0, 0): [(net.onward, 1)],
        (0, 2): [(net.corner, 0), (rest.corner, 0), (far, 0), (over, 1), (rest.onward_x, 2)],
        (0, 3): [(net.relay_of, 2, 0), (net.relay_of, 3, 1), (rest.onward_y, 2)],
        (1, 0): [(net.sides, 1), (net.onward, 2), (rest.onward_x, 3)],
        (1, 2): [(near, 1)],
        (1, 3): [(net.corner, 1), (net.corner_of, 2, 1), (rest.corner, 1)],
        (2, 0): [(far, 1), (over, 2), (rest.onward_y, 3)],
        (2, 3): [(net.sides, 2), (net.relay_of, 3, 0), (net.onward, 3), (net.corner_of, 3, 1)],
        (3, 0): [(near, 2)],
        (3, 2): [(net.corner_of, 2, 0), (rest.corner, 2), (over, 3)],
        (4, 0): [(net.sides, 3), (far, 2)],
        (4, 3): [(net.corner_of, 3, 0), (rest.corner, 3)],
        (5, 0): [(near, 3)],
        (6, 0): [(far, 3)],
    }

    net.relay(1)
    net.relay_of(2, 1)
    net.sides(0)
    over(0)
    for c in kept:
        c.wait()
    near(0)
    for c in fetched:
        c.wait()
    work.prepare()

    def body(i, carry):
        slot = i % 2
        u = unit_of(i)

        def hook(point):
            for (k, at), actions in plan.items():
                if at == point:

                    @pl.when(i == k)
                    def _(actions=actions):
                        for action, *values in actions:
                            action(*values)

        hook(0)

        for c in loads(u, slot):
            c.wait()

        @pl.when(i >= 2)
        def _():
            for c in stores(unit_of(i - 2), slot):
                c.wait()

        work.run(slot, u, gates, grad_gates, hook)
        for c in stores(u, slot):
            c.start()
        return carry

    lax.fori_loop(0, n_units, body, 0)
    for i in (n_units - 2, n_units - 1):
        for c in stores(unit_of(jnp.int32(i)), i % 2):
            c.wait()
    copies.close()
    rest.copies.close()


def expert_call(own, own_gates, grads, w_gate, w_up, w_down, shared, n_dp, capacity, collective_id):
    own_rows, model = own.shape
    blocks = 2 * n_dp
    width = w_down.shape[0]
    bf16 = jnp.bfloat16
    rows = n_dp * capacity
    n_planes = n_dp // 4
    vmem = pl.BlockSpec(memory_space=pltpu.VMEM)
    everyone = jax.ShapeDtypeStruct((blocks, own_rows, model), bf16)
    all_gates = (blocks,) + own_gates.shape
    return pl.pallas_call(
        functools.partial(expert_kernel, n_dp),
        out_shape=[
            everyone,
            everyone,
            everyone,
            everyone,
            jax.ShapeDtypeStruct(all_gates, jnp.float32),
            jax.ShapeDtypeStruct((rows, model), bf16),
            jax.ShapeDtypeStruct((rows, model), bf16),
            jax.ShapeDtypeStruct((3, rows, width), bf16),
            jax.ShapeDtypeStruct((blocks * own_rows, 384), bf16),
        ],
        in_specs=[ANY] * 7,
        out_specs=[ANY, ANY, ANY, ANY, vmem, ANY, ANY, ANY, ANY],
        input_output_aliases={2: 1},
        scratch_shapes=ExpertWork.scratch(model, width, capacity, own_rows)
        + [pltpu.VMEM(w.shape, bf16) for w in (w_gate, w_up, w_down, shared)]
        + [
            pltpu.SemaphoreType.DMA((4, 4)),
            pltpu.VMEM(all_gates, jnp.float32),
            pltpu.SemaphoreType.DMA((2, 2)),
            pltpu.SemaphoreType.DMA((2, 6)),
            pltpu.SemaphoreType.DMA((2,)),
            pltpu.SemaphoreType.DMA((14 * n_planes, 2)),
            pltpu.SemaphoreType.DMA((14 * n_planes, 2)),
            pltpu.SemaphoreType.DMA((14 * n_planes, 1)),
            pltpu.SemaphoreType.DMA((14 * n_planes, 1)),
        ],
        compiler_params=pltpu.CompilerParams(
            collective_id=collective_id, has_side_effects=True, vmem_limit_bytes=60 << 20
        ),
    )(own, own_gates, grads, w_gate, w_up, w_down, shared)


def gather_plan(
    tokens,
    attention_gain,
    expert_norm_gain,
    query_projection,
    key_projection,
    value_projection,
    output_projection,
    router,
    shared_gate_matrix,
    shared_up_matrix,
    shared_down_matrix,
    expert_gate_matrix,
    expert_up_matrix,
    expert_down_matrix,
    document_lengths,
    expert_indices,
    cotangent,
):
    n_dp = lax.axis_size(DP)
    x = lax.axis_index(TENSOR)
    dp = lax.axis_index(DP)
    own_rows, model_dim = tokens.shape
    sequence_length = own_rows * 2
    experts = n_dp
    top_k = expert_indices.shape[1]
    capacity = sequence_length * top_k * 4 // (3 * experts)
    bf16, f32 = jnp.bfloat16, jnp.float32

    def dot(a, b):
        return jnp.dot(a, b, preferred_element_type=f32)

    width = attention_gain.shape[0]
    lanes = 2 * width
    tile = jnp.concatenate(
        [router.T, attention_gain[None], expert_norm_gain[None], jnp.zeros((-(experts + 2) % 16, width), bf16)]
    )
    tile = lax.dynamic_update_slice(jnp.zeros((tile.shape[0], lanes), bf16), tile, (0, x * width))
    rotary_cosine, rotary_sine = rotation(sequence_length, HEAD_SIZE)
    cosine = jnp.concatenate([rotary_cosine, rotary_cosine], axis=1)
    sine = jnp.concatenate([-rotary_sine, rotary_sine], axis=1)
    doc_ends = jnp.cumsum(document_lengths[0])
    positions = jnp.arange(sequence_length, dtype=jnp.int32)
    doc_ids = jnp.sum((positions[:, None] >= doc_ends[None, :]).astype(jnp.int32), axis=-1)
    allowed = (doc_ids[:, None] == doc_ids[None, :]) & (positions[:, None] >= positions[None, :])
    own_indices = lax.dynamic_slice_in_dim(expert_indices, x * own_rows, own_rows, 0)
    chosen = jnp.any(own_indices[None] == jnp.arange(experts, dtype=jnp.int32)[:, None, None], axis=2)
    axes = (0, 0, 0, 1)
    (
        query_all, key_all, value_all, out_all, cotangent_all, params, full_one, rows_of_query, key_rows,
        rows_of_value, attn_probs, mixed_heads, residual, normed_two, gates_t,
    ) = front(
        [query_projection, key_projection, value_projection, output_projection],
        axes, tokens, tile, cotangent, chosen.astype(f32), cosine, sine, allowed.astype(f32), n_dp, 1,
    )
    router_full = params[:experts]
    first_gain = params[experts].astype(f32)
    second_gain = params[experts + 1].astype(f32)

    hidden = shared_gate_matrix.shape[1] // n_dp
    hidden_pad = -(-hidden // 16) * 16

    def slices(transposed):
        blocks = transposed.reshape(n_dp, hidden, -1)
        return jnp.pad(blocks, ((0, 0), (0, hidden_pad - hidden), (0, 0)))

    shared_out = jnp.stack(
        [slices(shared_gate_matrix.T), slices(shared_up_matrix.T), slices(shared_down_matrix)], axis=1
    )
    shared_in = lax.all_to_all(shared_out, DP, split_axis=0, concat_axis=0, tiled=True)
    shared_rows = jnp.moveaxis(shared_in, 0, 2).reshape(3, hidden_pad, model_dim)

    shared_rows = jnp.pad(shared_rows, ((0, 0), (0, 128 - hidden_pad), (0, 0))).reshape(384, model_dim)
    (
        normed_all, cotangent_all, output_parts, normed_parts, grad_gate_parts, received, grad_rows, hidden_rows,
        shared_hidden,
    ) = (
        expert_call(
            normed_two, gates_t, cotangent_all, expert_gate_matrix[0].T, expert_up_matrix[0].T, expert_down_matrix[0],
            shared_rows, n_dp, capacity, 2,
        )
    )
    (
        grad_normed_two, grad_gates_t, expert_gate_gradient, expert_up_gradient, expert_down_gradient, shared_grads,
    ) = sum_everywhere(
        [normed_parts, grad_gate_parts],
        [f32, f32],
        [
            received, grad_rows, normed_all.reshape(-1, model_dim), cotangent_all.reshape(-1, model_dim),
            hidden_rows, shared_hidden,
        ],
        n_dp, 4,
    )
    shared_grads = shared_grads.reshape(3, 128, model_dim)[:, :hidden_pad]

    gates = gates_t.T
    scale_two = lax.rsqrt(jnp.mean(residual * residual, axis=-1, keepdims=True) + norm_eps)
    grad_gates = grad_gates_t.T
    grad_logits = (
        gates * (grad_gates - jnp.sum(gates * grad_gates, axis=-1, keepdims=True))
    ).astype(bf16)
    grad_normed_two = grad_normed_two + dot(grad_logits, router_full)
    grad_router_part = dot(normed_two.T, grad_logits)
    grad_residual, grad_gain_two = rms_back(grad_normed_two, residual, scale_two, second_gain)
    grad_residual = grad_residual + cotangent.astype(f32)
    small_grads = jnp.concatenate([grad_router_part.T, jnp.zeros((8, model_dim), f32).at[1].set(grad_gain_two)])
    by_place = small_grads.reshape(-1, n_dp // 4, 2, 2, 2 * width).transpose(0, 3, 2, 1, 4)
    small_grads = by_place.reshape(small_grads.shape)
    *weight_grads, grad_inputs, small_sums, ffn_own = backward(
        grad_residual.astype(bf16), mixed_heads, full_one, rows_of_query, key_rows, rows_of_value, attn_probs,
        [query_all, key_all, value_all, out_all], axes, cosine, sine, tokens, grad_residual, first_gain[None],
        small_grads, output_parts, n_dp, 6,
    )
    output = (residual + ffn_own).astype(bf16)
    mine = lax.dynamic_slice_in_dim(small_sums, x * width, width, 1)
    gain_one_own, gain_two_own, router_own = mine[experts], mine[experts + 1], mine[:experts].T
    returned = lax.all_to_all(
        shared_grads.reshape(3, hidden_pad, n_dp, -1).transpose(2, 0, 1, 3),
        DP, split_axis=0, concat_axis=0, tiled=True,
    )[:, :, :hidden]
    returned = returned.transpose(1, 0, 2, 3).reshape(3, n_dp * hidden, -1).astype(f32)
    return (
        output,
        grad_inputs,
        gain_one_own,
        gain_two_own,
        *weight_grads,
        router_own,
        returned[0].T,
        returned[1].T,
        returned[2],
        expert_gate_gradient.T[None],
        expert_up_gradient.T[None],
        expert_down_gradient[None],
    )


def shards(*arguments):
    tokens, expert_gate_matrix = arguments[0], arguments[11]
    n_dp, n_tensor = lax.axis_size(DP), lax.axis_size(TENSOR)
    gathered = n_dp * n_tensor * tokens.shape[0] * tokens.shape[1] * 2
    if n_tensor == 2 and n_dp % 4 == 0 and expert_gate_matrix.shape[0] == 1 and gathered <= 32 << 20:
        return gather_plan(*arguments)
    return exchange_plan(*arguments)


def solution(mesh):
    placed = (
        P((DP, TENSOR), None),
        P((DP, TENSOR)),
        P((DP, TENSOR)),
        P(DP, TENSOR),
        P(DP, TENSOR),
        P(DP, TENSOR),
        P(TENSOR, DP),
        P((DP, TENSOR), None),
        P(DP, TENSOR),
        P(DP, TENSOR),
        P(TENSOR, DP),
        P(DP, None, TENSOR),
        P(DP, None, TENSOR),
        P(DP, TENSOR, None),
        P(DP, None),
        P(DP, None),
        P((DP, TENSOR), None),
    )
    return jax.shard_map(
        shards,
        mesh=mesh,
        in_specs=placed,
        out_specs=(
            P((DP, TENSOR), None),
            P((DP, TENSOR), None),
            P((DP, TENSOR)),
            P((DP, TENSOR)),
            P(DP, TENSOR),
            P(DP, TENSOR),
            P(DP, TENSOR),
            P(TENSOR, DP),
            P((DP, TENSOR), None),
            P(DP, TENSOR),
            P(DP, TENSOR),
            P(TENSOR, DP),
            P(DP, None, TENSOR),
            P(DP, None, TENSOR),
            P(DP, TENSOR, None),
        ),
        check_vma=False,
    )
```
